32 devices in a mesh: narrow: 4 (over x, core), wide: 8 (over z, y).
Axes of the slice: x: 2, y: 2, z: 4, core: 2. Of those that a mesh axis runs over, the one named last changes fastest.
Arguments:
- images: bfloat16 [16, 788, 768], P('wide', 'narrow'), may hold values from -6 to 6
- cotangent: bfloat16 [16, 788, 768], P('wide', 'narrow'), may hold values from -6 to 6
- image_ids: int32 [16, 788], P('wide'), may hold values from 0 to 5, never falling along the last dimension, each value on 1 to 197 neighbouring positions
- patch_order: int32 [16, 6, 196], P('wide'), may hold values from 0 to 195, each once within a row
- qkv_weight: bfloat16 [4, 768, 2304], P('narrow'), may hold values from -0.21875 to 0.21875
- qv_bias: float32 [4, 2, 768], P('narrow'), may hold values from -3 to 3
- proj_weight: bfloat16 [4, 768, 768], P('narrow'), may hold values from -0.875 to 0.875
- rel_table: float32 [4, 732, 12], P('narrow'), may hold values from -4 to 4
- layer_scales: float32 [4, 2, 768], P('narrow'), may hold values from 0.3 to 1.5
- layer_norm_gains: float32 [4, 2, 768], P('narrow'), may hold values from 0.5 to 1.5
- norm_biases: float32 [4, 2, 768], P('narrow'), may hold values from -1 to 1
- fc1_weight: bfloat16 [4, 768, 3072], P('narrow'), may hold values from -0.21875 to 0.21875
- fc1_bias: float32 [4, 3072], P('narrow'), may hold values from -3 to 3
- fc2_weight: bfloat16 [4, 3072, 768], P('narrow'), may hold values from -0.109375 to 0.109375
- out_biases: float32 [4, 2, 768], P('narrow'), may hold values from -3 to 3
Outputs:
- encoded: bfloat16 [16, 788, 768], P('wide', 'narrow')
- images_grad: bfloat16 [16, 788, 768], P('wide', 'narrow')
- qkv_grad: float32 [4, 768, 2304], P('narrow', 'wide')
- qv_bias_grad: float32 [4, 2, 768], P('narrow')
- proj_grad: float32 [4, 768, 768], P('narrow', 'wide')
- rel_table_grad: float32 [4, 732, 12], P('narrow')
- layer_scales_grad: float32 [4, 2, 768], P('narrow')
- norm_gains_grad: float32 [4, 2, 768], P('narrow')
- norm_biases_grad: float32 [4, 2, 768], P('narrow')
- fc1_grad: float32 [4, 768, 3072], P('narrow', 'wide')
- fc1_bias_grad: float32 [4, 3072], P('narrow')
- fc2_grad: float32 [4, 3072, 768], P('narrow', 'wide')
- out_biases_grad: float32 [4, 2, 768], P('narrow')
The draws below stay inside these ranges and needn't reach their ends.
Inputs may be any that keep to these rules, and one draw needn't show every extreme that they name: `image_ids`: rows of one image lie together, images are numbered in order along each sequence, every one of the 6 images of a sequence has 1 to 197 rows, and in each sequence one image has exactly 197. `patch_order`: for each image of each sequence the last dimension holds every patch number once.
All inputs are finite; a program needn't handle non-finite values.
Results may differ from the reference program's by a relative error of at most 0.03.
Values may be sent and summed in bfloat16 or wider, within the bound.
A program may use at most 320 MiB of HBM per device.

```python
import math
import jax
import jax.numpy as jnp
import numpy as np
from jax import lax

D = 768
HEADS = 12
FF = 3072
GRID = 14
IMGS = 6
SEQ_LEN = 788
LAYERS = 4
PATCHES = 196
REL = 732
SEQUENCES = 16


def steps_of(rng, extent, cuts, smallest, high):
    factor_of, own = 1.0, jax.random.fold_in(rng, 6)
    for dim, parts in cuts:
        heights = jnp.exp(jax.random.uniform(jax.random.fold_in(own, dim), (parts,), jnp.float32, smallest / len(cuts), high / len(cuts)))
        factor_of = factor_of * jnp.repeat(heights, extent[dim] // parts).reshape([-1 if axis == dim else 1 for axis in range(len(extent))])
    return factor_of


def length_profile(number_of, total, most, skew):
    weights = [(1 << 20) // math.isqrt(grade ** skew) + 1 for grade in range(2, number_of + 1)]
    spare, holding = total - most - (number_of - 1), [1] * (number_of - 1)
    while spare > 0:
        movable = [i for i in range(number_of - 1) if holding[i] < most]
        pool, budget = sum([weights[i] for i in movable]), spare
        for i in movable:
            addition = min(most - holding[i], max(1, budget * weights[i] // pool), spare)
            holding[i] = holding[i] + addition
            spare = spare - addition
    return np.array([most] + holding)


def ragged(key, count, total, reach, lean):
    if count == 2:
        one = jax.random.randint(key, (), max(1, total - reach), min(reach, total - 1) + 1)
        return jnp.stack([one, total - one])
    tallies = jnp.asarray(length_profile(count, total, reach, lean), jnp.int32)
    couples = (count - 1) // 2
    source_of, sink = tallies[1:1 + 2 * couples:2], tallies[2:2 + 2 * couples:2]
    slack = jnp.minimum(source_of - 1, reach - sink)
    shifted = jax.random.randint(jax.random.fold_in(key, 1), (couples,), 0, 1 << 20) % (slack + 1)
    tallies = tallies.at[1:1 + 2 * couples:2].set(source_of - shifted).at[2:2 + 2 * couples:2].set(sink + shifted)
    return tallies[jax.random.permutation(jax.random.fold_in(key, 2), count)]


def noise(stream_key, extent, scale, reach, pieces=(), kind=jnp.bfloat16):
    gain = steps_of(stream_key, extent, pieces, -0.22, 0.18) if pieces else 1.0
    array = jax.random.normal(stream_key, extent, jnp.float32) * scale * gain
    return jnp.minimum(jnp.maximum(array, -reach), reach).astype(kind)


def setup_inputs(seed: int = 0) -> dict:
    arg_keys = jax.random.split(jax.random.key(seed), 16)
    images = noise(arg_keys[0], (SEQUENCES, SEQ_LEN, D), 1.0, 6.0, ((0, 8), (1, 4)))
    cotangent = noise(arg_keys[1], (SEQUENCES, SEQ_LEN, D), 1.0, 6.0, ((0, 8), (1, 4)))
    image_ids = jax.vmap(lambda own: jnp.searchsorted(jnp.cumsum(ragged(own, IMGS, SEQ_LEN, GRID * GRID + 1, 0)), jnp.arange(SEQ_LEN), side="right"))(jax.random.split(arg_keys[2], SEQUENCES)).reshape((SEQUENCES, SEQ_LEN)).astype(jnp.int32)
    patch_order = jax.vmap(lambda own: jax.random.permutation(own, PATCHES))(jax.random.split(arg_keys[3], SEQUENCES * IMGS)).reshape((SEQUENCES, IMGS, PATCHES)).astype(jnp.int32)
    qkv_weight = noise(arg_keys[4], (LAYERS, D, 3 * D), D ** -0.5, 0.21875, ((0, 4),))
    qv_bias = noise(arg_keys[5], (LAYERS, 2, D), 0.5, 3.0, ((0, 4),), jnp.float32)
    proj_weight = noise(arg_keys[6], (LAYERS, D, D), (D // 16) ** -0.5, 0.875, ((0, 4),))
    rel_table = noise(arg_keys[7], (LAYERS, REL, HEADS), 1.0, 4.0, ((0, 4),), jnp.float32)
    layer_scales = jnp.clip(jnp.exp(math.log(1.5) - 1.60943787 * jax.random.uniform(arg_keys[8], (LAYERS, 2, D), jnp.float32) ** steps_of(arg_keys[8], (LAYERS, 2, D), ((0, 4),), -0.2, 0.2)), 0.3, 1.5)
    layer_norm_gains = jnp.clip(1.0 + 0.1 * jax.random.normal(arg_keys[9], (LAYERS, 2, D), jnp.float32), 0.5, 1.5)
    norm_biases = noise(arg_keys[10], (LAYERS, 2, D), 0.2, 1.0, ((0, 4),), jnp.float32)
    fc1_weight = noise(arg_keys[11], (LAYERS, D, FF), D ** -0.5, 0.21875, ((0, 4),))
    fc1_bias = noise(arg_keys[12], (LAYERS, FF), 0.5, 3.0, ((0, 4),), jnp.float32)
    fc2_weight = noise(arg_keys[13], (LAYERS, FF, D), FF ** -0.5, 0.109375, ((0, 4),))
    out_biases = noise(arg_keys[14], (LAYERS, 2, D), 0.5, 3.0, ((0, 4),), jnp.float32)
    return dict(images=images, cotangent=cotangent, image_ids=image_ids, patch_order=patch_order, qkv_weight=qkv_weight, qv_bias=qv_bias, proj_weight=proj_weight, rel_table=rel_table, layer_scales=layer_scales, layer_norm_gains=layer_norm_gains, norm_biases=norm_biases, fc1_weight=fc1_weight, fc1_bias=fc1_bias, fc2_weight=fc2_weight, out_biases=out_biases)


@jax.custom_vjp
def low(v):
    return lax.optimization_barrier(v.astype(jnp.bfloat16)).astype(jnp.float32)

@jax.custom_vjp
def low_back(v):
    return v

def low_keep(v):
    return (low(v), None)

def low_pass(kept, grad):
    return (grad,)

def back_keep(v):
    return (v, None)

def back_low(kept, grad):
    return (low(grad),)
low.defvjp(low_keep, low_pass)
low_back.defvjp(back_keep, back_low)
EPSILON = 1e-06
NEGATIVE = -1000000000.0
EXACT_MATMUL = lax.Precision.HIGHEST

def relative_index(row_images, patch_perm):
    seq_rows = row_images.shape[0]
    image_count = patch_perm.shape[0]
    patch_count = patch_perm.shape[1]
    members = (row_images[:, None] == jnp.arange(image_count, dtype=jnp.int32)[None, :]).astype(jnp.int32)
    image_rows = lax.optimization_barrier(jnp.sum(members, axis=0))
    image_start = jnp.cumsum(image_rows) - image_rows
    first_row = lax.optimization_barrier(jnp.sum(members * image_start[None, :], axis=1)).astype(jnp.int32)
    offsets = jnp.arange(seq_rows, dtype=jnp.int32) - first_row
    is_class = offsets == 0
    within = jnp.clip(offsets - 1, 0, patch_count - 1)
    patch_id = jnp.take(patch_perm.reshape(-1), (row_images * patch_count + within).astype(jnp.int32))
    grid_row = patch_id // GRID
    grid_col = patch_id % GRID
    rel_span = 2 * GRID - 1
    rel_count = rel_span * rel_span + 3
    pair_index = (grid_row[:, None] - grid_row[None, :] + GRID - 1) * rel_span + (grid_col[:, None] - grid_col[None, :] + GRID - 1)
    pair_index = jnp.where(is_class[:, None], rel_count - 3, pair_index)
    pair_index = jnp.where(is_class[None, :], rel_count - 2, pair_index)
    pair_index = jnp.where(is_class[:, None] & is_class[None, :], rel_count - 1, pair_index)
    return (pair_index.astype(jnp.int32), row_images[:, None] == row_images[None, :])

def norm_rows(values, gain_row, shift_row):
    centred = values - lax.optimization_barrier(jnp.mean(values, axis=-1, keepdims=True))
    spread = lax.optimization_barrier(jnp.mean(centred * centred, axis=-1, keepdims=True))
    return centred * lax.rsqrt(spread + EPSILON) * gain_row + shift_row

def block_forward(inputs, layer_weights, pair_index, same_image):
    qkv_mat, qv_vec, proj_mat, table_rows, scale_rows, gain_rows, shift_rows, fc1_mat, fc1_vec, fc2_mat, outb_rows = layer_weights
    model_width = inputs.shape[-1]
    head_count = table_rows.shape[-1]
    head_dim = model_width // head_count
    seq_rows = inputs.shape[0]
    score_scale = head_dim ** (-0.5)
    normed = low(norm_rows(inputs, gain_rows[0], shift_rows[0]))
    bias_row = jnp.concatenate([qv_vec[0], jnp.zeros_like(qv_vec[0]), qv_vec[1]])
    mixed = low(low_back(jnp.dot(normed, qkv_mat, precision=EXACT_MATMUL) + bias_row))
    queries = mixed[:, :model_width].reshape(seq_rows, head_count, head_dim)
    key_rows = mixed[:, model_width:2 * model_width].reshape(seq_rows, head_count, head_dim)
    values = mixed[:, 2 * model_width:].reshape(seq_rows, head_count, head_dim)
    rel_bias = jnp.transpose(jnp.take(table_rows, pair_index, axis=0), (2, 0, 1))
    logits = jnp.einsum('ihd,jhd->hij', queries, key_rows, precision=EXACT_MATMUL)
    scores = low_back(logits * score_scale + rel_bias)
    masked = jnp.where(same_image[None, :, :], scores, NEGATIVE)
    probs_low = low(jax.nn.softmax(masked, axis=-1))
    attention_output = jnp.einsum('hij,jhd->ihd', probs_low, values, precision=EXACT_MATMUL).reshape(seq_rows, model_width)
    attention_output = low(low_back(attention_output))
    branch = low_back(jnp.dot(attention_output, proj_mat, precision=EXACT_MATMUL) + outb_rows[0])
    middle = inputs + scale_rows[0] * branch
    normed_two = low(norm_rows(middle, gain_rows[1], shift_rows[1]))
    hidden = low_back(jnp.dot(normed_two, fc1_mat, precision=EXACT_MATMUL) + fc1_vec)
    active = low(jax.nn.gelu(hidden, approximate=False))
    branch_two = low_back(jnp.dot(active, fc2_mat, precision=EXACT_MATMUL) + outb_rows[1])
    return middle + scale_rows[1] * branch_two

def encode_sequence(all_weights, tokens, row_images, patch_perm):
    pair_index, same_image = relative_index(row_images, patch_perm)
    state = tokens
    for section_id in range(LAYERS):
        layer_weights = tuple((member[section_id] for member in all_weights))
        state = block_forward(state, layer_weights, pair_index, same_image)
        if section_id + 1 < LAYERS:
            state = low(low_back(state))
    return state

def reference(images, cotangent, image_ids, patch_order, qkv_weight, qv_bias, proj_weight, rel_table, layer_scales, layer_norm_gains, norm_biases, fc1_weight, fc1_bias, fc2_weight, out_biases):
    params = tuple((member.astype(jnp.float32) for member in (qkv_weight, qv_bias, proj_weight, rel_table, layer_scales, layer_norm_gains, norm_biases, fc1_weight, fc1_bias, fc2_weight, out_biases)))
    saved_sequence = jax.checkpoint(encode_sequence)

    def forward(tokens, all_weights):
        return lax.map(lambda seq_item: saved_sequence(all_weights, seq_item[0], seq_item[1], seq_item[2]), (tokens, image_ids, patch_order))
    encoded, pullback = jax.vjp(forward, images.astype(jnp.float32), params)
    images_grad, grads = pullback(cotangent.astype(jnp.float32))
    return (encoded.astype(jnp.bfloat16), images_grad.astype(jnp.bfloat16), grads[0], grads[1], grads[2], grads[3], grads[4], grads[5], grads[6], grads[7], grads[8], grads[9], grads[10])
```

```python
import functools

import jax
import jax.numpy as jnp
from jax import lax
from jax.experimental import pallas as pl
from jax.experimental.pallas import tpu as pltpu
from jax.sharding import PartitionSpec as P

EPSILON = 1e-06
HALF_ROOT = 0.7071067811865476
DENSITY_NORM = 0.3989422804014327
GRID = 14
SPAN = 2 * GRID - 1
PITCH = 16
SLOTS = GRID * PITCH
LANES = 256
CLASS_SLOT = 15
WIDE = 32
STRIP = 512
HEAD_ROWS = 16
F32 = jnp.float32
BF16 = jnp.bfloat16
NEGATIVE = -1000000000.0
LAG = 3
LAG_BACK = 2
TILE = 80
VMEM_LIMIT = 56 * 1024 * 1024

GAIN_A, SHIFT_A, GAIN_B, SHIFT_B, SCALE_A, SCALE_B, OUT_A, OUT_B, FC1_BIAS = range(9)
SUM_DF, SUM_SCALE_B, SUM_GAIN_B, SUM_SHIFT_B, SUM_DA, SUM_SCALE_A = range(6)


def nn(a, b):
    return lax.dot_general(a, b, (((1,), (0,)), ((), ())), preferred_element_type=F32)


def nt(a, b):
    return lax.dot_general(a, b, (((1,), (1,)), ((), ())), preferred_element_type=F32)


def tn(a, b):
    return lax.dot_general(a, b, (((0,), (0,)), ((), ())), preferred_element_type=F32)


def exact(a, b, dims):
    return lax.dot_general(a, b, (dims, ((), ())), precision=lax.Precision.HIGHEST, preferred_element_type=F32)


def iota(shape, axis):
    return lax.broadcasted_iota(jnp.int32, shape, axis)


def row_tile(t):
    return pl.ds(pl.multiple_of(t * TILE, 16), TILE)


def vec(vec_ref, k):
    return vec_ref[k:k + 1, :]


def row_stats(v):
    centred = v - jnp.mean(v, axis=-1, keepdims=True)
    inverse = lax.rsqrt(jnp.mean(centred * centred, axis=-1, keepdims=True) + EPSILON)
    return centred * inverse, inverse


def norm_tiles(src_ref, dst_ref, vec_ref, gain, shift):
    @pl.loop(0, src_ref.shape[0] // TILE)
    def _(t):
        rows = row_tile(t)
        unit, _ = row_stats(src_ref[rows, :].astype(F32))
        dst_ref[rows, :] = (unit * vec(vec_ref, gain) + vec(vec_ref, shift)).astype(BF16)


def extra_rows(first, lanes):
    row = iota((16, lanes), 0)
    out = jnp.zeros((16, lanes), F32)
    for k, value in enumerate(first):
        out = jnp.where(row == k, value, out)
    return out.astype(BF16)


def split3(v):
    hi = v.astype(BF16).astype(F32)
    mid = (v - hi).astype(BF16).astype(F32)
    return hi, mid, v - hi - mid


def attn_fwd_kernel(keep, pick_ref, ws_ref, x_ref, vec_ref, own_ref, other_ref, bias_ref, b_ref, et_ref, mask_ref,
                    o_ref, *rest):
    if keep:
        n1_ref, zt_ref, ot_ref, lse_ref, wt, n1t, sem = rest
    else:
        n1_ref, zt_ref, ot_ref, wt, n1t, sem = rest
    heads = b_ref.shape[0]
    width = x_ref.shape[1]
    hd = width // heads
    i = pl.program_id(0)

    @pl.when(i == 0)
    def _():
        @pl.when(pick_ref[0] == 1)
        def _():
            pltpu.make_async_copy(own_ref, wt, sem).start()

        @pl.when(pick_ref[0] == 0)
        def _():
            pltpu.make_async_copy(other_ref, wt, sem).start()

        o_ref[...] = jnp.zeros_like(o_ref)
        norm_tiles(x_ref, n1_ref, vec_ref, GAIN_A, SHIFT_A)
        pltpu.make_async_copy(own_ref, wt, sem).wait()

    ws = pl.multiple_of(ws_ref[i], 16)
    n1t[...] = tn(n1_ref[pl.ds(ws, SLOTS), :], et_ref[0]).astype(BF16)

    @pl.loop(0, 3)
    def _(c):
        rows = pl.ds(pl.multiple_of(c * width, width), width)
        factor = jnp.where(c == 0, hd ** -0.5, 1.0)
        zt_ref[0, rows, :] = ((nn(wt[rows, :], n1t[...]) + bias_ref[rows, :]) * factor).astype(BF16)

    ones_q = extra_rows([1.0], LANES)
    mask_k = extra_rows([mask_ref[0]], SLOTS)
    ones_v = extra_rows([1.0], SLOTS)

    def scores(h):
        r = h * hd
        qt = jnp.concatenate([zt_ref[0, r:r + hd, :], ones_q], axis=0)
        kt = jnp.concatenate([zt_ref[0, width + r:width + r + hd, :SLOTS], mask_k], axis=0)
        return tn(kt, qt)

    def soft(h, s):
        s = s + b_ref[h]
        m = jnp.max(s, axis=0, keepdims=True)
        return m, jnp.exp(s - m).astype(BF16)

    def finish(h, m, e):
        r = h * hd
        vt = jnp.concatenate([zt_ref[0, 2 * width + r:2 * width + r + hd, :SLOTS], ones_v], axis=0)
        o = nn(vt, e)
        total = o[hd:hd + 1]
        ot_ref[0, r:r + hd, :] = (o[:hd] * (1.0 / total)).astype(BF16)
        if keep:
            lse_ref[0, h:h + 1, :] = m + jnp.log(total)

    s, e = {}, {}
    for t in range(heads + 2 * LAG):
        if t < heads:
            s[t] = scores(t)
        if 0 <= t - LAG < heads:
            e[t - LAG] = soft(t - LAG, s.pop(t - LAG))
        if t - 2 * LAG >= 0:
            finish(t - 2 * LAG, *e.pop(t - 2 * LAG))

    win = pl.ds(ws, SLOTS)
    o_ref[win, :] = (o_ref[win, :].astype(F32) + nt(et_ref[0], ot_ref[0])).astype(BF16)


def attn_bwd_kernel(want, pick_ref, ws_ref, da_ref, own_ref, other_ref, b_ref, et_ref, mask_ref, zt_ref, ot_ref,
                    lse_ref, dz_ref, *rest):
    if want:
        db_ref, dat, dot, dzt = rest
    else:
        dat, dot, dzt = rest
    heads = b_ref.shape[0]
    width = da_ref.shape[1]
    hd = width // heads
    i = pl.program_id(0)

    @pl.when(i == 0)
    def _():
        dz_ref[...] = jnp.zeros_like(dz_ref)
        if want:
            db_ref[...] = jnp.zeros_like(db_ref)
        dzt[...] = jnp.zeros_like(dzt)

    ws = pl.multiple_of(ws_ref[i], 16)
    win = pl.ds(ws, SLOTS)
    dat[...] = tn(da_ref[win, :], et_ref[0]).astype(BF16)
    proj = jnp.where(pick_ref[0] == 1, own_ref[...], other_ref[...])
    dot[...] = nn(proj, dat[...]).astype(BF16)
    extra_k = extra_rows([mask_ref[0], 1.0, 1.0, 1.0], SLOTS)
    extra_v = extra_rows([1.0, 1.0, 1.0], SLOTS)

    def parts(h):
        r = h * hd
        return (zt_ref[0, r:r + hd, :], zt_ref[0, width + r:width + r + hd, :SLOTS],
                zt_ref[0, 2 * width + r:2 * width + r + hd, :SLOTS], dot[r:r + hd, :])

    def products(h):
        qt, kt, vt, dt = parts(h)
        r = h * hd
        delta = jnp.sum(dt.astype(F32) * ot_ref[0, r:r + hd, :].astype(F32), axis=0, keepdims=True)
        extra_q = extra_rows([1.0, *split3(-lse_ref[0, h:h + 1, :])], LANES)
        extra_d = extra_rows(split3(-delta), LANES)
        s = tn(jnp.concatenate([kt, extra_k], axis=0), jnp.concatenate([qt, extra_q], axis=0))
        dp = tn(jnp.concatenate([vt, extra_v], axis=0), jnp.concatenate([dt, extra_d], axis=0))
        return s, dp

    def middle(h, s, dp):
        p = jnp.exp(s + b_ref[h])
        ds = p * dp
        if want:
            db_ref[h] += ds
        return p.astype(BF16), ds.astype(BF16)

    def finish(h, p, ds):
        qt, kt, vt, dt = parts(h)
        r = h * hd
        dzt[2 * width + r:2 * width + r + hd, :SLOTS] = nt(dt, p).astype(BF16)
        dzt[width + r:width + r + hd, :SLOTS] = nt(qt, ds).astype(BF16)
        dzt[r:r + hd, :] = (nn(kt, ds) * hd ** -0.5).astype(BF16)

    s, e = {}, {}
    for t in range(heads + 2 * LAG_BACK):
        if t < heads:
            s[t] = products(t)
        if 0 <= t - LAG_BACK < heads:
            e[t - LAG_BACK] = middle(t - LAG_BACK, *s.pop(t - LAG_BACK))
        if t - 2 * LAG_BACK >= 0:
            finish(t - 2 * LAG_BACK, *e.pop(t - 2 * LAG_BACK))

    for c in range(3):
        cols = slice(c * width, (c + 1) * width)
        dz_ref[win, cols] = (dz_ref[win, cols].astype(F32) + nt(et_ref[0], dzt[cols, :])).astype(BF16)


def spread(count):
    entry = iota((count, SPAN * WIDE), 0)
    lane = iota((count, SPAN * WIDE), 1)
    return jnp.where((entry == lane // WIDE * SPAN + lane % WIDE) & (lane % WIDE < SPAN), 1.0, 0.0).astype(F32)


def squeeze():
    lane = iota((SPAN * WIDE, STRIP), 0)
    to = iota((SPAN * WIDE, STRIP), 1)
    return jnp.where(lane == to // PITCH * WIDE + to % PITCH, 1.0, 0.0).astype(F32)


def bias_kernel(table_ref, b_ref, shifted, strips):
    heads = b_ref.shape[0]
    table = table_ref[...]
    wide = exact(table, spread(table.shape[1]), ((1,), (0,)))
    for c in range(PITCH):
        shifted[c * HEAD_ROWS:(c + 1) * HEAD_ROWS, :] = pltpu.roll(wide, (c - GRID + 1) % (SPAN * WIDE), 1)
    packed = exact(shifted[...], squeeze(), ((1,), (0,)))
    for k in range(strips.shape[0]):
        strips[k] = packed[:, k * 128:(k + 1) * 128]
    row = iota((SLOTS, LANES), 0)
    col = iota((SLOTS, LANES), 1)
    for h in range(heads):
        strip = jnp.concatenate([strips[k, pl.ds(h, PITCH, stride=HEAD_ROWS), :] for k in range(strips.shape[0])], axis=1)
        for r in range(GRID):
            at = PITCH * (GRID - 1 - r)
            b_ref[h, r * PITCH:(r + 1) * PITCH, :] = strip[:, at:at + LANES]
        query, key, both = [table_ref[h:h + 1, SPAN * SPAN + k:SPAN * SPAN + k + 1] for k in range(3)]
        full = jnp.where(col == CLASS_SLOT, query, b_ref[h])
        b_ref[h] = jnp.where(row == CLASS_SLOT, jnp.where(col == CLASS_SLOT, both, key), full)


def bias_back_kernel(db_ref, table_ref, strips, classes):
    heads = db_ref.shape[0]
    row = iota((SLOTS, LANES), 0)
    col = iota((SLOTS, LANES), 1)
    is_row = row == CLASS_SLOT
    is_col = col == CLASS_SLOT
    entry = iota((1, table_ref.shape[1]), 1) - SPAN * SPAN
    strips[...] = jnp.zeros_like(strips)
    classes[...] = jnp.zeros_like(classes)
    for h in range(heads):
        full = db_ref[h]
        query = jnp.sum(jnp.where(is_col & ~is_row, full, 0.0), keepdims=True)
        key = jnp.sum(jnp.where(is_row & ~is_col, full, 0.0), keepdims=True)
        both = jnp.sum(jnp.where(is_row & is_col, full, 0.0), keepdims=True)
        classes[h:h + 1, :] = jnp.where(entry == 0, query, jnp.where(entry == 1, key, jnp.where(entry == 2, both, 0.0)))
        plain = jnp.where(is_row | is_col, 0.0, full)
        total = jnp.zeros((PITCH, STRIP), F32)
        for r in range(GRID):
            part = jnp.concatenate([plain[r * PITCH:(r + 1) * PITCH, :], jnp.zeros((PITCH, STRIP - LANES), F32)],
                                   axis=1)
            total = total + pltpu.roll(part, PITCH * (GRID - 1 - r), 1)
        for k in range(strips.shape[0]):
            strips[k, pl.ds(h, PITCH, stride=HEAD_ROWS), :] = total[:, k * 128:(k + 1) * 128]
    wide = exact(jnp.concatenate([strips[k] for k in range(strips.shape[0])], axis=1), squeeze(), ((1,), (1,)))
    gathered = jnp.zeros((HEAD_ROWS, SPAN * WIDE), F32)
    for c in range(GRID):
        gathered = gathered + pltpu.roll(wide[c * HEAD_ROWS:(c + 1) * HEAD_ROWS, :], (GRID - 1 - c) % (SPAN * WIDE), 1)
    table_ref[...] = exact(gathered, spread(table_ref.shape[1]), ((1,), (1,))) + classes[...]


def mlp_fwd_kernel(keep, pick_ref, x_ref, o_ref, proj_own, proj_other, vec_ref, fc1_own, fc1_other, fc2_own, fc2_other,
                   y_ref, *rest):
    if keep:
        m_ref, n2_ref, a_ref, f_ref, g_ref, slope_ref, acc = rest
    else:
        m_ref, n2_ref, acc = rest
    j = pl.program_id(0)
    mine = pick_ref[0] == 1

    @pl.when(j == 0)
    def _():
        a = nn(o_ref[...], jnp.where(mine, proj_own[...], proj_other[...])) + vec(vec_ref, OUT_A)
        if keep:
            a_ref[...] = a.astype(BF16)
        m_ref[...] = x_ref[...].astype(F32) + vec(vec_ref, SCALE_A) * a
        acc[...] = jnp.zeros_like(acc)
        norm_tiles(m_ref, n2_ref, vec_ref, GAIN_B, SHIFT_B)

    u = nn(n2_ref[...], jnp.where(mine, fc1_own[...], fc1_other[...])) + vec_ref[pl.ds(FC1_BIAS + j, 1), :]
    cdf = 0.5 * (1.0 + lax.erf(u * HALF_ROOT))
    g = (u * cdf).astype(BF16)
    if keep:
        g_ref[...] = g
        slope_ref[...] = (cdf + u * (jnp.exp(-0.5 * u * u) * DENSITY_NORM)).astype(BF16)
    acc[...] += nn(g, jnp.where(mine, fc2_own[...], fc2_other[...]))

    @pl.when(j == pl.num_programs(0) - 1)
    def _():
        @pl.loop(0, acc.shape[0] // TILE)
        def _(t):
            rows = row_tile(t)
            f = acc[rows, :] + vec(vec_ref, OUT_B)
            if keep:
                f_ref[rows, :] = f.astype(BF16)
            y_ref[rows, :] = (m_ref[rows, :] + vec(vec_ref, SCALE_B) * f).astype(BF16)


def norm_back_tiles(count, src_ref, grad_ref, vec_ref, gain, emit):
    def body(t, sums):
        rows = row_tile(t)
        unit, inverse = row_stats(src_ref[rows, :].astype(F32))
        grad = grad_ref[rows, :]
        scaled = grad * vec(vec_ref, gain)
        mean_one = jnp.mean(scaled, axis=-1, keepdims=True)
        mean_two = jnp.mean(scaled * unit, axis=-1, keepdims=True)
        more = emit(rows, inverse * (scaled - mean_one - unit * mean_two))
        if not count:
            return sums
        return tuple(s + jnp.sum(v, axis=0, keepdims=True) for s, v in zip(sums, (grad * unit, grad) + more))

    zero = jnp.zeros((1, grad_ref.shape[1]), F32)
    return lax.fori_loop(0, grad_ref.shape[0] // TILE, body, (zero,) * count)


def mlp_bwd_kernel(want, pick_ref, dy_ref, m_ref, vec_ref, slope_ref, fc1_own, fc1_other, fc2_own, fc2_other, *rest):
    if want:
        (n2_ref, g_ref, a_ref, f_ref, dm_ref, da_ref, fc1_give, fc1_keep, fc2_give, fc2_keep, sums_ref, df, acc) = rest
    else:
        dm_ref, da_ref, df, acc = rest
    j = pl.program_id(0)
    steps = pl.num_programs(0)
    mine = pick_ref[0] == 1
    core = pick_ref[1]
    width = dy_ref.shape[1]

    @pl.when(j == 0)
    def _():
        acc[...] = jnp.zeros_like(acc)
        if want:
            sums_ref[...] = jnp.zeros_like(sums_ref)
        zero = jnp.zeros((1, width), F32)

        def body(t, sums):
            rows = row_tile(t)
            dy = dy_ref[rows, :].astype(F32)
            scaled = (dy * vec(vec_ref, SCALE_B)).astype(BF16)
            df[rows, :] = scaled
            if not want:
                return sums
            return (sums[0] + jnp.sum(scaled.astype(F32), axis=0, keepdims=True),
                    sums[1] + jnp.sum(dy * f_ref[rows, :].astype(F32), axis=0, keepdims=True))

        sums = lax.fori_loop(0, df.shape[0] // TILE, body, (zero, zero) if want else ())
        if want:
            sums_ref[SUM_DF:SUM_DF + 1, :] = sums[0]
            sums_ref[SUM_SCALE_B:SUM_SCALE_B + 1, :] = sums[1]

    fc1 = jnp.where(mine, fc1_own[...], fc1_other[...])
    fc2 = jnp.where(mine, fc2_own[...], fc2_other[...])
    du = (nt(df[...], fc2) * slope_ref[...].astype(F32)).astype(BF16)
    acc[...] += nt(du, fc1)
    if want:
        at = lax.rem(j + (1 - core) * (steps // 2), steps)
        sums_ref[pl.ds(FC1_BIAS + at, 1), :] = jnp.sum(du.astype(F32), axis=0, keepdims=True)
        grad = tn(g_ref[...], df[...]).astype(BF16)
        low, high = grad[:, :width // 2], grad[:, width // 2:]
        fc2_keep[...] = jnp.where(core == 0, low, high)
        fc2_give[...] = jnp.where(core == 0, high, low)
        grad1 = tn(n2_ref[...], du).astype(BF16)

        @pl.when(j < steps // 2)
        def _():
            fc1_give[...] = grad1

        @pl.when(j >= steps // 2)
        def _():
            fc1_keep[...] = grad1

    @pl.when(j == steps - 1)
    def _():
        def emit(rows, dv):
            dm = dy_ref[rows, :].astype(F32) + dv
            da = (dm * vec(vec_ref, SCALE_A)).astype(BF16)
            dm_ref[rows, :] = dm
            da_ref[rows, :] = da
            return (da.astype(F32), dm * a_ref[rows, :].astype(F32)) if want else ()

        sums = norm_back_tiles(4 if want else 0, m_ref, acc, vec_ref, GAIN_B, emit)
        for k, s in zip((SUM_GAIN_B, SUM_SHIFT_B, SUM_DA, SUM_SCALE_A), sums):
            sums_ref[k:k + 1, :] = s


def attn_tail_kernel(want, pick_ref, x_ref, dm_ref, vec_ref, dz_ref, wt_own, wt_other, *rest):
    if want:
        n1_ref, o_ref, da_ref, dx_ref, qkv_give, qkv_keep, proj_give, proj_keep, bias_ref, sums_ref, acc = rest
    else:
        dx_ref, acc = rest
    j = pl.program_id(0)
    core = pick_ref[1]
    width = x_ref.shape[1]

    @pl.when(j == 0)
    def _():
        acc[...] = jnp.zeros_like(acc)
        if want:
            sums_ref[...] = jnp.zeros_like(sums_ref)
            grad = tn(o_ref[...], da_ref[...]).astype(BF16)
            low, high = grad[:, :width // 2], grad[:, width // 2:]
            proj_keep[...] = jnp.where(core == 0, low, high)
            proj_give[...] = jnp.where(core == 0, high, low)

    dz = dz_ref[...]
    acc[...] += nn(dz, jnp.where(pick_ref[0] == 1, wt_own[...], wt_other[...]))
    if want:
        bias_ref[0] = jnp.broadcast_to(jnp.sum(dz.astype(F32), axis=0, keepdims=True), bias_ref.shape[1:])
        grad1 = tn(n1_ref[...], dz).astype(BF16)

        @pl.when(j == 0)
        def _():
            qkv_give[...] = grad1

        @pl.when(j == 1)
        def _():
            qkv_keep[...] = grad1

    @pl.when(j == pl.num_programs(0) - 1)
    def _():
        def emit(rows, dv):
            dx_ref[rows, :] = (dm_ref[rows, :] + dv).astype(BF16)
            return ()

        sums = norm_back_tiles(2 if want else 0, x_ref, acc, vec_ref, GAIN_A, emit)
        for k, s in enumerate(sums):
            sums_ref[k:k + 1, :] = s


def params():
    return pltpu.CompilerParams(vmem_limit_bytes=VMEM_LIMIT)


def shaped(*arrays):
    return [jax.ShapeDtypeStruct(s, d) for s, d in arrays]


def whole(shape):
    return pl.BlockSpec(shape, lambda *_: (0,) * len(shape))


def per_image(shape):
    return pl.BlockSpec((1,) + shape, lambda i, *_: (i,) + (0,) * len(shape))


def call(kernel, name, prefetched, grid, inputs, outputs, scratch):
    return pl.pallas_call(
        kernel,
        grid_spec=pltpu.PrefetchScalarGridSpec(
            num_scalar_prefetch=len(prefetched), grid=grid, in_specs=[s for _, s in inputs],
            out_specs=[s for _, _, s in outputs], scratch_shapes=scratch),
        out_shape=[jax.ShapeDtypeStruct(s, d) for s, d, _ in outputs],
        compiler_params=params(), name=name,
    )(*prefetched, *[a for a, _ in inputs])


def attn_fwd(keep, x, w, meta):
    ws, et, mask = meta
    rows, width = x.shape
    heads = w["bias"].shape[0]
    imgs = et.shape[0]
    anywhere = pl.BlockSpec(memory_space=pl.ANY)
    inputs = [(x, whole(x.shape)), (w["vectors"], whole(w["vectors"].shape)), (w["qkv_t"][0], anywhere),
              (w["qkv_t"][1], anywhere), (w["qkv_bias"], whole(w["qkv_bias"].shape)), (w["bias"], whole(w["bias"].shape)),
              (et, per_image(et.shape[1:])), (mask, per_image(mask.shape[1:]))]
    outputs = [((rows, width), BF16, whole((rows, width)))]
    scratch = [pltpu.VMEM((3 * width, width), BF16), pltpu.VMEM((width, LANES), BF16), pltpu.SemaphoreType.DMA]
    if keep:
        outputs += [((rows, width), BF16, whole((rows, width))),
                    ((imgs, 3 * width, LANES), BF16, per_image((3 * width, LANES))),
                    ((imgs, width, LANES), BF16, per_image((width, LANES))),
                    ((imgs, heads, LANES), F32, per_image((heads, LANES)))]
    else:
        scratch = [pltpu.VMEM((rows, width), BF16), pltpu.VMEM((1, 3 * width, LANES), BF16),
                   pltpu.VMEM((1, width, LANES), BF16)] + scratch
    return call(functools.partial(attn_fwd_kernel, keep), "attn_fwd_keep" if keep else "attn_fwd", [w["pick"], ws],
                (imgs,), inputs, outputs, scratch)


def attn_bwd(want, da, w, meta, kept):
    ws, et, mask = meta
    rows, width = da.shape
    bias = w["bias"]
    imgs = et.shape[0]
    proj = whole((width, width))
    zt, ot, lse = kept["zt"], kept["ot"], kept["lse"]
    inputs = [(da, whole(da.shape)), (w["proj"][0], proj), (w["proj"][1], proj), (bias, whole(bias.shape)),
              (et, per_image(et.shape[1:])), (mask, per_image(mask.shape[1:])), (zt, per_image(zt.shape[1:])),
              (ot, per_image(ot.shape[1:])), (lse, per_image(lse.shape[1:]))]
    outputs = [((rows, 3 * width), BF16, whole((rows, 3 * width)))]
    if want:
        outputs += [(bias.shape, F32, whole(bias.shape))]
    scratch = [pltpu.VMEM((width, LANES), BF16), pltpu.VMEM((width, LANES), BF16), pltpu.VMEM((3 * width, LANES), BF16)]
    return call(functools.partial(attn_bwd_kernel, want), "attn_bwd_all" if want else "attn_bwd", [w["pick"], ws],
                (imgs,), inputs, outputs, scratch)


def build_bias(table):
    heads = 12
    return pl.pallas_call(
        bias_kernel, out_shape=jax.ShapeDtypeStruct((heads, SLOTS, LANES), F32),
        scratch_shapes=[pltpu.VMEM((PITCH * HEAD_ROWS, SPAN * WIDE), F32), pltpu.VMEM((STRIP // 128, PITCH * HEAD_ROWS, 128), F32)],
        compiler_params=params(), name="bias_build",
    )(table)


def table_back(db, lanes):
    return pl.pallas_call(
        bias_back_kernel, out_shape=jax.ShapeDtypeStruct((HEAD_ROWS, lanes), F32),
        scratch_shapes=[pltpu.VMEM((STRIP // 128, PITCH * HEAD_ROWS, 128), F32), pltpu.VMEM((HEAD_ROWS, lanes), F32)],
        compiler_params=params(), name="bias_back",
    )(db)


def chosen(which, block, to_index):
    def index(j, pick):
        used = pick[0] if which == 0 else 1 - pick[0]
        return tuple(k * used for k in to_index(j, pick))
    return pl.BlockSpec(block, index)


def both(pair, block, to_index):
    return [(pair[k], chosen(k, block, to_index)) for k in range(2)]


def mlp_fwd(keep, x, o, w):
    rows, width = x.shape
    hidden = w["fc1"][0].shape[1]
    full = whole((rows, width))
    proj = whole((width, width))
    inputs = [(x, full), (o, full), (w["proj"][0], proj), (w["proj"][1], proj),
              (w["vectors"], whole(w["vectors"].shape)),
              *both(w["fc1"], (width, width), lambda j, p: (0, j)), *both(w["fc2"], (width, width), lambda j, p: (j, 0))]
    outputs = [((rows, width), BF16, full)]
    scratch = [pltpu.VMEM((rows, width), F32)]
    if keep:
        part = pl.BlockSpec((rows, width), lambda j, p: (0, j))
        outputs += [((rows, width), F32, full)] + [((rows, width), BF16, full)] * 3 + [((rows, hidden), BF16, part)] * 2
    else:
        scratch = [pltpu.VMEM((rows, width), F32), pltpu.VMEM((rows, width), BF16)] + scratch
    return call(functools.partial(mlp_fwd_kernel, keep), "mlp_fwd_keep" if keep else "mlp_fwd", [w["pick"]],
                (hidden // width,), inputs, outputs, scratch)


def mlp_bwd(want, dy, w, kept):
    rows, width = dy.shape
    hidden = w["fc1"][0].shape[1]
    steps = hidden // width
    full = whole((rows, width))

    def at(j, pick):
        return lax.rem(j + (1 - pick[1]) * (steps // 2), steps)

    part = pl.BlockSpec((rows, width), lambda j, p: (0, at(j, p)))
    inputs = [(dy, full), (kept["m"], full), (w["vectors"], whole(w["vectors"].shape)), (kept["slope"], part),
              *both(w["fc1"], (width, width), lambda j, p: (0, at(j, p))),
              *both(w["fc2"], (width, width), lambda j, p: (at(j, p), 0))]
    outputs = [((rows, width), F32, full), ((rows, width), BF16, full)]
    if want:
        inputs += [(kept["n2"], full), (kept["g"], part), (kept["a"], full), (kept["f"], full)]
        half = pl.BlockSpec((width, width // 2), lambda j, p: (at(j, p), 0))
        give = pl.BlockSpec((width, width), lambda j, p: (0, jnp.minimum(j, steps // 2 - 1)))
        stay = pl.BlockSpec((width, width), lambda j, p: (0, jnp.maximum(j - steps // 2, 0)))
        outputs += [((width, hidden // 2), BF16, give), ((width, hidden // 2), BF16, stay),
                    ((hidden, width // 2), BF16, half), ((hidden, width // 2), BF16, half),
                    ((16, width), F32, whole((16, width)))]
    scratch = [pltpu.VMEM((rows, width), BF16), pltpu.VMEM((rows, width), F32)]
    return call(functools.partial(mlp_bwd_kernel, want), "mlp_bwd_all" if want else "mlp_bwd", [w["pick"]],
                (steps,), inputs, outputs, scratch)


def attn_tail(want, x, dm, dz, da, w, kept):
    rows, width = x.shape
    part = 3 * width // 2
    full = whole((rows, width))

    def at(j, pick):
        return lax.rem(j + 1 - pick[1], 2)

    inputs = [(x, full), (dm, full), (w["vectors"], whole(w["vectors"].shape)),
              (dz, pl.BlockSpec((rows, part), lambda j, p: (0, at(j, p)))),
              *both(w["qkv_t"], (part, width), lambda j, p: (at(j, p), 0))]
    outputs = [((rows, width), BF16, full)]
    if want:
        inputs += [(kept["n1"], full), (kept["o"], full), (da, full)]
        outputs += [((width, part), BF16, whole((width, part)))] * 2
        outputs += [((width, width // 2), BF16, whole((width, width // 2)))] * 2
        outputs += [((2, 8, part), F32, pl.BlockSpec((1, 8, part), lambda j, p: (at(j, p), 0, 0))),
                    ((8, width), F32, whole((8, width)))]
    return call(functools.partial(attn_tail_kernel, want), "attn_tail_all" if want else "attn_tail", [w["pick"]],
                (2,), inputs, outputs, [pltpu.VMEM((rows, width), F32)])


def sequence_meta(ids, order, rows):
    imgs, patches = order.shape
    image = jnp.arange(imgs, dtype=jnp.int32)
    start = jnp.sum((ids[None, :] < image[:, None]).astype(jnp.int32), axis=1)
    count = jnp.sum((ids[None, :] == image[:, None]).astype(jnp.int32), axis=1)
    ws = jnp.minimum(start // 16 * 16, rows - SLOTS)
    slot = jnp.arange(LANES, dtype=jnp.int32)
    is_class = slot == CLASS_SLOT
    is_patch = (slot % PITCH < GRID) & (slot < SLOTS)
    patch = jnp.where(is_patch, slot // PITCH * GRID + slot % PITCH, -1)
    place = jnp.arange(1, patches + 1, dtype=jnp.int32)
    offset = jnp.sum(jnp.where(order[:, None, :] == patch[None, :, None], place, 0), axis=2)
    valid = (is_class | is_patch)[None, :] & (offset < count[:, None])
    local = jnp.where(valid, offset + (start - ws)[:, None], -1)
    row = jnp.arange(SLOTS, dtype=jnp.int32)
    et = (local[:, None, :] == row[None, :, None]).astype(BF16)
    mask = jnp.where(valid, 0.0, NEGATIVE).astype(F32)[:, None, :SLOTS]
    return ws, et, mask


def layer_forward(x, w, meta, keep):
    out = attn_fwd(keep, x, w, meta)
    if not keep:
        return mlp_fwd(False, x, out[0], w)[0], None
    o, n1, zt, ot, lse = out
    y, m, n2, a, f, g, slope = mlp_fwd(True, x, o, w)
    return y, dict(x=x, n1=n1, o=o, zt=zt, ot=ot, lse=lse, a=a, m=m, n2=n2, g=g, slope=slope, f=f)


def layer_backward(dy, w, kept, meta, want):
    out = mlp_bwd(want, dy, w, kept)
    dm, da = out[:2]
    back = attn_bwd(want, da, w, meta, kept)
    last = attn_tail(want, kept["x"], dm, back[0], da, w, kept)
    if not want:
        return last[0], None, None
    fc1_give, fc1_keep, fc2_give, fc2_keep, sums_b = out[2:]
    dx, qkv_give, qkv_keep, proj_give, proj_keep, bias, sums_a = last
    width = dy.shape[1]
    bias = bias[:, 0].reshape(1, -1)
    small = jnp.concatenate([sums_b, sums_a[:2], bias[:, :width], bias[:, 2 * width:], jnp.zeros((4, width), F32),
                             table_back(back[1], width)])
    halves = [(fc2_keep, fc2_give), (fc1_keep, fc1_give), (proj_keep, proj_give), (qkv_keep, qkv_give)]
    return dx, halves, small


def shards(images, cotangent, image_ids, patch_order, qkv_weight, qv_bias, proj_weight, rel_table, layer_scales,
           layer_norm_gains, norm_biases, fc1_weight, fc1_bias, fc2_weight, out_biases):
    me = lax.axis_index("narrow")
    at_wide = lax.axis_index("wide")
    wide = lax.axis_size("wide")
    core = me % 2
    first = me < 2
    quarter, width = images.shape[1:]
    rows = 4 * quarter
    padded = -(-rows // TILE) * TILE
    entries, heads = rel_table.shape[1:]
    flips = {k: [(d, d ^ k) for d in range(4)] for k in (1, 2, 3)}

    def swap(v, k):
        return lax.ppermute(v, "narrow", flips[k])

    def swap_wide(v, k):
        return lax.ppermute(v, "wide", [(d, d ^ k) for d in range(wide)])

    def pick(v, index):
        return lax.dynamic_index_in_dim(v, index, 0, keepdims=False)

    smalls = jnp.concatenate([layer_norm_gains[0, :1], norm_biases[0, :1], layer_norm_gains[0, 1:], norm_biases[0, 1:],
                              layer_scales[0], out_biases[0], fc1_bias.reshape(-1, width), qv_bias[0],
                              jnp.zeros((2, width), F32)])
    table = jnp.pad(rel_table[0].T, ((0, HEAD_ROWS - heads), (0, width - entries)))
    own = [qkv_weight[0].T, smalls, table, proj_weight[0], fc1_weight[0], fc2_weight[0]]
    other = [swap(v, 1) for v in own]
    bias_at = FC1_BIAS + fc1_bias.shape[1] // width
    weights = []
    for layer in range(2):
        vectors = jnp.where(core == layer, smalls, other[1])
        qkv_bias = jnp.concatenate([vectors[bias_at], jnp.zeros((width,), F32), vectors[bias_at + 1]])
        weights.append(dict(
            pick=jnp.stack([(core == layer).astype(jnp.int32), core]), vectors=vectors, qkv_bias=qkv_bias[:, None],
            bias=build_bias(jnp.where(core == layer, table, other[2])),
            **{name: (own[k], other[k]) for name, k in (("qkv_t", 0), ("proj", 3), ("fc1", 4), ("fc2", 5))}))

    meta = sequence_meta(pick(image_ids, core), pick(patch_order, core), padded)

    mine = jnp.where(first, images, cotangent)
    theirs = jnp.where(first, cotangent, images)
    pieces = [pick(mine, core), swap(pick(mine, 1 - core), 1), swap(pick(theirs, core), 2),
              swap(pick(theirs, 1 - core), 3)]
    rows_in = jnp.zeros((padded, width), BF16)
    for k, piece in enumerate(pieces):
        rows_in = lax.dynamic_update_slice(rows_in, piece, ((me ^ k) * quarter, 0))

    def run_forward(x, keep):
        y, kept_one = layer_forward(x, weights[0], meta, keep)
        y, kept_two = layer_forward(y, weights[1], meta, keep)
        return y, (kept_one, kept_two)

    middle, _ = run_forward(rows_in, False)
    x_in = jnp.where(first, rows_in, swap(middle, 2))
    y_out, kept = run_forward(x_in, True)

    back, _, _ = layer_backward(rows_in, weights[1], kept[1], meta, False)
    back, _, _ = layer_backward(back, weights[0], kept[0], meta, False)
    dy_in = jnp.where(first, swap(back, 2), rows_in)

    def reduced(halves):
        out = []
        for keep, give in halves:
            got = swap(give, 1)
            n = wide
            r, c = keep.shape[0] // wide, keep.shape[1]
            step = 1
            while n > 1:
                bit = at_wide // step % 2
                pair = [v.reshape(n // 2, 2, r, c) for v in (keep, got)]
                total = [lax.dynamic_index_in_dim(v, 1 - bit, 1, keepdims=False).astype(F32) for v in pair]
                got_next = swap_wide((total[0] + total[1]).astype(BF16), step)
                rest = [lax.dynamic_index_in_dim(v, bit, 1, keepdims=False).astype(F32) for v in pair]
                keep, got = (rest[0] + rest[1]).astype(BF16), got_next
                n, step = n // 2, 2 * step
            out.append((keep.astype(F32) + got.astype(F32)).reshape(r, c))
        return out

    mid, halves_two, small_two = layer_backward(dy_in, weights[1], kept[1], meta, True)
    shares_two = reduced(halves_two)
    dx, halves_one, small_one = layer_backward(mid, weights[0], kept[0], meta, True)

    result = jnp.where(first, dx, y_out)[:rows].reshape(4, quarter, width)
    same = (pick(result, me), swap(pick(result, me ^ 1), 1))
    across = (swap(pick(result, me ^ 2), 2), swap(pick(result, me ^ 3), 3))
    same = jnp.where(core == 0, jnp.stack(same), jnp.stack(same[::-1]))
    across = jnp.where(core == 0, jnp.stack(across), jnp.stack(across[::-1]))
    encoded = jnp.where(first, across, same)
    images_grad = jnp.where(first, same, across)

    shares_one = reduced(halves_one)
    shares = []
    for one, two in zip(shares_one, shares_two):
        stay = jnp.where(core == 0, one, two)
        got = swap(jnp.where(core == 0, two, one).astype(BF16), 1).astype(F32)
        shares.append(jnp.where(core == 0, jnp.concatenate([stay, got], 1), jnp.concatenate([got, stay], 1))[None])
    totals = jnp.where(core == 0, small_one, small_two) + swap(jnp.where(core == 0, small_two, small_one), 1)
    step = 1
    while step < wide:
        totals = totals + swap_wide(totals, step)
        step *= 2
    tail = totals[16:24]
    return (
        encoded,
        images_grad,
        shares[3],
        tail[2:4][None],
        shares[2],
        totals[24:24 + heads, :entries].T[None],
        jnp.stack([totals[SUM_SCALE_A], totals[SUM_SCALE_B]])[None],
        jnp.stack([tail[0], totals[SUM_GAIN_B]])[None],
        jnp.stack([tail[1], totals[SUM_SHIFT_B]])[None],
        shares[1],
        totals[FC1_BIAS:bias_at].reshape(1, -1),
        shares[0],
        jnp.stack([totals[SUM_DA], totals[SUM_DF]])[None],
    )


def solution(mesh):
    by_layer = P("narrow", None, None)
    by_rows = P("wide", "narrow", None)
    by_both = P("narrow", "wide", None)
    in_specs = (by_rows, by_rows, P("wide", None), P("wide", None, None)) + (by_layer,) * 8 + (
        P("narrow", None), by_layer, by_layer)
    out_specs = (by_rows, by_rows, by_both, by_layer, by_both, by_layer, by_layer, by_layer, by_layer, by_both,
                 P("narrow", None), by_both, by_layer)
    return jax.shard_map(shards, mesh=mesh, in_specs=in_specs, out_specs=out_specs, check_vma=False)
```

```python
import functools

import jax
import jax.numpy as jnp
from jax import lax
from jax.experimental import pallas as pl
from jax.experimental.pallas import tpu as pltpu
from jax.sharding import PartitionSpec as P

EPSILON = 1e-06
HALF_ROOT = 0.7071067811865476
DENSITY_NORM = 0.3989422804014327
GRID = 14
SPAN = 2 * GRID - 1
PITCH = 16
SLOTS = GRID * PITCH
LANES = 256
CLASS_SLOT = 15
WIDE = 32
STRIP = 512
HEAD_ROWS = 16
F32 = jnp.float32
BF16 = jnp.bfloat16
NEGATIVE = -1000000000.0
LAG = 3
LAG_BACK = 2
TILE = 80

GAIN_A, SHIFT_A, GAIN_B, SHIFT_B, SCALE_A, SCALE_B, OUT_A, OUT_B, FC1_BIAS = range(9)
SUM_DF, SUM_SCALE_B, SUM_GAIN_B, SUM_SHIFT_B, SUM_DA, SUM_SCALE_A = range(6)


def nn(a, b):
    return lax.dot_general(a, b, (((1,), (0,)), ((), ())), preferred_element_type=F32)


def nt(a, b):
    return lax.dot_general(a, b, (((1,), (1,)), ((), ())), preferred_element_type=F32)


def tn(a, b):
    return lax.dot_general(a, b, (((0,), (0,)), ((), ())), preferred_element_type=F32)


def exact(a, b, dims):
    return lax.dot_general(a, b, (dims, ((), ())), precision=lax.Precision.HIGHEST, preferred_element_type=F32)


def iota(shape, axis):
    return lax.broadcasted_iota(jnp.int32, shape, axis)


def row_tile(t):
    return pl.ds(pl.multiple_of(t * TILE, 16), TILE)


def vec(vec_ref, k):
    return vec_ref[k:k + 1, :]


def row_stats(v):
    centred = v - jnp.mean(v, axis=-1, keepdims=True)
    inverse = lax.rsqrt(jnp.mean(centred * centred, axis=-1, keepdims=True) + EPSILON)
    return centred * inverse, inverse


def norm_tiles(src_ref, dst_ref, vec_ref, gain, shift):
    @pl.loop(0, src_ref.shape[0] // TILE)
    def _(t):
        rows = row_tile(t)
        unit, _ = row_stats(src_ref[rows, :].astype(F32))
        dst_ref[rows, :] = (unit * vec(vec_ref, gain) + vec(vec_ref, shift)).astype(BF16)


def extra_rows(first, lanes):
    row = iota((16, lanes), 0)
    out = jnp.zeros((16, lanes), F32)
    for k, value in enumerate(first):
        out = jnp.where(row == k, value, out)
    return out.astype(BF16)


def split3(v):
    hi = v.astype(BF16).astype(F32)
    mid = (v - hi).astype(BF16).astype(F32)
    return hi, mid, v - hi - mid


def attn_fwd_kernel(keep, pick_ref, ws_ref, x_ref, vec_ref, own_ref, other_ref, bias_ref, b_ref, et_ref, mask_ref,
                    o_ref, *rest):
    if keep:
        n1_ref, zt_ref, ot_ref, lse_ref, wt, n1t, sem = rest
    else:
        n1_ref, zt_ref, ot_ref, wt, n1t, sem = rest
    heads = b_ref.shape[0]
    width = x_ref.shape[1]
    hd = width // heads
    i = pl.program_id(0)

    @pl.when(i == 0)
    def _():
        @pl.when(pick_ref[0] == 1)
        def _():
            pltpu.make_async_copy(own_ref, wt, sem).start()

        @pl.when(pick_ref[0] == 0)
        def _():
            pltpu.make_async_copy(other_ref, wt, sem).start()

        o_ref[...] = jnp.zeros_like(o_ref)
        norm_tiles(x_ref, n1_ref, vec_ref, GAIN_A, SHIFT_A)
        pltpu.make_async_copy(own_ref, wt, sem).wait()

    ws = pl.multiple_of(ws_ref[i], 16)
    n1t[...] = tn(n1_ref[pl.ds(ws, SLOTS), :], et_ref[0]).astype(BF16)

    @pl.loop(0, 3)
    def _(c):
        rows = pl.ds(pl.multiple_of(c * width, width), width)
        factor = jnp.where(c == 0, hd ** -0.5, 1.0)
        zt_ref[0, rows, :] = ((nn(wt[rows, :], n1t[...]) + bias_ref[rows, :]) * factor).astype(BF16)

    ones_q = extra_rows([1.0], LANES)
    mask_k = extra_rows([mask_ref[0]], SLOTS)
    ones_v = extra_rows([1.0], SLOTS)

    def scores(h):
        r = h * hd
        qt = jnp.concatenate([zt_ref[0, r:r + hd, :], ones_q], axis=0)
        kt = jnp.concatenate([zt_ref[0, width + r:width + r + hd, :SLOTS], mask_k], axis=0)
        return tn(kt, qt)

    def soft(h, s):
        s = s + b_ref[h]
        m = jnp.max(s, axis=0, keepdims=True)
        return m, jnp.exp(s - m).astype(BF16)

    def finish(h, m, e):
        r = h * hd
        vt = jnp.concatenate([zt_ref[0, 2 * width + r:2 * width + r + hd, :SLOTS], ones_v], axis=0)
        o = nn(vt, e)
        total = o[hd:hd + 1]
        ot_ref[0, r:r + hd, :] = (o[:hd] * (1.0 / total)).astype(BF16)
        if keep:
            lse_ref[0, h:h + 1, :] = m + jnp.log(total)

    s, e = {}, {}
    for t in range(heads + 2 * LAG):
        if t < heads:
            s[t] = scores(t)
        if 0 <= t - LAG < heads:
            e[t - LAG] = soft(t - LAG, s.pop(t - LAG))
        if t - 2 * LAG >= 0:
            finish(t - 2 * LAG, *e.pop(t - 2 * LAG))

    win = pl.ds(ws, SLOTS)
    o_ref[win, :] = (o_ref[win, :].astype(F32) + nt(et_ref[0], ot_ref[0])).astype(BF16)


def attn_bwd_kernel(want, pick_ref, ws_ref, da_ref, own_ref, other_ref, b_ref, et_ref, mask_ref, zt_ref, ot_ref,
                    lse_ref, dz_ref, *rest):
    if want:
        db_ref, dat, dot, dzt = rest
    else:
        dat, dot, dzt = rest
    heads = b_ref.shape[0]
    width = da_ref.shape[1]
    hd = width // heads
    i = pl.program_id(0)

    @pl.when(i == 0)
    def _():
        dz_ref[...] = jnp.zeros_like(dz_ref)
        if want:
            db_ref[...] = jnp.zeros_like(db_ref)
        dzt[...] = jnp.zeros_like(dzt)

    ws = pl.multiple_of(ws_ref[i], 16)
    win = pl.ds(ws, SLOTS)
    dat[...] = tn(da_ref[win, :], et_ref[0]).astype(BF16)
    proj = jnp.where(pick_ref[0] == 1, own_ref[...], other_ref[...])
    dot[...] = nn(proj, dat[...]).astype(BF16)
    extra_k = extra_rows([mask_ref[0], 1.0, 1.0, 1.0], SLOTS)
    extra_v = extra_rows([1.0, 1.0, 1.0], SLOTS)

    def parts(h):
        r = h * hd
        return (zt_ref[0, r:r + hd, :], zt_ref[0, width + r:width + r + hd, :SLOTS],
                zt_ref[0, 2 * width + r:2 * width + r + hd, :SLOTS], dot[r:r + hd, :])

    def products(h):
        qt, kt, vt, dt = parts(h)
        r = h * hd
        delta = jnp.sum(dt.astype(F32) * ot_ref[0, r:r + hd, :].astype(F32), axis=0, keepdims=True)
        extra_q = extra_rows([1.0, *split3(-lse_ref[0, h:h + 1, :])], LANES)
        extra_d = extra_rows(split3(-delta), LANES)
        s = tn(jnp.concatenate([kt, extra_k], axis=0), jnp.concatenate([qt, extra_q], axis=0))
        dp = tn(jnp.concatenate([vt, extra_v], axis=0), jnp.concatenate([dt, extra_d], axis=0))
        return s, dp

    def middle(h, s, dp):
        p = jnp.exp(s + b_ref[h])
        ds = p * dp
        if want:
            db_ref[h] += ds
        return p.astype(BF16), ds.astype(BF16)

    def finish(h, p, ds):
        qt, kt, vt, dt = parts(h)
        r = h * hd
        dzt[2 * width + r:2 * width + r + hd, :SLOTS] = nt(dt, p).astype(BF16)
        dzt[width + r:width + r + hd, :SLOTS] = nt(qt, ds).astype(BF16)
        dzt[r:r + hd, :] = (nn(kt, ds) * hd ** -0.5).astype(BF16)

    s, e = {}, {}
    for t in range(heads + 2 * LAG_BACK):
        if t < heads:
            s[t] = products(t)
        if 0 <= t - LAG_BACK < heads:
            e[t - LAG_BACK] = middle(t - LAG_BACK, *s.pop(t - LAG_BACK))
        if t - 2 * LAG_BACK >= 0:
            finish(t - 2 * LAG_BACK, *e.pop(t - 2 * LAG_BACK))

    for c in range(3):
        cols = slice(c * width, (c + 1) * width)
        dz_ref[win, cols] = (dz_ref[win, cols].astype(F32) + nt(et_ref[0], dzt[cols, :])).astype(BF16)


def spread(count):
    entry = iota((count, SPAN * WIDE), 0)
    lane = iota((count, SPAN * WIDE), 1)
    return jnp.where((entry == lane // WIDE * SPAN + lane % WIDE) & (lane % WIDE < SPAN), 1.0, 0.0).astype(F32)


def squeeze():
    lane = iota((SPAN * WIDE, STRIP), 0)
    to = iota((SPAN * WIDE, STRIP), 1)
    return jnp.where(lane == to // PITCH * WIDE + to % PITCH, 1.0, 0.0).astype(F32)


def bias_kernel(table_ref, b_ref, shifted, strips):
    heads = b_ref.shape[0]
    table = table_ref[...]
    wide = exact(table, spread(table.shape[1]), ((1,), (0,)))
    for c in range(PITCH):
        shifted[c * HEAD_ROWS:(c + 1) * HEAD_ROWS, :] = pltpu.roll(wide, (c - GRID + 1) % (SPAN * WIDE), 1)
    packed = exact(shifted[...], squeeze(), ((1,), (0,)))
    for k in range(strips.shape[0]):
        strips[k] = packed[:, k * 128:(k + 1) * 128]
    row = iota((SLOTS, LANES), 0)
    col = iota((SLOTS, LANES), 1)
    for h in range(heads):
        strip = jnp.concatenate([strips[k, pl.ds(h, PITCH, stride=HEAD_ROWS), :] for k in range(strips.shape[0])], axis=1)
        for r in range(GRID):
            at = PITCH * (GRID - 1 - r)
            b_ref[h, r * PITCH:(r + 1) * PITCH, :] = strip[:, at:at + LANES]
        query, key, both = [table_ref[h:h + 1, SPAN * SPAN + k:SPAN * SPAN + k + 1] for k in range(3)]
        full = jnp.where(col == CLASS_SLOT, query, b_ref[h])
        b_ref[h] = jnp.where(row == CLASS_SLOT, jnp.where(col == CLASS_SLOT, both, key), full)


def bias_back_kernel(db_ref, table_ref, strips, classes):
    heads = db_ref.shape[0]
    row = iota((SLOTS, LANES), 0)
    col = iota((SLOTS, LANES), 1)
    is_row = row == CLASS_SLOT
    is_col = col == CLASS_SLOT
    entry = iota((1, table_ref.shape[1]), 1) - SPAN * SPAN
    strips[...] = jnp.zeros_like(strips)
    classes[...] = jnp.zeros_like(classes)
    for h in range(heads):
        full = db_ref[h]
        query = jnp.sum(jnp.where(is_col & ~is_row, full, 0.0), keepdims=True)
        key = jnp.sum(jnp.where(is_row & ~is_col, full, 0.0), keepdims=True)
        both = jnp.sum(jnp.where(is_row & is_col, full, 0.0), keepdims=True)
        classes[h:h + 1, :] = jnp.where(entry == 0, query, jnp.where(entry == 1, key, jnp.where(entry == 2, both, 0.0)))
        plain = jnp.where(is_row | is_col, 0.0, full)
        total = jnp.zeros((PITCH, STRIP), F32)
        for r in range(GRID):
            part = jnp.concatenate([plain[r * PITCH:(r + 1) * PITCH, :], jnp.zeros((PITCH, STRIP - LANES), F32)],
                                   axis=1)
            total = total + pltpu.roll(part, PITCH * (GRID - 1 - r), 1)
        for k in range(strips.shape[0]):
            strips[k, pl.ds(h, PITCH, stride=HEAD_ROWS), :] = total[:, k * 128:(k + 1) * 128]
    wide = exact(jnp.concatenate([strips[k] for k in range(strips.shape[0])], axis=1), squeeze(), ((1,), (1,)))
    gathered = jnp.zeros((HEAD_ROWS, SPAN * WIDE), F32)
    for c in range(GRID):
        gathered = gathered + pltpu.roll(wide[c * HEAD_ROWS:(c + 1) * HEAD_ROWS, :], (GRID - 1 - c) % (SPAN * WIDE), 1)
    table_ref[...] = exact(gathered, spread(table_ref.shape[1]), ((1,), (1,))) + classes[...]


def mlp_fwd_kernel(keep, pick_ref, x_ref, o_ref, proj_own, proj_other, vec_ref, fc1_own, fc1_other, fc2_own, fc2_other,
                   y_ref, *rest):
    if keep:
        m_ref, n2_ref, a_ref, f_ref, g_ref, slope_ref, acc = rest
    else:
        m_ref, n2_ref, acc = rest
    j = pl.program_id(0)
    mine = pick_ref[0] == 1

    @pl.when(j == 0)
    def _():
        a = nn(o_ref[...], jnp.where(mine, proj_own[...], proj_other[...])) + vec(vec_ref, OUT_A)
        if keep:
            a_ref[...] = a.astype(BF16)
        m_ref[...] = x_ref[...].astype(F32) + vec(vec_ref, SCALE_A) * a
        acc[...] = jnp.zeros_like(acc)
        norm_tiles(m_ref, n2_ref, vec_ref, GAIN_B, SHIFT_B)

    u = nn(n2_ref[...], jnp.where(mine, fc1_own[...], fc1_other[...])) + vec_ref[pl.ds(FC1_BIAS + j, 1), :]
    cdf = 0.5 * (1.0 + lax.erf(u * HALF_ROOT))
    g = (u * cdf).astype(BF16)
    if keep:
        g_ref[...] = g
        slope_ref[...] = (cdf + u * (jnp.exp(-0.5 * u * u) * DENSITY_NORM)).astype(BF16)
    acc[...] += nn(g, jnp.where(mine, fc2_own[...], fc2_other[...]))

    @pl.when(j == pl.num_programs(0) - 1)
    def _():
        @pl.loop(0, acc.shape[0] // TILE)
        def _(t):
            rows = row_tile(t)
            f = acc[rows, :] + vec(vec_ref, OUT_B)
            if keep:
                f_ref[rows, :] = f.astype(BF16)
            y_ref[rows, :] = (m_ref[rows, :] + vec(vec_ref, SCALE_B) * f).astype(BF16)


def norm_back_tiles(count, src_ref, grad_ref, vec_ref, gain, emit):
    def body(t, sums):
        rows = row_tile(t)
        unit, inverse = row_stats(src_ref[rows, :].astype(F32))
        grad = grad_ref[rows, :]
        scaled = grad * vec(vec_ref, gain)
        mean_one = jnp.mean(scaled, axis=-1, keepdims=True)
        mean_two = jnp.mean(scaled * unit, axis=-1, keepdims=True)
        more = emit(rows, inverse * (scaled - mean_one - unit * mean_two))
        if not count:
            return sums
        return tuple(s + jnp.sum(v, axis=0, keepdims=True) for s, v in zip(sums, (grad * unit, grad) + more))

    zero = jnp.zeros((1, grad_ref.shape[1]), F32)
    return lax.fori_loop(0, grad_ref.shape[0] // TILE, body, (zero,) * count)


def mlp_bwd_kernel(want, pick_ref, dy_ref, m_ref, vec_ref, slope_ref, fc1_own, fc1_other, fc2_own, fc2_other, *rest):
    if want:
        (n2_ref, g_ref, a_ref, f_ref, dm_ref, da_ref, fc1_give, fc1_keep, fc2_give, fc2_keep, sums_ref, df, acc) = rest
    else:
        dm_ref, da_ref, df, acc = rest
    j = pl.program_id(0)
    steps = pl.num_programs(0)
    mine = pick_ref[0] == 1
    core = pick_ref[1]
    width = dy_ref.shape[1]

    @pl.when(j == 0)
    def _():
        acc[...] = jnp.zeros_like(acc)
        if want:
            sums_ref[...] = jnp.zeros_like(sums_ref)
        zero = jnp.zeros((1, width), F32)

        def body(t, sums):
            rows = row_tile(t)
            dy = dy_ref[rows, :].astype(F32)
            scaled = (dy * vec(vec_ref, SCALE_B)).astype(BF16)
            df[rows, :] = scaled
            if not want:
                return sums
            return (sums[0] + jnp.sum(scaled.astype(F32), axis=0, keepdims=True),
                    sums[1] + jnp.sum(dy * f_ref[rows, :].astype(F32), axis=0, keepdims=True))

        sums = lax.fori_loop(0, df.shape[0] // TILE, body, (zero, zero) if want else ())
        if want:
            sums_ref[SUM_DF:SUM_DF + 1, :] = sums[0]
            sums_ref[SUM_SCALE_B:SUM_SCALE_B + 1, :] = sums[1]

    fc1 = jnp.where(mine, fc1_own[...], fc1_other[...])
    fc2 = jnp.where(mine, fc2_own[...], fc2_other[...])
    du = (nt(df[...], fc2) * slope_ref[...].astype(F32)).astype(BF16)
    acc[...] += nt(du, fc1)
    if want:
        at = lax.rem(j + (1 - core) * (steps // 2), steps)
        sums_ref[pl.ds(FC1_BIAS + at, 1), :] = jnp.sum(du.astype(F32), axis=0, keepdims=True)
        grad = tn(g_ref[...], df[...]).astype(BF16)
        low, high = grad[:, :width // 2], grad[:, width // 2:]
        fc2_keep[...] = jnp.where(core == 0, low, high)
        fc2_give[...] = jnp.where(core == 0, high, low)
        grad1 = tn(n2_ref[...], du).astype(BF16)

        @pl.when(j < steps // 2)
        def _():
            fc1_give[...] = grad1

        @pl.when(j >= steps // 2)
        def _():
            fc1_keep[...] = grad1

    @pl.when(j == steps - 1)
    def _():
        def emit(rows, dv):
            dm = dy_ref[rows, :].astype(F32) + dv
            da = (dm * vec(vec_ref, SCALE_A)).astype(BF16)
            dm_ref[rows, :] = dm
            da_ref[rows, :] = da
            return (da.astype(F32), dm * a_ref[rows, :].astype(F32)) if want else ()

        sums = norm_back_tiles(4 if want else 0, m_ref, acc, vec_ref, GAIN_B, emit)
        for k, s in zip((SUM_GAIN_B, SUM_SHIFT_B, SUM_DA, SUM_SCALE_A), sums):
            sums_ref[k:k + 1, :] = s


def attn_tail_kernel(want, pick_ref, x_ref, dm_ref, vec_ref, dz_ref, wt_own, wt_other, *rest):
    if want:
        n1_ref, o_ref, da_ref, dx_ref, give_ref, keep_ref, bias_ref, sums_ref, acc = rest
    else:
        dx_ref, acc = rest
    j = pl.program_id(0)
    core = pick_ref[1]
    width = x_ref.shape[1]

    @pl.when(j == 0)
    def _():
        acc[...] = jnp.zeros_like(acc)
        if want:
            sums_ref[...] = jnp.zeros_like(sums_ref)
            grad = tn(o_ref[...], da_ref[...]).astype(BF16)
            low, high = grad[:, :width // 2], grad[:, width // 2:]
            keep_ref[:, 3 * width // 2:] = jnp.where(core == 0, low, high)
            give_ref[:, 3 * width // 2:] = jnp.where(core == 0, high, low)

    dz = dz_ref[...]
    acc[...] += nn(dz, jnp.where(pick_ref[0] == 1, wt_own[...], wt_other[...]))
    if want:
        bias_ref[0] = jnp.broadcast_to(jnp.sum(dz.astype(F32), axis=0, keepdims=True), bias_ref.shape[1:])
        grad1 = tn(n1_ref[...], dz).astype(BF16)

        @pl.when(j == 0)
        def _():
            give_ref[:, :3 * width // 2] = grad1

        @pl.when(j == 1)
        def _():
            keep_ref[:, :3 * width // 2] = grad1

    @pl.when(j == pl.num_programs(0) - 1)
    def _():
        def emit(rows, dv):
            dx_ref[rows, :] = (dm_ref[rows, :] + dv).astype(BF16)
            return ()

        sums = norm_back_tiles(2 if want else 0, x_ref, acc, vec_ref, GAIN_A, emit)
        for k, s in enumerate(sums):
            sums_ref[k:k + 1, :] = s


TAKES = dict(attn_fwd=20, attn_fwd_keep=21, mlp_fwd=15, mlp_fwd_keep=19, mlp_bwd=15, mlp_bwd_all=27, attn_bwd=20,
             attn_bwd_all=21, attn_tail=9, attn_tail_all=16, bias_build=6, bias_back=9)


VMEM = dict(attn_fwd=60, attn_fwd_keep=60, mlp_fwd=60, mlp_fwd_keep=60, mlp_bwd=60, mlp_bwd_all=60, attn_bwd=60,
            attn_bwd_all=60, attn_tail=60, attn_tail_all=60, bias_build=60, bias_back=60)


def cost(name):
    return pl.CostEstimate(flops=TAKES[name] * 800_000_000, bytes_accessed=TAKES[name] * 3_000_000, transcendentals=0)


def params(name):
    return pltpu.CompilerParams(vmem_limit_bytes=VMEM[name] * 1024 * 1024)


def shaped(*arrays):
    return [jax.ShapeDtypeStruct(s, d) for s, d in arrays]


def whole(shape):
    return pl.BlockSpec(shape, lambda *_: (0,) * len(shape))


def once(shape):
    return pl.BlockSpec(shape, lambda *_: (0,) * len(shape), pipeline_mode=pl.Buffered(1))


def per_image(shape):
    return pl.BlockSpec((1,) + shape, lambda i, *_: (i,) + (0,) * len(shape))


def call(kernel, name, prefetched, grid, inputs, outputs, scratch, after=()):
    count = len(prefetched) + len(inputs)

    def body(*refs):
        kernel(*refs[:count], *refs[count + len(after):])

    inputs = inputs + [(a, pl.BlockSpec(memory_space=pl.ANY)) for a in after]
    return pl.pallas_call(
        body,
        grid_spec=pltpu.PrefetchScalarGridSpec(
            num_scalar_prefetch=len(prefetched), grid=grid, in_specs=[s for _, s in inputs],
            out_specs=[s for _, _, s in outputs], scratch_shapes=scratch),
        out_shape=[jax.ShapeDtypeStruct(s, d) for s, d, _ in outputs],
        compiler_params=params(name), name=name, cost_estimate=cost(name),
    )(*prefetched, *[a for a, _ in inputs])


def attn_fwd(keep, x, w, meta):
    ws, et, mask = meta
    rows, width = x.shape
    heads = w["bias"].shape[0]
    imgs = et.shape[0]
    anywhere = pl.BlockSpec(memory_space=pl.ANY)
    inputs = [(x, once(x.shape)), (w["vectors"], once(w["vectors"].shape)), (w["qkv_t"][0], anywhere),
              (w["qkv_t"][1], anywhere), (w["qkv_bias"], once(w["qkv_bias"].shape)), (w["bias"], once(w["bias"].shape)),
              (et, per_image(et.shape[1:])), (mask, per_image(mask.shape[1:]))]
    outputs = [((rows, width), BF16, whole((rows, width)))]
    scratch = [pltpu.VMEM((3 * width, width), BF16), pltpu.VMEM((width, LANES), BF16), pltpu.SemaphoreType.DMA]
    if keep:
        outputs += [((rows, width), BF16, whole((rows, width))),
                    ((imgs, 3 * width, LANES), BF16, per_image((3 * width, LANES))),
                    ((imgs, width, LANES), BF16, per_image((width, LANES))),
                    ((imgs, heads, LANES), F32, per_image((heads, LANES)))]
    else:
        scratch = [pltpu.VMEM((rows, width), BF16), pltpu.VMEM((1, 3 * width, LANES), BF16),
                   pltpu.VMEM((1, width, LANES), BF16)] + scratch
    return call(functools.partial(attn_fwd_kernel, keep), "attn_fwd_keep" if keep else "attn_fwd", [w["pick"], ws],
                (imgs,), inputs, outputs, scratch)


def attn_bwd(want, da, w, meta, kept, after=()):
    ws, et, mask = meta
    rows, width = da.shape
    bias = w["bias"]
    imgs = et.shape[0]
    single_proj = once((width, width))
    zt, ot, lse = kept["zt"], kept["ot"], kept["lse"]
    inputs = [(da, once(da.shape)), (w["proj"][0], single_proj), (w["proj"][1], single_proj), (bias, once(bias.shape)),
              (et, per_image(et.shape[1:])), (mask, per_image(mask.shape[1:])), (zt, per_image(zt.shape[1:])),
              (ot, per_image(ot.shape[1:])), (lse, per_image(lse.shape[1:]))]
    outputs = [((rows, 3 * width), BF16, whole((rows, 3 * width)))]
    if want:
        outputs += [(bias.shape, F32, whole(bias.shape))]
    scratch = [pltpu.VMEM((width, LANES), BF16), pltpu.VMEM((width, LANES), BF16), pltpu.VMEM((3 * width, LANES), BF16)]
    return call(functools.partial(attn_bwd_kernel, want), "attn_bwd_all" if want else "attn_bwd", [w["pick"], ws],
                (imgs,), inputs, outputs, scratch, after)


def build_bias(table):
    heads = 12
    return pl.pallas_call(
        bias_kernel, out_shape=jax.ShapeDtypeStruct((heads, SLOTS, LANES), F32),
        scratch_shapes=[pltpu.VMEM((PITCH * HEAD_ROWS, SPAN * WIDE), F32), pltpu.VMEM((STRIP // 128, PITCH * HEAD_ROWS, 128), F32)],
        compiler_params=params("bias_build"), name="bias_build", cost_estimate=cost("bias_build"),
    )(table)


def table_back(db, lanes, after=()):
    return call(bias_back_kernel, "bias_back", [], (1,), [(db, once(db.shape))],
                [((HEAD_ROWS, lanes), F32, whole((HEAD_ROWS, lanes)))],
                [pltpu.VMEM((STRIP // 128, PITCH * HEAD_ROWS, 128), F32), pltpu.VMEM((HEAD_ROWS, lanes), F32)], after)[0]


def chosen(which, block, to_index):
    def index(j, pick):
        used = pick[0] if which == 0 else 1 - pick[0]
        return tuple(k * used for k in to_index(j, pick))
    return pl.BlockSpec(block, index)


def both(pair, block, to_index):
    return [(pair[k], chosen(k, block, to_index)) for k in range(2)]


def mlp_fwd(keep, x, o, w):
    rows, width = x.shape
    hidden = w["fc1"][0].shape[1]
    full = whole((rows, width))
    single = once((rows, width))
    single_proj = once((width, width))
    inputs = [(x, single), (o, single), (w["proj"][0], single_proj), (w["proj"][1], single_proj),
              (w["vectors"], once(w["vectors"].shape)),
              *both(w["fc1"], (width, width), lambda j, p: (0, j)), *both(w["fc2"], (width, width), lambda j, p: (j, 0))]
    outputs = [((rows, width), BF16, full)]
    scratch = [pltpu.VMEM((rows, width), F32)]
    if keep:
        part = pl.BlockSpec((rows, width), lambda j, p: (0, j))
        outputs += [((rows, width), F32, full)] + [((rows, width), BF16, full)] * 3 + [((rows, hidden), BF16, part)] * 2
    else:
        scratch = [pltpu.VMEM((rows, width), F32), pltpu.VMEM((rows, width), BF16)] + scratch
    return call(functools.partial(mlp_fwd_kernel, keep), "mlp_fwd_keep" if keep else "mlp_fwd", [w["pick"]],
                (hidden // width,), inputs, outputs, scratch)


def mlp_bwd(want, dy, w, kept):
    rows, width = dy.shape
    hidden = w["fc1"][0].shape[1]
    steps = hidden // width
    full = whole((rows, width))
    single = once((rows, width))

    def at(j, pick):
        return lax.rem(j + (1 - pick[1]) * (steps // 2), steps)

    part = pl.BlockSpec((rows, width), lambda j, p: (0, at(j, p)))
    inputs = [(dy, single), (kept["m"], single), (w["vectors"], once(w["vectors"].shape)), (kept["slope"], part),
              *both(w["fc1"], (width, width), lambda j, p: (0, at(j, p))),
              *both(w["fc2"], (width, width), lambda j, p: (at(j, p), 0))]
    outputs = [((rows, width), F32, full), ((rows, width), BF16, full)]
    if want:
        inputs += [(kept["n2"], single), (kept["g"], part), (kept["a"], single), (kept["f"], single)]
        half = pl.BlockSpec((width, width // 2), lambda j, p: (at(j, p), 0))
        give = pl.BlockSpec((width, width), lambda j, p: (0, jnp.minimum(j, steps // 2 - 1)))
        stay = pl.BlockSpec((width, width), lambda j, p: (0, jnp.maximum(j - steps // 2, 0)))
        outputs += [((width, hidden // 2), BF16, give), ((width, hidden // 2), BF16, stay),
                    ((hidden, width // 2), BF16, half), ((hidden, width // 2), BF16, half),
                    ((16, width), F32, whole((16, width)))]
    scratch = [pltpu.VMEM((rows, width), BF16), pltpu.VMEM((rows, width), F32)]
    return call(functools.partial(mlp_bwd_kernel, want), "mlp_bwd_all" if want else "mlp_bwd", [w["pick"]],
                (steps,), inputs, outputs, scratch)


def attn_tail(want, x, dm, dz, da, w, kept, after=()):
    rows, width = x.shape
    part = 3 * width // 2
    full = whole((rows, width))
    single = once((rows, width))

    def at(j, pick):
        return lax.rem(j + 1 - pick[1], 2)

    inputs = [(x, single), (dm, single), (w["vectors"], once(w["vectors"].shape)),
              (dz, pl.BlockSpec((rows, part), lambda j, p: (0, at(j, p)))),
              *both(w["qkv_t"], (part, width), lambda j, p: (at(j, p), 0))]
    outputs = [((rows, width), BF16, full)]
    if want:
        inputs += [(kept["n1"], single), (kept["o"], single), (da, single)]
        outputs += [((width, 2 * width), BF16, whole((width, 2 * width)))] * 2
        outputs += [((2, 8, part), F32, pl.BlockSpec((1, 8, part), lambda j, p: (at(j, p), 0, 0))),
                    ((8, width), F32, whole((8, width)))]
    return call(functools.partial(attn_tail_kernel, want), "attn_tail_all" if want else "attn_tail", [w["pick"]],
                (2,), inputs, outputs, [pltpu.VMEM((rows, width), F32)], after)


def sequence_meta(ids, order, rows):
    imgs, patches = order.shape
    image = jnp.arange(imgs, dtype=jnp.int32)
    start = jnp.sum((ids[None, :] < image[:, None]).astype(jnp.int32), axis=1)
    count = jnp.sum((ids[None, :] == image[:, None]).astype(jnp.int32), axis=1)
    ws = jnp.minimum(start // 16 * 16, rows - SLOTS)
    slot = jnp.arange(LANES, dtype=jnp.int32)
    is_class = slot == CLASS_SLOT
    is_patch = (slot % PITCH < GRID) & (slot < SLOTS)
    patch = jnp.where(is_patch, slot // PITCH * GRID + slot % PITCH, -1)
    place = jnp.arange(1, patches + 1, dtype=jnp.int32)
    offset = jnp.sum(jnp.where(order[:, None, :] == patch[None, :, None], place, 0), axis=2)
    valid = (is_class | is_patch)[None, :] & (offset < count[:, None])
    local = jnp.where(valid, offset + (start - ws)[:, None], -1)
    row = jnp.arange(SLOTS, dtype=jnp.int32)
    et = (local[:, None, :] == row[None, :, None]).astype(BF16)
    mask = jnp.where(valid, 0.0, NEGATIVE).astype(F32)[:, None, :SLOTS]
    return ws, et, mask


def layer_forward(x, w, meta, keep):
    out = attn_fwd(keep, x, w, meta)
    if not keep:
        return mlp_fwd(False, x, out[0], w)[0], None
    o, n1, zt, ot, lse = out
    y, m, n2, a, f, g, slope = mlp_fwd(True, x, o, w)
    return y, dict(x=x, n1=n1, o=o, zt=zt, ot=ot, lse=lse, a=a, m=m, n2=n2, g=g, slope=slope, f=f)


def layer_back(dy, w, kept, meta):
    dm, da = mlp_bwd(False, dy, w, kept)
    dz = attn_bwd(False, da, w, meta, kept)[0]
    return attn_tail(False, kept["x"], dm, dz, da, w, kept)[0]


def later(arrays, token):
    if token is None:
        return list(arrays)
    return list(lax.optimization_barrier((*arrays, token)))[:-1]


class Reducer:
    def __init__(self, keep, give, swap_core, swap_wide, at_wide, wide):
        self.shape = (keep.shape[0] // wide, keep.shape[1])
        self.keep, self.got = keep, swap_core(give)
        self.swap_wide, self.at_wide = swap_wide, at_wide
        self.left, self.bit = wide, 1
        self.sent = []

    def parts(self):
        return [v.reshape((self.left,) + self.shape) for v in (self.keep, self.got)]

    def step(self, token=None):
        if self.left == 1:
            return
        mine = self.at_wide // self.bit % 2
        self.got, = later([self.got], token)
        pair = [v.reshape((self.left // 2, 2) + self.shape) for v in self.parts()]
        part = [[lax.dynamic_index_in_dim(v, k, 1, keepdims=False).astype(F32) for v in pair] for k in (1 - mine, mine)]
        self.sent = [(part[0][0] + part[0][1]).astype(BF16)]
        self.keep = (part[1][0] + part[1][1]).astype(BF16)
        self.got = self.swap_wide(self.sent[0], self.bit)
        self.left, self.bit = self.left // 2, 2 * self.bit

    def finish(self, token=None):
        while self.left > 1:
            self.step(token)
        self.got, = later([self.got], token)
        keep, got = self.parts()
        return keep[0].astype(F32) + got[0].astype(F32)


def last_sums_kernel(counts, swaps, *refs):
    arrays = len(counts)
    parts = refs[:2 * arrays]
    small_ref = refs[2 * arrays]
    outs = refs[2 * arrays + 1:3 * arrays + 1]
    small_out = refs[3 * arrays + 1]
    scratch = list(refs[3 * arrays + 2:])
    send_sem, recv_sem, local_sem = scratch[-3:]
    small_got = scratch[-4]
    bufs = [[scratch.pop(0) for _ in range(2 + 3 * (n.bit_length() - 1))] for n in counts]
    me = lax.axis_index("narrow")
    at = lax.axis_index("wide")
    bits = [1, 2, 4]
    half = [at // bit % 2 for bit in bits]
    partners = [{"narrow": me + 1 - 2 * (me % 2)}] + [{"wide": at + bit * (1 - 2 * b)} for bit, b in zip(bits, half)]

    barrier = pltpu.get_barrier_semaphore()
    for partner in partners:
        pl.semaphore_signal(barrier, inc=1, device_id=partner, device_id_type=pl.DeviceIdType.MESH)
    pl.semaphore_wait(barrier, len(partners))

    def remote(src, dst, row, hop):
        return pltpu.make_async_remote_copy(src_ref=src, dst_ref=dst, send_sem=send_sem.at[row, hop],
                                            recv_sem=recv_sem.at[row, hop], device_id=partners[hop],
                                            device_id_type=pl.DeviceIdType.MESH)

    pending = {}

    def begin(k):
        first, second = parts[2 * k], parts[2 * k + 1]
        copies = [pltpu.make_async_copy(first, bufs[k][0], local_sem.at[k, 0])]
        if swaps[k]:
            copies.append(remote(second, bufs[k][1], k, 0))
        else:
            copies.append(pltpu.make_async_copy(second, bufs[k][1], local_sem.at[k, 1]))
        for c in copies:
            c.start()
        pending[k] = copies

    def hop(k, n):
        for c in pending[k]:
            c.wait()
        level = counts[k].bit_length() - n.bit_length()
        mine, got = (bufs[k][0], bufs[k][1]) if level == 0 else bufs[k][2 + 3 * (level - 1) + 1:2 + 3 * level]
        send, stay, come = bufs[k][2 + 3 * level:5 + 3 * level]
        which = 3 - (n.bit_length() - 1)
        b = half[which]

        def add(i, to, index):
            to[i] = (mine[index].astype(F32) + got[index].astype(F32)).astype(BF16)

        @pl.loop(0, n // 2)
        def _(i):
            add(i, send, 2 * i + 1 - b)

        copy = remote(send, come, k, which + 1)
        copy.start()
        pending[k] = [copy]

        @pl.loop(0, n // 2)
        def _(i):
            add(i, stay, 2 * i + b)

    def end(k):
        for c in pending[k]:
            c.wait()
        stay, come = bufs[k][-2:]
        outs[k][...] = stay[0].astype(F32) + come[0].astype(F32)

    small = {}

    def small_send(h):
        copy = remote(small_out, small_got.at[h], arrays, h)
        copy.start()
        small[h] = copy

    def small_take(h):
        small[h].wait()
        small_out[...] += small_got[h]

    fc2, fc1, attn = range(3)
    small_out[...] = small_ref[...]
    small_send(0)
    for k in range(arrays):
        begin(k)
    small_take(0)
    small_send(2)
    hop(fc1, 8)
    hop(fc2, 4)
    hop(attn, 8)
    small_take(2)
    small_send(3)
    hop(fc2, 2)
    small_take(3)
    small_send(1)
    hop(fc1, 4)
    end(fc2)
    hop(fc1, 2)
    hop(attn, 4)
    end(fc1)
    hop(attn, 2)
    small_take(1)
    end(attn)


def last_sums(pairs, swaps, small):
    counts = [p.shape[0] for p, _ in pairs]
    anywhere = pl.BlockSpec(memory_space=pl.ANY)
    vmem = pl.BlockSpec(memory_space=pltpu.VMEM)
    scratch = []
    for (p, _), n in zip(pairs, counts):
        block = p.shape[1:]
        scratch += [pltpu.VMEM((n,) + block, BF16)] * 2
        while n > 1:
            n //= 2
            scratch += [pltpu.VMEM((n,) + block, BF16)] * 3
    scratch += [pltpu.VMEM((4,) + small.shape, F32)]
    scratch += [pltpu.SemaphoreType.DMA((len(pairs) + 1, 4)), pltpu.SemaphoreType.DMA((len(pairs) + 1, 4)),
                pltpu.SemaphoreType.DMA((len(pairs), 2))]
    return pl.pallas_call(
        functools.partial(last_sums_kernel, counts, swaps),
        in_specs=[anywhere] * (2 * len(pairs)) + [vmem],
        out_specs=[vmem] * (len(pairs) + 1),
        out_shape=[jax.ShapeDtypeStruct(p.shape[1:], F32) for p, _ in pairs] + [jax.ShapeDtypeStruct(small.shape, F32)],
        scratch_shapes=scratch,
        compiler_params=pltpu.CompilerParams(vmem_limit_bytes=56 * 1024 * 1024, collective_id=0, has_side_effects=True),
        cost_estimate=pl.CostEstimate(flops=0, bytes_accessed=300_000_000, transcendentals=0), name="last_sums",
    )(*[v for pair in pairs for v in pair], small)


def shards(images, cotangent, image_ids, patch_order, qkv_weight, qv_bias, proj_weight, rel_table, layer_scales,
           layer_norm_gains, norm_biases, fc1_weight, fc1_bias, fc2_weight, out_biases):
    me = lax.axis_index("narrow")
    at_wide = lax.axis_index("wide")
    wide = lax.axis_size("wide")
    core = me % 2
    first = me < 2
    quarter, width = images.shape[1:]
    rows = 4 * quarter
    padded = -(-rows // TILE) * TILE
    entries, heads = rel_table.shape[1:]
    flips = {k: [(d, d ^ k) for d in range(4)] for k in (1, 2, 3)}

    def swap(v, k):
        return lax.ppermute(v, "narrow", flips[k])

    def swap_wide(v, k):
        return lax.ppermute(v, "wide", [(d, d ^ k) for d in range(wide)])

    def pick(v, index):
        return lax.dynamic_index_in_dim(v, index, 0, keepdims=False)

    smalls = jnp.concatenate([layer_norm_gains[0, :1], norm_biases[0, :1], layer_norm_gains[0, 1:], norm_biases[0, 1:],
                              layer_scales[0], out_biases[0], fc1_bias.reshape(-1, width), qv_bias[0],
                              jnp.zeros((2, width), F32)])
    table = jnp.pad(rel_table[0].T, ((0, HEAD_ROWS - heads), (0, width - entries)))
    own = [qkv_weight[0].T, smalls, table, proj_weight[0], fc1_weight[0], fc2_weight[0]]
    other = [swap(v, 1) for v in own]
    bias_at = FC1_BIAS + fc1_bias.shape[1] // width
    weights = []
    for layer in range(2):
        vectors = jnp.where(core == layer, smalls, other[1])
        qkv_bias = jnp.concatenate([vectors[bias_at], jnp.zeros((width,), F32), vectors[bias_at + 1]])
        weights.append(dict(
            pick=jnp.stack([(core == layer).astype(jnp.int32), core]), vectors=vectors, qkv_bias=qkv_bias[:, None],
            bias=build_bias(jnp.where(core == layer, table, other[2])),
            **{name: (own[k], other[k]) for name, k in (("qkv_t", 0), ("proj", 3), ("fc1", 4), ("fc2", 5))}))

    meta = sequence_meta(pick(image_ids, core), pick(patch_order, core), padded)

    mine = jnp.where(first, images, cotangent)
    theirs = jnp.where(first, cotangent, images)
    pieces = [pick(mine, core), swap(pick(mine, 1 - core), 1), swap(pick(theirs, core), 2),
              swap(pick(theirs, 1 - core), 3)]
    rows_in = jnp.zeros((padded, width), BF16)
    for k, piece in enumerate(pieces):
        rows_in = lax.dynamic_update_slice(rows_in, piece, ((me ^ k) * quarter, 0))

    def run_forward(x, keep):
        y, kept_one = layer_forward(x, weights[0], meta, keep)
        y, kept_two = layer_forward(y, weights[1], meta, keep)
        return y, (kept_one, kept_two)

    middle, _ = run_forward(rows_in, False)
    x_in = jnp.where(first, rows_in, swap(middle, 2))
    y_out, kept = run_forward(x_in, True)

    back = layer_back(layer_back(rows_in, weights[1], kept[1], meta), weights[0], kept[0], meta)
    dy_in = jnp.where(first, swap(back, 2), rows_in)

    def reducer(keep, give):
        return Reducer(keep, give, lambda v: swap(v, 1), swap_wide, at_wide, wide)

    def mlp_part(dy, w, kept_one):
        dm, da, fc1_give, fc1_keep, fc2_give, fc2_keep, sums = mlp_bwd(True, dy, w, kept_one)
        return dm, da, [reducer(fc2_keep, fc2_give), reducer(fc1_keep, fc1_give)], sums

    def tail_part(dm, da, dz, w, kept_one, after, start=True):
        dx, give, keep, bias, sums = attn_tail(True, kept_one["x"], dm, dz, da, w, kept_one, after)
        bias = bias[:, 0].reshape(1, -1)
        rows_of = jnp.concatenate([sums[:2], bias[:, :width], bias[:, 2 * width:], jnp.zeros((4, width), F32)])
        halves = (keep, give)
        if start:
            return dx, reducer(*halves), rows_of
        return dx, [v.reshape(wide, -1, v.shape[1]) for v in halves], rows_of

    dm, da, fc_two, sums_two = mlp_part(dy_in, weights[1], kept[1])
    dz, db_two = attn_bwd(True, da, weights[1], meta, kept[1])
    for r in fc_two:
        r.step(dz)
    mid, attn_two, tail_two = tail_part(dm, da, dz, weights[1], kept[1], sum((r.sent for r in fc_two), []))
    dm, da, fc_one, sums_one = mlp_part(mid, weights[0], kept[0])
    for r in fc_two + [attn_two]:
        r.step(da)
    dz, db_one = attn_bwd(True, da, weights[0], meta, kept[0], sum((r.sent for r in fc_two + [attn_two]), []))
    for r in fc_one[:1] + fc_two + [attn_two]:
        r.step(dz)
    dx, attn_one, tail_one = tail_part(dm, da, dz, weights[0], kept[0],
                                       sum((r.sent for r in fc_one[:1] + fc_two + [attn_two]), []), wide != 8)
    small = jnp.concatenate([sums_two, tail_two, table_back(db_two, width, [dx]),
                             sums_one, tail_one, table_back(db_one, width, [dx])])

    result = jnp.where(first, dx, y_out)[:rows].reshape(4, quarter, width)
    same = (pick(result, me), swap(pick(result, me ^ 1), 1))
    across = (swap(pick(result, me ^ 2), 2), swap(pick(result, me ^ 3), 3))
    same = jnp.where(core == 0, jnp.stack(same), jnp.stack(same[::-1]))
    across = jnp.where(core == 0, jnp.stack(across), jnp.stack(across[::-1]))
    encoded = jnp.where(first, across, same)
    images_grad = jnp.where(first, same, across)

    attn_two.step(dx)
    small, = later([small], attn_two.sent[0])
    shares_two = [r.finish(dx) for r in fc_two + [attn_two]]
    if wide == 8:
        ends = [fc_one[0].parts(), fc_one[1].parts(), attn_one]
        *shares_one, small = last_sums(ends, (False, False, True), small)
    else:
        shares_one = [r.finish() for r in fc_one + [attn_one]]
        small = small + swap(small, 1)
        for k in range(wide.bit_length() - 1):
            small = small + swap_wide(small, 1 << k)
    shares = []
    for keep, give in zip(shares_one, shares_two):
        stay = jnp.where(core == 0, keep, give)
        got = swap(jnp.where(core == 0, give, keep).astype(BF16), 1).astype(F32)
        shares.append((jnp.where(core == 0, stay, got), jnp.where(core == 0, got, stay)))
    totals_two, totals_one = small[:40], small[40:]
    fc2, fc1, attn = shares
    qkv = jnp.concatenate([v[:, :3 * width // 2] for v in attn], axis=1)
    proj = jnp.concatenate([v[:, 3 * width // 2:] for v in attn], axis=1)
    totals = jnp.where(core == 0, totals_one, totals_two)
    tail = totals[16:24]
    return (
        encoded,
        images_grad,
        qkv[None],
        tail[2:4][None],
        proj[None],
        totals[24:24 + heads, :entries].T[None],
        jnp.stack([totals[SUM_SCALE_A], totals[SUM_SCALE_B]])[None],
        jnp.stack([tail[0], totals[SUM_GAIN_B]])[None],
        jnp.stack([tail[1], totals[SUM_SHIFT_B]])[None],
        jnp.concatenate(fc1, axis=1)[None],
        totals[FC1_BIAS:bias_at].reshape(1, -1),
        jnp.concatenate(fc2, axis=1)[None],
        jnp.stack([totals[SUM_DA], totals[SUM_DF]])[None],
    )


def solution(mesh):
    by_layer = P("narrow", None, None)
    by_rows = P("wide", "narrow", None)
    by_both = P("narrow", "wide", None)
    in_specs = (by_rows, by_rows, P("wide", None), P("wide", None, None)) + (by_layer,) * 8 + (
        P("narrow", None), by_layer, by_layer)
    out_specs = (by_rows, by_rows, by_both, by_layer, by_both, by_layer, by_layer, by_layer, by_layer, by_both,
                 P("narrow", None), by_both, by_layer)
    return jax.shard_map(shards, mesh=mesh, in_specs=in_specs, out_specs=out_specs, check_vma=False)
```

```python
import functools

import jax
import jax.numpy as jnp
from jax import lax
from jax.experimental import pallas as pl
from jax.experimental.pallas import tpu as pltpu
from jax.sharding import PartitionSpec as P

EPSILON = 1e-06
HALF_ROOT = 0.7071067811865476
DENSITY_NORM = 0.3989422804014327
GRID = 14
SPAN = 2 * GRID - 1
PITCH = 16
SLOTS = GRID * PITCH
LANES = 256
CLASS_SLOT = 15
WIDE = 32
STRIP = 512
HEAD_ROWS = 16
F32 = jnp.float32
BF16 = jnp.bfloat16
NEGATIVE = -1000000000.0
LAG = 3
LAG_BACK = 2
TILE = 80

GAIN_A, SHIFT_A, GAIN_B, SHIFT_B, SCALE_A, SCALE_B, OUT_A, OUT_B, FC1_BIAS = range(9)
QKV_BIAS = 12
SUM_DF, SUM_SCALE_B, SUM_GAIN_B, SUM_SHIFT_B, SUM_DA, SUM_SCALE_A = range(6)


def nn(a, b):
    return lax.dot_general(a, b, (((1,), (0,)), ((), ())), preferred_element_type=F32)


def nt(a, b):
    return lax.dot_general(a, b, (((1,), (1,)), ((), ())), preferred_element_type=F32)


def tn(a, b):
    return lax.dot_general(a, b, (((0,), (0,)), ((), ())), preferred_element_type=F32)


def iota(shape, axis):
    return lax.broadcasted_iota(jnp.int32, shape, axis)


def row_tile(t):
    return pl.ds(pl.multiple_of(t * TILE, 16), TILE)


def vec(vec_ref, k):
    return vec_ref[k:k + 1, :]


def row_stats(v):
    centred = v - jnp.mean(v, axis=-1, keepdims=True)
    inverse = lax.rsqrt(jnp.mean(centred * centred, axis=-1, keepdims=True) + EPSILON)
    return centred * inverse, inverse


def norm_tiles(src_ref, dst_ref, vec_ref, gain, shift):
    @pl.loop(0, src_ref.shape[0] // TILE)
    def _(t):
        rows = row_tile(t)
        unit, _ = row_stats(src_ref[rows, :].astype(F32))
        dst_ref[rows, :] = (unit * vec(vec_ref, gain) + vec(vec_ref, shift)).astype(BF16)


def extra_rows(first, lanes):
    row = iota((16, lanes), 0)
    out = jnp.zeros((16, lanes), F32)
    for k, value in enumerate(first):
        out = jnp.where(row == k, value, out)
    return out.astype(BF16)


def split3(v):
    hi = v.astype(BF16).astype(F32)
    mid = (v - hi).astype(BF16).astype(F32)
    return hi, mid, v - hi - mid


class Weights:
    def __init__(self, core, own, other, dst, sems):
        self.core, self.own, self.other, self.dst, self.sems = core, own, other, dst, sems

    def start(self, name, layer, chunk=None):
        src, slot = (lambda ref: ref), None
        if name == "fc1":
            src = lambda ref: ref.at[:, pl.ds(pl.multiple_of(chunk * ref.shape[0], 128), ref.shape[0])]
        if name == "fc2":
            src = lambda ref: ref.at[pl.ds(pl.multiple_of(chunk * ref.shape[1], 128), ref.shape[1]), :]
        dst, sem = self.place(name, chunk)

        @pl.when(self.core == layer)
        def _():
            pltpu.make_async_copy(src(self.own[name]), dst, sem).start()

        @pl.when(self.core != layer)
        def _():
            pltpu.make_async_copy(src(self.other[name]), dst, sem).start()

    def place(self, name, chunk):
        if chunk is None:
            return self.dst[name], self.sems[name]
        return self.dst[name].at[lax.rem(chunk, 2)], self.sems[name].at[lax.rem(chunk, 2)]

    def wait(self, name, chunk=None):
        dst, sem = self.place(name, chunk)
        pltpu.make_async_copy(dst, dst, sem).wait()

    def start_fc(self, layer, chunk):
        self.start("fc1", layer, chunk)
        self.start("fc2", layer, chunk)


MATRICES = ("qkv", "proj", "fc1", "fc2")


def weight_scratch(width):
    dma = pltpu.SemaphoreType.DMA
    return [pltpu.VMEM((width, 3 * width), BF16), pltpu.VMEM((width, width), BF16),
            pltpu.VMEM((2, width, width), BF16), pltpu.VMEM((2, width, width), BF16), dma, dma, dma((2,)), dma((2,))]


def weights_of(core, refs, scratch):
    return Weights(core, dict(zip(MATRICES, refs[:4])), dict(zip(MATRICES, refs[4:8])), dict(zip(MATRICES, scratch[:4])),
                   dict(zip(MATRICES, scratch[4:8])))


def forward_kernel(keep, core_ref, ws_ref, x_ref, vec_refs, *refs):
    b_refs, et_ref, mask_ref, y_ref = refs[8:10], refs[10], refs[11], refs[12]
    if keep:
        xs_ref, n1_ref, o_ref, m_ref, n2_ref, a_ref, f_ref, zt_ref, ot_ref, lse_ref, g_ref, slope_ref = refs[13:25]
        scratch = refs[25:]
    else:
        n1_ref, o_ref, m_ref, n2_ref, zt_ref, ot_ref = refs[13:19]
        scratch = refs[19:]
    w = weights_of(core_ref[0], refs[:8], scratch[:8])
    x, b, bias, n1t, acc, wt, b_sem = scratch[8:]
    layer, t = pl.program_id(0), pl.program_id(1)
    imgs = et_ref.shape[0]
    heads = b.shape[0]
    width = x.shape[1]
    hd = width // heads
    chunks = pl.num_programs(1) - imgs
    at = (0,) if keep else ()
    vec_ref = vec_refs.at[layer]

    def start_b(k):
        pltpu.make_async_copy(b_refs[k], b, b_sem).start()

    @pl.when((layer == 0) & (t == 0))
    def _():
        w.start("qkv", 0)
        start_b(0)
        w.start("proj", 0)
        w.start_fc(0, 0)
        w.start_fc(0, 1)
        x[...] = x_ref[...]

    @pl.when(t == 0)
    def _():
        if keep:
            xs_ref[0] = x[...]
        o_ref[...] = jnp.zeros_like(o_ref)
        columns = vec_ref[8:16, :].T
        bias[0:width, :] = jnp.broadcast_to(columns[:, QKV_BIAS - 8:QKV_BIAS - 7], (width, 128))
        bias[width:2 * width, :] = jnp.zeros((width, 128), F32)
        bias[2 * width:, :] = jnp.broadcast_to(columns[:, QKV_BIAS - 7:QKV_BIAS - 6], (width, 128))
        norm_tiles(x, n1_ref.at[at] if keep else n1_ref, vec_ref, GAIN_A, SHIFT_A)
        w.wait("qkv")
        for c in range(3):
            part = slice(c * width, (c + 1) * width)
            wt[part, :] = w.dst["qkv"][:, part].T

    def full(ref):
        return ref.at[0] if keep else ref

    n1_now, o_now, m_now, n2_now = full(n1_ref), full(o_ref), full(m_ref), full(n2_ref)
    zt, ot = (zt_ref.at[0, 0], ot_ref.at[0, 0]) if keep else (zt_ref, ot_ref)

    @pl.when(t < imgs)
    def _():
        ws = pl.multiple_of(ws_ref[t], 16)
        et = et_ref[t]
        n1t[...] = tn(n1_now[pl.ds(ws, SLOTS), :], et).astype(BF16)

        @pl.loop(0, 3)
        def _(c):
            rows = pl.ds(pl.multiple_of(c * width, width), width)
            factor = jnp.where(c == 0, hd ** -0.5, 1.0)
            column = bias[rows, :]
            add = jnp.concatenate([column] * (LANES // 128), axis=1)
            zt[rows, :] = ((nn(wt[rows, :], n1t[...]) + add) * factor).astype(BF16)

        @pl.when(t == 0)
        def _():
            pltpu.make_async_copy(b, b, b_sem).wait()

        ones_q = extra_rows([1.0], LANES)
        mask_k = extra_rows([mask_ref[t]], SLOTS)
        ones_v = extra_rows([1.0], SLOTS)

        def scores(h):
            r = h * hd
            qt = jnp.concatenate([zt[r:r + hd, :], ones_q], axis=0)
            kt = jnp.concatenate([zt[width + r:width + r + hd, :SLOTS], mask_k], axis=0)
            return tn(kt, qt)

        def soft(h, s):
            s = s + b[h]
            m = jnp.max(s, axis=0, keepdims=True)
            return m, jnp.exp(s - m).astype(BF16)

        def finish(h, m, e):
            r = h * hd
            vt = jnp.concatenate([zt[2 * width + r:2 * width + r + hd, :SLOTS], ones_v], axis=0)
            o = nn(vt, e)
            total = o[hd:hd + 1]
            ot[r:r + hd, :] = (o[:hd] * (1.0 / total)).astype(BF16)
            if keep:
                lse_ref[0, 0, h:h + 1, :] = m + jnp.log(total)

        s, e = {}, {}
        for k in range(heads + 2 * LAG):
            if k < heads:
                s[k] = scores(k)
            if 0 <= k - LAG < heads:
                e[k - LAG] = soft(k - LAG, s.pop(k - LAG))
            if k - 2 * LAG >= 0:
                finish(k - 2 * LAG, *e.pop(k - 2 * LAG))

        win = pl.ds(ws, SLOTS)
        o_now[win, :] = (o_now[win, :].astype(F32) + nt(et, ot[...])).astype(BF16)

    j = t - imgs

    @pl.when((t == imgs) & (layer == 0))
    def _():
        w.start("qkv", 1)
        start_b(1)

    @pl.when(t == imgs)
    def _():
        w.wait("proj")
        a = nn(o_now[...], w.dst["proj"][...]) + vec(vec_ref, OUT_A)
        if keep:
            a_ref[0] = a.astype(BF16)
        m_now[...] = x[...].astype(F32) + vec(vec_ref, SCALE_A) * a
        acc[...] = jnp.zeros_like(acc)
        norm_tiles(m_now, n2_now, vec_ref, GAIN_B, SHIFT_B)

    @pl.when((t == imgs) & (layer == 0))
    def _():
        w.start("proj", 1)

    @pl.when(t >= imgs)
    def _():
        slot = lax.rem(j, 2)
        w.wait("fc1", j)
        w.wait("fc2", j)
        u = nn(n2_now[...], w.dst["fc1"][slot]) + vec_ref[pl.ds(FC1_BIAS + j, 1), :]
        cdf = 0.5 * (1.0 + lax.erf(u * HALF_ROOT))
        g = (u * cdf).astype(BF16)
        if keep:
            g_ref[0] = g
            slope_ref[0] = (cdf + u * (jnp.exp(-0.5 * u * u) * DENSITY_NORM)).astype(BF16)
        acc[...] += nn(g, w.dst["fc2"][slot])

        @pl.when(j + 2 < chunks)
        def _():
            w.start_fc(layer, j + 2)

        @pl.when((j + 2 >= chunks) & (layer == 0))
        def _():
            w.start_fc(1, j + 2 - chunks)

    @pl.when(j == chunks - 1)
    def _():
        @pl.loop(0, acc.shape[0] // TILE)
        def _(k):
            rows = row_tile(k)
            f = acc[rows, :] + vec(vec_ref, OUT_B)
            if keep:
                f_ref[0, rows, :] = f.astype(BF16)
            x[rows, :] = (m_now[rows, :] + vec(vec_ref, SCALE_B) * f).astype(BF16)

        @pl.when(layer == 1)
        def _():
            y_ref[...] = x[...]


def attn_bwd_kernel(pick_ref, ws_ref, da_ref, own_ref, other_ref, b_ref, et_ref, mask_ref, zt_ref, ot_ref, lse_ref,
                    dz_ref, db_ref, dat, dot, dzt):
    width = da_ref.shape[1]
    i = pl.program_id(0)

    @pl.when(i == 0)
    def _():
        dz_ref[...] = jnp.zeros_like(dz_ref)
        db_ref[...] = jnp.zeros_like(db_ref)
        dzt[...] = jnp.zeros_like(dzt)

    win = pl.ds(pl.multiple_of(ws_ref[i], 16), SLOTS)
    et = et_ref[0]
    dat[...] = tn(da_ref[win, :], et).astype(BF16)
    proj = jnp.where(pick_ref[0] == 1, own_ref[...], other_ref[...])
    dot[...] = nn(proj, dat[...]).astype(BF16)
    attn_back_image(et, mask_ref[0], zt_ref, ot_ref, lse_ref, b_ref, dat, dot, dzt, db_ref)
    for c in range(3):
        cols = slice(c * width, (c + 1) * width)
        dz_ref[win, cols] = (dz_ref[win, cols].astype(F32) + nt(et, dzt[cols, :])).astype(BF16)


def attn_back_image(et, mask, zt, ot, lse_ref, b, dat, dot, dzt, db_ref):
    heads = b.shape[0]
    width = dat.shape[0]
    hd = width // heads
    extra_k = extra_rows([mask, 1.0, 1.0, 1.0], SLOTS)
    extra_v = extra_rows([1.0, 1.0, 1.0], SLOTS)

    def parts(h):
        r = h * hd
        return (zt[r:r + hd, :], zt[width + r:width + r + hd, :SLOTS], zt[2 * width + r:2 * width + r + hd, :SLOTS],
                dot[r:r + hd, :])

    def products(h):
        qt, kt, vt, dt = parts(h)
        r = h * hd
        delta = jnp.sum(dt.astype(F32) * ot[r:r + hd, :].astype(F32), axis=0, keepdims=True)
        extra_q = extra_rows([1.0, *split3(-lse_ref[h:h + 1, :])], LANES)
        extra_d = extra_rows(split3(-delta), LANES)
        s = tn(jnp.concatenate([kt, extra_k], axis=0), jnp.concatenate([qt, extra_q], axis=0))
        dp = tn(jnp.concatenate([vt, extra_v], axis=0), jnp.concatenate([dt, extra_d], axis=0))
        return s, dp

    def middle(h, s, dp):
        p = jnp.exp(s + b[h])
        ds = p * dp
        if db_ref is not None:
            db_ref[h] += ds
        return p.astype(BF16), ds.astype(BF16)

    def finish(h, p, ds):
        qt, kt, vt, dt = parts(h)
        r = h * hd
        dzt[2 * width + r:2 * width + r + hd, :SLOTS] = nt(dt, p).astype(BF16)
        dzt[width + r:width + r + hd, :SLOTS] = nt(qt, ds).astype(BF16)
        dzt[r:r + hd, :] = (nn(kt, ds) * hd ** -0.5).astype(BF16)

    s, e = {}, {}
    for t in range(heads + 2 * LAG_BACK):
        if t < heads:
            s[t] = products(t)
        if 0 <= t - LAG_BACK < heads:
            e[t - LAG_BACK] = middle(t - LAG_BACK, *s.pop(t - LAG_BACK))
        if t - 2 * LAG_BACK >= 0:
            finish(t - 2 * LAG_BACK, *e.pop(t - 2 * LAG_BACK))


def backward_kernel(core_ref, ws_ref, dy_ref, vec_refs, *refs):
    b_refs, et_ref, mask_ref = refs[8:10], refs[10], refs[11]
    m_ref, x_ref, slope_ref, zt_ref, ot_ref, lse_ref, dx_ref = refs[12:19]
    scratch = refs[19:]
    w = weights_of(core_ref[0], refs[:8], scratch[:8])
    dy, df, acc, dm, da, dz, dat, dot, dzt, b, b_sem = scratch[8:]
    step, t = pl.program_id(0), pl.program_id(1)
    layer = 1 - step
    imgs = et_ref.shape[0]
    width = dy.shape[1]
    chunks = pl.num_programs(1) - imgs - 1
    vec_ref = vec_refs.at[layer]

    def start_b(k):
        pltpu.make_async_copy(b_refs[k], b, b_sem).start()

    @pl.when((step == 0) & (t == 0))
    def _():
        w.start_fc(1, 0)
        w.start_fc(1, 1)
        w.start("proj", 1)
        start_b(1)
        w.start("qkv", 1)
        dy[...] = dy_ref[...]

    @pl.when((step == 1) & (t == 0))
    def _():
        w.start("qkv", 0)

    @pl.when(t == 0)
    def _():
        acc[...] = jnp.zeros_like(acc)

        @pl.loop(0, df.shape[0] // TILE)
        def _(k):
            rows = row_tile(k)
            df[rows, :] = (dy[rows, :].astype(F32) * vec(vec_ref, SCALE_B)).astype(BF16)

    @pl.when(t < chunks)
    def _():
        slot = lax.rem(t, 2)
        w.wait("fc1", t)
        w.wait("fc2", t)
        du = (nt(df[...], w.dst["fc2"][slot]) * slope_ref[...].astype(F32)).astype(BF16)
        acc[...] += nt(du, w.dst["fc1"][slot])

        @pl.when(t + 2 < chunks)
        def _():
            w.start_fc(layer, t + 2)

        @pl.when((t + 2 >= chunks) & (step == 0))
        def _():
            w.start_fc(0, t + 2 - chunks)

    @pl.when(t == chunks - 1)
    def _():
        def emit(rows, dv):
            value = dy[rows, :].astype(F32) + dv
            dm[rows, :] = value
            da[rows, :] = (value * vec(vec_ref, SCALE_A)).astype(BF16)
            return ()

        norm_back_tiles(0, m_ref, acc, vec_ref, GAIN_B, emit)
        dz[...] = jnp.zeros_like(dz)
        dzt[...] = jnp.zeros_like(dzt)
        w.wait("proj")
        pltpu.make_async_copy(b, b, b_sem).wait()

    @pl.when((t >= chunks) & (t < chunks + imgs))
    def _():
        i = t - chunks
        et = et_ref[i]
        win = pl.ds(pl.multiple_of(ws_ref[i], 16), SLOTS)
        dat[...] = tn(da[win, :], et).astype(BF16)
        dot[...] = nn(w.dst["proj"][...], dat[...]).astype(BF16)
        attn_back_image(et, mask_ref[i], zt_ref, ot_ref, lse_ref, b, dat, dot, dzt, None)
        for c in range(3):
            cols = slice(c * width, (c + 1) * width)
            dz[win, cols] = (dz[win, cols].astype(F32) + nt(et, dzt[cols, :])).astype(BF16)

    @pl.when(t == chunks + imgs)
    def _():
        @pl.when(step == 0)
        def _():
            w.start("proj", 0)
            start_b(0)

        w.wait("qkv")
        acc[...] = nt(dz[:, :width], w.dst["qkv"][:, :width])
        for c in range(1, 3):
            cols = slice(c * width, (c + 1) * width)
            acc[...] += nt(dz[:, cols], w.dst["qkv"][:, cols])

        def emit(rows, dv):
            dy[rows, :] = (dm[rows, :] + dv).astype(BF16)
            return ()

        norm_back_tiles(0, x_ref, acc, vec_ref, GAIN_A, emit)

        @pl.when(step == 1)
        def _():
            dx_ref[...] = dy[...]


def spread(count):
    entry = iota((count, SPAN * WIDE), 0)
    lane = iota((count, SPAN * WIDE), 1)
    return jnp.where((entry == lane // WIDE * SPAN + lane % WIDE) & (lane % WIDE < SPAN), 1.0, 0.0).astype(BF16)


def squeeze():
    lane = iota((SPAN * WIDE, STRIP), 0)
    to = iota((SPAN * WIDE, STRIP), 1)
    return jnp.where(lane == to // PITCH * WIDE + to % PITCH, 1.0, 0.0).astype(BF16)


def placed(product, v, onehot):
    return sum(product(part.astype(BF16), onehot) for part in split3(v))


def strip_rows(layer, head):
    return pl.ds(layer * HEAD_ROWS + head, PITCH, stride=2 * HEAD_ROWS)


def bias_kernel(table_ref, *refs):
    b_refs, (shifted, strips) = refs[:2], refs[2:]
    rows = table_ref.shape[0]
    heads = b_refs[0].shape[0]
    wide = placed(nn, table_ref[...], spread(table_ref.shape[1]))
    for c in range(PITCH):
        shifted[c * rows:(c + 1) * rows, :] = pltpu.roll(wide, (c - GRID + 1) % (SPAN * WIDE), 1)
    packed = placed(nn, shifted[...], squeeze())
    for k in range(strips.shape[0]):
        strips[k] = packed[:, k * 128:(k + 1) * 128]
    row = iota((SLOTS, LANES), 0)
    col = iota((SLOTS, LANES), 1)
    for layer, b_ref in enumerate(b_refs):
        for h in range(heads):
            strip = jnp.concatenate([strips[k, strip_rows(layer, h), :] for k in range(strips.shape[0])], axis=1)
            for r in range(GRID):
                at = PITCH * (GRID - 1 - r)
                b_ref[h, r * PITCH:(r + 1) * PITCH, :] = strip[:, at:at + LANES]
            mine = layer * HEAD_ROWS + h
            query, key, both = [table_ref[mine:mine + 1, SPAN * SPAN + k:SPAN * SPAN + k + 1] for k in range(3)]
            full = jnp.where(col == CLASS_SLOT, query, b_ref[h])
            b_ref[h] = jnp.where(row == CLASS_SLOT, jnp.where(col == CLASS_SLOT, both, key), full)


def bias_back_kernel(one_ref, two_ref, table_ref, held, strips, classes, sems):
    copies = [pltpu.make_async_copy(ref, held.at[k], sems.at[k]) for k, ref in enumerate((one_ref, two_ref))]
    for c in copies:
        c.start()
    heads = held.shape[1]
    row = iota((SLOTS, LANES), 0)
    col = iota((SLOTS, LANES), 1)
    is_row = row == CLASS_SLOT
    is_col = col == CLASS_SLOT
    entry = iota((1, table_ref.shape[1]), 1) - SPAN * SPAN
    strips[...] = jnp.zeros_like(strips)
    classes[...] = jnp.zeros_like(classes)
    for layer in range(2):
        copies[layer].wait()
        for h in range(heads):
            full = held[layer, h]
            query = jnp.sum(jnp.where(is_col & ~is_row, full, 0.0), keepdims=True)
            key = jnp.sum(jnp.where(is_row & ~is_col, full, 0.0), keepdims=True)
            both = jnp.sum(jnp.where(is_row & is_col, full, 0.0), keepdims=True)
            mine = layer * HEAD_ROWS + h
            classes[mine:mine + 1, :] = jnp.where(
                entry == 0, query, jnp.where(entry == 1, key, jnp.where(entry == 2, both, 0.0)))
            plain = jnp.where(is_row | is_col, 0.0, full)
            total = jnp.zeros((PITCH, STRIP), F32)
            for r in range(GRID):
                part = jnp.concatenate([plain[r * PITCH:(r + 1) * PITCH, :], jnp.zeros((PITCH, STRIP - LANES), F32)],
                                       axis=1)
                total = total + pltpu.roll(part, PITCH * (GRID - 1 - r), 1)
            for k in range(strips.shape[0]):
                strips[k, strip_rows(layer, h), :] = total[:, k * 128:(k + 1) * 128]
    rows = table_ref.shape[0]
    wide = placed(nt, jnp.concatenate([strips[k] for k in range(strips.shape[0])], axis=1), squeeze())
    gathered = jnp.zeros((rows, SPAN * WIDE), F32)
    for c in range(GRID):
        gathered = gathered + pltpu.roll(wide[c * rows:(c + 1) * rows, :], (GRID - 1 - c) % (SPAN * WIDE), 1)
    table_ref[...] = placed(nt, gathered, spread(table_ref.shape[1])) + classes[...]


def norm_back_tiles(count, src_ref, grad_ref, vec_ref, gain, emit):
    def body(t, sums):
        rows = row_tile(t)
        unit, inverse = row_stats(src_ref[rows, :].astype(F32))
        grad = grad_ref[rows, :]
        scaled = grad * vec(vec_ref, gain)
        mean_one = jnp.mean(scaled, axis=-1, keepdims=True)
        mean_two = jnp.mean(scaled * unit, axis=-1, keepdims=True)
        more = emit(rows, inverse * (scaled - mean_one - unit * mean_two))
        if not count:
            return sums
        return tuple(s + jnp.sum(v, axis=0, keepdims=True) for s, v in zip(sums, (grad * unit, grad) + more))

    zero = jnp.zeros((1, grad_ref.shape[1]), F32)
    return lax.fori_loop(0, grad_ref.shape[0] // TILE, body, (zero,) * count)


def mlp_bwd_kernel(want, pick_ref, dy_ref, m_ref, vec_ref, slope_ref, fc1_own, fc1_other, fc2_own, fc2_other, *rest):
    if want:
        (n2_ref, g_ref, a_ref, f_ref, dm_ref, da_ref, fc1_give, fc1_keep, fc2_give, fc2_keep, sums_ref, df, acc) = rest
    else:
        dm_ref, da_ref, df, acc = rest
    j = pl.program_id(0)
    steps = pl.num_programs(0)
    mine = pick_ref[0] == 1
    core = pick_ref[1]
    width = dy_ref.shape[1]

    @pl.when(j == 0)
    def _():
        acc[...] = jnp.zeros_like(acc)
        if want:
            sums_ref[...] = jnp.zeros_like(sums_ref)
        zero = jnp.zeros((1, width), F32)

        def body(t, sums):
            rows = row_tile(t)
            dy = dy_ref[rows, :].astype(F32)
            scaled = (dy * vec(vec_ref, SCALE_B)).astype(BF16)
            df[rows, :] = scaled
            if not want:
                return sums
            return (sums[0] + jnp.sum(scaled.astype(F32), axis=0, keepdims=True),
                    sums[1] + jnp.sum(dy * f_ref[rows, :].astype(F32), axis=0, keepdims=True))

        sums = lax.fori_loop(0, df.shape[0] // TILE, body, (zero, zero) if want else ())
        if want:
            sums_ref[SUM_DF:SUM_DF + 1, :] = sums[0]
            sums_ref[SUM_SCALE_B:SUM_SCALE_B + 1, :] = sums[1]

    fc1 = jnp.where(mine, fc1_own[...], fc1_other[...])
    fc2 = jnp.where(mine, fc2_own[...], fc2_other[...])
    du = (nt(df[...], fc2) * slope_ref[...].astype(F32)).astype(BF16)
    acc[...] += nt(du, fc1)
    if want:
        at = lax.rem(j + (1 - core) * (steps // 2), steps)
        sums_ref[pl.ds(FC1_BIAS + at, 1), :] = jnp.sum(du.astype(F32), axis=0, keepdims=True)
        grad = tn(g_ref[...], df[...]).astype(BF16)
        low, high = grad[:, :width // 2], grad[:, width // 2:]
        fc2_keep[...] = jnp.where(core == 0, low, high)
        fc2_give[...] = jnp.where(core == 0, high, low)
        grad1 = tn(n2_ref[...], du).astype(BF16)

        @pl.when(j < steps // 2)
        def _():
            fc1_give[...] = grad1

        @pl.when(j >= steps // 2)
        def _():
            fc1_keep[...] = grad1

    @pl.when(j == steps - 1)
    def _():
        def emit(rows, dv):
            dm = dy_ref[rows, :].astype(F32) + dv
            da = (dm * vec(vec_ref, SCALE_A)).astype(BF16)
            dm_ref[rows, :] = dm
            da_ref[rows, :] = da
            return (da.astype(F32), dm * a_ref[rows, :].astype(F32)) if want else ()

        sums = norm_back_tiles(4 if want else 0, m_ref, acc, vec_ref, GAIN_B, emit)
        for k, s in zip((SUM_GAIN_B, SUM_SHIFT_B, SUM_DA, SUM_SCALE_A), sums):
            sums_ref[k:k + 1, :] = s


def attn_tail_kernel(want, pick_ref, x_ref, dm_ref, vec_ref, dz_ref, wt_own, wt_other, *rest):
    if want:
        n1_ref, o_ref, da_ref, dx_ref, give_ref, keep_ref, bias_ref, sums_ref, acc = rest
    else:
        dx_ref, acc = rest
    j = pl.program_id(0)
    core = pick_ref[1]
    width = x_ref.shape[1]

    @pl.when(j == 0)
    def _():
        acc[...] = jnp.zeros_like(acc)
        if want:
            sums_ref[...] = jnp.zeros_like(sums_ref)
            grad = tn(o_ref[...], da_ref[...]).astype(BF16)
            low, high = grad[:, :width // 2], grad[:, width // 2:]
            keep_ref[:, 3 * width // 2:] = jnp.where(core == 0, low, high)
            give_ref[:, 3 * width // 2:] = jnp.where(core == 0, high, low)

    dz = dz_ref[...]
    acc[...] += nt(dz, jnp.where(pick_ref[0] == 1, wt_own[...], wt_other[...]))
    if want:
        bias_ref[0] = jnp.broadcast_to(jnp.sum(dz.astype(F32), axis=0, keepdims=True), bias_ref.shape[1:])
        grad1 = tn(n1_ref[...], dz).astype(BF16)

        @pl.when(j == 0)
        def _():
            give_ref[:, :3 * width // 2] = grad1

        @pl.when(j == 1)
        def _():
            keep_ref[:, :3 * width // 2] = grad1

    @pl.when(j == pl.num_programs(0) - 1)
    def _():
        def emit(rows, dv):
            dx_ref[rows, :] = (dm_ref[rows, :] + dv).astype(BF16)
            return ()

        sums = norm_back_tiles(2 if want else 0, x_ref, acc, vec_ref, GAIN_A, emit)
        for k, s in enumerate(sums):
            sums_ref[k:k + 1, :] = s


TAKES = dict(backward=85, forward=75, forward_keep=85, mlp_bwd=15, mlp_bwd_all=27, attn_bwd=20, attn_bwd_all=21, attn_tail=9,
             attn_tail_all=16, bias_build=6, bias_back=9)


VMEM = dict(backward=60, forward=60, forward_keep=60, mlp_bwd=60, mlp_bwd_all=60, attn_bwd=60, attn_bwd_all=60, attn_tail=60,
            attn_tail_all=60, bias_build=60, bias_back=60)


def cost(name):
    return pl.CostEstimate(flops=TAKES[name] * 800_000_000, bytes_accessed=TAKES[name] * 3_000_000, transcendentals=0)


def params(name):
    return pltpu.CompilerParams(vmem_limit_bytes=VMEM[name] * 1024 * 1024)


def shaped(*arrays):
    return [jax.ShapeDtypeStruct(s, d) for s, d in arrays]


def whole(shape):
    return pl.BlockSpec(shape, lambda *_: (0,) * len(shape))


def once(shape):
    return pl.BlockSpec(shape, lambda *_: (0,) * len(shape), pipeline_mode=pl.Buffered(1))


def per_image(shape):
    return pl.BlockSpec((1,) + shape, lambda i, *_: (i,) + (0,) * len(shape))


def call(kernel, name, prefetched, grid, inputs, outputs, scratch, after=()):
    count = len(prefetched) + len(inputs)

    def body(*refs):
        kernel(*refs[:count], *refs[count + len(after):])

    inputs = inputs + [(a, pl.BlockSpec(memory_space=pl.ANY)) for a in after]
    return pl.pallas_call(
        body,
        grid_spec=pltpu.PrefetchScalarGridSpec(
            num_scalar_prefetch=len(prefetched), grid=grid, in_specs=[s for _, s in inputs],
            out_specs=[s for _, _, s in outputs], scratch_shapes=scratch),
        out_shape=[jax.ShapeDtypeStruct(s, d) for s, d, _ in outputs],
        compiler_params=params(name), name=name, cost_estimate=cost(name),
    )(*prefetched, *[a for a, _ in inputs])


def forward(keep, x, section, meta):
    core, ws, et, mask = meta
    rows, width = x.shape
    biases = section["bias"]
    heads = biases[0].shape[0]
    hidden = section["own"]["fc1"].shape[1]
    imgs = et.shape[0]
    chunks = hidden // width
    anywhere = pl.BlockSpec(memory_space=pl.ANY)
    vectors = section["vectors"]
    inputs = [(x, once(x.shape)), (vectors, once(vectors.shape))]
    inputs += [(section[side][name], anywhere) for side in ("own", "other") for name in MATRICES]
    inputs += [(v, anywhere) for v in biases] + [(et, once(et.shape)), (mask, once(mask.shape))]
    outputs = [((rows, width), BF16, whole((rows, width)))]
    low = [pltpu.VMEM((rows, width), BF16)]
    scratch = weight_scratch(width) + low + [
        pltpu.VMEM(biases[0].shape, F32), pltpu.VMEM((3 * width, 128), F32), pltpu.VMEM((width, LANES), BF16),
        pltpu.VMEM((rows, width), F32), pltpu.VMEM((3 * width, width), BF16), pltpu.SemaphoreType.DMA]
    if keep:
        def of_layer(kind):
            return (2, rows, width), kind, pl.BlockSpec((1, rows, width), lambda l, t, *_: (l, 0, 0))

        def of_image(*shape, kind=BF16):
            return ((2, imgs) + shape, kind,
                    pl.BlockSpec((1, 1) + shape, lambda l, t, *_: (l, jnp.minimum(t, imgs - 1), 0, 0)))

        of_chunk = ((2, rows, hidden), BF16,
                    pl.BlockSpec((1, rows, width), lambda l, t, *_: (l, 0, jnp.maximum(t - imgs, 0))))
        outputs += [of_layer(BF16), of_layer(BF16), of_layer(BF16), of_layer(F32), of_layer(BF16), of_layer(BF16),
                    of_layer(BF16), of_image(3 * width, LANES), of_image(width, LANES),
                    of_image(heads, LANES, kind=F32), of_chunk, of_chunk]
    else:
        scratch = low * 2 + [pltpu.VMEM((rows, width), F32)] + low + [
            pltpu.VMEM((3 * width, LANES), BF16), pltpu.VMEM((width, LANES), BF16)] + scratch
    return call(functools.partial(forward_kernel, keep), "forward_keep" if keep else "forward", [core, ws],
                (2, imgs + chunks), inputs, outputs, scratch)


def backward(dy, section, meta, kept):
    core, ws, et, mask = meta
    rows, width = dy.shape
    biases = section["bias"]
    imgs = et.shape[0]
    chunks = section["own"]["fc1"].shape[1] // width
    anywhere = pl.BlockSpec(memory_space=pl.ANY)
    vectors = section["vectors"]
    inputs = [(dy, once(dy.shape)), (vectors, once(vectors.shape))]
    inputs += [(section[side][name], anywhere) for side in ("own", "other") for name in MATRICES]
    inputs += [(v, anywhere) for v in biases] + [(et, once(et.shape)), (mask, once(mask.shape))]
    of_layer = pl.BlockSpec((None, rows, width), lambda l, t, *_: (1 - l, 0, 0))
    inputs += [(kept["m"], of_layer), (kept["x"], of_layer)]
    inputs += [(kept["slope"], pl.BlockSpec((None, rows, width),
                                            lambda l, t, *_: (1 - l, 0, jnp.minimum(t, chunks - 1))))]
    for name in ("zt", "ot", "lse"):
        v = kept[name]
        inputs += [(v, pl.BlockSpec((None, None) + v.shape[2:],
                                    lambda l, t, *_: (1 - l, jnp.clip(t - chunks, 0, imgs - 1), 0, 0)))]
    low, high = pltpu.VMEM((rows, width), BF16), pltpu.VMEM((rows, width), F32)
    slots = pltpu.VMEM((width, LANES), BF16)
    scratch = weight_scratch(width) + [
        low, low, high, high, low, pltpu.VMEM((rows, 3 * width), BF16), slots, slots,
        pltpu.VMEM((3 * width, LANES), BF16), pltpu.VMEM(biases[0].shape, F32), pltpu.SemaphoreType.DMA]
    return call(backward_kernel, "backward", [core, ws], (2, chunks + imgs + 1), inputs,
                [((rows, width), BF16, whole((rows, width)))], scratch)[0]


def attn_bwd(da, w, meta, kept, after=()):
    _, ws, et, mask = meta
    rows, width = da.shape
    bias = w["bias"]
    imgs = et.shape[0]
    single_proj = once((width, width))
    layer = w["layer"]

    def kept_image(name):
        v = kept[name]
        return v, pl.BlockSpec((None, None) + v.shape[2:], lambda i, *_: (layer, i, 0, 0))

    inputs = [(da, once(da.shape)), (w["proj"][0], single_proj), (w["proj"][1], single_proj), (bias, once(bias.shape)),
              (et, per_image(et.shape[1:])), (mask, per_image(mask.shape[1:])), kept_image("zt"),
              kept_image("ot"), kept_image("lse")]
    outputs = [((rows, 3 * width), BF16, whole((rows, 3 * width)))]
    outputs += [(bias.shape, F32, whole(bias.shape))]
    scratch = [pltpu.VMEM((width, LANES), BF16), pltpu.VMEM((width, LANES), BF16), pltpu.VMEM((3 * width, LANES), BF16)]
    return call(attn_bwd_kernel, "attn_bwd_all", [w["pick"], ws],
                (imgs,), inputs, outputs, scratch, after)


def build_bias(tables, heads):
    shape = (heads, SLOTS, LANES)
    rows = tables.shape[0]
    return call(bias_kernel, "bias_build", [], (1,), [(tables, once(tables.shape))], [(shape, F32, whole(shape))] * 2,
                [pltpu.VMEM((PITCH * rows, SPAN * WIDE), F32), pltpu.VMEM((STRIP // 128, PITCH * rows, 128), F32)])


def table_back(one, two, lanes, after=()):
    rows = 2 * HEAD_ROWS
    anywhere = pl.BlockSpec(memory_space=pl.ANY)
    return call(bias_back_kernel, "bias_back", [], (1,), [(one, anywhere), (two, anywhere)],
                [((rows, lanes), F32, whole((rows, lanes)))],
                [pltpu.VMEM((2,) + one.shape, F32), pltpu.VMEM((STRIP // 128, PITCH * rows, 128), F32),
                 pltpu.VMEM((rows, lanes), F32), pltpu.SemaphoreType.DMA((2,))], after)[0]


def chosen(which, block, to_index):
    def index(j, pick):
        used = pick[0] if which == 0 else 1 - pick[0]
        return tuple(k * used for k in to_index(j, pick))
    return pl.BlockSpec(block, index)


def both(pair, block, to_index):
    return [(pair[k], chosen(k, block, to_index)) for k in range(2)]


def kept_whole(kept, name, w):
    v, layer = kept[name], w["layer"]
    return v, pl.BlockSpec((None,) + v.shape[1:], lambda *_: (layer, 0, 0), pipeline_mode=pl.Buffered(1))


def mlp_bwd(want, dy, w, kept):
    rows, width = dy.shape
    hidden = w["fc1"][0].shape[1]
    steps = hidden // width
    full = whole((rows, width))
    single = once((rows, width))

    def at(j, pick):
        return lax.rem(j + (1 - pick[1]) * (steps // 2), steps)

    layer = w["layer"]
    part = pl.BlockSpec((None, rows, width), lambda j, p: (layer, 0, at(j, p)))
    inputs = [(dy, single), kept_whole(kept, "m", w), (w["vectors"], once(w["vectors"].shape)), (kept["slope"], part),
              *both(w["fc1"], (width, width), lambda j, p: (0, at(j, p))),
              *both(w["fc2"], (width, width), lambda j, p: (at(j, p), 0))]
    outputs = [((rows, width), F32, full), ((rows, width), BF16, full)]
    if want:
        inputs += [kept_whole(kept, "n2", w), (kept["g"], part), kept_whole(kept, "a", w), kept_whole(kept, "f", w)]
        half = pl.BlockSpec((width, width // 2), lambda j, p: (at(j, p), 0))
        give = pl.BlockSpec((width, width), lambda j, p: (0, jnp.minimum(j, steps // 2 - 1)))
        stay = pl.BlockSpec((width, width), lambda j, p: (0, jnp.maximum(j - steps // 2, 0)))
        outputs += [((width, hidden // 2), BF16, give), ((width, hidden // 2), BF16, stay),
                    ((hidden, width // 2), BF16, half), ((hidden, width // 2), BF16, half),
                    ((16, width), F32, whole((16, width)))]
    scratch = [pltpu.VMEM((rows, width), BF16), pltpu.VMEM((rows, width), F32)]
    return call(functools.partial(mlp_bwd_kernel, want), "mlp_bwd_all" if want else "mlp_bwd", [w["pick"]],
                (steps,), inputs, outputs, scratch)


def attn_tail(want, dm, dz, da, w, kept, after=()):
    rows, width = dm.shape
    part = 3 * width // 2
    full = whole((rows, width))
    single = once((rows, width))

    def at(j, pick):
        return lax.rem(j + 1 - pick[1], 2)

    inputs = [kept_whole(kept, "x", w), (dm, single), (w["vectors"], once(w["vectors"].shape)),
              (dz, pl.BlockSpec((rows, part), lambda j, p: (0, at(j, p)))),
              *both(w["qkv"], (width, part), lambda j, p: (0, at(j, p)))]
    outputs = [((rows, width), BF16, full)]
    if want:
        inputs += [kept_whole(kept, "n1", w), kept_whole(kept, "o", w), (da, single)]
        outputs += [((width, 2 * width), BF16, whole((width, 2 * width)))] * 2
        outputs += [((2, 8, part), F32, pl.BlockSpec((1, 8, part), lambda j, p: (at(j, p), 0, 0))),
                    ((8, width), F32, whole((8, width)))]
    return call(functools.partial(attn_tail_kernel, want), "attn_tail_all" if want else "attn_tail", [w["pick"]],
                (2,), inputs, outputs, [pltpu.VMEM((rows, width), F32)], after)


def sequence_meta(ids, order, rows):
    imgs, patches = order.shape
    image = jnp.arange(imgs, dtype=jnp.int32)
    start = jnp.sum((ids[None, :] < image[:, None]).astype(jnp.int32), axis=1)
    count = jnp.sum((ids[None, :] == image[:, None]).astype(jnp.int32), axis=1)
    ws = jnp.minimum(start // 16 * 16, rows - SLOTS)
    slot = jnp.arange(LANES, dtype=jnp.int32)
    is_class = slot == CLASS_SLOT
    is_patch = (slot % PITCH < GRID) & (slot < SLOTS)
    patch = jnp.where(is_patch, slot // PITCH * GRID + slot % PITCH, -1)
    place = jnp.arange(1, patches + 1, dtype=jnp.int32)
    offset = jnp.sum(jnp.where(order[:, None, :] == patch[None, :, None], place, 0), axis=2)
    valid = (is_class | is_patch)[None, :] & (offset < count[:, None])
    local = jnp.where(valid, offset + (start - ws)[:, None], -1)
    row = jnp.arange(SLOTS, dtype=jnp.int32)
    et = (local[:, None, :] == row[None, :, None]).astype(BF16)
    mask = jnp.where(valid, 0.0, NEGATIVE).astype(F32)[:, None, :SLOTS]
    return ws, et, mask


KEPT = ("x", "n1", "o", "m", "n2", "a", "f", "zt", "ot", "lse", "g", "slope")


def later(arrays, token):
    if token is None:
        return list(arrays)
    return list(lax.optimization_barrier((*arrays, token)))[:-1]


class Reducer:
    def __init__(self, keep, give, swap_core, swap_wide, at_wide, wide):
        shape = (wide, keep.shape[0] // wide, keep.shape[1])
        self.parts = [v.reshape(shape) for v in (keep, swap_core(give))]
        self.swap_wide, self.at_wide = swap_wide, at_wide
        self.left, self.bit = wide, 1
        self.sent = []

    def hold(self, token):
        self.parts[-1], = later([self.parts[-1]], token)

    def added(self, parts):
        return sum(v.astype(F32) for v in parts)

    def step(self, token=None):
        if self.left == 1:
            return
        self.hold(token)
        mine = self.at_wide // self.bit % 2
        pairs = [v.reshape((self.left // 2, 2) + v.shape[1:]) for v in self.parts]
        self.sent = [self.added(lax.dynamic_index_in_dim(v, 1 - mine, 1, keepdims=False) for v in pairs).astype(BF16)]
        self.parts = [lax.dynamic_index_in_dim(v, mine, 1, keepdims=False) for v in pairs]
        self.parts.append(self.swap_wide(self.sent[0], self.bit))
        self.left, self.bit = self.left // 2, 2 * self.bit

    def two(self):
        return [self.added(self.parts[:-1]).astype(BF16), self.parts[-1]]

    def finish(self, token=None):
        while self.left > 1:
            self.step(token)
        self.hold(token)
        return self.added(self.parts)[0]


FC2, FC1, FC1_MORE, ATTN, ATTN_MORE, OTHER, OTHER_MORE = range(7)
SMALL, ROWS = 7, 8
CORE, Y, Z0, Z1, FINAL = range(5)


def last_sums_kernel(cuts, counts, *refs):
    pairs, (fc2_two, fc1_two, small_ref, rows_ref) = refs[:8], refs[8:12]
    out_fc2, out_fc1, out_attn, small_out, rows_out = refs[12:17]
    scratch = list(refs[17:])
    send_sem, recv_sem, local_sem = scratch[-3:]
    small_got = scratch[-4]
    me = lax.axis_index("narrow")
    at = lax.axis_index("wide")
    core = me % 2
    half = {hop: at // bit % 2 for hop, bit in ((Y, 1), (Z0, 2), (Z1, 4))}
    core_partner = {"narrow": me + 1 - 2 * core}
    across = {"narrow": me + 2 - 4 * (me // 2)}
    corner = {"narrow": 3 - me}
    partners = {CORE: core_partner, FINAL: core_partner}
    for hop, bit in ((Y, 1), (Z0, 2), (Z1, 4)):
        partners[hop] = {"wide": at + bit * (1 - 2 * half[hop])}
    greeted = [core_partner, across, corner] + [partners[hop] for hop in (Y, Z0, Z1)]
    barrier = pltpu.get_barrier_semaphore()
    for partner in greeted:
        pl.semaphore_signal(barrier, inc=1, device_id=partner, device_id_type=pl.DeviceIdType.MESH)
    pl.semaphore_wait(barrier, len(greeted))

    def remote(src, dst, row, hop, device=None):
        return pltpu.make_async_remote_copy(
            src_ref=src, dst_ref=dst, send_sem=send_sem.at[row, hop], recv_sem=recv_sem.at[row, hop],
            device_id=partners[hop] if device is None else device, device_id_type=pl.DeviceIdType.MESH)

    first, second, levels, last = {}, {}, {}, {}
    for p, (k, cut) in enumerate(cuts):
        n = counts[p]
        mine, come = scratch.pop(0), scratch.pop(0)
        first[p] = (pairs[2 * k].at[:, :, cut], mine)
        second[p] = (pairs[2 * k + 1].at[:, :, cut], come)
        levels[p] = [(None, mine, come)]
        while n > 1:
            n //= 2
            levels[p].append((scratch.pop(0), scratch.pop(0), scratch.pop(0)))
        if p < OTHER:
            last[p] = (scratch.pop(0), scratch.pop(0))
    other = {p: scratch.pop(0) for p in (OTHER, OTHER_MORE)}
    pending = {}

    def begin(p):
        pending[p] = [pltpu.make_async_copy(*first[p], local_sem.at[p, 0])]
        if p in (ATTN, ATTN_MORE):
            pending[p].append(remote(*second[p], p, CORE))
        else:
            pending[p].append(pltpu.make_async_copy(*second[p], local_sem.at[p, 1]))
        for c in pending[p]:
            c.start()

    def wait(p):
        for c in pending[p]:
            c.wait()

    def hop(p, n):
        wait(p)
        level = counts[p].bit_length() - n.bit_length()
        _, mine, come = levels[p][level]
        send, stay, next_come = levels[p][level + 1]
        which = {8: Y, 4: Z0, 2: Z1}[n]
        b = half[which]

        def add(to, i, index):
            to[i] = (mine[index].astype(F32) + come[index].astype(F32)).astype(BF16)

        @pl.loop(0, n // 2)
        def _(i):
            add(send, i, 2 * i + 1 - b)

        copy = remote(send, next_come, p, which)
        copy.start()
        pending[p] = [copy]

        @pl.loop(0, n // 2)
        def _(i):
            add(stay, i, 2 * i + b)

    def total(p):
        wait(p)
        _, stay, come = levels[p][-1]
        return stay[0].astype(F32) + come[0].astype(F32)

    outs = {FC2: out_fc2, FC1: out_fc1, FC1_MORE: out_fc1, ATTN: out_attn, ATTN_MORE: out_attn}
    others = {FC2: fc2_two, FC1: fc1_two, FC1_MORE: fc1_two}

    def end(p):
        cut = cuts[p][1]
        one = total(p)
        two = (others[p][:, cut] if p in others else other[p + OTHER - ATTN][...]).astype(F32)
        give, come = last[p]
        give[...] = jnp.where(core == 0, two, one).astype(BF16)
        copy = remote(give, come, p, FINAL)
        copy.start()
        pending[p] = [copy]
        outs[p][core, :, cut] = jnp.where(core == 0, one, two)

    def close(p):
        wait(p)
        outs[p][1 - core, :, cuts[p][1]] = last[p][1][...].astype(F32)

    small = {}

    def small_send(h):
        small[h] = remote(small_out, small_got.at[h], SMALL, h)
        small[h].start()

    def small_take(h):
        small[h].wait()
        small_out[...] += small_got[h]

    small_out[...] = small_ref[...]
    small_send(CORE)
    for p in (FC1, FC1_MORE, FC2, ATTN, ATTN_MORE, OTHER, OTHER_MORE):
        begin(p)
    row_copies = []
    for k, (device, block) in enumerate(((core_partner, me + 1 - 2 * core), (across, me + 2 - 4 * (me // 2)),
                                         (corner, 3 - me))):
        row_copies.append(remote(rows_ref.at[block], rows_out.at[k], ROWS, k, device))
        row_copies[-1].start()
    small_take(CORE)
    small_send(Z0)
    hop(FC1, 8)
    hop(FC1_MORE, 8)
    hop(FC2, 4)
    hop(ATTN, 8)
    hop(ATTN_MORE, 8)
    hop(OTHER, 2)
    hop(OTHER_MORE, 2)
    small_take(Z0)
    small_send(Z1)
    hop(FC2, 2)
    hop(FC1, 4)
    small_take(Z1)
    small_send(Y)
    hop(FC1_MORE, 4)
    hop(FC1, 2)
    end(FC2)
    for p in (OTHER, OTHER_MORE):
        other[p][...] = total(p).astype(BF16)
    hop(ATTN, 4)
    hop(FC1_MORE, 2)
    end(FC1)
    hop(ATTN_MORE, 4)
    hop(ATTN, 2)
    end(FC1_MORE)
    hop(ATTN_MORE, 2)
    small_take(Y)
    end(ATTN)
    for p in (FC2, FC1, FC1_MORE):
        close(p)
    for c in row_copies:
        c.wait()
    end(ATTN_MORE)
    close(ATTN)
    close(ATTN_MORE)


def last_sums(pairs, fc2_two, fc1_two, small, rows):
    anywhere = pl.BlockSpec(memory_space=pl.ANY)
    vmem = pl.BlockSpec(memory_space=pltpu.VMEM)
    scratch, cuts, counts = [], [], []
    for k, many in enumerate((1, 2, 2, 2)):
        p = pairs[k][0]
        size = p.shape[2] // many
        for c in range(many):
            n, block = p.shape[0], (p.shape[1], size)
            cuts.append((k, slice(c * size, (c + 1) * size)))
            counts.append(n)
            scratch += [pltpu.VMEM((n,) + block, BF16)] * 2
            while n > 1:
                n //= 2
                scratch += [pltpu.VMEM((n,) + block, BF16)] * 3
            if k < 3:
                scratch += [pltpu.VMEM(block, BF16)] * 2
    scratch += [pltpu.VMEM((pairs[3][0].shape[1], pairs[3][0].shape[2] // 2), BF16)] * 2
    scratch += [pltpu.VMEM((4,) + small.shape, F32)]
    scratch += [pltpu.SemaphoreType.DMA((9, 5)), pltpu.SemaphoreType.DMA((9, 5)), pltpu.SemaphoreType.DMA((7, 2))]
    return pl.pallas_call(
        functools.partial(last_sums_kernel, cuts, counts),
        in_specs=[anywhere] * 8 + [vmem] * 3 + [anywhere],
        out_specs=[vmem] * 5,
        out_shape=[jax.ShapeDtypeStruct((2,) + p.shape[1:], F32) for p, _ in pairs[:3]]
        + [jax.ShapeDtypeStruct(small.shape, F32), jax.ShapeDtypeStruct((3,) + rows.shape[1:], BF16)],
        scratch_shapes=scratch,
        compiler_params=pltpu.CompilerParams(vmem_limit_bytes=58 * 1024 * 1024, collective_id=0, has_side_effects=True),
        cost_estimate=pl.CostEstimate(flops=0, bytes_accessed=300_000_000, transcendentals=0), name="last_sums",
    )(*[v for pair in pairs for v in pair], fc2_two, fc1_two, small, rows)


def shards(images, cotangent, image_ids, patch_order, qkv_weight, qv_bias, proj_weight, rel_table, layer_scales,
           layer_norm_gains, norm_biases, fc1_weight, fc1_bias, fc2_weight, out_biases):
    me = lax.axis_index("narrow")
    at_wide = lax.axis_index("wide")
    wide = lax.axis_size("wide")
    core = me % 2
    first = me < 2
    quarter, width = images.shape[1:]
    rows = 4 * quarter
    padded = -(-rows // TILE) * TILE
    entries, heads = rel_table.shape[1:]
    flips = {k: [(d, d ^ k) for d in range(4)] for k in (1, 2, 3)}

    def swap(v, k):
        return lax.ppermute(v, "narrow", flips[k])

    def swap_wide(v, k):
        return lax.ppermute(v, "wide", [(d, d ^ k) for d in range(wide)])

    def pick(v, index):
        return lax.dynamic_index_in_dim(v, index, 0, keepdims=False)

    smalls = jnp.concatenate([layer_norm_gains[0, :1], norm_biases[0, :1], layer_norm_gains[0, 1:], norm_biases[0, 1:],
                              layer_scales[0], out_biases[0], fc1_bias.reshape(-1, width), qv_bias[0],
                              jnp.zeros((2, width), F32)])
    table = jnp.pad(rel_table[0].T, ((0, HEAD_ROWS - heads), (0, width - entries)))
    own = [qkv_weight[0], smalls, table, proj_weight[0], fc1_weight[0], fc2_weight[0]]
    other = [swap(v, 1) for v in own]
    bias_at = FC1_BIAS + fc1_bias.shape[1] // width
    biases = build_bias(jnp.concatenate([jnp.where(core == k, table, other[2]) for k in range(2)]), heads)
    weights = []
    for layer in range(2):
        vectors = jnp.where(core == layer, smalls, other[1])
        weights.append(dict(
            layer=layer, pick=jnp.stack([(core == layer).astype(jnp.int32), core]), vectors=vectors, bias=biases[layer],
            **{name: (own[k], other[k]) for name, k in (("qkv", 0), ("proj", 3), ("fc1", 4), ("fc2", 5))}))

    section = dict(
        vectors=jnp.stack([w["vectors"] for w in weights]), bias=[w["bias"] for w in weights],
        own={name: weights[0][name][0] for name in MATRICES}, other={name: weights[0][name][1] for name in MATRICES})
    meta = (core[None],) + sequence_meta(pick(image_ids, core), pick(patch_order, core), padded)

    mine = jnp.where(first, images, cotangent)
    theirs = jnp.where(first, cotangent, images)
    pieces = [pick(mine, core), swap(pick(mine, 1 - core), 1), swap(pick(theirs, core), 2),
              swap(pick(theirs, 1 - core), 3)]
    rows_in = jnp.zeros((padded, width), BF16)
    for k, piece in enumerate(pieces):
        rows_in = lax.dynamic_update_slice(rows_in, piece, ((me ^ k) * quarter, 0))

    middle, = forward(False, rows_in, section, meta)
    x_in = jnp.where(first, rows_in, swap(middle, 2))
    y_out, *parts = forward(True, x_in, section, meta)
    kept = dict(zip(KEPT, parts))

    back = backward(rows_in, section, meta, kept)
    dy_in = jnp.where(first, swap(back, 2), rows_in)

    def reducer(keep, give):
        return Reducer(keep, give, lambda v: swap(v, 1), swap_wide, at_wide, wide)

    def mlp_part(dy, w, kept_one):
        dm, da, fc1_give, fc1_keep, fc2_give, fc2_keep, sums = mlp_bwd(True, dy, w, kept_one)
        return dm, da, [reducer(fc2_keep, fc2_give), reducer(fc1_keep, fc1_give)], sums

    def tail_part(dm, da, dz, w, kept_one, after, start=True):
        dx, give, keep, bias, sums = attn_tail(True, dm, dz, da, w, kept_one, after)
        bias = bias[:, 0].reshape(1, -1)
        rows_of = jnp.concatenate([sums[:2], bias[:, :width], bias[:, 2 * width:], jnp.zeros((4, width), F32)])
        halves = (keep, give)
        if start:
            return dx, reducer(*halves), rows_of
        return dx, [v.reshape(wide, -1, v.shape[1]) for v in halves], rows_of

    dm, da, fc_two, sums_two = mlp_part(dy_in, weights[1], kept)
    dz, db_two = attn_bwd(da, weights[1], meta, kept)
    for r in fc_two:
        r.step(dz)
    mid, attn_two, tail_two = tail_part(dm, da, dz, weights[1], kept, sum((r.sent for r in fc_two), []))
    dm, da, fc_one, sums_one = mlp_part(mid, weights[0], kept)
    for r in fc_two + [attn_two]:
        r.step(da)
    dz, db_one = attn_bwd(da, weights[0], meta, kept, sum((r.sent for r in fc_two + [attn_two]), []))
    for r in fc_one[:1] + fc_two + [attn_two]:
        r.step(dz)
    dx, attn_one, tail_one = tail_part(dm, da, dz, weights[0], kept,
                                       sum((r.sent for r in fc_one[:1] + fc_two + [attn_two]), []), wide != 8)
    folded = table_back(db_one, db_two, width, [dx])
    small = jnp.concatenate([sums_two, tail_two, folded[HEAD_ROWS:], sums_one, tail_one, folded[:HEAD_ROWS]])

    result = jnp.where(first, dx, y_out)[:rows].reshape(4, quarter, width)
    if wide == 8:
        result = jnp.pad(result, ((0, 0), (0, -quarter % 16), (0, 0)))
        pairs = [fc_one[0].two(), fc_one[1].two(), attn_one, attn_two.two()]
        *shares, small, others = last_sums(pairs, *[r.finish(dx).astype(BF16) for r in fc_two], small, result)
        fc2, fc1, attn = [(v[0], v[1]) for v in shares]
        mine, others = pick(result, me)[:quarter], [others[k, :quarter] for k in range(3)]
    else:
        mine, others = pick(result, me), [swap(pick(result, me ^ k), k) for k in (1, 2, 3)]
        small = small + swap(small, 1)
        for k in range(wide.bit_length() - 1):
            small = small + swap_wide(small, 1 << k)
        shares = []
        for one, two in zip(fc_one + [attn_one], fc_two + [attn_two]):
            one, two = one.finish(), two.finish()
            stay = jnp.where(core == 0, one, two)
            got = swap(jnp.where(core == 0, two, one).astype(BF16), 1).astype(F32)
            shares.append((jnp.where(core == 0, stay, got), jnp.where(core == 0, got, stay)))
        fc2, fc1, attn = shares
    same, across = [mine, others[0]], others[1:]
    same = jnp.where(core == 0, jnp.stack(same), jnp.stack(same[::-1]))
    across = jnp.where(core == 0, jnp.stack(across), jnp.stack(across[::-1]))
    encoded = jnp.where(first, across, same)
    images_grad = jnp.where(first, same, across)
    totals_two, totals_one = small[:40], small[40:]
    qkv = jnp.concatenate([v[:, :3 * width // 2] for v in attn], axis=1)
    proj = jnp.concatenate([v[:, 3 * width // 2:] for v in attn], axis=1)
    totals = jnp.where(core == 0, totals_one, totals_two)
    tail = totals[16:24]
    return (
        encoded,
        images_grad,
        qkv[None],
        tail[2:4][None],
        proj[None],
        totals[24:24 + heads, :entries].T[None],
        jnp.stack([totals[SUM_SCALE_A], totals[SUM_SCALE_B]])[None],
        jnp.stack([tail[0], totals[SUM_GAIN_B]])[None],
        jnp.stack([tail[1], totals[SUM_SHIFT_B]])[None],
        jnp.concatenate(fc1, axis=1)[None],
        totals[FC1_BIAS:bias_at].reshape(1, -1),
        jnp.concatenate(fc2, axis=1)[None],
        jnp.stack([totals[SUM_DA], totals[SUM_DF]])[None],
    )


def solution(mesh):
    by_layer = P("narrow", None, None)
    by_rows = P("wide", "narrow", None)
    by_both = P("narrow", "wide", None)
    in_specs = (by_rows, by_rows, P("wide", None), P("wide", None, None)) + (by_layer,) * 8 + (
        P("narrow", None), by_layer, by_layer)
    out_specs = (by_rows, by_rows, by_both, by_layer, by_both, by_layer, by_layer, by_layer, by_layer, by_both,
                 P("narrow", None), by_both, by_layer)
    return jax.shard_map(shards, mesh=mesh, in_specs=in_specs, out_specs=out_specs, check_vma=False)
```

```python
import functools

import jax
import jax.numpy as jnp
from jax import lax
from jax.experimental import pallas as pl
from jax.experimental.pallas import tpu as pltpu
from jax.sharding import PartitionSpec as P

EPSILON = 1e-06
HALF_ROOT = 0.7071067811865476
DENSITY_NORM = 0.3989422804014327
GRID = 14
SPAN = 2 * GRID - 1
PITCH = 16
SLOTS = GRID * PITCH
LANES = 256
CLASS_SLOT = 15
WIDE = 32
STRIP = 512
HEAD_ROWS = 16
F32 = jnp.float32
BF16 = jnp.bfloat16
NEGATIVE = -1000000000.0
LAG = 3
LAG_BACK = 2
TILE = 80

GAIN_A, SHIFT_A, GAIN_B, SHIFT_B, SCALE_A, SCALE_B, OUT_A, OUT_B, FC1_BIAS = range(9)
QKV_BIAS = 12
SUM_DF, SUM_SCALE_B, SUM_GAIN_B, SUM_SHIFT_B, SUM_DA, SUM_SCALE_A = range(6)
SUM_GAIN_A, SUM_SHIFT_A, SUM_Q, SUM_V = range(4)


def nn(a, b):
    return lax.dot_general(a, b, (((1,), (0,)), ((), ())), preferred_element_type=F32)


def nt(a, b):
    return lax.dot_general(a, b, (((1,), (1,)), ((), ())), preferred_element_type=F32)


def tn(a, b):
    return lax.dot_general(a, b, (((0,), (0,)), ((), ())), preferred_element_type=F32)


def iota(shape, axis):
    return lax.broadcasted_iota(jnp.int32, shape, axis)


def row_tile(t):
    return pl.ds(pl.multiple_of(t * TILE, 16), TILE)


def vec(vec_ref, k):
    return vec_ref[k:k + 1, :]


def row_stats(v):
    centred = v - jnp.mean(v, axis=-1, keepdims=True)
    inverse = lax.rsqrt(jnp.mean(centred * centred, axis=-1, keepdims=True) + EPSILON)
    return centred * inverse, inverse


def norm_tiles(src_ref, dst_ref, vec_ref, gain, shift):
    @pl.loop(0, src_ref.shape[0] // TILE)
    def _(t):
        rows = row_tile(t)
        unit, _ = row_stats(src_ref[rows, :].astype(F32))
        dst_ref[rows, :] = (unit * vec(vec_ref, gain) + vec(vec_ref, shift)).astype(BF16)


def extra_rows(first, lanes):
    row = iota((16, lanes), 0)
    out = jnp.zeros((16, lanes), F32)
    for k, value in enumerate(first):
        out = jnp.where(row == k, value, out)
    return out.astype(BF16)


def split3(v):
    hi = v.astype(BF16).astype(F32)
    mid = (v - hi).astype(BF16).astype(F32)
    return hi, mid, v - hi - mid


class Weights:
    def __init__(self, core, own, other, dst, sems):
        self.core, self.own, self.other, self.dst, self.sems = core, own, other, dst, sems

    def start(self, name, layer, chunk=None):
        src, slot = (lambda ref: ref), None
        if name == "fc1":
            src = lambda ref: ref.at[:, pl.ds(pl.multiple_of(chunk * ref.shape[0], 128), ref.shape[0])]
        if name == "fc2":
            src = lambda ref: ref.at[pl.ds(pl.multiple_of(chunk * ref.shape[1], 128), ref.shape[1]), :]
        dst, sem = self.place(name, chunk)

        @pl.when(self.core == layer)
        def _():
            pltpu.make_async_copy(src(self.own[name]), dst, sem).start()

        @pl.when(self.core != layer)
        def _():
            pltpu.make_async_copy(src(self.other[name]), dst, sem).start()

    def place(self, name, chunk):
        if chunk is None:
            return self.dst[name], self.sems[name]
        return self.dst[name].at[lax.rem(chunk, 2)], self.sems[name].at[lax.rem(chunk, 2)]

    def wait(self, name, chunk=None):
        dst, sem = self.place(name, chunk)
        pltpu.make_async_copy(dst, dst, sem).wait()

    def start_fc(self, layer, chunk):
        self.start("fc1", layer, chunk)
        self.start("fc2", layer, chunk)


MATRICES = ("qkv", "proj", "fc1", "fc2")


def weight_scratch(width):
    dma = pltpu.SemaphoreType.DMA
    return [pltpu.VMEM((width, 3 * width), BF16), pltpu.VMEM((width, width), BF16),
            pltpu.VMEM((2, width, width), BF16), pltpu.VMEM((2, width, width), BF16), dma, dma, dma((2,)), dma((2,))]


def weights_of(core, refs, scratch):
    return Weights(core, dict(zip(MATRICES, refs[:4])), dict(zip(MATRICES, refs[4:8])), dict(zip(MATRICES, scratch[:4])),
                   dict(zip(MATRICES, scratch[4:8])))


def forward_kernel(keep, core_ref, ws_ref, x_ref, vec_refs, *refs):
    b_refs, et_ref, mask_ref, y_ref = refs[8:10], refs[10], refs[11], refs[12]
    if keep:
        xs_ref, n1_ref, o_ref, m_ref, n2_ref, a_ref, f_ref, zt_ref, ot_ref, lse_ref, g_ref, slope_ref = refs[13:25]
        scratch = refs[25:]
    else:
        n1_ref, o_ref, m_ref, n2_ref, zt_ref, ot_ref = refs[13:19]
        scratch = refs[19:]
    w = weights_of(core_ref[0], refs[:8], scratch[:8])
    x, b, bias, n1t, acc, wt, b_sem = scratch[8:]
    layer, t = pl.program_id(0), pl.program_id(1)
    imgs = et_ref.shape[0]
    heads = b.shape[0]
    width = x.shape[1]
    hd = width // heads
    chunks = pl.num_programs(1) - imgs
    at = (0,) if keep else ()
    vec_ref = vec_refs.at[layer]

    def start_b(k):
        pltpu.make_async_copy(b_refs[k], b, b_sem).start()

    @pl.when((layer == 0) & (t == 0))
    def _():
        w.start("qkv", 0)
        start_b(0)
        w.start("proj", 0)
        w.start_fc(0, 0)
        w.start_fc(0, 1)
        x[...] = x_ref[...]

    @pl.when(t == 0)
    def _():
        if keep:
            xs_ref[0] = x[...]
        o_ref[...] = jnp.zeros_like(o_ref)
        columns = vec_ref[8:16, :].T
        bias[0:width, :] = jnp.broadcast_to(columns[:, QKV_BIAS - 8:QKV_BIAS - 7], (width, 128))
        bias[width:2 * width, :] = jnp.zeros((width, 128), F32)
        bias[2 * width:, :] = jnp.broadcast_to(columns[:, QKV_BIAS - 7:QKV_BIAS - 6], (width, 128))
        norm_tiles(x, n1_ref.at[at] if keep else n1_ref, vec_ref, GAIN_A, SHIFT_A)
        w.wait("qkv")
        for c in range(3):
            part = slice(c * width, (c + 1) * width)
            wt[part, :] = w.dst["qkv"][:, part].T

    def full(ref):
        return ref.at[0] if keep else ref

    n1_now, o_now, m_now, n2_now = full(n1_ref), full(o_ref), full(m_ref), full(n2_ref)
    zt, ot = (zt_ref.at[0, 0], ot_ref.at[0, 0]) if keep else (zt_ref, ot_ref)

    @pl.when(t < imgs)
    def _():
        ws = pl.multiple_of(ws_ref[t], 16)
        et = et_ref[t]
        n1t[...] = tn(n1_now[pl.ds(ws, SLOTS), :], et).astype(BF16)

        @pl.loop(0, 3)
        def _(c):
            rows = pl.ds(pl.multiple_of(c * width, width), width)
            factor = jnp.where(c == 0, hd ** -0.5, 1.0)
            column = bias[rows, :]
            add = jnp.concatenate([column] * (LANES // 128), axis=1)
            zt[rows, :] = ((nn(wt[rows, :], n1t[...]) + add) * factor).astype(BF16)

        @pl.when(t == 0)
        def _():
            pltpu.make_async_copy(b, b, b_sem).wait()

        ones_q = extra_rows([1.0], LANES)
        mask_k = extra_rows([mask_ref[t]], SLOTS)
        ones_v = extra_rows([1.0], SLOTS)

        def scores(h):
            r = h * hd
            qt = jnp.concatenate([zt[r:r + hd, :], ones_q], axis=0)
            kt = jnp.concatenate([zt[width + r:width + r + hd, :SLOTS], mask_k], axis=0)
            return tn(kt, qt)

        def soft(h, s):
            s = s + b[h]
            m = jnp.max(s, axis=0, keepdims=True)
            return m, jnp.exp(s - m).astype(BF16)

        def finish(h, m, e):
            r = h * hd
            vt = jnp.concatenate([zt[2 * width + r:2 * width + r + hd, :SLOTS], ones_v], axis=0)
            o = nn(vt, e)
            total = o[hd:hd + 1]
            ot[r:r + hd, :] = (o[:hd] * (1.0 / total)).astype(BF16)
            if keep:
                lse_ref[0, 0, h:h + 1, :] = m + jnp.log(total)

        s, e = {}, {}
        for k in range(heads + 2 * LAG):
            if k < heads:
                s[k] = scores(k)
            if 0 <= k - LAG < heads:
                e[k - LAG] = soft(k - LAG, s.pop(k - LAG))
            if k - 2 * LAG >= 0:
                finish(k - 2 * LAG, *e.pop(k - 2 * LAG))

        win = pl.ds(ws, SLOTS)
        o_now[win, :] = (o_now[win, :].astype(F32) + nt(et, ot[...])).astype(BF16)

    j = t - imgs

    @pl.when((t == imgs) & (layer == 0))
    def _():
        w.start("qkv", 1)
        start_b(1)

    @pl.when(t == imgs)
    def _():
        w.wait("proj")
        a = nn(o_now[...], w.dst["proj"][...]) + vec(vec_ref, OUT_A)
        if keep:
            a_ref[0] = a.astype(BF16)
        m_now[...] = x[...].astype(F32) + vec(vec_ref, SCALE_A) * a
        acc[...] = jnp.zeros_like(acc)
        norm_tiles(m_now, n2_now, vec_ref, GAIN_B, SHIFT_B)

    @pl.when((t == imgs) & (layer == 0))
    def _():
        w.start("proj", 1)

    @pl.when(t >= imgs)
    def _():
        slot = lax.rem(j, 2)
        w.wait("fc1", j)
        w.wait("fc2", j)
        u = nn(n2_now[...], w.dst["fc1"][slot]) + vec_ref[pl.ds(FC1_BIAS + j, 1), :]
        cdf = 0.5 * (1.0 + lax.erf(u * HALF_ROOT))
        g = (u * cdf).astype(BF16)
        if keep:
            g_ref[0] = g
            slope_ref[0] = (cdf + u * (jnp.exp(-0.5 * u * u) * DENSITY_NORM)).astype(BF16)
        acc[...] += nn(g, w.dst["fc2"][slot])

        @pl.when(j + 2 < chunks)
        def _():
            w.start_fc(layer, j + 2)

        @pl.when((j + 2 >= chunks) & (layer == 0))
        def _():
            w.start_fc(1, j + 2 - chunks)

    @pl.when(j == chunks - 1)
    def _():
        @pl.loop(0, acc.shape[0] // TILE)
        def _(k):
            rows = row_tile(k)
            f = acc[rows, :] + vec(vec_ref, OUT_B)
            if keep:
                f_ref[0, rows, :] = f.astype(BF16)
            x[rows, :] = (m_now[rows, :] + vec(vec_ref, SCALE_B) * f).astype(BF16)

        @pl.when(layer == 1)
        def _():
            y_ref[...] = x[...]


def attn_bwd_kernel(pick_ref, ws_ref, da_ref, own_ref, other_ref, b_ref, et_ref, mask_ref, zt_ref, ot_ref, lse_ref,
                    dz_ref, db_ref, dat, dot, dzt):
    width = da_ref.shape[1]
    i = pl.program_id(0)

    @pl.when(i == 0)
    def _():
        dz_ref[...] = jnp.zeros_like(dz_ref)
        db_ref[...] = jnp.zeros_like(db_ref)
        dzt[...] = jnp.zeros_like(dzt)

    win = pl.ds(pl.multiple_of(ws_ref[i], 16), SLOTS)
    et = et_ref[0]
    dat[...] = tn(da_ref[win, :], et).astype(BF16)
    proj = jnp.where(pick_ref[0] == 1, own_ref[...], other_ref[...])
    dot[...] = nn(proj, dat[...]).astype(BF16)
    attn_back_image(et, mask_ref[0], zt_ref, ot_ref, lse_ref, b_ref, dat, dot, dzt, db_ref)
    for c in range(3):
        cols = slice(c * width, (c + 1) * width)
        dz_ref[win, cols] = (dz_ref[win, cols].astype(F32) + nt(et, dzt[cols, :])).astype(BF16)


def attn_back_image(et, mask, zt, ot, lse_ref, b, dat, dot, dzt, db_ref):
    heads = b.shape[0]
    width = dat.shape[0]
    hd = width // heads
    extra_k = extra_rows([mask, 1.0, 1.0, 1.0], SLOTS)
    extra_v = extra_rows([1.0, 1.0, 1.0], SLOTS)

    def parts(h):
        r = h * hd
        return (zt[r:r + hd, :], zt[width + r:width + r + hd, :SLOTS], zt[2 * width + r:2 * width + r + hd, :SLOTS],
                dot[r:r + hd, :])

    def products(h):
        qt, kt, vt, dt = parts(h)
        r = h * hd
        delta = jnp.sum(dt.astype(F32) * ot[r:r + hd, :].astype(F32), axis=0, keepdims=True)
        extra_q = extra_rows([1.0, *split3(-lse_ref[h:h + 1, :])], LANES)
        extra_d = extra_rows(split3(-delta), LANES)
        s = tn(jnp.concatenate([kt, extra_k], axis=0), jnp.concatenate([qt, extra_q], axis=0))
        dp = tn(jnp.concatenate([vt, extra_v], axis=0), jnp.concatenate([dt, extra_d], axis=0))
        return s, dp

    def middle(h, s, dp):
        p = jnp.exp(s + b[h])
        ds = p * dp
        if db_ref is not None:
            db_ref[h] += ds
        return p.astype(BF16), ds.astype(BF16)

    def finish(h, p, ds):
        qt, kt, vt, dt = parts(h)
        r = h * hd
        dzt[2 * width + r:2 * width + r + hd, :SLOTS] = nt(dt, p).astype(BF16)
        dzt[width + r:width + r + hd, :SLOTS] = nt(qt, ds).astype(BF16)
        dzt[r:r + hd, :] = (nn(kt, ds) * hd ** -0.5).astype(BF16)

    s, e = {}, {}
    for t in range(heads + 2 * LAG_BACK):
        if t < heads:
            s[t] = products(t)
        if 0 <= t - LAG_BACK < heads:
            e[t - LAG_BACK] = middle(t - LAG_BACK, *s.pop(t - LAG_BACK))
        if t - 2 * LAG_BACK >= 0:
            finish(t - 2 * LAG_BACK, *e.pop(t - 2 * LAG_BACK))


def backward_kernel(core_ref, ws_ref, dy_ref, vec_refs, *refs):
    b_refs, et_ref, mask_ref = refs[8:10], refs[10], refs[11]
    m_ref, x_ref, slope_ref, zt_ref, ot_ref, lse_ref, dx_ref = refs[12:19]
    scratch = refs[19:]
    w = weights_of(core_ref[0], refs[:8], scratch[:8])
    dy, df, acc, dm, da, dz, dat, dot, dzt, b, b_sem = scratch[8:]
    step, t = pl.program_id(0), pl.program_id(1)
    layer = 1 - step
    imgs = et_ref.shape[0]
    width = dy.shape[1]
    chunks = pl.num_programs(1) - imgs - 1
    vec_ref = vec_refs.at[layer]

    def start_b(k):
        pltpu.make_async_copy(b_refs[k], b, b_sem).start()

    @pl.when((step == 0) & (t == 0))
    def _():
        w.start_fc(1, 0)
        w.start_fc(1, 1)
        w.start("proj", 1)
        start_b(1)
        w.start("qkv", 1)
        dy[...] = dy_ref[...]

    @pl.when((step == 1) & (t == 0))
    def _():
        w.start("qkv", 0)

    @pl.when(t == 0)
    def _():
        acc[...] = jnp.zeros_like(acc)

        @pl.loop(0, df.shape[0] // TILE)
        def _(k):
            rows = row_tile(k)
            df[rows, :] = (dy[rows, :].astype(F32) * vec(vec_ref, SCALE_B)).astype(BF16)

    @pl.when(t < chunks)
    def _():
        slot = lax.rem(t, 2)
        w.wait("fc1", t)
        w.wait("fc2", t)
        du = (nt(df[...], w.dst["fc2"][slot]) * slope_ref[...].astype(F32)).astype(BF16)
        acc[...] += nt(du, w.dst["fc1"][slot])

        @pl.when(t + 2 < chunks)
        def _():
            w.start_fc(layer, t + 2)

        @pl.when((t + 2 >= chunks) & (step == 0))
        def _():
            w.start_fc(0, t + 2 - chunks)

    @pl.when(t == chunks - 1)
    def _():
        def emit(rows, dv):
            value = dy[rows, :].astype(F32) + dv
            dm[rows, :] = value
            da[rows, :] = (value * vec(vec_ref, SCALE_A)).astype(BF16)
            return ()

        norm_back_tiles(0, m_ref, acc, vec_ref, GAIN_B, emit)
        dz[...] = jnp.zeros_like(dz)
        dzt[...] = jnp.zeros_like(dzt)
        w.wait("proj")
        pltpu.make_async_copy(b, b, b_sem).wait()

    @pl.when((t >= chunks) & (t < chunks + imgs))
    def _():
        i = t - chunks
        et = et_ref[i]
        win = pl.ds(pl.multiple_of(ws_ref[i], 16), SLOTS)
        dat[...] = tn(da[win, :], et).astype(BF16)
        dot[...] = nn(w.dst["proj"][...], dat[...]).astype(BF16)
        attn_back_image(et, mask_ref[i], zt_ref, ot_ref, lse_ref, b, dat, dot, dzt, None)
        for c in range(3):
            cols = slice(c * width, (c + 1) * width)
            dz[win, cols] = (dz[win, cols].astype(F32) + nt(et, dzt[cols, :])).astype(BF16)

    @pl.when(t == chunks + imgs)
    def _():
        @pl.when(step == 0)
        def _():
            w.start("proj", 0)
            start_b(0)

        w.wait("qkv")
        acc[...] = nt(dz[:, :width], w.dst["qkv"][:, :width])
        for c in range(1, 3):
            cols = slice(c * width, (c + 1) * width)
            acc[...] += nt(dz[:, cols], w.dst["qkv"][:, cols])

        def emit(rows, dv):
            dy[rows, :] = (dm[rows, :] + dv).astype(BF16)
            return ()

        norm_back_tiles(0, x_ref, acc, vec_ref, GAIN_A, emit)

        @pl.when(step == 1)
        def _():
            dx_ref[...] = dy[...]


def spread(count):
    entry = iota((count, SPAN * WIDE), 0)
    lane = iota((count, SPAN * WIDE), 1)
    return jnp.where((entry == lane // WIDE * SPAN + lane % WIDE) & (lane % WIDE < SPAN), 1.0, 0.0).astype(BF16)


def squeeze():
    lane = iota((SPAN * WIDE, STRIP), 0)
    to = iota((SPAN * WIDE, STRIP), 1)
    return jnp.where(lane == to // PITCH * WIDE + to % PITCH, 1.0, 0.0).astype(BF16)


def placed(product, v, onehot):
    return sum(product(part.astype(BF16), onehot) for part in split3(v))


def strip_rows(layer, head):
    return pl.ds(layer * HEAD_ROWS + head, PITCH, stride=2 * HEAD_ROWS)


def bias_kernel(table_ref, *refs):
    b_refs, (shifted, strips) = refs[:2], refs[2:]
    rows = table_ref.shape[0]
    heads = b_refs[0].shape[0]
    wide = placed(nn, table_ref[...], spread(table_ref.shape[1]))
    for c in range(PITCH):
        shifted[c * rows:(c + 1) * rows, :] = pltpu.roll(wide, (c - GRID + 1) % (SPAN * WIDE), 1)
    packed = placed(nn, shifted[...], squeeze())
    for k in range(strips.shape[0]):
        strips[k] = packed[:, k * 128:(k + 1) * 128]
    row = iota((SLOTS, LANES), 0)
    col = iota((SLOTS, LANES), 1)
    for layer, b_ref in enumerate(b_refs):
        for h in range(heads):
            strip = jnp.concatenate([strips[k, strip_rows(layer, h), :] for k in range(strips.shape[0])], axis=1)
            for r in range(GRID):
                at = PITCH * (GRID - 1 - r)
                b_ref[h, r * PITCH:(r + 1) * PITCH, :] = strip[:, at:at + LANES]
            mine = layer * HEAD_ROWS + h
            query, key, both = [table_ref[mine:mine + 1, SPAN * SPAN + k:SPAN * SPAN + k + 1] for k in range(3)]
            full = jnp.where(col == CLASS_SLOT, query, b_ref[h])
            b_ref[h] = jnp.where(row == CLASS_SLOT, jnp.where(col == CLASS_SLOT, both, key), full)


def bias_back_kernel(db_ref, table_ref, strips, classes):
    table_ref[...] = folded(db_ref, strips, classes)


def folded(db_ref, strips, classes):
    heads = db_ref.shape[0]
    row = iota((SLOTS, LANES), 0)
    col = iota((SLOTS, LANES), 1)
    is_row = row == CLASS_SLOT
    is_col = col == CLASS_SLOT
    entry = iota((1, classes.shape[1]), 1) - SPAN * SPAN
    strips[...] = jnp.zeros_like(strips)
    classes[...] = jnp.zeros_like(classes)
    for h in range(heads):
        full = db_ref[h]
        query = jnp.sum(jnp.where(is_col & ~is_row, full, 0.0), keepdims=True)
        key = jnp.sum(jnp.where(is_row & ~is_col, full, 0.0), keepdims=True)
        both = jnp.sum(jnp.where(is_row & is_col, full, 0.0), keepdims=True)
        classes[h:h + 1, :] = jnp.where(
            entry == 0, query, jnp.where(entry == 1, key, jnp.where(entry == 2, both, 0.0)))
        plain = jnp.where(is_row | is_col, 0.0, full)
        total = jnp.zeros((PITCH, STRIP), F32)
        for r in range(GRID):
            part = jnp.concatenate([plain[r * PITCH:(r + 1) * PITCH, :], jnp.zeros((PITCH, STRIP - LANES), F32)],
                                   axis=1)
            total = total + pltpu.roll(part, PITCH * (GRID - 1 - r), 1)
        for k in range(strips.shape[0]):
            strips[k, pl.ds(h, PITCH, stride=HEAD_ROWS), :] = total[:, k * 128:(k + 1) * 128]
    rows = classes.shape[0]
    wide = placed(nt, jnp.concatenate([strips[k] for k in range(strips.shape[0])], axis=1), squeeze())
    gathered = jnp.zeros((rows, SPAN * WIDE), F32)
    for c in range(GRID):
        gathered = gathered + pltpu.roll(wide[c * rows:(c + 1) * rows, :], (GRID - 1 - c) % (SPAN * WIDE), 1)
    return placed(nt, gathered, spread(classes.shape[1])) + classes[...]


def norm_back_tiles(count, src_ref, grad_ref, vec_ref, gain, emit):
    def body(t, sums):
        rows = row_tile(t)
        unit, inverse = row_stats(src_ref[rows, :].astype(F32))
        grad = grad_ref[rows, :]
        scaled = grad * vec(vec_ref, gain)
        mean_one = jnp.mean(scaled, axis=-1, keepdims=True)
        mean_two = jnp.mean(scaled * unit, axis=-1, keepdims=True)
        more = emit(rows, inverse * (scaled - mean_one - unit * mean_two))
        if not count:
            return sums
        return tuple(s + jnp.sum(v, axis=0, keepdims=True) for s, v in zip(sums, (grad * unit, grad) + more))

    zero = jnp.zeros((1, grad_ref.shape[1]), F32)
    return lax.fori_loop(0, grad_ref.shape[0] // TILE, body, (zero,) * count)


def mlp_bwd_kernel(want, pick_ref, dy_ref, m_ref, vec_ref, slope_ref, fc1_own, fc1_other, fc2_own, fc2_other, *rest):
    if want:
        (n2_ref, g_ref, a_ref, f_ref, dm_ref, da_ref, fc1_give, fc1_keep, fc2_give, fc2_keep, sums_ref, df, acc) = rest
    else:
        dm_ref, da_ref, df, acc = rest
    j = pl.program_id(0)
    steps = pl.num_programs(0)
    mine = pick_ref[0] == 1
    core = pick_ref[1]
    width = dy_ref.shape[1]

    @pl.when(j == 0)
    def _():
        acc[...] = jnp.zeros_like(acc)
        if want:
            sums_ref[...] = jnp.zeros_like(sums_ref)
        zero = jnp.zeros((1, width), F32)

        def body(t, sums):
            rows = row_tile(t)
            dy = dy_ref[rows, :].astype(F32)
            scaled = (dy * vec(vec_ref, SCALE_B)).astype(BF16)
            df[rows, :] = scaled
            if not want:
                return sums
            return (sums[0] + jnp.sum(scaled.astype(F32), axis=0, keepdims=True),
                    sums[1] + jnp.sum(dy * f_ref[rows, :].astype(F32), axis=0, keepdims=True))

        sums = lax.fori_loop(0, df.shape[0] // TILE, body, (zero, zero) if want else ())
        if want:
            sums_ref[SUM_DF:SUM_DF + 1, :] = sums[0]
            sums_ref[SUM_SCALE_B:SUM_SCALE_B + 1, :] = sums[1]

    fc1 = jnp.where(mine, fc1_own[...], fc1_other[...])
    fc2 = jnp.where(mine, fc2_own[...], fc2_other[...])
    du = (nt(df[...], fc2) * slope_ref[...].astype(F32)).astype(BF16)
    acc[...] += nt(du, fc1)
    if want:
        at = lax.rem(j + (1 - core) * (steps // 2), steps)
        sums_ref[pl.ds(FC1_BIAS + at, 1), :] = jnp.sum(du.astype(F32), axis=0, keepdims=True)
        grad = tn(g_ref[...], df[...]).astype(BF16)
        low, high = grad[:, :width // 2], grad[:, width // 2:]
        fc2_keep[...] = jnp.where(core == 0, low, high)
        fc2_give[...] = jnp.where(core == 0, high, low)
        grad1 = tn(n2_ref[...], du).astype(BF16)

        @pl.when(j < steps // 2)
        def _():
            fc1_give[...] = grad1

        @pl.when(j >= steps // 2)
        def _():
            fc1_keep[...] = grad1

    @pl.when(j == steps - 1)
    def _():
        def emit(rows, dv):
            dm = dy_ref[rows, :].astype(F32) + dv
            da = (dm * vec(vec_ref, SCALE_A)).astype(BF16)
            dm_ref[rows, :] = dm
            da_ref[rows, :] = da
            return (da.astype(F32), dm * a_ref[rows, :].astype(F32)) if want else ()

        sums = norm_back_tiles(4 if want else 0, m_ref, acc, vec_ref, GAIN_B, emit)
        for k, s in zip((SUM_GAIN_B, SUM_SHIFT_B, SUM_DA, SUM_SCALE_A), sums):
            sums_ref[k:k + 1, :] = s


def attn_tail_kernel(want, pick_ref, x_ref, dm_ref, vec_ref, dz_ref, wt_own, wt_other, *rest):
    if want:
        n1_ref, o_ref, da_ref, dx_ref, give_ref, keep_ref, sums_ref, acc = rest
    else:
        dx_ref, acc = rest
    j = pl.program_id(0)
    core = pick_ref[1]
    width = x_ref.shape[1]

    @pl.when(j == 0)
    def _():
        acc[...] = jnp.zeros_like(acc)
        if want:
            sums_ref[...] = jnp.zeros_like(sums_ref)
            grad = tn(o_ref[...], da_ref[...]).astype(BF16)
            low, high = grad[:, :width // 2], grad[:, width // 2:]
            keep_ref[:, 3 * width // 2:] = jnp.where(core == 0, low, high)
            give_ref[:, 3 * width // 2:] = jnp.where(core == 0, high, low)

    dz = dz_ref[...]
    acc[...] += nt(dz, jnp.where(pick_ref[0] == 1, wt_own[...], wt_other[...]))
    if want:
        half = lax.rem(j + 1 - core, 2)
        columns = jnp.sum(dz.astype(F32), axis=0, keepdims=True)

        @pl.when(half == 0)
        def _():
            sums_ref[SUM_Q:SUM_Q + 1, :] = columns[:, :width]

        @pl.when(half == 1)
        def _():
            sums_ref[SUM_V:SUM_V + 1, :] = columns[:, width // 2:]

        grad1 = tn(n1_ref[...], dz).astype(BF16)

        @pl.when(j == 0)
        def _():
            give_ref[:, :3 * width // 2] = grad1

        @pl.when(j == 1)
        def _():
            keep_ref[:, :3 * width // 2] = grad1

    @pl.when(j == pl.num_programs(0) - 1)
    def _():
        def emit(rows, dv):
            dx_ref[rows, :] = (dm_ref[rows, :] + dv).astype(BF16)
            return ()

        sums = norm_back_tiles(2 if want else 0, x_ref, acc, vec_ref, GAIN_A, emit)
        for k, s in enumerate(sums):
            sums_ref[k:k + 1, :] = s


TAKES = dict(backward=85, forward=75, forward_keep=85, mlp_bwd=15, mlp_bwd_all=27, attn_bwd=20, attn_bwd_all=21, attn_tail=9,
             attn_tail_all=16, bias_build=6, bias_back=9)


VMEM = dict(backward=60, forward=60, forward_keep=60, mlp_bwd=60, mlp_bwd_all=60, attn_bwd=60, attn_bwd_all=60, attn_tail=60,
            attn_tail_all=60, bias_build=60, bias_back=60)


def cost(name):
    return pl.CostEstimate(flops=TAKES[name] * 800_000_000, bytes_accessed=TAKES[name] * 3_000_000, transcendentals=0)


def params(name):
    return pltpu.CompilerParams(vmem_limit_bytes=VMEM[name] * 1024 * 1024)


def shaped(*arrays):
    return [jax.ShapeDtypeStruct(s, d) for s, d in arrays]


def whole(shape):
    return pl.BlockSpec(shape, lambda *_: (0,) * len(shape))


def once(shape):
    return pl.BlockSpec(shape, lambda *_: (0,) * len(shape), pipeline_mode=pl.Buffered(1))


def per_image(shape):
    return pl.BlockSpec((1,) + shape, lambda i, *_: (i,) + (0,) * len(shape))


def call(kernel, name, prefetched, grid, inputs, outputs, scratch, after=()):
    count = len(prefetched) + len(inputs)

    def body(*refs):
        kernel(*refs[:count], *refs[count + len(after):])

    inputs = inputs + [(a, pl.BlockSpec(memory_space=pl.ANY)) for a in after]
    return pl.pallas_call(
        body,
        grid_spec=pltpu.PrefetchScalarGridSpec(
            num_scalar_prefetch=len(prefetched), grid=grid, in_specs=[s for _, s in inputs],
            out_specs=[s for _, _, s in outputs], scratch_shapes=scratch),
        out_shape=[jax.ShapeDtypeStruct(s, d) for s, d, _ in outputs],
        compiler_params=params(name), name=name, cost_estimate=cost(name),
    )(*prefetched, *[a for a, _ in inputs])


def forward(keep, x, section, meta):
    core, ws, et, mask = meta
    rows, width = x.shape
    biases = section["bias"]
    heads = biases[0].shape[0]
    hidden = section["own"]["fc1"].shape[1]
    imgs = et.shape[0]
    chunks = hidden // width
    anywhere = pl.BlockSpec(memory_space=pl.ANY)
    vectors = section["vectors"]
    inputs = [(x, once(x.shape)), (vectors, once(vectors.shape))]
    inputs += [(section[side][name], anywhere) for side in ("own", "other") for name in MATRICES]
    inputs += [(v, anywhere) for v in biases] + [(et, once(et.shape)), (mask, once(mask.shape))]
    outputs = [((rows, width), BF16, whole((rows, width)))]
    low = [pltpu.VMEM((rows, width), BF16)]
    scratch = weight_scratch(width) + low + [
        pltpu.VMEM(biases[0].shape, F32), pltpu.VMEM((3 * width, 128), F32), pltpu.VMEM((width, LANES), BF16),
        pltpu.VMEM((rows, width), F32), pltpu.VMEM((3 * width, width), BF16), pltpu.SemaphoreType.DMA]
    if keep:
        def of_layer(kind):
            return (2, rows, width), kind, pl.BlockSpec((1, rows, width), lambda l, t, *_: (l, 0, 0))

        def of_image(*shape, kind=BF16):
            return ((2, imgs) + shape, kind,
                    pl.BlockSpec((1, 1) + shape, lambda l, t, *_: (l, jnp.minimum(t, imgs - 1), 0, 0)))

        of_chunk = ((2, rows, hidden), BF16,
                    pl.BlockSpec((1, rows, width), lambda l, t, *_: (l, 0, jnp.maximum(t - imgs, 0))))
        outputs += [of_layer(BF16), of_layer(BF16), of_layer(BF16), of_layer(F32), of_layer(BF16), of_layer(BF16),
                    of_layer(BF16), of_image(3 * width, LANES), of_image(width, LANES),
                    of_image(heads, LANES, kind=F32), of_chunk, of_chunk]
    else:
        scratch = low * 2 + [pltpu.VMEM((rows, width), F32)] + low + [
            pltpu.VMEM((3 * width, LANES), BF16), pltpu.VMEM((width, LANES), BF16)] + scratch
    return call(functools.partial(forward_kernel, keep), "forward_keep" if keep else "forward", [core, ws],
                (2, imgs + chunks), inputs, outputs, scratch)


def backward(dy, section, meta, kept):
    core, ws, et, mask = meta
    rows, width = dy.shape
    biases = section["bias"]
    imgs = et.shape[0]
    chunks = section["own"]["fc1"].shape[1] // width
    anywhere = pl.BlockSpec(memory_space=pl.ANY)
    vectors = section["vectors"]
    inputs = [(dy, once(dy.shape)), (vectors, once(vectors.shape))]
    inputs += [(section[side][name], anywhere) for side in ("own", "other") for name in MATRICES]
    inputs += [(v, anywhere) for v in biases] + [(et, once(et.shape)), (mask, once(mask.shape))]
    of_layer = pl.BlockSpec((None, rows, width), lambda l, t, *_: (1 - l, 0, 0))
    inputs += [(kept["m"], of_layer), (kept["x"], of_layer)]
    inputs += [(kept["slope"], pl.BlockSpec((None, rows, width),
                                            lambda l, t, *_: (1 - l, 0, jnp.minimum(t, chunks - 1))))]
    for name in ("zt", "ot", "lse"):
        v = kept[name]
        inputs += [(v, pl.BlockSpec((None, None) + v.shape[2:],
                                    lambda l, t, *_: (1 - l, jnp.clip(t - chunks, 0, imgs - 1), 0, 0)))]
    low, high = pltpu.VMEM((rows, width), BF16), pltpu.VMEM((rows, width), F32)
    slots = pltpu.VMEM((width, LANES), BF16)
    scratch = weight_scratch(width) + [
        low, low, high, high, low, pltpu.VMEM((rows, 3 * width), BF16), slots, slots,
        pltpu.VMEM((3 * width, LANES), BF16), pltpu.VMEM(biases[0].shape, F32), pltpu.SemaphoreType.DMA]
    return call(backward_kernel, "backward", [core, ws], (2, chunks + imgs + 1), inputs,
                [((rows, width), BF16, whole((rows, width)))], scratch)[0]


def attn_bwd(da, w, meta, kept, after=()):
    _, ws, et, mask = meta
    rows, width = da.shape
    bias = w["bias"]
    imgs = et.shape[0]
    single_proj = once((width, width))
    layer = w["layer"]

    def kept_image(name):
        v = kept[name]
        return v, pl.BlockSpec((None, None) + v.shape[2:], lambda i, *_: (layer, i, 0, 0))

    inputs = [(da, once(da.shape)), (w["proj"][0], single_proj), (w["proj"][1], single_proj), (bias, once(bias.shape)),
              (et, per_image(et.shape[1:])), (mask, per_image(mask.shape[1:])), kept_image("zt"),
              kept_image("ot"), kept_image("lse")]
    outputs = [((rows, 3 * width), BF16, whole((rows, 3 * width)))]
    outputs += [(bias.shape, F32, whole(bias.shape))]
    scratch = [pltpu.VMEM((width, LANES), BF16), pltpu.VMEM((width, LANES), BF16), pltpu.VMEM((3 * width, LANES), BF16)]
    return call(attn_bwd_kernel, "attn_bwd_all", [w["pick"], ws],
                (imgs,), inputs, outputs, scratch, after)


def build_bias(tables, heads):
    shape = (heads, SLOTS, LANES)
    rows = tables.shape[0]
    return call(bias_kernel, "bias_build", [], (1,), [(tables, once(tables.shape))], [(shape, F32, whole(shape))] * 2,
                [pltpu.VMEM((PITCH * rows, SPAN * WIDE), F32), pltpu.VMEM((STRIP // 128, PITCH * rows, 128), F32)])


def table_back(db, lanes, after=()):
    return call(bias_back_kernel, "bias_back", [], (1,), [(db, once(db.shape))],
                [((HEAD_ROWS, lanes), F32, whole((HEAD_ROWS, lanes)))],
                [pltpu.VMEM((STRIP // 128, PITCH * HEAD_ROWS, 128), F32), pltpu.VMEM((HEAD_ROWS, lanes), F32)],
                after)[0]


def chosen(which, block, to_index):
    def index(j, pick):
        used = pick[0] if which == 0 else 1 - pick[0]
        return tuple(k * used for k in to_index(j, pick))
    return pl.BlockSpec(block, index)


def both(pair, block, to_index):
    return [(pair[k], chosen(k, block, to_index)) for k in range(2)]


def kept_whole(kept, name, w):
    v, layer = kept[name], w["layer"]
    return v, pl.BlockSpec((None,) + v.shape[1:], lambda *_: (layer, 0, 0), pipeline_mode=pl.Buffered(1))


def mlp_bwd(want, dy, w, kept, after=()):
    rows, width = dy.shape
    hidden = w["fc1"][0].shape[1]
    steps = hidden // width
    full = whole((rows, width))
    single = once((rows, width))

    def at(j, pick):
        return lax.rem(j + (1 - pick[1]) * (steps // 2), steps)

    layer = w["layer"]
    part = pl.BlockSpec((None, rows, width), lambda j, p: (layer, 0, at(j, p)))
    inputs = [(dy, single), kept_whole(kept, "m", w), (w["vectors"], once(w["vectors"].shape)), (kept["slope"], part),
              *both(w["fc1"], (width, width), lambda j, p: (0, at(j, p))),
              *both(w["fc2"], (width, width), lambda j, p: (at(j, p), 0))]
    outputs = [((rows, width), F32, full), ((rows, width), BF16, full)]
    if want:
        inputs += [kept_whole(kept, "n2", w), (kept["g"], part), kept_whole(kept, "a", w), kept_whole(kept, "f", w)]
        half = pl.BlockSpec((width, width // 2), lambda j, p: (at(j, p), 0))
        give = pl.BlockSpec((width, width), lambda j, p: (0, jnp.minimum(j, steps // 2 - 1)))
        stay = pl.BlockSpec((width, width), lambda j, p: (0, jnp.maximum(j - steps // 2, 0)))
        outputs += [((width, hidden // 2), BF16, give), ((width, hidden // 2), BF16, stay),
                    ((hidden, width // 2), BF16, half), ((hidden, width // 2), BF16, half),
                    ((16, width), F32, whole((16, width)))]
    scratch = [pltpu.VMEM((rows, width), BF16), pltpu.VMEM((rows, width), F32)]
    return call(functools.partial(mlp_bwd_kernel, want), "mlp_bwd_all" if want else "mlp_bwd", [w["pick"]],
                (steps,), inputs, outputs, scratch, after)


def attn_tail(want, dm, dz, da, w, kept, after=()):
    rows, width = dm.shape
    part = 3 * width // 2
    full = whole((rows, width))
    single = once((rows, width))

    def at(j, pick):
        return lax.rem(j + 1 - pick[1], 2)

    inputs = [kept_whole(kept, "x", w), (dm, single), (w["vectors"], once(w["vectors"].shape)),
              (dz, pl.BlockSpec((rows, part), lambda j, p: (0, at(j, p)))),
              *both(w["qkv"], (width, part), lambda j, p: (0, at(j, p)))]
    outputs = [((rows, width), BF16, full)]
    if want:
        inputs += [kept_whole(kept, "n1", w), kept_whole(kept, "o", w), (da, single)]
        outputs += [((width, 2 * width), BF16, whole((width, 2 * width)))] * 2
        outputs += [((8, width), F32, whole((8, width)))]
    return call(functools.partial(attn_tail_kernel, want), "attn_tail_all" if want else "attn_tail", [w["pick"]],
                (2,), inputs, outputs, [pltpu.VMEM((rows, width), F32)], after)


def sequence_meta(ids, order, rows):
    imgs, patches = order.shape
    image = jnp.arange(imgs, dtype=jnp.int32)
    start = jnp.sum((ids[None, :] < image[:, None]).astype(jnp.int32), axis=1)
    count = jnp.sum((ids[None, :] == image[:, None]).astype(jnp.int32), axis=1)
    ws = jnp.minimum(start // 16 * 16, rows - SLOTS)
    slot = jnp.arange(LANES, dtype=jnp.int32)
    is_class = slot == CLASS_SLOT
    is_patch = (slot % PITCH < GRID) & (slot < SLOTS)
    patch = jnp.where(is_patch, slot // PITCH * GRID + slot % PITCH, -1)
    place = jnp.arange(1, patches + 1, dtype=jnp.int32)
    offset = jnp.sum(jnp.where(order[:, None, :] == patch[None, :, None], place, 0), axis=2)
    valid = (is_class | is_patch)[None, :] & (offset < count[:, None])
    local = jnp.where(valid, offset + (start - ws)[:, None], -1)
    row = jnp.arange(SLOTS, dtype=jnp.int32)
    et = (local[:, None, :] == row[None, :, None]).astype(BF16)
    mask = jnp.where(valid, 0.0, NEGATIVE).astype(F32)[:, None, :SLOTS]
    return ws, et, mask


KEPT = ("x", "n1", "o", "m", "n2", "a", "f", "zt", "ot", "lse", "g", "slope")


def later(arrays, token):
    if token is None:
        return list(arrays)
    return list(lax.optimization_barrier((*arrays, token)))[:-1]


class Reducer:
    def __init__(self, keep, give, swap_core, swap_wide, at_wide, wide, at_once=None):
        self.swap_wide, self.at_wide = swap_wide, at_wide
        if at_once is not None:
            send, stay = at_once
            self.sent, self.parts = [send], [stay]
            self.left, self.bit = wide // 2, 2
            return
        shape = (wide, keep.shape[0] // wide, keep.shape[1])
        self.parts = [v.reshape(shape) for v in (keep, swap_core(give))]
        self.left, self.bit = wide, 1
        self.sent = []

    def launch(self, token=None):
        self.parts.append(self.swap_wide(later(self.sent, token)[0], 1))
        return self

    def hold(self, token):
        self.parts[-1], = later([self.parts[-1]], token)

    def added(self, parts):
        return sum(v.astype(F32) for v in parts)

    def step(self, token=None):
        if self.left == 1:
            return
        self.hold(token)
        mine = self.at_wide // self.bit % 2
        pairs = [v.reshape((self.left // 2, 2) + v.shape[1:]) for v in self.parts]
        self.sent = [self.added(lax.dynamic_index_in_dim(v, 1 - mine, 1, keepdims=False) for v in pairs).astype(BF16)]
        self.parts = [lax.dynamic_index_in_dim(v, mine, 1, keepdims=False) for v in pairs]
        self.parts.append(self.swap_wide(self.sent[0], self.bit))
        self.left, self.bit = self.left // 2, 2 * self.bit

    def two(self):
        return [self.added(self.parts[:-1]).astype(BF16), self.parts[-1]]

    def finish(self, token=None):
        while self.left > 1:
            self.step(token)
        self.hold(token)
        return self.added(self.parts)[0]


def swap_sums_kernel(count, *refs):
    keeps, gives, outs = refs[:count], refs[count:2 * count], refs[2 * count:4 * count]
    mine, come = refs[4 * count:5 * count], refs[5 * count:6 * count]
    local_sem, send_sem, recv_sem = refs[6 * count:]
    me = lax.axis_index("narrow")
    b = lax.axis_index("wide") % 2
    partner = {"narrow": me + 1 - 2 * (me % 2)}
    barrier = pltpu.get_barrier_semaphore()
    pl.semaphore_signal(barrier, inc=1, device_id=partner, device_id_type=pl.DeviceIdType.MESH)
    pl.semaphore_wait(barrier, 1)
    copies = []
    for k in range(count):
        remote = pltpu.make_async_remote_copy(
            src_ref=gives[k], dst_ref=come[k], send_sem=send_sem.at[k], recv_sem=recv_sem.at[k], device_id=partner,
            device_id_type=pl.DeviceIdType.MESH)
        local = pltpu.make_async_copy(keeps[k], mine[k], local_sem.at[k])
        remote.start()
        local.start()
        copies.append((remote, local))
    for k in range(count):
        for copy in copies[k]:
            copy.wait()
        send, stay = outs[2 * k:2 * k + 2]

        @pl.loop(0, send.shape[0])
        def _(i):
            for to, index in ((send, 2 * i + 1 - b), (stay, 2 * i + b)):
                to[i] = (mine[k][index].astype(F32) + come[k][index].astype(F32)).astype(BF16)


def swap_sums(halves, wide):
    count = len(halves)
    blocks = [(keep.shape[0] // wide, keep.shape[1]) for keep, _ in halves]
    anywhere = pl.BlockSpec(memory_space=pl.ANY)
    dma = pltpu.SemaphoreType.DMA
    out = pl.pallas_call(
        functools.partial(swap_sums_kernel, count), in_specs=[anywhere] * 2 * count,
        out_specs=[pl.BlockSpec(memory_space=pltpu.VMEM)] * 2 * count,
        out_shape=[jax.ShapeDtypeStruct((wide // 2,) + block, BF16) for block in blocks for _ in range(2)],
        scratch_shapes=[pltpu.VMEM((wide,) + block, BF16) for _ in range(2) for block in blocks]
        + [dma((count,))] * 3,
        compiler_params=pltpu.CompilerParams(vmem_limit_bytes=60 * 1024 * 1024, collective_id=count,
                                             has_side_effects=True),
        cost_estimate=pl.CostEstimate(flops=0, bytes_accessed=30_000_000, transcendentals=0), name="swap_sums",
    )(*[h[k].reshape((wide,) + block) for k in range(2) for h, block in zip(halves, blocks)])
    return [(out[2 * k], out[2 * k + 1]) for k in range(count)]


FC2, FC1, FC1_MORE, ATTN, ATTN_MORE, SMALL, ROWS = range(7)
ROW_STEP, ROW_WINDOW = 192, 224
CORE, Y, Z0, Z1, FINAL = range(5)


def last_sums_kernel(cuts, counts, *refs):
    pairs, twos, small_refs, db_refs, row_refs = refs[:6], refs[6:12], refs[12:16], refs[16:18], refs[18:20]
    out_fc2, out_fc1, out_attn, small_out, rows_out = refs[20:25]
    scratch = list(refs[25:])
    db, strips, classes, db_sem, row_buf, row_sem, small_low = scratch[-11:-4]
    small_got, send_sem, recv_sem, local_sem = scratch[-4:]
    me = lax.axis_index("narrow")
    at = lax.axis_index("wide")
    core = me % 2
    half = {hop: at // bit % 2 for hop, bit in ((Y, 1), (Z0, 2), (Z1, 4))}
    core_partner = {"narrow": me + 1 - 2 * core}
    across = {"narrow": me + 2 - 4 * (me // 2)}
    corner = {"narrow": 3 - me}
    partners = {CORE: core_partner, FINAL: core_partner}
    for hop, bit in ((Y, 1), (Z0, 2), (Z1, 4)):
        partners[hop] = {"wide": at + bit * (1 - 2 * half[hop])}
    greeted = [core_partner, across, corner] + [partners[hop] for hop in (Y, Z0, Z1)]
    barrier = pltpu.get_barrier_semaphore()
    for partner in greeted:
        pl.semaphore_signal(barrier, inc=1, device_id=partner, device_id_type=pl.DeviceIdType.MESH)
    pl.semaphore_wait(barrier, len(greeted))

    def remote(src, dst, row, hop, device=None):
        return pltpu.make_async_remote_copy(
            src_ref=src, dst_ref=dst, send_sem=send_sem.at[row, hop], recv_sem=recv_sem.at[row, hop],
            device_id=partners[hop] if device is None else device, device_id_type=pl.DeviceIdType.MESH)

    first, second, levels, last = {}, {}, {}, {}
    for p, (k, cut) in enumerate(cuts):
        n = counts[p]
        mine, come = scratch.pop(0), scratch.pop(0)
        first[p] = (pairs[2 * k].at[:, :, cut], mine)
        second[p] = (pairs[2 * k + 1].at[:, :, cut], come)
        levels[p] = [(None, mine, come)]
        while n > 1:
            n //= 2
            levels[p].append((scratch.pop(0), scratch.pop(0), scratch.pop(0)))
        last[p] = (scratch.pop(0), scratch.pop(0))
    pending = {}

    def begin(p):
        pending[p] = [pltpu.make_async_copy(*first[p], local_sem.at[p, 0])]
        if p in (ATTN, ATTN_MORE):
            pending[p].append(remote(*second[p], p, CORE))
        else:
            pending[p].append(pltpu.make_async_copy(*second[p], local_sem.at[p, 1]))
        for c in pending[p]:
            c.start()

    def wait(p):
        for c in pending[p]:
            c.wait()

    def hop(p, n):
        wait(p)
        level = counts[p].bit_length() - n.bit_length()
        _, mine, come = levels[p][level]
        send, stay, next_come = levels[p][level + 1]
        which = {8: Y, 4: Z0, 2: Z1}[n]
        b = half[which]

        def add(to, i, index):
            to[i] = (mine[index].astype(F32) + come[index].astype(F32)).astype(BF16)

        @pl.loop(0, n // 2)
        def _(i):
            add(send, i, 2 * i + 1 - b)

        copy = remote(send, next_come, p, which)
        copy.start()
        pending[p] = [copy]

        @pl.loop(0, n // 2)
        def _(i):
            add(stay, i, 2 * i + b)

    def total(p):
        wait(p)
        _, stay, come = levels[p][-1]
        return stay[0].astype(F32) + come[0].astype(F32)

    outs = {FC2: out_fc2, FC1: out_fc1, FC1_MORE: out_fc1, ATTN: out_attn, ATTN_MORE: out_attn}
    others = {FC2: twos[:2], FC1: twos[2:4], FC1_MORE: twos[2:4], ATTN: twos[4:], ATTN_MORE: twos[4:]}

    def end(p):
        cut = cuts[p][1]
        one = total(p)
        two = sum(ref[0, :, cut].astype(F32) for ref in others[p])
        give, come = last[p]
        give[...] = jnp.where(core == 0, two, one).astype(BF16)
        copy = remote(give, come, p, FINAL)
        copy.start()
        pending[p] = [copy]
        outs[p][core, :, cut] = jnp.where(core == 0, one, two)

    def close(p):
        wait(p)
        outs[p][1 - core, :, cuts[p][1]] = last[p][1][...].astype(F32)

    small = {}

    def small_send(h):
        small_low[...] = small_out[...].astype(BF16)
        small[h] = remote(small_low, small_got.at[h], SMALL, h)
        small[h].start()

    def small_take(h):
        small[h].wait()
        small_out[...] = small_low[...].astype(F32) + small_got[h].astype(F32)

    for p in (ATTN, ATTN_MORE, FC2, FC1, FC1_MORE):
        begin(p)
    db_copies = [pltpu.make_async_copy(ref, db.at[k], db_sem.at[k]) for k, ref in enumerate(db_refs)]
    for c in db_copies:
        c.start()
    row_copies = []
    for k, (device, block) in enumerate(((core_partner, me + 1 - 2 * core), (across, me + 2 - 4 * (me // 2)),
                                         (corner, 3 - me))):
        window = pl.ds(pl.multiple_of(block * ROW_STEP, 16), ROW_WINDOW)
        row_copies.append(remote(row_buf.at[window, :], rows_out.at[k], ROWS, k, device))
    for k in range(2):
        @pl.when(me // 2 == k)
        def _():
            pltpu.make_async_copy(row_refs[k], row_buf, row_sem).start()

    hop(FC2, 2)
    hop(FC1, 4)
    hop(FC1_MORE, 4)
    hop(ATTN, 8)
    hop(ATTN_MORE, 8)
    pltpu.make_async_copy(row_refs[0], row_buf, row_sem).wait()
    for c in row_copies:
        c.start()
    row = 0
    for ref in small_refs:
        small_out[row:row + ref.shape[0], :] = ref[...]
        row += ref.shape[0]
    db_copies[0].wait()
    small_out[row:row + HEAD_ROWS, :] = folded(db.at[0], strips, classes)
    end(FC2)
    hop(FC1, 2)
    db_copies[1].wait()
    small_out[row + HEAD_ROWS:, :] = folded(db.at[1], strips, classes)
    small_send(CORE)
    hop(FC1_MORE, 2)
    small_take(CORE)
    small_send(Z0)
    hop(ATTN, 4)
    end(FC1)
    end(FC1_MORE)
    hop(ATTN_MORE, 4)
    small_take(Z0)
    small_send(Y)
    hop(ATTN, 2)
    for p in (FC2, FC1, FC1_MORE):
        close(p)
    hop(ATTN_MORE, 2)
    small_take(Y)
    small_send(Z1)
    end(ATTN)
    for c in row_copies:
        c.wait()
    end(ATTN_MORE)
    small_take(Z1)
    close(ATTN)
    close(ATTN_MORE)


def last_sums(pairs, two, small, db, rows):
    anywhere = pl.BlockSpec(memory_space=pl.ANY)
    vmem = pl.BlockSpec(memory_space=pltpu.VMEM)
    scratch, cuts, counts = [], [], []
    for k, many in enumerate((1, 2, 2)):
        p = pairs[k][0]
        size = p.shape[2] // many
        for c in range(many):
            n, block = p.shape[0], (p.shape[1], size)
            cuts.append((k, slice(c * size, (c + 1) * size)))
            counts.append(n)
            scratch += [pltpu.VMEM((n,) + block, BF16)] * 2
            while n > 1:
                n //= 2
                scratch += [pltpu.VMEM((n,) + block, BF16)] * 3
            scratch += [pltpu.VMEM(block, BF16)] * 2
    lanes = small[0].shape[1]
    count = sum(v.shape[0] for v in small) + 2 * HEAD_ROWS
    scratch += [pltpu.VMEM((2,) + db[0].shape, F32), pltpu.VMEM((STRIP // 128, PITCH * HEAD_ROWS, 128), F32),
                pltpu.VMEM((HEAD_ROWS, lanes), F32), pltpu.SemaphoreType.DMA((2,)),
                pltpu.VMEM(rows[0].shape, BF16), pltpu.SemaphoreType.DMA, pltpu.VMEM((count, lanes), BF16),
                pltpu.VMEM((4, count, lanes), BF16)]
    scratch += [pltpu.SemaphoreType.DMA((7, 5)), pltpu.SemaphoreType.DMA((7, 5)), pltpu.SemaphoreType.DMA((5, 2))]
    return pl.pallas_call(
        functools.partial(last_sums_kernel, cuts, counts),
        in_specs=[anywhere] * 6 + [vmem] * 10 + [anywhere] * 4,
        out_specs=[vmem] * 5,
        out_shape=[jax.ShapeDtypeStruct((2,) + p.shape[1:], F32) for p, _ in pairs]
        + [jax.ShapeDtypeStruct((count, lanes), F32), jax.ShapeDtypeStruct((3, ROW_WINDOW, lanes), BF16)],
        scratch_shapes=scratch,
        compiler_params=pltpu.CompilerParams(vmem_limit_bytes=60 * 1024 * 1024, collective_id=0, has_side_effects=True),
        cost_estimate=pl.CostEstimate(flops=0, bytes_accessed=300_000_000, transcendentals=0), name="last_sums",
    )(*[v for pair in pairs for v in pair], *two, *small, *db, *rows)


def shards(images, cotangent, image_ids, patch_order, qkv_weight, qv_bias, proj_weight, rel_table, layer_scales,
           layer_norm_gains, norm_biases, fc1_weight, fc1_bias, fc2_weight, out_biases):
    me = lax.axis_index("narrow")
    at_wide = lax.axis_index("wide")
    wide = lax.axis_size("wide")
    core = me % 2
    first = me < 2
    quarter, width = images.shape[1:]
    rows = 4 * quarter
    padded = -(-rows // TILE) * TILE
    entries, heads = rel_table.shape[1:]
    flips = {k: [(d, d ^ k) for d in range(4)] for k in (1, 2, 3)}

    def swap(v, k):
        return lax.ppermute(v, "narrow", flips[k])

    def swap_wide(v, k):
        return lax.ppermute(v, "wide", [(d, d ^ k) for d in range(wide)])

    def pick(v, index):
        return lax.dynamic_index_in_dim(v, index, 0, keepdims=False)

    smalls = jnp.concatenate([layer_norm_gains[0, :1], norm_biases[0, :1], layer_norm_gains[0, 1:], norm_biases[0, 1:],
                              layer_scales[0], out_biases[0], fc1_bias.reshape(-1, width), qv_bias[0],
                              jnp.zeros((2, width), F32)])
    table = jnp.pad(rel_table[0].T, ((0, HEAD_ROWS - heads), (0, width - entries)))
    own = [qkv_weight[0], smalls, table, proj_weight[0], fc1_weight[0], fc2_weight[0]]
    other = [swap(v, 1) for v in own]
    bias_at = FC1_BIAS + fc1_bias.shape[1] // width
    biases = build_bias(jnp.concatenate([jnp.where(core == k, table, other[2]) for k in range(2)]), heads)
    weights = []
    for layer in range(2):
        vectors = jnp.where(core == layer, smalls, other[1])
        weights.append(dict(
            layer=layer, pick=jnp.stack([(core == layer).astype(jnp.int32), core]), vectors=vectors, bias=biases[layer],
            **{name: (own[k], other[k]) for name, k in (("qkv", 0), ("proj", 3), ("fc1", 4), ("fc2", 5))}))

    section = dict(
        vectors=jnp.stack([w["vectors"] for w in weights]), bias=[w["bias"] for w in weights],
        own={name: weights[0][name][0] for name in MATRICES}, other={name: weights[0][name][1] for name in MATRICES})
    meta = (core[None],) + sequence_meta(pick(image_ids, core), pick(patch_order, core), padded)

    mine = jnp.where(first, images, cotangent)
    theirs = jnp.where(first, cotangent, images)
    pieces = [pick(mine, core), swap(pick(mine, 1 - core), 1), swap(pick(theirs, core), 2),
              swap(pick(theirs, 1 - core), 3)]
    rows_in = jnp.zeros((padded, width), BF16)
    for k, piece in enumerate(pieces):
        rows_in = lax.dynamic_update_slice(rows_in, piece, ((me ^ k) * quarter, 0))

    middle, = forward(False, rows_in, section, meta)
    x_in = jnp.where(first, rows_in, swap(middle, 2))
    y_out, *parts = forward(True, x_in, section, meta)
    kept = dict(zip(KEPT, parts))

    back = backward(rows_in, section, meta, kept)
    dy_in = jnp.where(first, swap(back, 2), rows_in)

    def reducer(keep, give, at_once=None):
        return Reducer(keep, give, lambda v: swap(v, 1), swap_wide, at_wide, wide, at_once)

    def mlp_part(dy, w, kept_one, after=()):
        dm, da, fc1_give, fc1_keep, fc2_give, fc2_keep, sums = mlp_bwd(True, dy, w, kept_one, after)
        return dm, da, [(fc2_keep, fc2_give), (fc1_keep, fc1_give)], sums

    def tail_part(dm, da, dz, w, kept_one, after):
        dx, give, keep, sums = attn_tail(True, dm, dz, da, w, kept_one, after)
        return dx, keep, give, sums

    def sent(*reducers):
        return [v for r in reducers for v in r.sent]

    def reducers(halves):
        return [reducer(*h, at_once) for h, at_once in zip(halves, swap_sums(halves, wide))]

    dm, da, halves, sums_two = mlp_part(dy_in, weights[1], kept)
    fc_two = [reducer(*h) for h in halves]
    dz, db_two = attn_bwd(da, weights[1], meta, kept)
    for r in fc_two:
        r.step(dz)
    mid, *halves, tail_two = tail_part(dm, da, dz, weights[1], kept, sent(*fc_two))
    attn_two = reducers([halves])[0].launch()
    fc_two[0].step(mid)
    dm, da, halves, sums_one = mlp_part(mid, weights[0], kept, sent(attn_two, fc_two[0]))
    fc_one = reducers(halves)
    fc_one[0].launch()
    for r in fc_two + [attn_two]:
        r.step(fc_one[0].sent[0])
    dz, db_one = attn_bwd(da, weights[0], meta, kept, sent(*fc_two, *fc_one, attn_two))
    fc_one[0].step(dz)
    fc_one[1].launch(dz)
    for r in (fc_two[1], attn_two):
        r.step(dz)
    ready = [r.two()[0] for r in fc_one + fc_two + [attn_two]]
    dx, *halves, tail_one = tail_part(dm, da, dz, weights[0], kept, sent(*fc_one, fc_two[1], attn_two) + ready)

    if wide == 8:
        pairs = [(ready[0], fc_one[0].parts[-1]), (ready[1], fc_one[1].parts[-1]),
                 [v.reshape(wide, -1, v.shape[1]) for v in halves]]
        two = [v for k, r in enumerate(fc_two + [attn_two]) for v in (ready[2 + k], r.parts[-1])]
        *shares, small, others = last_sums(pairs, two, [sums_two, tail_two, sums_one, tail_one], [db_two, db_one],
                                           [dx, y_out])
        fc2, fc1, attn = [(v[0], v[1]) for v in shares]
        mine = lax.dynamic_slice_in_dim(jnp.where(first, dx, y_out), quarter * me, quarter, 0)
        others = lax.dynamic_slice_in_dim(others, (quarter - ROW_STEP) * me, quarter, 1)
    else:
        result = jnp.where(first, dx, y_out)[:rows].reshape(4, quarter, width)
        mine, others = pick(result, me), [swap(pick(result, me ^ k), k) for k in (1, 2, 3)]
        small = jnp.concatenate([sums_two, tail_two, sums_one, tail_one, table_back(db_two, width),
                                 table_back(db_one, width)])
        small = small + swap(small, 1)
        for k in range(wide.bit_length() - 1):
            small = small + swap_wide(small, 1 << k)
        shares = []
        for one, two in zip(fc_one + [reducer(*halves)], fc_two + [attn_two]):
            one, two = one.finish(), two.finish()
            stay = jnp.where(core == 0, one, two)
            got = swap(jnp.where(core == 0, two, one).astype(BF16), 1).astype(F32)
            shares.append((jnp.where(core == 0, stay, got), jnp.where(core == 0, got, stay)))
        fc2, fc1, attn = shares
    same, across = [mine, others[0]], others[1:]
    same = jnp.where(core == 0, jnp.stack(same), jnp.stack(same[::-1]))
    across = jnp.where(core == 0, jnp.stack(across), jnp.stack(across[::-1]))
    encoded = jnp.where(first, across, same)
    images_grad = jnp.where(first, same, across)
    qkv = jnp.concatenate([v[:, :3 * width // 2] for v in attn], axis=1)
    proj = jnp.concatenate([v[:, 3 * width // 2:] for v in attn], axis=1)
    tables = small[48:].reshape(2, HEAD_ROWS, width)
    totals = jnp.where(core == 0, small[24:48], small[:24])
    table_grad = jnp.where(core == 0, tables[1], tables[0])
    tail = totals[16:]
    return (
        encoded,
        images_grad,
        qkv[None],
        tail[SUM_Q:SUM_V + 1][None],
        proj[None],
        table_grad[:heads, :entries].T[None],
        jnp.stack([totals[SUM_SCALE_A], totals[SUM_SCALE_B]])[None],
        jnp.stack([tail[SUM_GAIN_A], totals[SUM_GAIN_B]])[None],
        jnp.stack([tail[SUM_SHIFT_A], totals[SUM_SHIFT_B]])[None],
        jnp.concatenate(fc1, axis=1)[None],
        totals[FC1_BIAS:bias_at].reshape(1, -1),
        jnp.concatenate(fc2, axis=1)[None],
        jnp.stack([totals[SUM_DA], totals[SUM_DF]])[None],
    )


def solution(mesh):
    by_layer = P("narrow", None, None)
    by_rows = P("wide", "narrow", None)
    by_both = P("narrow", "wide", None)
    in_specs = (by_rows, by_rows, P("wide", None), P("wide", None, None)) + (by_layer,) * 8 + (
        P("narrow", None), by_layer, by_layer)
    out_specs = (by_rows, by_rows, by_both, by_layer, by_both, by_layer, by_layer, by_layer, by_layer, by_both,
                 P("narrow", None), by_both, by_layer)
    return jax.shard_map(shards, mesh=mesh, in_specs=in_specs, out_specs=out_specs, check_vma=False)
```

```python
import functools

import jax
import jax.numpy as jnp
from jax import lax
from jax.experimental import pallas as pl
from jax.experimental.pallas import tpu as pltpu
from jax.sharding import PartitionSpec as P

EPSILON = 1e-06
HALF_ROOT = 0.7071067811865476
DENSITY_NORM = 0.3989422804014327
GRID = 14
SPAN = 2 * GRID - 1
PITCH = 16
SLOTS = GRID * PITCH
LANES = 256
CLASS_SLOT = 15
WIDE = 32
STRIP = 512
HEAD_ROWS = 16
F32 = jnp.float32
BF16 = jnp.bfloat16
NEGATIVE = -1000000000.0
LAG = 3
LAG_BACK = 2
TILE = 400

GAIN_A, SHIFT_A, GAIN_B, SHIFT_B, SCALE_A, SCALE_B, OUT_A, OUT_B, FC1_BIAS = range(9)
QKV_BIAS = 12
SUM_DF, SUM_SCALE_B, SUM_GAIN_B, SUM_SHIFT_B, SUM_DA, SUM_SCALE_A = range(6)
SUM_GAIN_A, SUM_SHIFT_A, SUM_Q, SUM_V = range(4)


def nn(a, b):
    return lax.dot_general(a, b, (((1,), (0,)), ((), ())), preferred_element_type=F32)


def nt(a, b):
    return lax.dot_general(a, b, (((1,), (1,)), ((), ())), preferred_element_type=F32)


def tn(a, b):
    return lax.dot_general(a, b, (((0,), (0,)), ((), ())), preferred_element_type=F32)


def iota(shape, axis):
    return lax.broadcasted_iota(jnp.int32, shape, axis)


def row_tile(t):
    return pl.ds(pl.multiple_of(t * TILE, 16), TILE)


def vec(vec_ref, k):
    return vec_ref[k:k + 1, :]


def row_stats(v):
    centred = v - jnp.mean(v, axis=-1, keepdims=True)
    inverse = lax.rsqrt(jnp.mean(centred * centred, axis=-1, keepdims=True) + EPSILON)
    return centred * inverse, inverse


def norm_tiles(src_ref, dst_ref, vec_ref, gain, shift):
    @pl.loop(0, src_ref.shape[0] // TILE)
    def _(t):
        rows = row_tile(t)
        unit, _ = row_stats(src_ref[rows, :].astype(F32))
        dst_ref[rows, :] = (unit * vec(vec_ref, gain) + vec(vec_ref, shift)).astype(BF16)


def extra_rows(first, lanes):
    row = iota((16, lanes), 0)
    out = jnp.zeros((16, lanes), F32)
    for k, value in enumerate(first):
        out = jnp.where(row == k, value, out)
    return out.astype(BF16)


def split3(v):
    hi = v.astype(BF16).astype(F32)
    mid = (v - hi).astype(BF16).astype(F32)
    return hi, mid, v - hi - mid


class Weights:
    def __init__(self, core, own, other, dst, sems):
        self.core, self.own, self.other, self.dst, self.sems = core, own, other, dst, sems

    def start(self, name, layer, chunk=None):
        src, slot = (lambda ref: ref), None
        if name == "fc1":
            src = lambda ref: ref.at[:, pl.ds(pl.multiple_of(chunk * ref.shape[0], 128), ref.shape[0])]
        if name == "fc2":
            src = lambda ref: ref.at[pl.ds(pl.multiple_of(chunk * ref.shape[1], 128), ref.shape[1]), :]
        dst, sem = self.place(name, chunk)

        @pl.when(self.core == layer)
        def _():
            pltpu.make_async_copy(src(self.own[name]), dst, sem).start()

        @pl.when(self.core != layer)
        def _():
            pltpu.make_async_copy(src(self.other[name]), dst, sem).start()

    def place(self, name, chunk):
        if chunk is None:
            return self.dst[name], self.sems[name]
        return self.dst[name].at[lax.rem(chunk, 2)], self.sems[name].at[lax.rem(chunk, 2)]

    def wait(self, name, chunk=None):
        dst, sem = self.place(name, chunk)
        pltpu.make_async_copy(dst, dst, sem).wait()

    def start_fc(self, layer, chunk):
        self.start("fc1", layer, chunk)
        self.start("fc2", layer, chunk)


MATRICES = ("qkv", "proj", "fc1", "fc2")


def weight_scratch(width):
    dma = pltpu.SemaphoreType.DMA
    return [pltpu.VMEM((width, 3 * width), BF16), pltpu.VMEM((width, width), BF16),
            pltpu.VMEM((2, width, width), BF16), pltpu.VMEM((2, width, width), BF16), dma, dma, dma((2,)), dma((2,))]


def weights_of(core, refs, scratch):
    return Weights(core, dict(zip(MATRICES, refs[:4])), dict(zip(MATRICES, refs[4:8])), dict(zip(MATRICES, scratch[:4])),
                   dict(zip(MATRICES, scratch[4:8])))


def forward_kernel(keep, core_ref, ws_ref, x_first, x_second, vec_refs, *refs):
    b_refs, et_ref, mask_ref, y_ref = refs[8:10], refs[10], refs[11], refs[12]
    if keep:
        xs_ref, n1_ref, o_ref, m_ref, n2_ref, a_ref, f_ref, zt_ref, ot_ref, lse_ref, g_ref, slope_ref = refs[13:25]
        scratch = refs[25:]
    else:
        n1_ref, o_ref, m_ref, n2_ref, zt_ref, ot_ref = refs[13:19]
        scratch = refs[19:]
    w = weights_of(core_ref[0], refs[:8], scratch[:8])
    x, b, bias, n1t, acc, wt, b_sem, x_sem = scratch[8:]
    layer, t = pl.program_id(0), pl.program_id(1)
    imgs = et_ref.shape[0]
    heads = b.shape[0]
    width = x.shape[1]
    hd = width // heads
    chunks = pl.num_programs(1) - imgs
    at = (0,) if keep else ()
    vec_ref = vec_refs.at[layer]

    def start_b(k):
        pltpu.make_async_copy(b_refs[k], b, b_sem).start()

    @pl.when((layer == 0) & (t == 0))
    def _():
        for k, ref in enumerate((x_first, x_second)):
            @pl.when(core_ref[1] == k)
            def _():
                pltpu.make_async_copy(ref, x, x_sem).start()

        w.start("qkv", 0)
        start_b(0)
        w.start("proj", 0)
        w.start_fc(0, 0)
        w.start_fc(0, 1)
        pltpu.make_async_copy(x_first, x, x_sem).wait()

    @pl.when(t == 0)
    def _():
        if keep:
            xs_ref[0] = x[...]
        o_ref[...] = jnp.zeros_like(o_ref)
        columns = vec_ref[8:16, :].T
        bias[0:width, :] = jnp.broadcast_to(columns[:, QKV_BIAS - 8:QKV_BIAS - 7], (width, 128))
        bias[width:2 * width, :] = jnp.zeros((width, 128), F32)
        bias[2 * width:, :] = jnp.broadcast_to(columns[:, QKV_BIAS - 7:QKV_BIAS - 6], (width, 128))
        norm_tiles(x, n1_ref.at[at] if keep else n1_ref, vec_ref, GAIN_A, SHIFT_A)
        w.wait("qkv")
        for c in range(3):
            part = slice(c * width, (c + 1) * width)
            wt[part, :] = w.dst["qkv"][:, part].T

    def full(ref):
        return ref.at[0] if keep else ref

    n1_now, o_now, m_now, n2_now = full(n1_ref), full(o_ref), full(m_ref), full(n2_ref)
    zt, ot = (zt_ref.at[0, 0], ot_ref.at[0, 0]) if keep else (zt_ref, ot_ref)

    @pl.when(t < imgs)
    def _():
        ws = pl.multiple_of(ws_ref[t], 16)
        et = et_ref[t]
        n1t[...] = tn(n1_now[pl.ds(ws, SLOTS), :], et).astype(BF16)

        @pl.loop(0, 3)
        def _(c):
            rows = pl.ds(pl.multiple_of(c * width, width), width)
            factor = jnp.where(c == 0, hd ** -0.5, 1.0)
            column = bias[rows, :]
            add = jnp.concatenate([column] * (LANES // 128), axis=1)
            zt[rows, :] = ((nn(wt[rows, :], n1t[...]) + add) * factor).astype(BF16)

        @pl.when(t == 0)
        def _():
            pltpu.make_async_copy(b, b, b_sem).wait()

        ones_q = extra_rows([1.0], LANES)
        mask_k = extra_rows([mask_ref[t]], SLOTS)
        ones_v = extra_rows([1.0], SLOTS)

        def scores(h):
            r = h * hd
            qt = jnp.concatenate([zt[r:r + hd, :], ones_q], axis=0)
            kt = jnp.concatenate([zt[width + r:width + r + hd, :SLOTS], mask_k], axis=0)
            return tn(kt, qt)

        def soft(h, s):
            s = s + b[h]
            m = jnp.max(s, axis=0, keepdims=True)
            return m, jnp.exp(s - m).astype(BF16)

        def finish(h, m, e):
            r = h * hd
            vt = jnp.concatenate([zt[2 * width + r:2 * width + r + hd, :SLOTS], ones_v], axis=0)
            o = nn(vt, e)
            total = o[hd:hd + 1]
            ot[r:r + hd, :] = (o[:hd] * (1.0 / total)).astype(BF16)
            if keep:
                lse_ref[0, 0, h:h + 1, :] = m + jnp.log(total)

        s, e = {}, {}
        for k in range(heads + 2 * LAG):
            if k < heads:
                s[k] = scores(k)
            if 0 <= k - LAG < heads:
                e[k - LAG] = soft(k - LAG, s.pop(k - LAG))
            if k - 2 * LAG >= 0:
                finish(k - 2 * LAG, *e.pop(k - 2 * LAG))

        win = pl.ds(ws, SLOTS)
        o_now[win, :] = (o_now[win, :].astype(F32) + nt(et, ot[...])).astype(BF16)

    j = t - imgs

    @pl.when((t == imgs) & (layer == 0))
    def _():
        w.start("qkv", 1)
        start_b(1)

    @pl.when(t == imgs)
    def _():
        w.wait("proj")
        a = nn(o_now[...], w.dst["proj"][...]) + vec(vec_ref, OUT_A)
        if keep:
            a_ref[0] = a.astype(BF16)
        m_now[...] = x[...].astype(F32) + vec(vec_ref, SCALE_A) * a
        acc[...] = jnp.zeros_like(acc)
        norm_tiles(m_now, n2_now, vec_ref, GAIN_B, SHIFT_B)

    @pl.when((t == imgs) & (layer == 0))
    def _():
        w.start("proj", 1)

    @pl.when(t >= imgs)
    def _():
        slot = lax.rem(j, 2)
        w.wait("fc1", j)
        w.wait("fc2", j)
        u = nn(n2_now[...], w.dst["fc1"][slot]) + vec_ref[pl.ds(FC1_BIAS + j, 1), :]
        cdf = 0.5 * (1.0 + lax.erf(u * HALF_ROOT))
        g = (u * cdf).astype(BF16)
        if keep:
            g_ref[0] = g
            slope_ref[0] = (cdf + u * (jnp.exp(-0.5 * u * u) * DENSITY_NORM)).astype(BF16)
        acc[...] += nn(g, w.dst["fc2"][slot])

        @pl.when(j + 2 < chunks)
        def _():
            w.start_fc(layer, j + 2)

        @pl.when((j + 2 >= chunks) & (layer == 0))
        def _():
            w.start_fc(1, j + 2 - chunks)

    @pl.when(j == chunks - 1)
    def _():
        @pl.loop(0, acc.shape[0] // TILE)
        def _(k):
            rows = row_tile(k)
            f = acc[rows, :] + vec(vec_ref, OUT_B)
            if keep:
                f_ref[0, rows, :] = f.astype(BF16)
            x[rows, :] = (m_now[rows, :] + vec(vec_ref, SCALE_B) * f).astype(BF16)

        @pl.when(layer == 1)
        def _():
            y_ref[...] = x[...]


def attn_bwd_kernel(pick_ref, ws_ref, da_ref, own_ref, other_ref, b_ref, et_ref, mask_ref, zt_ref, ot_ref, lse_ref,
                    dz_ref, db_ref, dat, dot, dzt):
    width = da_ref.shape[1]
    i = pl.program_id(0)

    @pl.when(i == 0)
    def _():
        dz_ref[...] = jnp.zeros_like(dz_ref)
        db_ref[...] = jnp.zeros_like(db_ref)
        dzt[...] = jnp.zeros_like(dzt)

    win = pl.ds(pl.multiple_of(ws_ref[i], 16), SLOTS)
    et = et_ref[0]
    dat[...] = tn(da_ref[win, :], et).astype(BF16)
    proj = jnp.where(pick_ref[0] == 1, own_ref[...], other_ref[...])
    dot[...] = nn(proj, dat[...]).astype(BF16)
    attn_back_image(et, mask_ref[0], zt_ref, ot_ref, lse_ref, b_ref, dat, dot, dzt, db_ref)
    for c in range(3):
        cols = slice(c * width, (c + 1) * width)
        dz_ref[win, cols] = (dz_ref[win, cols].astype(F32) + nt(et, dzt[cols, :])).astype(BF16)


def attn_back_image(et, mask, zt, ot, lse_ref, b, dat, dot, dzt, db_ref):
    heads = b.shape[0]
    width = dat.shape[0]
    hd = width // heads
    extra_k = extra_rows([mask, 1.0, 1.0, 1.0], SLOTS)
    extra_v = extra_rows([1.0, 1.0, 1.0], SLOTS)

    def parts(h):
        r = h * hd
        return (zt[r:r + hd, :], zt[width + r:width + r + hd, :SLOTS], zt[2 * width + r:2 * width + r + hd, :SLOTS],
                dot[r:r + hd, :])

    def products(h):
        qt, kt, vt, dt = parts(h)
        r = h * hd
        delta = jnp.sum(dt.astype(F32) * ot[r:r + hd, :].astype(F32), axis=0, keepdims=True)
        extra_q = extra_rows([1.0, *split3(-lse_ref[h:h + 1, :])], LANES)
        extra_d = extra_rows(split3(-delta), LANES)
        s = tn(jnp.concatenate([kt, extra_k], axis=0), jnp.concatenate([qt, extra_q], axis=0))
        dp = tn(jnp.concatenate([vt, extra_v], axis=0), jnp.concatenate([dt, extra_d], axis=0))
        return s, dp

    def middle(h, s, dp):
        p = jnp.exp(s + b[h])
        ds = p * dp
        if db_ref is not None:
            db_ref[h] += ds
        return p.astype(BF16), ds.astype(BF16)

    def finish(h, p, ds):
        qt, kt, vt, dt = parts(h)
        r = h * hd
        dzt[2 * width + r:2 * width + r + hd, :SLOTS] = nt(dt, p).astype(BF16)
        dzt[width + r:width + r + hd, :SLOTS] = nt(qt, ds).astype(BF16)
        dzt[r:r + hd, :] = (nn(kt, ds) * hd ** -0.5).astype(BF16)

    s, e = {}, {}
    for t in range(heads + 2 * LAG_BACK):
        if t < heads:
            s[t] = products(t)
        if 0 <= t - LAG_BACK < heads:
            e[t - LAG_BACK] = middle(t - LAG_BACK, *s.pop(t - LAG_BACK))
        if t - 2 * LAG_BACK >= 0:
            finish(t - 2 * LAG_BACK, *e.pop(t - 2 * LAG_BACK))


def backward_kernel(core_ref, ws_ref, dy_ref, vec_refs, *refs):
    b_refs, et_ref, mask_ref = refs[8:10], refs[10], refs[11]
    m_ref, x_ref, slope_ref, zt_ref, ot_ref, lse_ref, dx_ref = refs[12:19]
    scratch = refs[19:]
    w = weights_of(core_ref[0], refs[:8], scratch[:8])
    dy, df, acc, dm, da, dz, dat, dot, dzt, b, b_sem = scratch[8:]
    step, t = pl.program_id(0), pl.program_id(1)
    layer = 1 - step
    imgs = et_ref.shape[0]
    width = dy.shape[1]
    chunks = pl.num_programs(1) - imgs - 1
    vec_ref = vec_refs.at[layer]

    def start_b(k):
        pltpu.make_async_copy(b_refs[k], b, b_sem).start()

    @pl.when((step == 0) & (t == 0))
    def _():
        w.start_fc(1, 0)
        w.start_fc(1, 1)
        w.start("proj", 1)
        start_b(1)
        w.start("qkv", 1)
        dy[...] = dy_ref[...]

    @pl.when((step == 1) & (t == 0))
    def _():
        w.start("qkv", 0)

    @pl.when(t == 0)
    def _():
        acc[...] = jnp.zeros_like(acc)

        @pl.loop(0, df.shape[0] // TILE)
        def _(k):
            rows = row_tile(k)
            df[rows, :] = (dy[rows, :].astype(F32) * vec(vec_ref, SCALE_B)).astype(BF16)

    @pl.when(t < chunks)
    def _():
        slot = lax.rem(t, 2)
        w.wait("fc1", t)
        w.wait("fc2", t)
        du = (nt(df[...], w.dst["fc2"][slot]) * slope_ref[...].astype(F32)).astype(BF16)
        acc[...] += nt(du, w.dst["fc1"][slot])

        @pl.when(t + 2 < chunks)
        def _():
            w.start_fc(layer, t + 2)

        @pl.when((t + 2 >= chunks) & (step == 0))
        def _():
            w.start_fc(0, t + 2 - chunks)

    @pl.when(t == chunks - 1)
    def _():
        def emit(rows, dv):
            value = dy[rows, :].astype(F32) + dv
            dm[rows, :] = value
            da[rows, :] = (value * vec(vec_ref, SCALE_A)).astype(BF16)
            return ()

        norm_back_tiles(0, m_ref, acc, vec_ref, GAIN_B, emit)
        dz[...] = jnp.zeros_like(dz)
        dzt[...] = jnp.zeros_like(dzt)
        w.wait("proj")
        pltpu.make_async_copy(b, b, b_sem).wait()

    @pl.when((t >= chunks) & (t < chunks + imgs))
    def _():
        i = t - chunks
        et = et_ref[i]
        win = pl.ds(pl.multiple_of(ws_ref[i], 16), SLOTS)
        dat[...] = tn(da[win, :], et).astype(BF16)
        dot[...] = nn(w.dst["proj"][...], dat[...]).astype(BF16)
        attn_back_image(et, mask_ref[i], zt_ref, ot_ref, lse_ref, b, dat, dot, dzt, None)
        for c in range(3):
            cols = slice(c * width, (c + 1) * width)
            dz[win, cols] = (dz[win, cols].astype(F32) + nt(et, dzt[cols, :])).astype(BF16)

    @pl.when(t == chunks + imgs)
    def _():
        @pl.when(step == 0)
        def _():
            w.start("proj", 0)
            start_b(0)

        w.wait("qkv")
        acc[...] = nt(dz[:, :width], w.dst["qkv"][:, :width])
        for c in range(1, 3):
            cols = slice(c * width, (c + 1) * width)
            acc[...] += nt(dz[:, cols], w.dst["qkv"][:, cols])

        def emit(rows, dv):
            dy[rows, :] = (dm[rows, :] + dv).astype(BF16)
            return ()

        norm_back_tiles(0, x_ref, acc, vec_ref, GAIN_A, emit)

        @pl.when(step == 1)
        def _():
            dx_ref[...] = dy[...]


def spread(count):
    entry = iota((count, SPAN * WIDE), 0)
    lane = iota((count, SPAN * WIDE), 1)
    return jnp.where((entry == lane // WIDE * SPAN + lane % WIDE) & (lane % WIDE < SPAN), 1.0, 0.0).astype(BF16)


def squeeze():
    lane = iota((SPAN * WIDE, STRIP), 0)
    to = iota((SPAN * WIDE, STRIP), 1)
    return jnp.where(lane == to // PITCH * WIDE + to % PITCH, 1.0, 0.0).astype(BF16)


def placed(product, v, onehot):
    return sum(product(part.astype(BF16), onehot) for part in split3(v))


def strip_rows(layer, head):
    return pl.ds(layer * HEAD_ROWS + head, PITCH, stride=2 * HEAD_ROWS)


def bias_kernel(table_ref, *refs):
    b_refs, (shifted, strips) = refs[:2], refs[2:]
    rows = table_ref.shape[0]
    heads = b_refs[0].shape[0]
    wide = placed(nn, table_ref[...], spread(table_ref.shape[1]))
    for c in range(PITCH):
        shifted[c * rows:(c + 1) * rows, :] = pltpu.roll(wide, (c - GRID + 1) % (SPAN * WIDE), 1)
    packed = placed(nn, shifted[...], squeeze())
    for k in range(strips.shape[0]):
        strips[k] = packed[:, k * 128:(k + 1) * 128]
    row = iota((SLOTS, LANES), 0)
    col = iota((SLOTS, LANES), 1)
    for layer, b_ref in enumerate(b_refs):
        for h in range(heads):
            strip = jnp.concatenate([strips[k, strip_rows(layer, h), :] for k in range(strips.shape[0])], axis=1)
            for r in range(GRID):
                at = PITCH * (GRID - 1 - r)
                b_ref[h, r * PITCH:(r + 1) * PITCH, :] = strip[:, at:at + LANES]
            mine = layer * HEAD_ROWS + h
            query, key, both = [table_ref[mine:mine + 1, SPAN * SPAN + k:SPAN * SPAN + k + 1] for k in range(3)]
            full = jnp.where(col == CLASS_SLOT, query, b_ref[h])
            b_ref[h] = jnp.where(row == CLASS_SLOT, jnp.where(col == CLASS_SLOT, both, key), full)


def bias_back_kernel(db_ref, table_ref, strips, classes):
    table_ref[...] = folded(db_ref, strips, classes)


def folded(db_ref, strips, classes):
    heads = db_ref.shape[0]
    row = iota((SLOTS, LANES), 0)
    col = iota((SLOTS, LANES), 1)
    is_row = row == CLASS_SLOT
    is_col = col == CLASS_SLOT
    entry = iota((1, classes.shape[1]), 1) - SPAN * SPAN
    strips[...] = jnp.zeros_like(strips)
    classes[...] = jnp.zeros_like(classes)
    for h in range(heads):
        full = db_ref[h]
        query = jnp.sum(jnp.where(is_col & ~is_row, full, 0.0), keepdims=True)
        key = jnp.sum(jnp.where(is_row & ~is_col, full, 0.0), keepdims=True)
        both = jnp.sum(jnp.where(is_row & is_col, full, 0.0), keepdims=True)
        classes[h:h + 1, :] = jnp.where(
            entry == 0, query, jnp.where(entry == 1, key, jnp.where(entry == 2, both, 0.0)))
        plain = jnp.where(is_row | is_col, 0.0, full)
        total = jnp.zeros((PITCH, STRIP), F32)
        for r in range(GRID):
            part = jnp.concatenate([plain[r * PITCH:(r + 1) * PITCH, :], jnp.zeros((PITCH, STRIP - LANES), F32)],
                                   axis=1)
            total = total + pltpu.roll(part, PITCH * (GRID - 1 - r), 1)
        for k in range(strips.shape[0]):
            strips[k, pl.ds(h, PITCH, stride=HEAD_ROWS), :] = total[:, k * 128:(k + 1) * 128]
    rows = classes.shape[0]
    wide = placed(nt, jnp.concatenate([strips[k] for k in range(strips.shape[0])], axis=1), squeeze())
    gathered = jnp.zeros((rows, SPAN * WIDE), F32)
    for c in range(GRID):
        gathered = gathered + pltpu.roll(wide[c * rows:(c + 1) * rows, :], (GRID - 1 - c) % (SPAN * WIDE), 1)
    return placed(nt, gathered, spread(classes.shape[1])) + classes[...]


def norm_back_tiles(count, src_ref, grad_ref, vec_ref, gain, emit):
    def body(t, sums):
        rows = row_tile(t)
        unit, inverse = row_stats(src_ref[rows, :].astype(F32))
        grad = grad_ref[rows, :]
        scaled = grad * vec(vec_ref, gain)
        mean_one = jnp.mean(scaled, axis=-1, keepdims=True)
        mean_two = jnp.mean(scaled * unit, axis=-1, keepdims=True)
        more = emit(rows, inverse * (scaled - mean_one - unit * mean_two))
        if not count:
            return sums
        return tuple(s + jnp.sum(v, axis=0, keepdims=True) for s, v in zip(sums, (grad * unit, grad) + more))

    zero = jnp.zeros((1, grad_ref.shape[1]), F32)
    return lax.fori_loop(0, grad_ref.shape[0] // TILE, body, (zero,) * count)


def mlp_bwd_kernel(want, pick_ref, dy_ref, m_ref, vec_ref, slope_ref, fc1_own, fc1_other, fc2_own, fc2_other, *rest):
    if want:
        (n2_ref, g_ref, a_ref, f_ref, dm_ref, da_ref, fc1_give, fc1_keep, fc2_give, fc2_keep, sums_ref, df, acc) = rest
    else:
        dm_ref, da_ref, df, acc = rest
    j = pl.program_id(0)
    steps = pl.num_programs(0)
    mine = pick_ref[0] == 1
    core = pick_ref[1]
    width = dy_ref.shape[1]

    @pl.when(j == 0)
    def _():
        acc[...] = jnp.zeros_like(acc)
        if want:
            sums_ref[...] = jnp.zeros_like(sums_ref)
        zero = jnp.zeros((1, width), F32)

        def body(t, sums):
            rows = row_tile(t)
            dy = dy_ref[rows, :].astype(F32)
            scaled = (dy * vec(vec_ref, SCALE_B)).astype(BF16)
            df[rows, :] = scaled
            if not want:
                return sums
            return (sums[0] + jnp.sum(scaled.astype(F32), axis=0, keepdims=True),
                    sums[1] + jnp.sum(dy * f_ref[rows, :].astype(F32), axis=0, keepdims=True))

        sums = lax.fori_loop(0, df.shape[0] // TILE, body, (zero, zero) if want else ())
        if want:
            sums_ref[SUM_DF:SUM_DF + 1, :] = sums[0]
            sums_ref[SUM_SCALE_B:SUM_SCALE_B + 1, :] = sums[1]

    fc1 = jnp.where(mine, fc1_own[...], fc1_other[...])
    fc2 = jnp.where(mine, fc2_own[...], fc2_other[...])
    du = (nt(df[...], fc2) * slope_ref[...].astype(F32)).astype(BF16)
    acc[...] += nt(du, fc1)
    if want:
        at = lax.rem(j + (1 - core) * (steps // 2), steps)
        sums_ref[pl.ds(FC1_BIAS + at, 1), :] = jnp.sum(du.astype(F32), axis=0, keepdims=True)
        grad = tn(g_ref[...], df[...]).astype(BF16)
        low, high = grad[:, :width // 2], grad[:, width // 2:]
        fc2_keep[...] = jnp.where(core == 0, low, high)
        fc2_give[...] = jnp.where(core == 0, high, low)
        grad1 = tn(n2_ref[...], du).astype(BF16)

        @pl.when(j < steps // 2)
        def _():
            fc1_give[...] = grad1

        @pl.when(j >= steps // 2)
        def _():
            fc1_keep[...] = grad1

    @pl.when(j == steps - 1)
    def _():
        def emit(rows, dv):
            dm = dy_ref[rows, :].astype(F32) + dv
            da = (dm * vec(vec_ref, SCALE_A)).astype(BF16)
            dm_ref[rows, :] = dm
            da_ref[rows, :] = da
            return (da.astype(F32), dm * a_ref[rows, :].astype(F32)) if want else ()

        sums = norm_back_tiles(4 if want else 0, m_ref, acc, vec_ref, GAIN_B, emit)
        for k, s in zip((SUM_GAIN_B, SUM_SHIFT_B, SUM_DA, SUM_SCALE_A), sums):
            sums_ref[k:k + 1, :] = s


def attn_tail_kernel(pick_ref, vec_ref, dz_ref, own_ref, other_ref, dm_ref, da_ref, x_refs, n1_refs, o_refs, dx_ref,
                     sums_ref, give_ref, keep_ref, o, da, n1, dz, wt, dm, x, give, keep, acc, sems, layer):
    core = pick_ref[1]
    width = x.shape[1]
    part = 3 * width // 2
    arrays = dict(o=(o_refs.at[layer], o), da=(da_ref, da), n1=(n1_refs.at[layer], n1), dm=(dm_ref, dm),
                  x=(x_refs.at[layer], x))
    place = {name: k for k, name in enumerate(arrays)}

    def load(name):
        src, dst = arrays[name]
        return pltpu.make_async_copy(src, dst, sems.at[place[name]])

    def columns(ref, k):
        half = core if k else 1 - core
        return ref.at[:, pl.ds(pl.multiple_of(half * part, 128), part)]

    def load_dz(k):
        return pltpu.make_async_copy(columns(dz_ref, k), dz.at[k], sems.at[5 + k])

    def load_wt(k):
        @pl.when(pick_ref[0] == 1)
        def _():
            pltpu.make_async_copy(columns(own_ref, k), wt.at[k], sems.at[7 + k]).start()

        @pl.when(pick_ref[0] == 0)
        def _():
            pltpu.make_async_copy(columns(other_ref, k), wt.at[k], sems.at[7 + k]).start()

    load("o").start()
    load("da").start()
    load("n1").start()
    load_dz(0).start()
    load_wt(0)
    load_dz(1).start()
    load_wt(1)
    load("dm").start()
    load("x").start()
    sums_ref[...] = jnp.zeros_like(sums_ref)
    load("o").wait()
    load("da").wait()
    grad = tn(o[...], da[...]).astype(BF16)
    low, high = grad[:, :width // 2], grad[:, width // 2:]
    give[:, part:] = jnp.where(core == 0, high, low)
    keep[:, part:] = jnp.where(core == 0, low, high)
    load("n1").wait()
    stores = []
    for k, (to, out) in enumerate(((give, give_ref), (keep, keep_ref))):
        load_dz(k).wait()
        half = core if k else 1 - core
        to[:, :part] = tn(n1[...], dz[k]).astype(BF16)
        stores.append(pltpu.make_async_copy(to, out, sems.at[9 + k]))
        stores[-1].start()
        totals = jnp.sum(dz[k].astype(F32), axis=0, keepdims=True)

        @pl.when(half == 0)
        def _():
            sums_ref[SUM_Q:SUM_Q + 1, :] = totals[:, :width]

        @pl.when(half == 1)
        def _():
            sums_ref[SUM_V:SUM_V + 1, :] = totals[:, width // 2:]

        pltpu.make_async_copy(wt.at[k], wt.at[k], sems.at[7 + k]).wait()
        if k == 0:
            acc[...] = nt(dz[k], wt[k])
        else:
            acc[...] += nt(dz[k], wt[k])
    load("dm").wait()
    load("x").wait()

    def emit(rows, dv):
        dx_ref[rows, :] = (dm[rows, :] + dv).astype(BF16)
        return ()

    sums = norm_back_tiles(2, x, acc, vec_ref, GAIN_A, emit)
    for k, v in zip((SUM_GAIN_A, SUM_SHIFT_A), sums):
        sums_ref[k:k + 1, :] = v
    for c in stores:
        c.wait()


TAKES = dict(backward=85, forward=75, forward_keep=85, mlp_bwd=15, mlp_bwd_all=27, attn_bwd=20, attn_bwd_all=21, attn_tail=9,
             attn_tail_all=16, bias_build=6, bias_back=9)


VMEM = dict(backward=60, forward=60, forward_keep=60, mlp_bwd=60, mlp_bwd_all=60, attn_bwd=60, attn_bwd_all=60, attn_tail=60,
            attn_tail_all=60, bias_build=60, bias_back=60)


def cost(name):
    return pl.CostEstimate(flops=TAKES[name] * 800_000_000, bytes_accessed=TAKES[name] * 3_000_000, transcendentals=0)


def params(name):
    return pltpu.CompilerParams(vmem_limit_bytes=VMEM[name] * 1024 * 1024)


def shaped(*arrays):
    return [jax.ShapeDtypeStruct(s, d) for s, d in arrays]


def whole(shape):
    return pl.BlockSpec(shape, lambda *_: (0,) * len(shape))


def once(shape):
    return pl.BlockSpec(shape, lambda *_: (0,) * len(shape), pipeline_mode=pl.Buffered(1))


def per_image(shape):
    return pl.BlockSpec((1,) + shape, lambda i, *_: (i,) + (0,) * len(shape))


def call(kernel, name, prefetched, grid, inputs, outputs, scratch, after=()):
    count = len(prefetched) + len(inputs)

    def body(*refs):
        kernel(*refs[:count], *refs[count + len(after):])

    inputs = inputs + [(a, pl.BlockSpec(memory_space=pl.ANY)) for a in after]
    return pl.pallas_call(
        body,
        grid_spec=pltpu.PrefetchScalarGridSpec(
            num_scalar_prefetch=len(prefetched), grid=grid, in_specs=[s for _, s in inputs],
            out_specs=[s for _, _, s in outputs], scratch_shapes=scratch),
        out_shape=[jax.ShapeDtypeStruct(s, d) for s, d, _ in outputs],
        compiler_params=params(name), name=name, cost_estimate=cost(name),
    )(*prefetched, *[a for a, _ in inputs])


def forward(keep, x_pair, section, meta):
    core, ws, et, mask = meta
    rows, width = x_pair[0].shape
    biases = section["bias"]
    heads = biases[0].shape[0]
    hidden = section["own"]["fc1"].shape[1]
    imgs = et.shape[0]
    chunks = hidden // width
    anywhere = pl.BlockSpec(memory_space=pl.ANY)
    vectors = section["vectors"]
    inputs = [(x, anywhere) for x in x_pair] + [(vectors, once(vectors.shape))]
    inputs += [(section[side][name], anywhere) for side in ("own", "other") for name in MATRICES]
    inputs += [(v, anywhere) for v in biases] + [(et, once(et.shape)), (mask, once(mask.shape))]
    outputs = [((rows, width), BF16, whole((rows, width)))]
    low = [pltpu.VMEM((rows, width), BF16)]
    scratch = weight_scratch(width) + low + [
        pltpu.VMEM(biases[0].shape, F32), pltpu.VMEM((3 * width, 128), F32), pltpu.VMEM((width, LANES), BF16),
        pltpu.VMEM((rows, width), F32), pltpu.VMEM((3 * width, width), BF16), pltpu.SemaphoreType.DMA, pltpu.SemaphoreType.DMA]
    if keep:
        def of_layer(kind):
            return (2, rows, width), kind, pl.BlockSpec((1, rows, width), lambda l, t, *_: (l, 0, 0))

        def of_image(*shape, kind=BF16):
            return ((2, imgs) + shape, kind,
                    pl.BlockSpec((1, 1) + shape, lambda l, t, *_: (l, jnp.minimum(t, imgs - 1), 0, 0)))

        of_chunk = ((2, rows, hidden), BF16,
                    pl.BlockSpec((1, rows, width), lambda l, t, *_: (l, 0, jnp.maximum(t - imgs, 0))))
        outputs += [of_layer(BF16), of_layer(BF16), of_layer(BF16), of_layer(F32), of_layer(BF16), of_layer(BF16),
                    of_layer(BF16), of_image(3 * width, LANES), of_image(width, LANES),
                    of_image(heads, LANES, kind=F32), of_chunk, of_chunk]
    else:
        scratch = low * 2 + [pltpu.VMEM((rows, width), F32)] + low + [
            pltpu.VMEM((3 * width, LANES), BF16), pltpu.VMEM((width, LANES), BF16)] + scratch
    return call(functools.partial(forward_kernel, keep), "forward_keep" if keep else "forward", [core, ws],
                (2, imgs + chunks), inputs, outputs, scratch)


def backward(dy, section, meta, kept):
    core, ws, et, mask = meta
    rows, width = dy.shape
    biases = section["bias"]
    imgs = et.shape[0]
    chunks = section["own"]["fc1"].shape[1] // width
    anywhere = pl.BlockSpec(memory_space=pl.ANY)
    vectors = section["vectors"]
    inputs = [(dy, once(dy.shape)), (vectors, once(vectors.shape))]
    inputs += [(section[side][name], anywhere) for side in ("own", "other") for name in MATRICES]
    inputs += [(v, anywhere) for v in biases] + [(et, once(et.shape)), (mask, once(mask.shape))]
    of_layer = pl.BlockSpec((None, rows, width), lambda l, t, *_: (1 - l, 0, 0))
    inputs += [(kept["m"], of_layer), (kept["x"], of_layer)]
    inputs += [(kept["slope"], pl.BlockSpec((None, rows, width),
                                            lambda l, t, *_: (1 - l, 0, jnp.minimum(t, chunks - 1))))]
    for name in ("zt", "ot", "lse"):
        v = kept[name]
        inputs += [(v, pl.BlockSpec((None, None) + v.shape[2:],
                                    lambda l, t, *_: (1 - l, jnp.clip(t - chunks, 0, imgs - 1), 0, 0)))]
    low, high = pltpu.VMEM((rows, width), BF16), pltpu.VMEM((rows, width), F32)
    slots = pltpu.VMEM((width, LANES), BF16)
    scratch = weight_scratch(width) + [
        low, low, high, high, low, pltpu.VMEM((rows, 3 * width), BF16), slots, slots,
        pltpu.VMEM((3 * width, LANES), BF16), pltpu.VMEM(biases[0].shape, F32), pltpu.SemaphoreType.DMA]
    return call(backward_kernel, "backward", [core, ws], (2, chunks + imgs + 1), inputs,
                [((rows, width), BF16, whole((rows, width)))], scratch)[0]


def attn_bwd(da, w, meta, kept, after=()):
    _, ws, et, mask = meta
    rows, width = da.shape
    bias = w["bias"]
    imgs = et.shape[0]
    single_proj = once((width, width))
    layer = w["layer"]

    def kept_image(name):
        v = kept[name]
        return v, pl.BlockSpec((None, None) + v.shape[2:], lambda i, *_: (layer, i, 0, 0))

    inputs = [(da, once(da.shape)), (w["proj"][0], single_proj), (w["proj"][1], single_proj), (bias, once(bias.shape)),
              (et, per_image(et.shape[1:])), (mask, per_image(mask.shape[1:])), kept_image("zt"),
              kept_image("ot"), kept_image("lse")]
    outputs = [((rows, 3 * width), BF16, whole((rows, 3 * width)))]
    outputs += [(bias.shape, F32, whole(bias.shape))]
    scratch = [pltpu.VMEM((width, LANES), BF16), pltpu.VMEM((width, LANES), BF16), pltpu.VMEM((3 * width, LANES), BF16)]
    return call(attn_bwd_kernel, "attn_bwd_all", [w["pick"], ws],
                (imgs,), inputs, outputs, scratch, after)


def build_bias(tables, heads):
    shape = (heads, SLOTS, LANES)
    rows = tables.shape[0]
    return call(bias_kernel, "bias_build", [], (1,), [(tables, once(tables.shape))], [(shape, F32, whole(shape))] * 2,
                [pltpu.VMEM((PITCH * rows, SPAN * WIDE), F32), pltpu.VMEM((STRIP // 128, PITCH * rows, 128), F32)])


def table_back(db, lanes, after=()):
    return call(bias_back_kernel, "bias_back", [], (1,), [(db, once(db.shape))],
                [((HEAD_ROWS, lanes), F32, whole((HEAD_ROWS, lanes)))],
                [pltpu.VMEM((STRIP // 128, PITCH * HEAD_ROWS, 128), F32), pltpu.VMEM((HEAD_ROWS, lanes), F32)],
                after)[0]


def chosen(which, block, to_index):
    def index(j, pick):
        used = pick[0] if which == 0 else 1 - pick[0]
        return tuple(k * used for k in to_index(j, pick))
    return pl.BlockSpec(block, index)


def both(pair, block, to_index):
    return [(pair[k], chosen(k, block, to_index)) for k in range(2)]


def kept_whole(kept, name, w):
    v, layer = kept[name], w["layer"]
    return v, pl.BlockSpec((None,) + v.shape[1:], lambda *_: (layer, 0, 0), pipeline_mode=pl.Buffered(1))


def mlp_bwd(want, dy, w, kept, after=()):
    rows, width = dy.shape
    hidden = w["fc1"][0].shape[1]
    steps = hidden // width
    full = whole((rows, width))
    single = once((rows, width))

    def at(j, pick):
        return lax.rem(j + (1 - pick[1]) * (steps // 2), steps)

    layer = w["layer"]
    part = pl.BlockSpec((None, rows, width), lambda j, p: (layer, 0, at(j, p)))
    inputs = [(dy, single), kept_whole(kept, "m", w), (w["vectors"], once(w["vectors"].shape)), (kept["slope"], part),
              *both(w["fc1"], (width, width), lambda j, p: (0, at(j, p))),
              *both(w["fc2"], (width, width), lambda j, p: (at(j, p), 0))]
    outputs = [((rows, width), F32, full), ((rows, width), BF16, full)]
    if want:
        inputs += [kept_whole(kept, "n2", w), (kept["g"], part), kept_whole(kept, "a", w), kept_whole(kept, "f", w)]
        half = pl.BlockSpec((width, width // 2), lambda j, p: (at(j, p), 0))
        give = pl.BlockSpec((width, width), lambda j, p: (0, jnp.minimum(j, steps // 2 - 1)))
        stay = pl.BlockSpec((width, width), lambda j, p: (0, jnp.maximum(j - steps // 2, 0)))
        outputs += [((width, hidden // 2), BF16, give), ((width, hidden // 2), BF16, stay),
                    ((hidden, width // 2), BF16, half), ((hidden, width // 2), BF16, half),
                    ((16, width), F32, whole((16, width)))]
    scratch = [pltpu.VMEM((rows, width), BF16), pltpu.VMEM((rows, width), F32)]
    return call(functools.partial(mlp_bwd_kernel, want), "mlp_bwd_all" if want else "mlp_bwd", [w["pick"]],
                (steps,), inputs, outputs, scratch, after)


def attn_tail(dm, dz, da, w, kept, after=()):
    rows, width = dm.shape
    part = 3 * width // 2
    layer = w["layer"]
    anywhere = pl.BlockSpec(memory_space=pl.ANY)
    inputs = [(w["vectors"], once(w["vectors"].shape))]
    inputs += [(v, anywhere) for v in (dz, *w["qkv"], dm, da, kept["x"], kept["n1"], kept["o"])]
    outputs = [((rows, width), BF16, whole((rows, width))), ((8, width), F32, whole((8, width)))]
    outputs += [((width, 2 * width), BF16, anywhere)] * 2
    low, high = pltpu.VMEM((rows, width), BF16), pltpu.VMEM((rows, width), F32)
    scratch = [low, low, low, pltpu.VMEM((2, rows, part), BF16), pltpu.VMEM((2, width, part), BF16), high, low,
               pltpu.VMEM((width, 2 * width), BF16), pltpu.VMEM((width, 2 * width), BF16), high,
               pltpu.SemaphoreType.DMA((11,))]
    dx, sums, give, keep = call(functools.partial(attn_tail_kernel, layer=layer), "attn_tail_all", [w["pick"]], (1,),
                                inputs, outputs, scratch, after)
    return dx, give, keep, sums


def sequence_meta(ids, order, rows):
    imgs, patches = order.shape
    image = jnp.arange(imgs, dtype=jnp.int32)
    start = jnp.sum((ids[None, :] < image[:, None]).astype(jnp.int32), axis=1)
    count = jnp.sum((ids[None, :] == image[:, None]).astype(jnp.int32), axis=1)
    ws = jnp.minimum(start // 16 * 16, rows - SLOTS)
    slot = jnp.arange(LANES, dtype=jnp.int32)
    is_class = slot == CLASS_SLOT
    is_patch = (slot % PITCH < GRID) & (slot < SLOTS)
    patch = jnp.where(is_patch, slot // PITCH * GRID + slot % PITCH, -1)
    place = jnp.arange(1, patches + 1, dtype=jnp.int32)
    offset = jnp.sum(jnp.where(order[:, None, :] == patch[None, :, None], place, 0), axis=2)
    valid = (is_class | is_patch)[None, :] & (offset < count[:, None])
    local = jnp.where(valid, offset + (start - ws)[:, None], -1)
    row = jnp.arange(SLOTS, dtype=jnp.int32)
    et = (local[:, None, :] == row[None, :, None]).astype(BF16)
    mask = jnp.where(valid, 0.0, NEGATIVE).astype(F32)[:, None, :SLOTS]
    return ws, et, mask


KEPT = ("x", "n1", "o", "m", "n2", "a", "f", "zt", "ot", "lse", "g", "slope")


def later(arrays, token):
    if token is None:
        return list(arrays)
    return list(lax.optimization_barrier((*arrays, token)))[:-1]


class Reducer:
    def __init__(self, keep, give, swap_core, swap_wide, at_wide, wide, at_once=None):
        self.swap_wide, self.at_wide = swap_wide, at_wide
        if at_once is not None:
            send, stay = at_once
            self.sent, self.parts = [send], [stay]
            self.left, self.bit = wide // 2, 2
            return
        shape = (wide, keep.shape[0] // wide, keep.shape[1])
        self.parts = [v.reshape(shape) for v in (keep, swap_core(give))]
        self.left, self.bit = wide, 1
        self.sent = []

    def launch(self, token=None):
        self.parts.append(self.swap_wide(later(self.sent, token)[0], 1))
        return self

    def hold(self, token):
        self.parts[-1], = later([self.parts[-1]], token)

    def added(self, parts):
        return sum(v.astype(F32) for v in parts)

    def step(self, token=None):
        if self.left == 1:
            return
        self.hold(token)
        mine = self.at_wide // self.bit % 2
        pairs = [v.reshape((self.left // 2, 2) + v.shape[1:]) for v in self.parts]
        self.sent = [self.added(lax.dynamic_index_in_dim(v, 1 - mine, 1, keepdims=False) for v in pairs).astype(BF16)]
        self.parts = [lax.dynamic_index_in_dim(v, mine, 1, keepdims=False) for v in pairs]
        self.parts.append(self.swap_wide(self.sent[0], self.bit))
        self.left, self.bit = self.left // 2, 2 * self.bit

    def two(self):
        return [self.added(self.parts[:-1]).astype(BF16), self.parts[-1]]

    def finish(self, token=None):
        while self.left > 1:
            self.step(token)
        self.hold(token)
        return self.added(self.parts)[0]


def swap_sums_kernel(count, *refs):
    keeps, gives, outs = refs[:count], refs[count:2 * count], refs[2 * count:4 * count]
    mine, come = refs[4 * count:5 * count], refs[5 * count:6 * count]
    local_sem, send_sem, recv_sem = refs[6 * count:]
    me = lax.axis_index("narrow")
    b = lax.axis_index("wide") % 2
    partner = {"narrow": me + 1 - 2 * (me % 2)}
    barrier = pltpu.get_barrier_semaphore()
    pl.semaphore_signal(barrier, inc=1, device_id=partner, device_id_type=pl.DeviceIdType.MESH)
    pl.semaphore_wait(barrier, 1)
    copies = []
    for k in range(count):
        remote = pltpu.make_async_remote_copy(
            src_ref=gives[k], dst_ref=come[k], send_sem=send_sem.at[k], recv_sem=recv_sem.at[k], device_id=partner,
            device_id_type=pl.DeviceIdType.MESH)
        local = pltpu.make_async_copy(keeps[k], mine[k], local_sem.at[k])
        remote.start()
        local.start()
        copies.append((remote, local))
    for k in range(count):
        for copy in copies[k]:
            copy.wait()
        send, stay = outs[2 * k:2 * k + 2]

        @pl.loop(0, send.shape[0])
        def _(i):
            for to, index in ((send, 2 * i + 1 - b), (stay, 2 * i + b)):
                to[i] = (mine[k][index].astype(F32) + come[k][index].astype(F32)).astype(BF16)


def swap_sums(halves, wide):
    count = len(halves)
    blocks = [(keep.shape[0] // wide, keep.shape[1]) for keep, _ in halves]
    anywhere = pl.BlockSpec(memory_space=pl.ANY)
    dma = pltpu.SemaphoreType.DMA
    out = pl.pallas_call(
        functools.partial(swap_sums_kernel, count), in_specs=[anywhere] * 2 * count,
        out_specs=[pl.BlockSpec(memory_space=pltpu.VMEM)] * 2 * count,
        out_shape=[jax.ShapeDtypeStruct((wide // 2,) + block, BF16) for block in blocks for _ in range(2)],
        scratch_shapes=[pltpu.VMEM((wide,) + block, BF16) for _ in range(2) for block in blocks]
        + [dma((count,))] * 3,
        compiler_params=pltpu.CompilerParams(vmem_limit_bytes=60 * 1024 * 1024, collective_id=count,
                                             has_side_effects=True),
        cost_estimate=pl.CostEstimate(flops=0, bytes_accessed=30_000_000, transcendentals=0), name="swap_sums",
    )(*[h[k].reshape((wide,) + block) for k in range(2) for h, block in zip(halves, blocks)])
    return [(out[2 * k], out[2 * k + 1]) for k in range(count)]


FC2, FC1, FC1_MORE, ATTN, ATTN_MORE, SMALL, ROWS = range(7)
ROW_STEP, ROW_WINDOW = 192, 224
CORE, Y, Z0, Z1, FINAL = range(5)


def last_sums_kernel(cuts, counts, *refs):
    pairs, twos, small_refs, db_refs, row_refs = refs[:6], refs[6:12], refs[12:16], refs[16:18], refs[18:20]
    out_fc2, out_fc1, out_attn, small_out, rows_out = refs[20:25]
    scratch = list(refs[25:])
    db, strips, classes, db_sem, row_buf, row_sem, small_low = scratch[-11:-4]
    small_got, send_sem, recv_sem, local_sem = scratch[-4:]
    me = lax.axis_index("narrow")
    at = lax.axis_index("wide")
    core = me % 2
    half = {hop: at // bit % 2 for hop, bit in ((Y, 1), (Z0, 2), (Z1, 4))}
    core_partner = {"narrow": me + 1 - 2 * core}
    across = {"narrow": me + 2 - 4 * (me // 2)}
    corner = {"narrow": 3 - me}
    partners = {CORE: core_partner, FINAL: core_partner}
    for hop, bit in ((Y, 1), (Z0, 2), (Z1, 4)):
        partners[hop] = {"wide": at + bit * (1 - 2 * half[hop])}
    greeted = [core_partner, across, corner] + [partners[hop] for hop in (Y, Z0, Z1)]
    barrier = pltpu.get_barrier_semaphore()
    for partner in greeted:
        pl.semaphore_signal(barrier, inc=1, device_id=partner, device_id_type=pl.DeviceIdType.MESH)
    pl.semaphore_wait(barrier, len(greeted))

    def remote(src, dst, row, hop, device=None):
        return pltpu.make_async_remote_copy(
            src_ref=src, dst_ref=dst, send_sem=send_sem.at[row, hop], recv_sem=recv_sem.at[row, hop],
            device_id=partners[hop] if device is None else device, device_id_type=pl.DeviceIdType.MESH)

    first, second, levels, last = {}, {}, {}, {}
    for p, (k, cut) in enumerate(cuts):
        n = counts[p]
        mine, come = scratch.pop(0), scratch.pop(0)
        first[p] = (pairs[2 * k].at[:, :, cut], mine)
        second[p] = (pairs[2 * k + 1].at[:, :, cut], come)
        levels[p] = [(None, mine, come)]
        while n > 1:
            n //= 2
            levels[p].append((scratch.pop(0), scratch.pop(0), scratch.pop(0)))
        last[p] = (scratch.pop(0), scratch.pop(0))
    pending = {}

    def begin(p):
        pending[p] = [pltpu.make_async_copy(*first[p], local_sem.at[p, 0])]
        if p in (ATTN, ATTN_MORE):
            pending[p].append(remote(*second[p], p, CORE))
        else:
            pending[p].append(pltpu.make_async_copy(*second[p], local_sem.at[p, 1]))
        for c in pending[p]:
            c.start()

    def wait(p):
        for c in pending[p]:
            c.wait()

    def hop(p, n):
        wait(p)
        level = counts[p].bit_length() - n.bit_length()
        _, mine, come = levels[p][level]
        send, stay, next_come = levels[p][level + 1]
        which = {8: Y, 4: Z0, 2: Z1}[n]
        b = half[which]

        def add(to, i, index):
            to[i] = (mine[index].astype(F32) + come[index].astype(F32)).astype(BF16)

        @pl.loop(0, n // 2)
        def _(i):
            add(send, i, 2 * i + 1 - b)

        copy = remote(send, next_come, p, which)
        copy.start()
        pending[p] = [copy]

        @pl.loop(0, n // 2)
        def _(i):
            add(stay, i, 2 * i + b)

    def total(p):
        wait(p)
        _, stay, come = levels[p][-1]
        return stay[0].astype(F32) + come[0].astype(F32)

    outs = {FC2: out_fc2, FC1: out_fc1, FC1_MORE: out_fc1, ATTN: out_attn, ATTN_MORE: out_attn}
    others = {FC2: twos[:2], FC1: twos[2:4], FC1_MORE: twos[2:4], ATTN: twos[4:], ATTN_MORE: twos[4:]}

    def end(p):
        cut = cuts[p][1]
        one = total(p)
        two = sum(ref[0, :, cut].astype(F32) for ref in others[p])
        give, come = last[p]
        give[...] = jnp.where(core == 0, two, one).astype(BF16)
        copy = remote(give, come, p, FINAL)
        copy.start()
        pending[p] = [copy]
        outs[p][core, :, cut] = jnp.where(core == 0, one, two)

    def close(p):
        wait(p)
        outs[p][1 - core, :, cuts[p][1]] = last[p][1][...].astype(F32)

    small = {}

    def small_send(h):
        small_low[...] = small_out[...].astype(BF16)
        small[h] = remote(small_low, small_got.at[h], SMALL, h)
        small[h].start()

    def small_take(h):
        small[h].wait()
        small_out[...] = small_low[...].astype(F32) + small_got[h].astype(F32)

    for p in (ATTN, ATTN_MORE, FC2, FC1, FC1_MORE):
        begin(p)
    db_copies = [pltpu.make_async_copy(ref, db.at[k], db_sem.at[k]) for k, ref in enumerate(db_refs)]
    for c in db_copies:
        c.start()
    row_copies = []
    for k, (device, block) in enumerate(((core_partner, me + 1 - 2 * core), (across, me + 2 - 4 * (me // 2)),
                                         (corner, 3 - me))):
        window = pl.ds(pl.multiple_of(block * ROW_STEP, 16), ROW_WINDOW)
        row_copies.append(remote(row_buf.at[window, :], rows_out.at[k], ROWS, k, device))
    for k in range(2):
        @pl.when(me // 2 == k)
        def _():
            pltpu.make_async_copy(row_refs[k], row_buf, row_sem).start()

    hop(FC2, 2)
    hop(FC1, 4)
    hop(FC1_MORE, 4)
    hop(ATTN, 8)
    hop(ATTN_MORE, 8)
    pltpu.make_async_copy(row_refs[0], row_buf, row_sem).wait()
    for c in row_copies:
        c.start()
    row = 0
    for ref in small_refs:
        small_out[row:row + ref.shape[0], :] = ref[...]
        row += ref.shape[0]
    db_copies[0].wait()
    small_out[row:row + HEAD_ROWS, :] = folded(db.at[0], strips, classes)
    end(FC2)
    hop(FC1, 2)
    db_copies[1].wait()
    small_out[row + HEAD_ROWS:, :] = folded(db.at[1], strips, classes)
    small_send(CORE)
    hop(FC1_MORE, 2)
    small_take(CORE)
    small_send(Z0)
    hop(ATTN, 4)
    end(FC1)
    end(FC1_MORE)
    hop(ATTN_MORE, 4)
    small_take(Z0)
    small_send(Y)
    hop(ATTN, 2)
    for p in (FC2, FC1, FC1_MORE):
        close(p)
    hop(ATTN_MORE, 2)
    small_take(Y)
    small_send(Z1)
    end(ATTN)
    for c in row_copies:
        c.wait()
    end(ATTN_MORE)
    small_take(Z1)
    close(ATTN)
    close(ATTN_MORE)


def last_sums(pairs, two, small, db, rows):
    anywhere = pl.BlockSpec(memory_space=pl.ANY)
    vmem = pl.BlockSpec(memory_space=pltpu.VMEM)
    scratch, cuts, counts = [], [], []
    for k, many in enumerate((1, 2, 2)):
        p = pairs[k][0]
        size = p.shape[2] // many
        for c in range(many):
            n, block = p.shape[0], (p.shape[1], size)
            cuts.append((k, slice(c * size, (c + 1) * size)))
            counts.append(n)
            scratch += [pltpu.VMEM((n,) + block, BF16)] * 2
            while n > 1:
                n //= 2
                scratch += [pltpu.VMEM((n,) + block, BF16)] * 3
            scratch += [pltpu.VMEM(block, BF16)] * 2
    lanes = small[0].shape[1]
    count = sum(v.shape[0] for v in small) + 2 * HEAD_ROWS
    scratch += [pltpu.VMEM((2,) + db[0].shape, F32), pltpu.VMEM((STRIP // 128, PITCH * HEAD_ROWS, 128), F32),
                pltpu.VMEM((HEAD_ROWS, lanes), F32), pltpu.SemaphoreType.DMA((2,)),
                pltpu.VMEM(rows[0].shape, BF16), pltpu.SemaphoreType.DMA, pltpu.VMEM((count, lanes), BF16),
                pltpu.VMEM((4, count, lanes), BF16)]
    scratch += [pltpu.SemaphoreType.DMA((7, 5)), pltpu.SemaphoreType.DMA((7, 5)), pltpu.SemaphoreType.DMA((5, 2))]
    return pl.pallas_call(
        functools.partial(last_sums_kernel, cuts, counts),
        in_specs=[anywhere] * 6 + [vmem] * 10 + [anywhere] * 4,
        out_specs=[vmem] * 5,
        out_shape=[jax.ShapeDtypeStruct((2,) + p.shape[1:], F32) for p, _ in pairs]
        + [jax.ShapeDtypeStruct((count, lanes), F32), jax.ShapeDtypeStruct((3, ROW_WINDOW, lanes), BF16)],
        scratch_shapes=scratch,
        compiler_params=pltpu.CompilerParams(vmem_limit_bytes=60 * 1024 * 1024, collective_id=0, has_side_effects=True),
        cost_estimate=pl.CostEstimate(flops=0, bytes_accessed=300_000_000, transcendentals=0), name="last_sums",
    )(*[v for pair in pairs for v in pair], *two, *small, *db, *rows)


def shards(images, cotangent, image_ids, patch_order, qkv_weight, qv_bias, proj_weight, rel_table, layer_scales,
           layer_norm_gains, norm_biases, fc1_weight, fc1_bias, fc2_weight, out_biases):
    me = lax.axis_index("narrow")
    at_wide = lax.axis_index("wide")
    wide = lax.axis_size("wide")
    core = me % 2
    first = me < 2
    quarter, width = images.shape[1:]
    rows = 4 * quarter
    padded = -(-rows // TILE) * TILE
    entries, heads = rel_table.shape[1:]
    flips = {k: [(d, d ^ k) for d in range(4)] for k in (1, 2, 3)}

    def swap(v, k):
        return lax.ppermute(v, "narrow", flips[k])

    def swap_wide(v, k):
        return lax.ppermute(v, "wide", [(d, d ^ k) for d in range(wide)])

    def pick(v, index):
        return lax.dynamic_index_in_dim(v, index, 0, keepdims=False)

    smalls = jnp.concatenate([layer_norm_gains[0, :1], norm_biases[0, :1], layer_norm_gains[0, 1:], norm_biases[0, 1:],
                              layer_scales[0], out_biases[0], fc1_bias.reshape(-1, width), qv_bias[0],
                              jnp.zeros((2, width), F32)])
    table = jnp.pad(rel_table[0].T, ((0, HEAD_ROWS - heads), (0, width - entries)))
    own_small = jnp.concatenate([smalls, table])
    other_small = swap(own_small, 1)
    own = dict(qkv=qkv_weight[0])
    own["proj"], own["fc1"], own["fc2"] = later([proj_weight[0], fc1_weight[0], fc2_weight[0]], other_small)
    other = {name: swap(own[name], 1) for name in MATRICES}
    bias_at = FC1_BIAS + fc1_bias.shape[1] // width
    both = [jnp.where(core == k, own_small, other_small) for k in range(2)]
    biases = build_bias(jnp.concatenate([v[16:] for v in both]), heads)
    weights = []
    for layer in range(2):
        vectors = both[layer][:16]
        weights.append(dict(
            layer=layer, pick=jnp.stack([(core == layer).astype(jnp.int32), core]), vectors=vectors, bias=biases[layer],
            **{name: (own[name], other[name]) for name in MATRICES}))

    section = dict(
        vectors=jnp.stack([w["vectors"] for w in weights]), bias=[w["bias"] for w in weights],
        own=own, other=other)
    meta = (jnp.stack([core, 1 - first.astype(jnp.int32)]),) + sequence_meta(pick(image_ids, core), pick(patch_order, core), padded)

    mine = jnp.where(first, images, cotangent)
    theirs = jnp.where(first, cotangent, images)
    pieces = [pick(mine, core), swap(pick(mine, 1 - core), 1), swap(pick(theirs, core), 2),
              swap(pick(theirs, 1 - core), 3)]
    rows_in = jnp.zeros((padded, width), BF16)
    for k, piece in enumerate(pieces):
        rows_in = lax.dynamic_update_slice(rows_in, piece, ((me ^ k) * quarter, 0))

    middle, = forward(False, (rows_in, rows_in), section, meta)
    y_out, *parts = forward(True, (rows_in, swap(middle, 2)), section, meta)
    kept = dict(zip(KEPT, parts))

    back = backward(rows_in, section, meta, kept)
    dy_in = jnp.where(first, swap(back, 2), rows_in)

    def reducer(keep, give, at_once=None):
        return Reducer(keep, give, lambda v: swap(v, 1), swap_wide, at_wide, wide, at_once)

    def mlp_part(dy, w, kept_one, after=()):
        dm, da, fc1_give, fc1_keep, fc2_give, fc2_keep, sums = mlp_bwd(True, dy, w, kept_one, after)
        return dm, da, [(fc2_keep, fc2_give), (fc1_keep, fc1_give)], sums

    def tail_part(dm, da, dz, w, kept_one, after=()):
        dx, give, keep, sums = attn_tail(dm, dz, da, w, kept_one, after)
        return dx, keep, give, sums

    def sent(*reducers):
        return [v for r in reducers for v in r.sent]

    def reducers(halves):
        return [reducer(*h, at_once) for h, at_once in zip(halves, swap_sums(halves, wide))]

    dm, da, halves, sums_two = mlp_part(dy_in, weights[1], kept)
    fc_two = [r.launch() for r in reducers(halves)]
    dz, db_two = attn_bwd(da, weights[1], meta, kept, sent(*fc_two))
    mid, *halves, tail_two = tail_part(dm, da, dz, weights[1], kept)
    attn_two = reducers([halves])[0].launch()
    for r in fc_two:
        r.step(mid)
    dm, da, halves, sums_one = mlp_part(mid, weights[0], kept, sent(attn_two, *fc_two))
    fc_one = reducers(halves)
    fc_one[0].launch()
    for r in fc_two + [attn_two]:
        r.step(fc_one[0].sent[0])
    dz, db_one = attn_bwd(da, weights[0], meta, kept, sent(*fc_two, *fc_one, attn_two))
    fc_one[0].step(dz)
    fc_one[1].launch(dz)
    attn_two.step(dz)
    ready = [r.two()[0] for r in fc_one + fc_two + [attn_two]]
    dx, *halves, tail_one = tail_part(dm, da, dz, weights[0], kept, sent(*fc_one, attn_two) + ready)

    if wide == 8:
        pairs = [(ready[0], fc_one[0].parts[-1]), (ready[1], fc_one[1].parts[-1]),
                 [v.reshape(wide, -1, v.shape[1]) for v in halves]]
        two = [v for k, r in enumerate(fc_two + [attn_two]) for v in (ready[2 + k], r.parts[-1])]
        *shares, small, others = last_sums(pairs, two, [sums_two, tail_two, sums_one, tail_one], [db_two, db_one],
                                           [dx, y_out])
        fc2, fc1, attn = [(v[0], v[1]) for v in shares]
        mine = lax.dynamic_slice_in_dim(jnp.where(first, dx, y_out), quarter * me, quarter, 0)
        others = lax.dynamic_slice_in_dim(others, (quarter - ROW_STEP) * me, quarter, 1)
    else:
        result = jnp.where(first, dx, y_out)[:rows].reshape(4, quarter, width)
        mine, others = pick(result, me), [swap(pick(result, me ^ k), k) for k in (1, 2, 3)]
        small = jnp.concatenate([sums_two, tail_two, sums_one, tail_one, table_back(db_two, width),
                                 table_back(db_one, width)])
        small = small + swap(small, 1)
        for k in range(wide.bit_length() - 1):
            small = small + swap_wide(small, 1 << k)
        shares = []
        for one, two in zip(fc_one + [reducer(*halves)], fc_two + [attn_two]):
            one, two = one.finish(), two.finish()
            stay = jnp.where(core == 0, one, two)
            got = swap(jnp.where(core == 0, two, one).astype(BF16), 1).astype(F32)
            shares.append((jnp.where(core == 0, stay, got), jnp.where(core == 0, got, stay)))
        fc2, fc1, attn = shares
    same, across = [mine, others[0]], others[1:]
    same = jnp.where(core == 0, jnp.stack(same), jnp.stack(same[::-1]))
    across = jnp.where(core == 0, jnp.stack(across), jnp.stack(across[::-1]))
    encoded = jnp.where(first, across, same)
    images_grad = jnp.where(first, same, across)
    qkv = jnp.concatenate([v[:, :3 * width // 2] for v in attn], axis=1)
    proj = jnp.concatenate([v[:, 3 * width // 2:] for v in attn], axis=1)
    tables = small[48:].reshape(2, HEAD_ROWS, width)
    totals = jnp.where(core == 0, small[24:48], small[:24])
    table_grad = jnp.where(core == 0, tables[1], tables[0])
    tail = totals[16:]
    return (
        encoded,
        images_grad,
        qkv[None],
        tail[SUM_Q:SUM_V + 1][None],
        proj[None],
        table_grad[:heads, :entries].T[None],
        jnp.stack([totals[SUM_SCALE_A], totals[SUM_SCALE_B]])[None],
        jnp.stack([tail[SUM_GAIN_A], totals[SUM_GAIN_B]])[None],
        jnp.stack([tail[SUM_SHIFT_A], totals[SUM_SHIFT_B]])[None],
        jnp.concatenate(fc1, axis=1)[None],
        totals[FC1_BIAS:bias_at].reshape(1, -1),
        jnp.concatenate(fc2, axis=1)[None],
        jnp.stack([totals[SUM_DA], totals[SUM_DF]])[None],
    )


def solution(mesh):
    by_layer = P("narrow", None, None)
    by_rows = P("wide", "narrow", None)
    by_both = P("narrow", "wide", None)
    in_specs = (by_rows, by_rows, P("wide", None), P("wide", None, None)) + (by_layer,) * 8 + (
        P("narrow", None), by_layer, by_layer)
    out_specs = (by_rows, by_rows, by_both, by_layer, by_both, by_layer, by_layer, by_layer, by_layer, by_both,
                 P("narrow", None), by_both, by_layer)
    return jax.shard_map(shards, mesh=mesh, in_specs=in_specs, out_specs=out_specs, check_vma=False)
```

```python
import functools

import jax
import jax.numpy as jnp
from jax import lax
from jax.experimental import pallas as pl
from jax.experimental.pallas import tpu as pltpu
from jax.sharding import PartitionSpec as P

EPSILON = 1e-06
HALF_ROOT = 0.7071067811865476
DENSITY_NORM = 0.3989422804014327
GRID = 14
SPAN = 2 * GRID - 1
PITCH = 16
SLOTS = GRID * PITCH
LANES = 256
CLASS_SLOT = 15
WIDE = 32
STRIP = 512
HEAD_ROWS = 16
F32 = jnp.float32
BF16 = jnp.bfloat16
NEGATIVE = -1000000000.0
LAG = 6
LAG_BACK = 2
TILE = 800

GAIN_A, SHIFT_A, GAIN_B, SHIFT_B, SCALE_A, SCALE_B, OUT_A, OUT_B, FC1_BIAS = range(9)
QKV_BIAS = 12
SUM_DF, SUM_SCALE_B, SUM_GAIN_B, SUM_SHIFT_B, SUM_DA, SUM_SCALE_A = range(6)
SUM_GAIN_A, SUM_SHIFT_A, SUM_Q, SUM_V = range(4)


def nn(a, b):
    return lax.dot_general(a, b, (((1,), (0,)), ((), ())), preferred_element_type=F32)


def nt(a, b):
    return lax.dot_general(a, b, (((1,), (1,)), ((), ())), preferred_element_type=F32)


def tn(a, b):
    return lax.dot_general(a, b, (((0,), (0,)), ((), ())), preferred_element_type=F32)


def iota(shape, axis):
    return lax.broadcasted_iota(jnp.int32, shape, axis)


def row_tile(t):
    return pl.ds(pl.multiple_of(t * TILE, 16), TILE)


def vec(vec_ref, k):
    return vec_ref[k:k + 1, :]


def row_stats(v):
    centred = v - jnp.mean(v, axis=-1, keepdims=True)
    inverse = lax.rsqrt(jnp.mean(centred * centred, axis=-1, keepdims=True) + EPSILON)
    return centred * inverse, inverse


def norm_tiles(src_ref, dst_ref, vec_ref, gain, shift):
    @pl.loop(0, src_ref.shape[0] // TILE)
    def _(t):
        rows = row_tile(t)
        unit, _ = row_stats(src_ref[rows, :].astype(F32))
        dst_ref[rows, :] = (unit * vec(vec_ref, gain) + vec(vec_ref, shift)).astype(BF16)


def extra_rows(first, lanes):
    row = iota((16, lanes), 0)
    out = jnp.zeros((16, lanes), F32)
    for k, value in enumerate(first):
        out = jnp.where(row == k, value, out)
    return out.astype(BF16)


def split3(v):
    hi = v.astype(BF16).astype(F32)
    mid = (v - hi).astype(BF16).astype(F32)
    return hi, mid, v - hi - mid


class Weights:
    def __init__(self, core, own, other, dst, sems):
        self.core, self.own, self.other, self.dst, self.sems = core, own, other, dst, sems

    def start(self, name, layer, chunk=None):
        src, slot = (lambda ref: ref), None
        if name == "fc1":
            src = lambda ref: ref.at[:, pl.ds(pl.multiple_of(chunk * ref.shape[0], 128), ref.shape[0])]
        if name == "fc2":
            src = lambda ref: ref.at[pl.ds(pl.multiple_of(chunk * ref.shape[1], 128), ref.shape[1]), :]
        dst, sem = self.place(name, chunk)

        @pl.when(self.core == layer)
        def _():
            pltpu.make_async_copy(src(self.own[name]), dst, sem).start()

        @pl.when(self.core != layer)
        def _():
            pltpu.make_async_copy(src(self.other[name]), dst, sem).start()

    def place(self, name, chunk):
        if chunk is None:
            return self.dst[name], self.sems[name]
        return self.dst[name].at[lax.rem(chunk, 2)], self.sems[name].at[lax.rem(chunk, 2)]

    def wait(self, name, chunk=None):
        dst, sem = self.place(name, chunk)
        pltpu.make_async_copy(dst, dst, sem).wait()

    def start_fc(self, layer, chunk):
        self.start("fc1", layer, chunk)
        self.start("fc2", layer, chunk)


MATRICES = ("qkv", "proj", "fc1", "fc2")


def weight_scratch(width):
    dma = pltpu.SemaphoreType.DMA
    return [pltpu.VMEM((width, 3 * width), BF16), pltpu.VMEM((width, width), BF16),
            pltpu.VMEM((2, width, width), BF16), pltpu.VMEM((2, width, width), BF16), dma, dma, dma((2,)), dma((2,))]


def weights_of(core, refs, scratch):
    return Weights(core, dict(zip(MATRICES, refs[:4])), dict(zip(MATRICES, refs[4:8])), dict(zip(MATRICES, scratch[:4])),
                   dict(zip(MATRICES, scratch[4:8])))


def forward_kernel(keep, core_ref, ws_ref, x_first, x_second, vec_refs, *refs):
    b_refs, et_ref, mask_ref, y_ref = refs[8:10], refs[10], refs[11], refs[12]
    if keep:
        xs_ref, n1_ref, o_ref, m_ref, n2_ref, a_ref, f_ref, zt_ref, ot_ref, lse_ref, g_ref, slope_ref = refs[13:25]
        scratch = refs[25:]
    else:
        n1_ref, o_ref, m_ref, n2_ref, zt_ref, ot_ref = refs[13:19]
        scratch = refs[19:]
    w = weights_of(core_ref[0], refs[:8], scratch[:8])
    x, b, bias, n1t, acc, wt, b_sem, x_sem = scratch[8:]
    layer, t = pl.program_id(0), pl.program_id(1)
    imgs = et_ref.shape[0]
    heads = b.shape[0]
    width = x.shape[1]
    hd = width // heads
    chunks = pl.num_programs(1) - imgs
    at = (0,) if keep else ()
    vec_ref = vec_refs.at[layer]

    def start_b(k):
        pltpu.make_async_copy(b_refs[k], b, b_sem).start()

    @pl.when((layer == 0) & (t == 0))
    def _():
        for k, ref in enumerate((x_first, x_second)):
            @pl.when(core_ref[1] == k)
            def _():
                pltpu.make_async_copy(ref, x, x_sem).start()

        w.start("qkv", 0)
        start_b(0)
        w.start("proj", 0)
        w.start_fc(0, 0)
        w.start_fc(0, 1)
        pltpu.make_async_copy(x_first, x, x_sem).wait()

    @pl.when(t == 0)
    def _():
        if keep:
            xs_ref[0] = x[...]
        o_ref[...] = jnp.zeros_like(o_ref)
        columns = vec_ref[8:16, :].T
        bias[0:width, :] = jnp.broadcast_to(columns[:, QKV_BIAS - 8:QKV_BIAS - 7], (width, 128))
        bias[width:2 * width, :] = jnp.zeros((width, 128), F32)
        bias[2 * width:, :] = jnp.broadcast_to(columns[:, QKV_BIAS - 7:QKV_BIAS - 6], (width, 128))
        norm_tiles(x, n1_ref.at[at] if keep else n1_ref, vec_ref, GAIN_A, SHIFT_A)
        w.wait("qkv")
        for c in range(3):
            part = slice(c * width, (c + 1) * width)
            wt[part, :] = w.dst["qkv"][:, part].T

    def full(ref):
        return ref.at[0] if keep else ref

    n1_now, o_now, m_now, n2_now = full(n1_ref), full(o_ref), full(m_ref), full(n2_ref)
    zt, ot = (zt_ref.at[0, 0], ot_ref.at[0, 0]) if keep else (zt_ref, ot_ref)

    @pl.when(t < imgs)
    def _():
        ws = pl.multiple_of(ws_ref[t], 16)
        et = et_ref[t]
        n1t[...] = tn(n1_now[pl.ds(ws, SLOTS), :], et).astype(BF16)

        @pl.loop(0, 3)
        def _(c):
            rows = pl.ds(pl.multiple_of(c * width, width), width)
            factor = jnp.where(c == 0, hd ** -0.5, 1.0)
            column = bias[rows, :]
            add = jnp.concatenate([column] * (LANES // 128), axis=1)
            zt[rows, :] = ((nn(wt[rows, :], n1t[...]) + add) * factor).astype(BF16)

        @pl.when(t == 0)
        def _():
            pltpu.make_async_copy(b, b, b_sem).wait()

        ones_q = extra_rows([1.0], LANES)
        mask_k = extra_rows([mask_ref[t]], SLOTS)
        ones_v = extra_rows([1.0], SLOTS)

        def scores(h):
            r = h * hd
            qt = jnp.concatenate([zt[r:r + hd, :], ones_q], axis=0)
            kt = jnp.concatenate([zt[width + r:width + r + hd, :SLOTS], mask_k], axis=0)
            return tn(kt, qt)

        def soft(h, s):
            s = s + b[h]
            m = jnp.max(s, axis=0, keepdims=True)
            return m, jnp.exp(s - m).astype(BF16)

        def finish(h, m, e):
            r = h * hd
            vt = jnp.concatenate([zt[2 * width + r:2 * width + r + hd, :SLOTS], ones_v], axis=0)
            o = nn(vt, e)
            total = o[hd:hd + 1]
            ot[r:r + hd, :] = (o[:hd] * (1.0 / total)).astype(BF16)
            if keep:
                lse_ref[0, 0, h:h + 1, :] = m + jnp.log(total)

        s, e = {}, {}
        for k in range(heads + 2 * LAG):
            if k < heads:
                s[k] = scores(k)
            if 0 <= k - LAG < heads:
                e[k - LAG] = soft(k - LAG, s.pop(k - LAG))
            if k - 2 * LAG >= 0:
                finish(k - 2 * LAG, *e.pop(k - 2 * LAG))

        win = pl.ds(ws, SLOTS)
        o_now[win, :] = (o_now[win, :].astype(F32) + nt(et, ot[...])).astype(BF16)

    j = t - imgs

    @pl.when((t == imgs) & (layer == 0))
    def _():
        w.start("qkv", 1)
        start_b(1)

    @pl.when(t == imgs)
    def _():
        w.wait("proj")
        a = nn(o_now[...], w.dst["proj"][...]) + vec(vec_ref, OUT_A)
        if keep:
            a_ref[0] = a.astype(BF16)
        m_now[...] = x[...].astype(F32) + vec(vec_ref, SCALE_A) * a
        acc[...] = jnp.zeros_like(acc)
        norm_tiles(m_now, n2_now, vec_ref, GAIN_B, SHIFT_B)

    @pl.when((t == imgs) & (layer == 0))
    def _():
        w.start("proj", 1)

    @pl.when(t >= imgs)
    def _():
        slot = lax.rem(j, 2)
        w.wait("fc1", j)
        w.wait("fc2", j)
        u = nn(n2_now[...], w.dst["fc1"][slot]) + vec_ref[pl.ds(FC1_BIAS + j, 1), :]
        cdf = 0.5 * (1.0 + lax.erf(u * HALF_ROOT))
        g = (u * cdf).astype(BF16)
        if keep:
            g_ref[0] = g
            slope_ref[0] = (cdf + u * (jnp.exp(-0.5 * u * u) * DENSITY_NORM)).astype(BF16)
        acc[...] += nn(g, w.dst["fc2"][slot])

        @pl.when(j + 2 < chunks)
        def _():
            w.start_fc(layer, j + 2)

        @pl.when((j + 2 >= chunks) & (layer == 0))
        def _():
            w.start_fc(1, j + 2 - chunks)

    @pl.when(j == chunks - 1)
    def _():
        @pl.loop(0, acc.shape[0] // TILE)
        def _(k):
            rows = row_tile(k)
            f = acc[rows, :] + vec(vec_ref, OUT_B)
            if keep:
                f_ref[0, rows, :] = f.astype(BF16)
            x[rows, :] = (m_now[rows, :] + vec(vec_ref, SCALE_B) * f).astype(BF16)

        @pl.when(layer == 1)
        def _():
            y_ref[...] = x[...]


def attn_bwd_kernel(pick_ref, ws_ref, da_ref, own_ref, other_ref, b_ref, et_ref, mask_ref, zt_ref, ot_ref, lse_ref,
                    dz_ref, db_ref, dat, dot, dzt):
    width = da_ref.shape[1]
    i = pl.program_id(0)

    @pl.when(i == 0)
    def _():
        dz_ref[...] = jnp.zeros_like(dz_ref)
        db_ref[...] = jnp.zeros_like(db_ref)
        dzt[...] = jnp.zeros_like(dzt)

    win = pl.ds(pl.multiple_of(ws_ref[i], 16), SLOTS)
    et = et_ref[0]
    dat[...] = tn(da_ref[win, :], et).astype(BF16)
    proj = jnp.where(pick_ref[0] == 1, own_ref[...], other_ref[...])
    dot[...] = nn(proj, dat[...]).astype(BF16)
    attn_back_image(et, mask_ref[0], zt_ref, ot_ref, lse_ref, b_ref, dat, dot, dzt, db_ref)
    for c in range(3):
        cols = slice(c * width, (c + 1) * width)
        dz_ref[win, cols] = (dz_ref[win, cols].astype(F32) + nt(et, dzt[cols, :])).astype(BF16)


def attn_back_image(et, mask, zt, ot, lse_ref, b, dat, dot, dzt, db_ref):
    heads = b.shape[0]
    width = dat.shape[0]
    hd = width // heads
    extra_k = extra_rows([mask, 1.0, 1.0, 1.0], SLOTS)
    extra_v = extra_rows([1.0, 1.0, 1.0], SLOTS)

    def parts(h):
        r = h * hd
        return (zt[r:r + hd, :], zt[width + r:width + r + hd, :SLOTS], zt[2 * width + r:2 * width + r + hd, :SLOTS],
                dot[r:r + hd, :])

    def products(h):
        qt, kt, vt, dt = parts(h)
        r = h * hd
        delta = jnp.sum(dt.astype(F32) * ot[r:r + hd, :].astype(F32), axis=0, keepdims=True)
        extra_q = extra_rows([1.0, *split3(-lse_ref[h:h + 1, :])], LANES)
        extra_d = extra_rows(split3(-delta), LANES)
        s = tn(jnp.concatenate([kt, extra_k], axis=0), jnp.concatenate([qt, extra_q], axis=0))
        dp = tn(jnp.concatenate([vt, extra_v], axis=0), jnp.concatenate([dt, extra_d], axis=0))
        return s, dp

    def middle(h, s, dp):
        p = jnp.exp(s + b[h])
        ds = p * dp
        if db_ref is not None:
            db_ref[h] += ds
        return p.astype(BF16), ds.astype(BF16)

    def finish(h, p, ds):
        qt, kt, vt, dt = parts(h)
        r = h * hd
        dzt[2 * width + r:2 * width + r + hd, :SLOTS] = nt(dt, p).astype(BF16)
        dzt[width + r:width + r + hd, :SLOTS] = nt(qt, ds).astype(BF16)
        dzt[r:r + hd, :] = (nn(kt, ds) * hd ** -0.5).astype(BF16)

    s, e = {}, {}
    for t in range(heads + 2 * LAG_BACK):
        if t < heads:
            s[t] = products(t)
        if 0 <= t - LAG_BACK < heads:
            e[t - LAG_BACK] = middle(t - LAG_BACK, *s.pop(t - LAG_BACK))
        if t - 2 * LAG_BACK >= 0:
            finish(t - 2 * LAG_BACK, *e.pop(t - 2 * LAG_BACK))


def backward_kernel(core_ref, ws_ref, dy_ref, vec_refs, *refs):
    b_refs, et_ref, mask_ref = refs[8:10], refs[10], refs[11]
    m_ref, x_ref, slope_ref, zt_ref, ot_ref, lse_ref, dx_ref = refs[12:19]
    scratch = refs[19:]
    w = weights_of(core_ref[0], refs[:8], scratch[:8])
    dy, df, acc, dm, da, dz, dat, dot, dzt, b, b_sem = scratch[8:]
    step, t = pl.program_id(0), pl.program_id(1)
    layer = 1 - step
    imgs = et_ref.shape[0]
    width = dy.shape[1]
    chunks = pl.num_programs(1) - imgs - 1
    vec_ref = vec_refs.at[layer]

    def start_b(k):
        pltpu.make_async_copy(b_refs[k], b, b_sem).start()

    @pl.when((step == 0) & (t == 0))
    def _():
        w.start_fc(1, 0)
        w.start_fc(1, 1)
        w.start("proj", 1)
        start_b(1)
        w.start("qkv", 1)
        dy[...] = dy_ref[...]

    @pl.when((step == 1) & (t == 0))
    def _():
        w.start("qkv", 0)

    @pl.when(t == 0)
    def _():
        acc[...] = jnp.zeros_like(acc)

        @pl.loop(0, df.shape[0] // TILE)
        def _(k):
            rows = row_tile(k)
            df[rows, :] = (dy[rows, :].astype(F32) * vec(vec_ref, SCALE_B)).astype(BF16)

    @pl.when(t < chunks)
    def _():
        slot = lax.rem(t, 2)
        w.wait("fc1", t)
        w.wait("fc2", t)
        du = (nt(df[...], w.dst["fc2"][slot]) * slope_ref[...].astype(F32)).astype(BF16)
        acc[...] += nt(du, w.dst["fc1"][slot])

        @pl.when(t + 2 < chunks)
        def _():
            w.start_fc(layer, t + 2)

        @pl.when((t + 2 >= chunks) & (step == 0))
        def _():
            w.start_fc(0, t + 2 - chunks)

    @pl.when(t == chunks - 1)
    def _():
        def emit(rows, dv):
            value = dy[rows, :].astype(F32) + dv
            dm[rows, :] = value
            da[rows, :] = (value * vec(vec_ref, SCALE_A)).astype(BF16)
            return ()

        norm_back_tiles(0, m_ref, acc, vec_ref, GAIN_B, emit)
        dz[...] = jnp.zeros_like(dz)
        dzt[...] = jnp.zeros_like(dzt)
        w.wait("proj")
        pltpu.make_async_copy(b, b, b_sem).wait()

    @pl.when((t >= chunks) & (t < chunks + imgs))
    def _():
        i = t - chunks
        et = et_ref[i]
        win = pl.ds(pl.multiple_of(ws_ref[i], 16), SLOTS)
        dat[...] = tn(da[win, :], et).astype(BF16)
        dot[...] = nn(w.dst["proj"][...], dat[...]).astype(BF16)
        attn_back_image(et, mask_ref[i], zt_ref, ot_ref, lse_ref, b, dat, dot, dzt, None)
        for c in range(3):
            cols = slice(c * width, (c + 1) * width)
            dz[win, cols] = (dz[win, cols].astype(F32) + nt(et, dzt[cols, :])).astype(BF16)

    @pl.when(t == chunks + imgs)
    def _():
        @pl.when(step == 0)
        def _():
            w.start("proj", 0)
            start_b(0)

        w.wait("qkv")
        acc[...] = nt(dz[:, :width], w.dst["qkv"][:, :width])
        for c in range(1, 3):
            cols = slice(c * width, (c + 1) * width)
            acc[...] += nt(dz[:, cols], w.dst["qkv"][:, cols])

        def emit(rows, dv):
            dy[rows, :] = (dm[rows, :] + dv).astype(BF16)
            return ()

        norm_back_tiles(0, x_ref, acc, vec_ref, GAIN_A, emit)

        @pl.when(step == 1)
        def _():
            dx_ref[...] = dy[...]


def spread(count):
    entry = iota((count, SPAN * WIDE), 0)
    lane = iota((count, SPAN * WIDE), 1)
    return jnp.where((entry == lane // WIDE * SPAN + lane % WIDE) & (lane % WIDE < SPAN), 1.0, 0.0).astype(BF16)


def squeeze():
    lane = iota((SPAN * WIDE, STRIP), 0)
    to = iota((SPAN * WIDE, STRIP), 1)
    return jnp.where(lane == to // PITCH * WIDE + to % PITCH, 1.0, 0.0).astype(BF16)


def placed(product, v, onehot):
    return sum(product(part.astype(BF16), onehot) for part in split3(v))


def strip_rows(layer, head):
    return pl.ds(layer * HEAD_ROWS + head, PITCH, stride=2 * HEAD_ROWS)


def bias_kernel(table_ref, *refs):
    b_refs, (shifted, strips) = refs[:2], refs[2:]
    rows = table_ref.shape[0]
    heads = b_refs[0].shape[0]
    wide = placed(nn, table_ref[...], spread(table_ref.shape[1]))
    for c in range(PITCH):
        shifted[c * rows:(c + 1) * rows, :] = pltpu.roll(wide, (c - GRID + 1) % (SPAN * WIDE), 1)
    packed = placed(nn, shifted[...], squeeze())
    for k in range(strips.shape[0]):
        strips[k] = packed[:, k * 128:(k + 1) * 128]
    row = iota((SLOTS, LANES), 0)
    col = iota((SLOTS, LANES), 1)
    for layer, b_ref in enumerate(b_refs):
        for h in range(heads):
            strip = jnp.concatenate([strips[k, strip_rows(layer, h), :] for k in range(strips.shape[0])], axis=1)
            for r in range(GRID):
                at = PITCH * (GRID - 1 - r)
                b_ref[h, r * PITCH:(r + 1) * PITCH, :] = strip[:, at:at + LANES]
            mine = layer * HEAD_ROWS + h
            query, key, both = [table_ref[mine:mine + 1, SPAN * SPAN + k:SPAN * SPAN + k + 1] for k in range(3)]
            full = jnp.where(col == CLASS_SLOT, query, b_ref[h])
            b_ref[h] = jnp.where(row == CLASS_SLOT, jnp.where(col == CLASS_SLOT, both, key), full)


def bias_back_kernel(db_ref, table_ref, strips, classes):
    table_ref[...] = folded(db_ref, strips, classes)


def folded(db_ref, strips, classes):
    heads = db_ref.shape[0]
    row = iota((SLOTS, LANES), 0)
    col = iota((SLOTS, LANES), 1)
    is_row = row == CLASS_SLOT
    is_col = col == CLASS_SLOT
    entry = iota((1, classes.shape[1]), 1) - SPAN * SPAN
    strips[...] = jnp.zeros_like(strips)
    classes[...] = jnp.zeros_like(classes)
    for h in range(heads):
        full = db_ref[h]
        query = jnp.sum(jnp.where(is_col & ~is_row, full, 0.0), keepdims=True)
        key = jnp.sum(jnp.where(is_row & ~is_col, full, 0.0), keepdims=True)
        both = jnp.sum(jnp.where(is_row & is_col, full, 0.0), keepdims=True)
        classes[h:h + 1, :] = jnp.where(
            entry == 0, query, jnp.where(entry == 1, key, jnp.where(entry == 2, both, 0.0)))
        plain = jnp.where(is_row | is_col, 0.0, full)
        total = jnp.zeros((PITCH, STRIP), F32)
        for r in range(GRID):
            part = jnp.concatenate([plain[r * PITCH:(r + 1) * PITCH, :], jnp.zeros((PITCH, STRIP - LANES), F32)],
                                   axis=1)
            total = total + pltpu.roll(part, PITCH * (GRID - 1 - r), 1)
        for k in range(strips.shape[0]):
            strips[k, pl.ds(h, PITCH, stride=HEAD_ROWS), :] = total[:, k * 128:(k + 1) * 128]
    rows = classes.shape[0]
    wide = placed(nt, jnp.concatenate([strips[k] for k in range(strips.shape[0])], axis=1), squeeze())
    gathered = jnp.zeros((rows, SPAN * WIDE), F32)
    for c in range(GRID):
        gathered = gathered + pltpu.roll(wide[c * rows:(c + 1) * rows, :], (GRID - 1 - c) % (SPAN * WIDE), 1)
    return placed(nt, gathered, spread(classes.shape[1])) + classes[...]


def norm_back_tiles(count, src_ref, grad_ref, vec_ref, gain, emit):
    def body(t, sums):
        rows = row_tile(t)
        unit, inverse = row_stats(src_ref[rows, :].astype(F32))
        grad = grad_ref[rows, :]
        scaled = grad * vec(vec_ref, gain)
        mean_one = jnp.mean(scaled, axis=-1, keepdims=True)
        mean_two = jnp.mean(scaled * unit, axis=-1, keepdims=True)
        more = emit(rows, inverse * (scaled - mean_one - unit * mean_two))
        if not count:
            return sums
        return tuple(s + jnp.sum(v, axis=0, keepdims=True) for s, v in zip(sums, (grad * unit, grad) + more))

    zero = jnp.zeros((1, grad_ref.shape[1]), F32)
    return lax.fori_loop(0, grad_ref.shape[0] // TILE, body, (zero,) * count)


def mlp_bwd_kernel(want, pick_ref, dy_ref, m_ref, vec_ref, slope_ref, fc1_own, fc1_other, fc2_own, fc2_other, *rest):
    if want:
        (n2_ref, g_ref, a_ref, f_ref, dm_ref, da_ref, fc1_give, fc1_keep, fc2_give, fc2_keep, sums_ref, df, acc) = rest
    else:
        dm_ref, da_ref, df, acc = rest
    j = pl.program_id(0)
    steps = pl.num_programs(0)
    mine = pick_ref[0] == 1
    core = pick_ref[1]
    width = dy_ref.shape[1]

    @pl.when(j == 0)
    def _():
        acc[...] = jnp.zeros_like(acc)
        if want:
            sums_ref[...] = jnp.zeros_like(sums_ref)
        zero = jnp.zeros((1, width), F32)

        def body(t, sums):
            rows = row_tile(t)
            dy = dy_ref[rows, :].astype(F32)
            scaled = (dy * vec(vec_ref, SCALE_B)).astype(BF16)
            df[rows, :] = scaled
            if not want:
                return sums
            return (sums[0] + jnp.sum(scaled.astype(F32), axis=0, keepdims=True),
                    sums[1] + jnp.sum(dy * f_ref[rows, :].astype(F32), axis=0, keepdims=True))

        sums = lax.fori_loop(0, df.shape[0] // TILE, body, (zero, zero) if want else ())
        if want:
            sums_ref[SUM_DF:SUM_DF + 1, :] = sums[0]
            sums_ref[SUM_SCALE_B:SUM_SCALE_B + 1, :] = sums[1]

    fc1 = jnp.where(mine, fc1_own[...], fc1_other[...])
    fc2 = jnp.where(mine, fc2_own[...], fc2_other[...])
    du = (nt(df[...], fc2) * slope_ref[...].astype(F32)).astype(BF16)
    acc[...] += nt(du, fc1)
    if want:
        at = lax.rem(j + (1 - core) * (steps // 2), steps)
        sums_ref[pl.ds(FC1_BIAS + at, 1), :] = jnp.sum(du.astype(F32), axis=0, keepdims=True)
        grad = tn(g_ref[...], df[...]).astype(BF16)
        low, high = grad[:, :width // 2], grad[:, width // 2:]
        fc2_keep[...] = jnp.where(core == 0, low, high)
        fc2_give[...] = jnp.where(core == 0, high, low)
        grad1 = tn(n2_ref[...], du).astype(BF16)

        @pl.when(j < steps // 2)
        def _():
            fc1_give[...] = grad1

        @pl.when(j >= steps // 2)
        def _():
            fc1_keep[...] = grad1

    @pl.when(j == steps - 1)
    def _():
        def emit(rows, dv):
            dm = dy_ref[rows, :].astype(F32) + dv
            da = (dm * vec(vec_ref, SCALE_A)).astype(BF16)
            dm_ref[rows, :] = dm
            da_ref[rows, :] = da
            return (da.astype(F32), dm * a_ref[rows, :].astype(F32)) if want else ()

        sums = norm_back_tiles(4 if want else 0, m_ref, acc, vec_ref, GAIN_B, emit)
        for k, s in zip((SUM_GAIN_B, SUM_SHIFT_B, SUM_DA, SUM_SCALE_A), sums):
            sums_ref[k:k + 1, :] = s


def attn_tail_kernel(pick_ref, vec_ref, dz_ref, own_ref, other_ref, dm_ref, da_ref, x_refs, n1_refs, o_refs, dx_ref,
                     sums_ref, give_ref, keep_ref, o, da, n1, dz, wt, dm, x, give, keep, acc, sems, layer):
    core = pick_ref[1]
    width = x.shape[1]
    part = 3 * width // 2
    arrays = dict(o=(o_refs.at[layer], o), da=(da_ref, da), n1=(n1_refs.at[layer], n1), dm=(dm_ref, dm),
                  x=(x_refs.at[layer], x))
    place = {name: k for k, name in enumerate(arrays)}

    def load(name):
        src, dst = arrays[name]
        return pltpu.make_async_copy(src, dst, sems.at[place[name]])

    def columns(ref, k):
        half = core if k else 1 - core
        return ref.at[:, pl.ds(pl.multiple_of(half * part, 128), part)]

    def load_dz(k):
        return pltpu.make_async_copy(columns(dz_ref, k), dz.at[k], sems.at[5 + k])

    def load_wt(k):
        @pl.when(pick_ref[0] == 1)
        def _():
            pltpu.make_async_copy(columns(own_ref, k), wt.at[k], sems.at[7 + k]).start()

        @pl.when(pick_ref[0] == 0)
        def _():
            pltpu.make_async_copy(columns(other_ref, k), wt.at[k], sems.at[7 + k]).start()

    load("o").start()
    load("da").start()
    load("n1").start()
    load_dz(0).start()
    load_wt(0)
    load_dz(1).start()
    load_wt(1)
    load("dm").start()
    load("x").start()
    sums_ref[...] = jnp.zeros_like(sums_ref)
    load("o").wait()
    load("da").wait()
    grad = tn(o[...], da[...]).astype(BF16)
    low, high = grad[:, :width // 2], grad[:, width // 2:]
    give[:, part:] = jnp.where(core == 0, high, low)
    keep[:, part:] = jnp.where(core == 0, low, high)
    load("n1").wait()
    stores = []
    for k, (to, out) in enumerate(((give, give_ref), (keep, keep_ref))):
        load_dz(k).wait()
        half = core if k else 1 - core
        to[:, :part] = tn(n1[...], dz[k]).astype(BF16)
        stores.append(pltpu.make_async_copy(to, out, sems.at[9 + k]))
        stores[-1].start()
        totals = jnp.sum(dz[k].astype(F32), axis=0, keepdims=True)

        @pl.when(half == 0)
        def _():
            sums_ref[SUM_Q:SUM_Q + 1, :] = totals[:, :width]

        @pl.when(half == 1)
        def _():
            sums_ref[SUM_V:SUM_V + 1, :] = totals[:, width // 2:]

        pltpu.make_async_copy(wt.at[k], wt.at[k], sems.at[7 + k]).wait()
        if k == 0:
            acc[...] = nt(dz[k], wt[k])
        else:
            acc[...] += nt(dz[k], wt[k])
    load("dm").wait()
    load("x").wait()

    def emit(rows, dv):
        dx_ref[rows, :] = (dm[rows, :] + dv).astype(BF16)
        return ()

    sums = norm_back_tiles(2, x, acc, vec_ref, GAIN_A, emit)
    for k, v in zip((SUM_GAIN_A, SUM_SHIFT_A), sums):
        sums_ref[k:k + 1, :] = v
    for c in stores:
        c.wait()


TAKES = dict(backward=85, forward=75, forward_keep=85, mlp_bwd=15, mlp_bwd_all=27, attn_bwd=20, attn_bwd_all=21, attn_tail=9,
             attn_tail_all=16, bias_build=6, bias_back=9)


VMEM = dict(backward=60, forward=60, forward_keep=60, mlp_bwd=60, mlp_bwd_all=60, attn_bwd=60, attn_bwd_all=60, attn_tail=60,
            attn_tail_all=60, bias_build=60, bias_back=60)


def cost(name):
    return pl.CostEstimate(flops=TAKES[name] * 800_000_000, bytes_accessed=TAKES[name] * 3_000_000, transcendentals=0)


def params(name):
    return pltpu.CompilerParams(vmem_limit_bytes=VMEM[name] * 1024 * 1024)


def shaped(*arrays):
    return [jax.ShapeDtypeStruct(s, d) for s, d in arrays]


def whole(shape):
    return pl.BlockSpec(shape, lambda *_: (0,) * len(shape))


def once(shape):
    return pl.BlockSpec(shape, lambda *_: (0,) * len(shape), pipeline_mode=pl.Buffered(1))


def per_image(shape):
    return pl.BlockSpec((1,) + shape, lambda i, *_: (i,) + (0,) * len(shape))


def call(kernel, name, prefetched, grid, inputs, outputs, scratch, after=()):
    count = len(prefetched) + len(inputs)

    def body(*refs):
        kernel(*refs[:count], *refs[count + len(after):])

    inputs = inputs + [(a, pl.BlockSpec(memory_space=pl.ANY)) for a in after]
    return pl.pallas_call(
        body,
        grid_spec=pltpu.PrefetchScalarGridSpec(
            num_scalar_prefetch=len(prefetched), grid=grid, in_specs=[s for _, s in inputs],
            out_specs=[s for _, _, s in outputs], scratch_shapes=scratch),
        out_shape=[jax.ShapeDtypeStruct(s, d) for s, d, _ in outputs],
        compiler_params=params(name), name=name, cost_estimate=cost(name),
    )(*prefetched, *[a for a, _ in inputs])


def forward(keep, x_pair, section, meta):
    core, ws, et, mask = meta
    rows, width = x_pair[0].shape
    biases = section["bias"]
    heads = biases[0].shape[0]
    hidden = section["own"]["fc1"].shape[1]
    imgs = et.shape[0]
    chunks = hidden // width
    anywhere = pl.BlockSpec(memory_space=pl.ANY)
    vectors = section["vectors"]
    inputs = [(x, anywhere) for x in x_pair] + [(vectors, once(vectors.shape))]
    inputs += [(section[side][name], anywhere) for side in ("own", "other") for name in MATRICES]
    inputs += [(v, anywhere) for v in biases] + [(et, once(et.shape)), (mask, once(mask.shape))]
    outputs = [((rows, width), BF16, whole((rows, width)))]
    low = [pltpu.VMEM((rows, width), BF16)]
    scratch = weight_scratch(width) + low + [
        pltpu.VMEM(biases[0].shape, F32), pltpu.VMEM((3 * width, 128), F32), pltpu.VMEM((width, LANES), BF16),
        pltpu.VMEM((rows, width), F32), pltpu.VMEM((3 * width, width), BF16), pltpu.SemaphoreType.DMA, pltpu.SemaphoreType.DMA]
    if keep:
        def of_layer(kind):
            return (2, rows, width), kind, pl.BlockSpec((1, rows, width), lambda l, t, *_: (l, 0, 0))

        def of_image(*shape, kind=BF16):
            return ((2, imgs) + shape, kind,
                    pl.BlockSpec((1, 1) + shape, lambda l, t, *_: (l, jnp.minimum(t, imgs - 1), 0, 0)))

        of_chunk = ((2, rows, hidden), BF16,
                    pl.BlockSpec((1, rows, width), lambda l, t, *_: (l, 0, jnp.maximum(t - imgs, 0))))
        outputs += [of_layer(BF16), of_layer(BF16), of_layer(BF16), of_layer(F32), of_layer(BF16), of_layer(BF16),
                    of_layer(BF16), of_image(3 * width, LANES), of_image(width, LANES),
                    of_image(heads, LANES, kind=F32), of_chunk, of_chunk]
    else:
        scratch = low * 2 + [pltpu.VMEM((rows, width), F32)] + low + [
            pltpu.VMEM((3 * width, LANES), BF16), pltpu.VMEM((width, LANES), BF16)] + scratch
    return call(functools.partial(forward_kernel, keep), "forward_keep" if keep else "forward", [core, ws],
                (2, imgs + chunks), inputs, outputs, scratch)


def backward(dy, section, meta, kept):
    core, ws, et, mask = meta
    rows, width = dy.shape
    biases = section["bias"]
    imgs = et.shape[0]
    chunks = section["own"]["fc1"].shape[1] // width
    anywhere = pl.BlockSpec(memory_space=pl.ANY)
    vectors = section["vectors"]
    inputs = [(dy, once(dy.shape)), (vectors, once(vectors.shape))]
    inputs += [(section[side][name], anywhere) for side in ("own", "other") for name in MATRICES]
    inputs += [(v, anywhere) for v in biases] + [(et, once(et.shape)), (mask, once(mask.shape))]
    of_layer = pl.BlockSpec((None, rows, width), lambda l, t, *_: (1 - l, 0, 0))
    inputs += [(kept["m"], of_layer), (kept["x"], of_layer)]
    inputs += [(kept["slope"], pl.BlockSpec((None, rows, width),
                                            lambda l, t, *_: (1 - l, 0, jnp.minimum(t, chunks - 1))))]
    for name in ("zt", "ot", "lse"):
        v = kept[name]
        inputs += [(v, pl.BlockSpec((None, None) + v.shape[2:],
                                    lambda l, t, *_: (1 - l, jnp.clip(t - chunks, 0, imgs - 1), 0, 0)))]
    low, high = pltpu.VMEM((rows, width), BF16), pltpu.VMEM((rows, width), F32)
    slots = pltpu.VMEM((width, LANES), BF16)
    scratch = weight_scratch(width) + [
        low, low, high, high, low, pltpu.VMEM((rows, 3 * width), BF16), slots, slots,
        pltpu.VMEM((3 * width, LANES), BF16), pltpu.VMEM(biases[0].shape, F32), pltpu.SemaphoreType.DMA]
    return call(backward_kernel, "backward", [core, ws], (2, chunks + imgs + 1), inputs,
                [((rows, width), BF16, whole((rows, width)))], scratch)[0]


def attn_bwd(da, w, meta, kept, after=()):
    _, ws, et, mask = meta
    rows, width = da.shape
    bias = w["bias"]
    imgs = et.shape[0]
    single_proj = once((width, width))
    layer = w["layer"]

    def kept_image(name):
        v = kept[name]
        return v, pl.BlockSpec((None, None) + v.shape[2:], lambda i, *_: (layer, i, 0, 0))

    inputs = [(da, once(da.shape)), (w["proj"][0], single_proj), (w["proj"][1], single_proj), (bias, once(bias.shape)),
              (et, per_image(et.shape[1:])), (mask, per_image(mask.shape[1:])), kept_image("zt"),
              kept_image("ot"), kept_image("lse")]
    outputs = [((rows, 3 * width), BF16, whole((rows, 3 * width)))]
    outputs += [(bias.shape, F32, whole(bias.shape))]
    scratch = [pltpu.VMEM((width, LANES), BF16), pltpu.VMEM((width, LANES), BF16), pltpu.VMEM((3 * width, LANES), BF16)]
    return call(attn_bwd_kernel, "attn_bwd_all", [w["pick"], ws],
                (imgs,), inputs, outputs, scratch, after)


def build_bias(tables, heads):
    shape = (heads, SLOTS, LANES)
    rows = tables.shape[0]
    return call(bias_kernel, "bias_build", [], (1,), [(tables, once(tables.shape))], [(shape, F32, whole(shape))] * 2,
                [pltpu.VMEM((PITCH * rows, SPAN * WIDE), F32), pltpu.VMEM((STRIP // 128, PITCH * rows, 128), F32)])


def table_back(db, lanes, after=()):
    return call(bias_back_kernel, "bias_back", [], (1,), [(db, once(db.shape))],
                [((HEAD_ROWS, lanes), F32, whole((HEAD_ROWS, lanes)))],
                [pltpu.VMEM((STRIP // 128, PITCH * HEAD_ROWS, 128), F32), pltpu.VMEM((HEAD_ROWS, lanes), F32)],
                after)[0]


def chosen(which, block, to_index):
    def index(j, pick):
        used = pick[0] if which == 0 else 1 - pick[0]
        return tuple(k * used for k in to_index(j, pick))
    return pl.BlockSpec(block, index)


def both(pair, block, to_index):
    return [(pair[k], chosen(k, block, to_index)) for k in range(2)]


def kept_whole(kept, name, w):
    v, layer = kept[name], w["layer"]
    return v, pl.BlockSpec((None,) + v.shape[1:], lambda *_: (layer, 0, 0), pipeline_mode=pl.Buffered(1))


def mlp_bwd(want, dy, w, kept, after=()):
    rows, width = dy.shape
    hidden = w["fc1"][0].shape[1]
    steps = hidden // width
    full = whole((rows, width))
    single = once((rows, width))

    def at(j, pick):
        return lax.rem(j + (1 - pick[1]) * (steps // 2), steps)

    layer = w["layer"]
    part = pl.BlockSpec((None, rows, width), lambda j, p: (layer, 0, at(j, p)))
    inputs = [(dy, single), kept_whole(kept, "m", w), (w["vectors"], once(w["vectors"].shape)), (kept["slope"], part),
              *both(w["fc1"], (width, width), lambda j, p: (0, at(j, p))),
              *both(w["fc2"], (width, width), lambda j, p: (at(j, p), 0))]
    outputs = [((rows, width), F32, full), ((rows, width), BF16, full)]
    if want:
        inputs += [kept_whole(kept, "n2", w), (kept["g"], part), kept_whole(kept, "a", w), kept_whole(kept, "f", w)]
        half = pl.BlockSpec((width, width // 2), lambda j, p: (at(j, p), 0))
        give = pl.BlockSpec((width, width), lambda j, p: (0, jnp.minimum(j, steps // 2 - 1)))
        stay = pl.BlockSpec((width, width), lambda j, p: (0, jnp.maximum(j - steps // 2, 0)))
        outputs += [((width, hidden // 2), BF16, give), ((width, hidden // 2), BF16, stay),
                    ((hidden, width // 2), BF16, half), ((hidden, width // 2), BF16, half),
                    ((16, width), F32, whole((16, width)))]
    scratch = [pltpu.VMEM((rows, width), BF16), pltpu.VMEM((rows, width), F32)]
    return call(functools.partial(mlp_bwd_kernel, want), "mlp_bwd_all" if want else "mlp_bwd", [w["pick"]],
                (steps,), inputs, outputs, scratch, after)


def attn_tail(dm, dz, da, w, kept, after=()):
    rows, width = dm.shape
    part = 3 * width // 2
    layer = w["layer"]
    anywhere = pl.BlockSpec(memory_space=pl.ANY)
    inputs = [(w["vectors"], once(w["vectors"].shape))]
    inputs += [(v, anywhere) for v in (dz, *w["qkv"], dm, da, kept["x"], kept["n1"], kept["o"])]
    outputs = [((rows, width), BF16, whole((rows, width))), ((8, width), F32, whole((8, width)))]
    outputs += [((width, 2 * width), BF16, anywhere)] * 2
    low, high = pltpu.VMEM((rows, width), BF16), pltpu.VMEM((rows, width), F32)
    scratch = [low, low, low, pltpu.VMEM((2, rows, part), BF16), pltpu.VMEM((2, width, part), BF16), high, low,
               pltpu.VMEM((width, 2 * width), BF16), pltpu.VMEM((width, 2 * width), BF16), high,
               pltpu.SemaphoreType.DMA((11,))]
    dx, sums, give, keep = call(functools.partial(attn_tail_kernel, layer=layer), "attn_tail_all", [w["pick"]], (1,),
                                inputs, outputs, scratch, after)
    return dx, give, keep, sums


def sequence_meta(ids, order, rows):
    imgs, patches = order.shape
    image = jnp.arange(imgs, dtype=jnp.int32)
    start = jnp.sum((ids[None, :] < image[:, None]).astype(jnp.int32), axis=1)
    count = jnp.sum((ids[None, :] == image[:, None]).astype(jnp.int32), axis=1)
    ws = jnp.minimum(start // 16 * 16, rows - SLOTS)
    slot = jnp.arange(LANES, dtype=jnp.int32)
    is_class = slot == CLASS_SLOT
    is_patch = (slot % PITCH < GRID) & (slot < SLOTS)
    patch = jnp.where(is_patch, slot // PITCH * GRID + slot % PITCH, -1)
    place = jnp.arange(1, patches + 1, dtype=jnp.int32)
    offset = jnp.sum(jnp.where(order[:, None, :] == patch[None, :, None], place, 0), axis=2)
    valid = (is_class | is_patch)[None, :] & (offset < count[:, None])
    local = jnp.where(valid, offset + (start - ws)[:, None], -1)
    row = jnp.arange(SLOTS, dtype=jnp.int32)
    et = (local[:, None, :] == row[None, :, None]).astype(BF16)
    mask = jnp.where(valid, 0.0, NEGATIVE).astype(F32)[:, None, :SLOTS]
    return ws, et, mask


KEPT = ("x", "n1", "o", "m", "n2", "a", "f", "zt", "ot", "lse", "g", "slope")


def later(arrays, token):
    if token is None:
        return list(arrays)
    return list(lax.optimization_barrier((*arrays, token)))[:-1]


class Reducer:
    def __init__(self, keep, give, swap_core, swap_wide, at_wide, wide, at_once=None):
        self.swap_wide, self.at_wide = swap_wide, at_wide
        if at_once is not None:
            send, stay = at_once
            self.sent, self.parts = [send], [stay]
            self.left, self.bit = wide // 2, 2
            return
        shape = (wide, keep.shape[0] // wide, keep.shape[1])
        self.parts = [v.reshape(shape) for v in (keep, swap_core(give))]
        self.left, self.bit = wide, 1
        self.sent = []

    def launch(self, token=None):
        self.parts.append(self.swap_wide(later(self.sent, token)[0], 1))
        return self

    def hold(self, token):
        self.parts[-1], = later([self.parts[-1]], token)

    def added(self, parts):
        return sum(v.astype(F32) for v in parts)

    def step(self, token=None):
        if self.left == 1:
            return
        self.hold(token)
        mine = self.at_wide // self.bit % 2
        pairs = [v.reshape((self.left // 2, 2) + v.shape[1:]) for v in self.parts]
        self.sent = [self.added(lax.dynamic_index_in_dim(v, 1 - mine, 1, keepdims=False) for v in pairs).astype(BF16)]
        self.parts = [lax.dynamic_index_in_dim(v, mine, 1, keepdims=False) for v in pairs]
        self.parts.append(self.swap_wide(self.sent[0], self.bit))
        self.left, self.bit = self.left // 2, 2 * self.bit

    def two(self):
        return [self.added(self.parts[:-1]).astype(BF16), self.parts[-1]]

    def finish(self, token=None):
        while self.left > 1:
            self.step(token)
        self.hold(token)
        return self.added(self.parts)[0]


def swap_sums_kernel(count, *refs):
    keeps, gives, outs = refs[:count], refs[count:2 * count], refs[2 * count:4 * count]
    mine, come = refs[4 * count:5 * count], refs[5 * count:6 * count]
    local_sem, send_sem, recv_sem = refs[6 * count:]
    me = lax.axis_index("narrow")
    b = lax.axis_index("wide") % 2
    partner = {"narrow": me + 1 - 2 * (me % 2)}
    barrier = pltpu.get_barrier_semaphore()
    pl.semaphore_signal(barrier, inc=1, device_id=partner, device_id_type=pl.DeviceIdType.MESH)
    pl.semaphore_wait(barrier, 1)
    copies = []
    for k in range(count):
        remote = pltpu.make_async_remote_copy(
            src_ref=gives[k], dst_ref=come[k], send_sem=send_sem.at[k], recv_sem=recv_sem.at[k], device_id=partner,
            device_id_type=pl.DeviceIdType.MESH)
        local = pltpu.make_async_copy(keeps[k], mine[k], local_sem.at[k])
        remote.start()
        local.start()
        copies.append((remote, local))
    for k in range(count):
        for copy in copies[k]:
            copy.wait()
        send, stay = outs[2 * k:2 * k + 2]

        @pl.loop(0, send.shape[0])
        def _(i):
            for to, index in ((send, 2 * i + 1 - b), (stay, 2 * i + b)):
                to[i] = (mine[k][index].astype(F32) + come[k][index].astype(F32)).astype(BF16)


def swap_sums(halves, wide):
    count = len(halves)
    blocks = [(keep.shape[0] // wide, keep.shape[1]) for keep, _ in halves]
    anywhere = pl.BlockSpec(memory_space=pl.ANY)
    dma = pltpu.SemaphoreType.DMA
    out = pl.pallas_call(
        functools.partial(swap_sums_kernel, count), in_specs=[anywhere] * 2 * count,
        out_specs=[pl.BlockSpec(memory_space=pltpu.VMEM)] * 2 * count,
        out_shape=[jax.ShapeDtypeStruct((wide // 2,) + block, BF16) for block in blocks for _ in range(2)],
        scratch_shapes=[pltpu.VMEM((wide,) + block, BF16) for _ in range(2) for block in blocks]
        + [dma((count,))] * 3,
        compiler_params=pltpu.CompilerParams(vmem_limit_bytes=60 * 1024 * 1024, collective_id=count,
                                             has_side_effects=True),
        cost_estimate=pl.CostEstimate(flops=0, bytes_accessed=30_000_000, transcendentals=0), name="swap_sums",
    )(*[h[k].reshape((wide,) + block) for k in range(2) for h, block in zip(halves, blocks)])
    return [(out[2 * k], out[2 * k + 1]) for k in range(count)]


FC2, FC1, FC1_MORE, ATTN, ATTN_MORE, SMALL, ROWS = range(7)
ROW_STEP, ROW_WINDOW = 192, 224
CORE, Y, Z0, Z1, FINAL = range(5)


def last_sums_kernel(cuts, counts, *refs):
    pairs, twos, small_refs, db_refs, row_refs = refs[:6], refs[6:12], refs[12:16], refs[16:18], refs[18:20]
    out_fc2, out_fc1, out_attn, small_out, rows_out = refs[20:25]
    scratch = list(refs[25:])
    db, strips, classes, db_sem, row_buf, row_sem, small_low = scratch[-11:-4]
    small_got, send_sem, recv_sem, local_sem = scratch[-4:]
    me = lax.axis_index("narrow")
    at = lax.axis_index("wide")
    core = me % 2
    half = {hop: at // bit % 2 for hop, bit in ((Y, 1), (Z0, 2), (Z1, 4))}
    core_partner = {"narrow": me + 1 - 2 * core}
    across = {"narrow": me + 2 - 4 * (me // 2)}
    corner = {"narrow": 3 - me}
    partners = {CORE: core_partner, FINAL: core_partner}
    for hop, bit in ((Y, 1), (Z0, 2), (Z1, 4)):
        partners[hop] = {"wide": at + bit * (1 - 2 * half[hop])}
    greeted = [core_partner, across, corner] + [partners[hop] for hop in (Y, Z0, Z1)]
    barrier = pltpu.get_barrier_semaphore()
    for partner in greeted:
        pl.semaphore_signal(barrier, inc=1, device_id=partner, device_id_type=pl.DeviceIdType.MESH)
    pl.semaphore_wait(barrier, len(greeted))

    def remote(src, dst, row, hop, device=None):
        return pltpu.make_async_remote_copy(
            src_ref=src, dst_ref=dst, send_sem=send_sem.at[row, hop], recv_sem=recv_sem.at[row, hop],
            device_id=partners[hop] if device is None else device, device_id_type=pl.DeviceIdType.MESH)

    first, second, levels, last = {}, {}, {}, {}
    for p, (k, cut) in enumerate(cuts):
        n = counts[p]
        mine, come = scratch.pop(0), scratch.pop(0)
        first[p] = (pairs[2 * k].at[:, :, cut], mine)
        second[p] = (pairs[2 * k + 1].at[:, :, cut], come)
        levels[p] = [(None, mine, come)]
        while n > 1:
            n //= 2
            levels[p].append((scratch.pop(0), scratch.pop(0), scratch.pop(0)))
        last[p] = (scratch.pop(0), scratch.pop(0))
    pending = {}

    def begin(p):
        pending[p] = [pltpu.make_async_copy(*first[p], local_sem.at[p, 0])]
        if p in (ATTN, ATTN_MORE):
            pending[p].append(remote(*second[p], p, CORE))
        else:
            pending[p].append(pltpu.make_async_copy(*second[p], local_sem.at[p, 1]))
        for c in pending[p]:
            c.start()

    def wait(p):
        for c in pending[p]:
            c.wait()

    def hop(p, n):
        wait(p)
        level = counts[p].bit_length() - n.bit_length()
        _, mine, come = levels[p][level]
        send, stay, next_come = levels[p][level + 1]
        which = {8: Y, 4: Z0, 2: Z1}[n]
        b = half[which]

        def add(to, i, index):
            to[i] = (mine[index].astype(F32) + come[index].astype(F32)).astype(BF16)

        @pl.loop(0, n // 2)
        def _(i):
            add(send, i, 2 * i + 1 - b)

        copy = remote(send, next_come, p, which)
        copy.start()
        pending[p] = [copy]

        @pl.loop(0, n // 2)
        def _(i):
            add(stay, i, 2 * i + b)

    def total(p):
        wait(p)
        _, stay, come = levels[p][-1]
        return stay[0].astype(F32) + come[0].astype(F32)

    outs = {FC2: out_fc2, FC1: out_fc1, FC1_MORE: out_fc1, ATTN: out_attn, ATTN_MORE: out_attn}
    others = {FC2: twos[:2], FC1: twos[2:4], FC1_MORE: twos[2:4], ATTN: twos[4:], ATTN_MORE: twos[4:]}

    def end(p):
        cut = cuts[p][1]
        one = total(p)
        two = sum(ref[0, :, cut].astype(F32) for ref in others[p])
        give, come = last[p]
        give[...] = jnp.where(core == 0, two, one).astype(BF16)
        copy = remote(give, come, p, FINAL)
        copy.start()
        pending[p] = [copy]
        outs[p][core, :, cut] = jnp.where(core == 0, one, two)

    def close(p):
        wait(p)
        outs[p][1 - core, :, cuts[p][1]] = last[p][1][...].astype(F32)

    small = {}

    def small_send(h):
        small_low[...] = small_out[...].astype(BF16)
        small[h] = remote(small_low, small_got.at[h], SMALL, h)
        small[h].start()

    def small_take(h):
        small[h].wait()
        small_out[...] = small_low[...].astype(F32) + small_got[h].astype(F32)

    for p in (ATTN, ATTN_MORE, FC2, FC1, FC1_MORE):
        begin(p)
    db_copies = [pltpu.make_async_copy(ref, db.at[k], db_sem.at[k]) for k, ref in enumerate(db_refs)]
    for c in db_copies:
        c.start()
    row_copies = []
    for k, (device, block) in enumerate(((core_partner, me + 1 - 2 * core), (across, me + 2 - 4 * (me // 2)),
                                         (corner, 3 - me))):
        window = pl.ds(pl.multiple_of(block * ROW_STEP, 16), ROW_WINDOW)
        row_copies.append(remote(row_buf.at[window, :], rows_out.at[k], ROWS, k, device))
    for k in range(2):
        @pl.when(me // 2 == k)
        def _():
            pltpu.make_async_copy(row_refs[k], row_buf, row_sem).start()

    hop(FC2, 2)
    hop(FC1, 4)
    hop(FC1_MORE, 4)
    hop(ATTN, 8)
    hop(ATTN_MORE, 8)
    pltpu.make_async_copy(row_refs[0], row_buf, row_sem).wait()
    for c in row_copies:
        c.start()
    row = 0
    for ref in small_refs:
        small_out[row:row + ref.shape[0], :] = ref[...]
        row += ref.shape[0]
    db_copies[0].wait()
    small_out[row:row + HEAD_ROWS, :] = folded(db.at[0], strips, classes)
    db_copies[1].wait()
    small_out[row + HEAD_ROWS:, :] = folded(db.at[1], strips, classes)
    small_send(CORE)
    end(FC2)
    hop(FC1, 2)
    hop(FC1_MORE, 2)
    small_take(CORE)
    small_send(Y)
    hop(ATTN, 4)
    end(FC1)
    end(FC1_MORE)
    hop(ATTN_MORE, 4)
    hop(ATTN, 2)
    for p in (FC2, FC1, FC1_MORE):
        close(p)
    small_take(Y)
    small_send(Z0)
    hop(ATTN_MORE, 2)
    end(ATTN)
    small_take(Z0)
    small_send(Z1)
    for c in row_copies:
        c.wait()
    end(ATTN_MORE)
    small_take(Z1)
    close(ATTN)
    close(ATTN_MORE)


def last_sums(pairs, two, small, db, rows):
    anywhere = pl.BlockSpec(memory_space=pl.ANY)
    vmem = pl.BlockSpec(memory_space=pltpu.VMEM)
    scratch, cuts, counts = [], [], []
    for k, many in enumerate((1, 2, 2)):
        p = pairs[k][0]
        size = p.shape[2] // many
        for c in range(many):
            n, block = p.shape[0], (p.shape[1], size)
            cuts.append((k, slice(c * size, (c + 1) * size)))
            counts.append(n)
            scratch += [pltpu.VMEM((n,) + block, BF16)] * 2
            while n > 1:
                n //= 2
                scratch += [pltpu.VMEM((n,) + block, BF16)] * 3
            scratch += [pltpu.VMEM(block, BF16)] * 2
    lanes = small[0].shape[1]
    count = sum(v.shape[0] for v in small) + 2 * HEAD_ROWS
    scratch += [pltpu.VMEM((2,) + db[0].shape, F32), pltpu.VMEM((STRIP // 128, PITCH * HEAD_ROWS, 128), F32),
                pltpu.VMEM((HEAD_ROWS, lanes), F32), pltpu.SemaphoreType.DMA((2,)),
                pltpu.VMEM(rows[0].shape, BF16), pltpu.SemaphoreType.DMA, pltpu.VMEM((count, lanes), BF16),
                pltpu.VMEM((4, count, lanes), BF16)]
    scratch += [pltpu.SemaphoreType.DMA((7, 5)), pltpu.SemaphoreType.DMA((7, 5)), pltpu.SemaphoreType.DMA((5, 2))]
    return pl.pallas_call(
        functools.partial(last_sums_kernel, cuts, counts),
        in_specs=[anywhere] * 6 + [vmem] * 10 + [anywhere] * 4,
        out_specs=[vmem] * 5,
        out_shape=[jax.ShapeDtypeStruct((2,) + p.shape[1:], F32) for p, _ in pairs]
        + [jax.ShapeDtypeStruct((count, lanes), F32), jax.ShapeDtypeStruct((3, ROW_WINDOW, lanes), BF16)],
        scratch_shapes=scratch,
        compiler_params=pltpu.CompilerParams(vmem_limit_bytes=60 * 1024 * 1024, collective_id=0, has_side_effects=True),
        cost_estimate=pl.CostEstimate(flops=0, bytes_accessed=300_000_000, transcendentals=0), name="last_sums",
    )(*[v for pair in pairs for v in pair], *two, *small, *db, *rows)


def shards(images, cotangent, image_ids, patch_order, qkv_weight, qv_bias, proj_weight, rel_table, layer_scales,
           layer_norm_gains, norm_biases, fc1_weight, fc1_bias, fc2_weight, out_biases):
    me = lax.axis_index("narrow")
    at_wide = lax.axis_index("wide")
    wide = lax.axis_size("wide")
    core = me % 2
    first = me < 2
    quarter, width = images.shape[1:]
    rows = 4 * quarter
    padded = -(-rows // TILE) * TILE
    entries, heads = rel_table.shape[1:]
    flips = {k: [(d, d ^ k) for d in range(4)] for k in (1, 2, 3)}

    def swap(v, k):
        return lax.ppermute(v, "narrow", flips[k])

    def swap_wide(v, k):
        return lax.ppermute(v, "wide", [(d, d ^ k) for d in range(wide)])

    def pick(v, index):
        return lax.dynamic_index_in_dim(v, index, 0, keepdims=False)

    smalls = jnp.concatenate([layer_norm_gains[0, :1], norm_biases[0, :1], layer_norm_gains[0, 1:], norm_biases[0, 1:],
                              layer_scales[0], out_biases[0], fc1_bias.reshape(-1, width), qv_bias[0],
                              jnp.zeros((2, width), F32)])
    table = jnp.pad(rel_table[0].T, ((0, HEAD_ROWS - heads), (0, width - entries)))
    own_small = jnp.concatenate([smalls, table])
    other_small = swap(own_small, 1)
    own = dict(qkv=qkv_weight[0])
    own["proj"], own["fc1"], own["fc2"] = later([proj_weight[0], fc1_weight[0], fc2_weight[0]], other_small)
    other = {name: swap(own[name], 1) for name in MATRICES}
    bias_at = FC1_BIAS + fc1_bias.shape[1] // width
    both = [jnp.where(core == k, own_small, other_small) for k in range(2)]
    biases = build_bias(jnp.concatenate([v[16:] for v in both]), heads)
    weights = []
    for layer in range(2):
        vectors = both[layer][:16]
        weights.append(dict(
            layer=layer, pick=jnp.stack([(core == layer).astype(jnp.int32), core]), vectors=vectors, bias=biases[layer],
            **{name: (own[name], other[name]) for name in MATRICES}))

    section = dict(
        vectors=jnp.stack([w["vectors"] for w in weights]), bias=[w["bias"] for w in weights],
        own=own, other=other)
    meta = (jnp.stack([core, 1 - first.astype(jnp.int32)]),) + sequence_meta(pick(image_ids, core), pick(patch_order, core), padded)

    mine = jnp.where(first, images, cotangent)
    theirs = jnp.where(first, cotangent, images)
    pieces = [pick(mine, core), swap(pick(mine, 1 - core), 1), swap(pick(theirs, core), 2),
              swap(pick(theirs, 1 - core), 3)]
    rows_in = jnp.zeros((padded, width), BF16)
    for k, piece in enumerate(pieces):
        rows_in = lax.dynamic_update_slice(rows_in, piece, ((me ^ k) * quarter, 0))

    middle, = forward(False, (rows_in, rows_in), section, meta)
    y_out, *parts = forward(True, (rows_in, swap(middle, 2)), section, meta)
    kept = dict(zip(KEPT, parts))

    back = backward(rows_in, section, meta, kept)
    dy_in = jnp.where(first, swap(back, 2), rows_in)

    def reducer(keep, give, at_once=None):
        return Reducer(keep, give, lambda v: swap(v, 1), swap_wide, at_wide, wide, at_once)

    def mlp_part(dy, w, kept_one, after=()):
        dm, da, fc1_give, fc1_keep, fc2_give, fc2_keep, sums = mlp_bwd(True, dy, w, kept_one, after)
        return dm, da, [(fc2_keep, fc2_give), (fc1_keep, fc1_give)], sums

    def tail_part(dm, da, dz, w, kept_one, after=()):
        dx, give, keep, sums = attn_tail(dm, dz, da, w, kept_one, after)
        return dx, keep, give, sums

    def sent(*reducers):
        return [v for r in reducers for v in r.sent]

    def reducers(halves):
        return [reducer(*h, at_once) for h, at_once in zip(halves, swap_sums(halves, wide))]

    dm, da, halves, sums_two = mlp_part(dy_in, weights[1], kept)
    fc_two = [r.launch() for r in reducers(halves)]
    dz, db_two = attn_bwd(da, weights[1], meta, kept, sent(*fc_two))
    mid, *halves, tail_two = tail_part(dm, da, dz, weights[1], kept)
    attn_two = reducers([halves])[0].launch()
    for r in fc_two:
        r.step(mid)
    dm, da, halves, sums_one = mlp_part(mid, weights[0], kept, sent(attn_two, *fc_two))
    fc_one = reducers(halves)
    fc_one[0].launch()
    for r in fc_two + [attn_two]:
        r.step(fc_one[0].sent[0])
    dz, db_one = attn_bwd(da, weights[0], meta, kept, sent(*fc_two, *fc_one, attn_two))
    fc_one[0].step(dz)
    fc_one[1].launch(dz)
    attn_two.step(dz)
    ready = [r.two()[0] for r in fc_one + fc_two + [attn_two]]
    dx, *halves, tail_one = tail_part(dm, da, dz, weights[0], kept, sent(*fc_one, attn_two) + ready)

    if wide == 8:
        pairs = [(ready[0], fc_one[0].parts[-1]), (ready[1], fc_one[1].parts[-1]),
                 [v.reshape(wide, -1, v.shape[1]) for v in halves]]
        two = [v for k, r in enumerate(fc_two + [attn_two]) for v in (ready[2 + k], r.parts[-1])]
        *shares, small, others = last_sums(pairs, two, [sums_two, tail_two, sums_one, tail_one], [db_two, db_one],
                                           [dx, y_out])
        fc2, fc1, attn = [(v[0], v[1]) for v in shares]
        mine = lax.dynamic_slice_in_dim(jnp.where(first, dx, y_out), quarter * me, quarter, 0)
        others = lax.dynamic_slice_in_dim(others, (quarter - ROW_STEP) * me, quarter, 1)
    else:
        result = jnp.where(first, dx, y_out)[:rows].reshape(4, quarter, width)
        mine, others = pick(result, me), [swap(pick(result, me ^ k), k) for k in (1, 2, 3)]
        small = jnp.concatenate([sums_two, tail_two, sums_one, tail_one, table_back(db_two, width),
                                 table_back(db_one, width)])
        small = small + swap(small, 1)
        for k in range(wide.bit_length() - 1):
            small = small + swap_wide(small, 1 << k)
        shares = []
        for one, two in zip(fc_one + [reducer(*halves)], fc_two + [attn_two]):
            one, two = one.finish(), two.finish()
            stay = jnp.where(core == 0, one, two)
            got = swap(jnp.where(core == 0, two, one).astype(BF16), 1).astype(F32)
            shares.append((jnp.where(core == 0, stay, got), jnp.where(core == 0, got, stay)))
        fc2, fc1, attn = shares
    same, across = [mine, others[0]], others[1:]
    same = jnp.where(core == 0, jnp.stack(same), jnp.stack(same[::-1]))
    across = jnp.where(core == 0, jnp.stack(across), jnp.stack(across[::-1]))
    encoded = jnp.where(first, across, same)
    images_grad = jnp.where(first, same, across)
    qkv = jnp.concatenate([v[:, :3 * width // 2] for v in attn], axis=1)
    proj = jnp.concatenate([v[:, 3 * width // 2:] for v in attn], axis=1)
    tables = small[48:].reshape(2, HEAD_ROWS, width)
    totals = jnp.where(core == 0, small[24:48], small[:24])
    table_grad = jnp.where(core == 0, tables[1], tables[0])
    tail = totals[16:]
    return (
        encoded,
        images_grad,
        qkv[None],
        tail[SUM_Q:SUM_V + 1][None],
        proj[None],
        table_grad[:heads, :entries].T[None],
        jnp.stack([totals[SUM_SCALE_A], totals[SUM_SCALE_B]])[None],
        jnp.stack([tail[SUM_GAIN_A], totals[SUM_GAIN_B]])[None],
        jnp.stack([tail[SUM_SHIFT_A], totals[SUM_SHIFT_B]])[None],
        jnp.concatenate(fc1, axis=1)[None],
        totals[FC1_BIAS:bias_at].reshape(1, -1),
        jnp.concatenate(fc2, axis=1)[None],
        jnp.stack([totals[SUM_DA], totals[SUM_DF]])[None],
    )


def solution(mesh):
    by_layer = P("narrow", None, None)
    by_rows = P("wide", "narrow", None)
    by_both = P("narrow", "wide", None)
    in_specs = (by_rows, by_rows, P("wide", None), P("wide", None, None)) + (by_layer,) * 8 + (
        P("narrow", None), by_layer, by_layer)
    out_specs = (by_rows, by_rows, by_both, by_layer, by_both, by_layer, by_layer, by_layer, by_layer, by_both,
                 P("narrow", None), by_both, by_layer)
    return jax.shard_map(shards, mesh=mesh, in_specs=in_specs, out_specs=out_specs, check_vma=False)
```

```python
import functools

import jax
import jax.numpy as jnp
from jax import lax
from jax.experimental import pallas as pl
from jax.experimental.pallas import tpu as pltpu
from jax.sharding import PartitionSpec as P

EPSILON = 1e-06
HALF_ROOT = 0.7071067811865476
DENSITY_NORM = 0.3989422804014327
GRID = 14
SPAN = 2 * GRID - 1
PITCH = 16
SLOTS = GRID * PITCH
LANES = 256
CLASS_SLOT = 15
WIDE = 32
STRIP = 512
HEAD_ROWS = 16
F32 = jnp.float32
BF16 = jnp.bfloat16
NEGATIVE = -1000000000.0
LAG = 6
LAG_BACK = 2
TILE = 800

GAIN_A, SHIFT_A, GAIN_B, SHIFT_B, SCALE_A, SCALE_B, OUT_A, OUT_B, FC1_BIAS = range(9)
QKV_BIAS = 12
SUM_DF, SUM_SCALE_B, SUM_GAIN_B, SUM_SHIFT_B, SUM_DA, SUM_SCALE_A = range(6)
SUM_GAIN_A, SUM_SHIFT_A, SUM_Q, SUM_V = range(4)


def nn(a, b):
    return lax.dot_general(a, b, (((1,), (0,)), ((), ())), preferred_element_type=F32)


def nt(a, b):
    return lax.dot_general(a, b, (((1,), (1,)), ((), ())), preferred_element_type=F32)


def tn(a, b):
    return lax.dot_general(a, b, (((0,), (0,)), ((), ())), preferred_element_type=F32)


def iota(shape, axis):
    return lax.broadcasted_iota(jnp.int32, shape, axis)


def row_tile(t):
    return pl.ds(pl.multiple_of(t * TILE, 16), TILE)


def vec(vec_ref, k):
    return vec_ref[k:k + 1, :]


def row_stats(v):
    centred = v - jnp.mean(v, axis=-1, keepdims=True)
    inverse = lax.rsqrt(jnp.mean(centred * centred, axis=-1, keepdims=True) + EPSILON)
    return centred * inverse, inverse


def norm_tiles(src_ref, dst_ref, vec_ref, gain, shift):
    @pl.loop(0, src_ref.shape[0] // TILE)
    def _(t):
        rows = row_tile(t)
        unit, _ = row_stats(src_ref[rows, :].astype(F32))
        dst_ref[rows, :] = (unit * vec(vec_ref, gain) + vec(vec_ref, shift)).astype(BF16)


def extra_rows(first, lanes):
    row = iota((16, lanes), 0)
    out = jnp.zeros((16, lanes), F32)
    for k, value in enumerate(first):
        out = jnp.where(row == k, value, out)
    return out.astype(BF16)


def split3(v):
    hi = v.astype(BF16).astype(F32)
    mid = (v - hi).astype(BF16).astype(F32)
    return hi, mid, v - hi - mid


class Weights:
    def __init__(self, core, own, other, dst, sems):
        self.core, self.own, self.other, self.dst, self.sems = core, own, other, dst, sems

    def start(self, name, layer, chunk=None):
        src, slot = (lambda ref: ref), None
        if name == "fc1":
            src = lambda ref: ref.at[:, pl.ds(pl.multiple_of(chunk * ref.shape[0], 128), ref.shape[0])]
        if name == "fc2":
            src = lambda ref: ref.at[pl.ds(pl.multiple_of(chunk * ref.shape[1], 128), ref.shape[1]), :]
        dst, sem = self.place(name, chunk)

        @pl.when(self.core == layer)
        def _():
            pltpu.make_async_copy(src(self.own[name]), dst, sem).start()

        @pl.when(self.core != layer)
        def _():
            pltpu.make_async_copy(src(self.other[name]), dst, sem).start()

    def place(self, name, chunk):
        if chunk is None:
            return self.dst[name], self.sems[name]
        return self.dst[name].at[lax.rem(chunk, 2)], self.sems[name].at[lax.rem(chunk, 2)]

    def wait(self, name, chunk=None):
        dst, sem = self.place(name, chunk)
        pltpu.make_async_copy(dst, dst, sem).wait()

    def start_fc(self, layer, chunk):
        self.start("fc1", layer, chunk)
        self.start("fc2", layer, chunk)


MATRICES = ("qkv", "proj", "fc1", "fc2")


def weight_scratch(width):
    dma = pltpu.SemaphoreType.DMA
    return [pltpu.VMEM((width, 3 * width), BF16), pltpu.VMEM((width, width), BF16),
            pltpu.VMEM((2, width, width), BF16), pltpu.VMEM((2, width, width), BF16), dma, dma, dma((2,)), dma((2,))]


def weights_of(core, refs, scratch):
    return Weights(core, dict(zip(MATRICES, refs[:4])), dict(zip(MATRICES, refs[4:8])), dict(zip(MATRICES, scratch[:4])),
                   dict(zip(MATRICES, scratch[4:8])))


def forward_kernel(keep, core_ref, ws_ref, x_first, x_second, vec_refs, *refs):
    b_refs, et_ref, mask_ref, y_ref = refs[8:10], refs[10], refs[11], refs[12]
    if keep:
        xs_ref, n1_ref, o_ref, m_ref, n2_ref, a_ref, f_ref, zt_ref, ot_ref, lse_ref, g_ref, slope_ref = refs[13:25]
        scratch = refs[25:]
    else:
        n1_ref, o_ref, m_ref, n2_ref, zt_ref, ot_ref = refs[13:19]
        scratch = refs[19:]
    w = weights_of(core_ref[0], refs[:8], scratch[:8])
    x, b, bias, n1t, acc, wt, b_sem, x_sem = scratch[8:]
    layer, t = pl.program_id(0), pl.program_id(1)
    imgs = et_ref.shape[0]
    heads = b.shape[0]
    width = x.shape[1]
    hd = width // heads
    chunks = pl.num_programs(1) - imgs
    at = (0,) if keep else ()
    vec_ref = vec_refs.at[layer]

    def start_b(k):
        pltpu.make_async_copy(b_refs[k], b, b_sem).start()

    @pl.when((layer == 0) & (t == 0))
    def _():
        for k, ref in enumerate((x_first, x_second)):
            @pl.when(core_ref[1] == k)
            def _():
                pltpu.make_async_copy(ref, x, x_sem).start()

        w.start("qkv", 0)
        start_b(0)
        w.start("proj", 0)
        w.start_fc(0, 0)
        w.start_fc(0, 1)
        pltpu.make_async_copy(x_first, x, x_sem).wait()

    @pl.when(t == 0)
    def _():
        if keep:
            xs_ref[0] = x[...]
        o_ref[...] = jnp.zeros_like(o_ref)
        columns = vec_ref[8:16, :].T
        bias[0:width, :] = jnp.broadcast_to(columns[:, QKV_BIAS - 8:QKV_BIAS - 7], (width, 128))
        bias[width:2 * width, :] = jnp.zeros((width, 128), F32)
        bias[2 * width:, :] = jnp.broadcast_to(columns[:, QKV_BIAS - 7:QKV_BIAS - 6], (width, 128))
        norm_tiles(x, n1_ref.at[at] if keep else n1_ref, vec_ref, GAIN_A, SHIFT_A)
        w.wait("qkv")
        for c in range(3):
            part = slice(c * width, (c + 1) * width)
            wt[part, :] = w.dst["qkv"][:, part].T

    def full(ref):
        return ref.at[0] if keep else ref

    n1_now, o_now, m_now, n2_now = full(n1_ref), full(o_ref), full(m_ref), full(n2_ref)
    zt, ot = (zt_ref.at[0, 0], ot_ref.at[0, 0]) if keep else (zt_ref, ot_ref)

    @pl.when(t < imgs)
    def _():
        ws = pl.multiple_of(ws_ref[t], 16)
        et = et_ref[t]
        n1t[...] = tn(n1_now[pl.ds(ws, SLOTS), :], et).astype(BF16)

        @pl.loop(0, 3)
        def _(c):
            rows = pl.ds(pl.multiple_of(c * width, width), width)
            factor = jnp.where(c == 0, hd ** -0.5, 1.0)
            column = bias[rows, :]
            add = jnp.concatenate([column] * (LANES // 128), axis=1)
            zt[rows, :] = ((nn(wt[rows, :], n1t[...]) + add) * factor).astype(BF16)

        @pl.when(t == 0)
        def _():
            pltpu.make_async_copy(b, b, b_sem).wait()

        ones_q = extra_rows([1.0], LANES)
        mask_k = extra_rows([mask_ref[t]], SLOTS)
        ones_v = extra_rows([1.0], SLOTS)

        def scores(h):
            r = h * hd
            qt = jnp.concatenate([zt[r:r + hd, :], ones_q], axis=0)
            kt = jnp.concatenate([zt[width + r:width + r + hd, :SLOTS], mask_k], axis=0)
            return tn(kt, qt)

        def soft(h, s):
            s = s + b[h]
            m = jnp.max(s, axis=0, keepdims=True)
            return m, jnp.exp(s - m).astype(BF16)

        def finish(h, m, e):
            r = h * hd
            vt = jnp.concatenate([zt[2 * width + r:2 * width + r + hd, :SLOTS], ones_v], axis=0)
            o = nn(vt, e)
            total = o[hd:hd + 1]
            ot[r:r + hd, :] = (o[:hd] * (1.0 / total)).astype(BF16)
            if keep:
                lse_ref[0, 0, h:h + 1, :] = m + jnp.log(total)

        s, e = {}, {}
        for k in range(heads + 2 * LAG):
            if k < heads:
                s[k] = scores(k)
            if 0 <= k - LAG < heads:
                e[k - LAG] = soft(k - LAG, s.pop(k - LAG))
            if k - 2 * LAG >= 0:
                finish(k - 2 * LAG, *e.pop(k - 2 * LAG))

        win = pl.ds(ws, SLOTS)
        o_now[win, :] = (o_now[win, :].astype(F32) + nt(et, ot[...])).astype(BF16)

    j = t - imgs

    @pl.when((t == imgs) & (layer == 0))
    def _():
        w.start("qkv", 1)
        start_b(1)

    @pl.when(t == imgs)
    def _():
        w.wait("proj")
        a = nn(o_now[...], w.dst["proj"][...]) + vec(vec_ref, OUT_A)
        if keep:
            a_ref[0] = a.astype(BF16)
        m_now[...] = x[...].astype(F32) + vec(vec_ref, SCALE_A) * a
        acc[...] = jnp.zeros_like(acc)
        norm_tiles(m_now, n2_now, vec_ref, GAIN_B, SHIFT_B)

    @pl.when((t == imgs) & (layer == 0))
    def _():
        w.start("proj", 1)

    @pl.when(t >= imgs)
    def _():
        slot = lax.rem(j, 2)
        w.wait("fc1", j)
        w.wait("fc2", j)
        u = nn(n2_now[...], w.dst["fc1"][slot]) + vec_ref[pl.ds(FC1_BIAS + j, 1), :]
        cdf = 0.5 * (1.0 + lax.erf(u * HALF_ROOT))
        g = (u * cdf).astype(BF16)
        if keep:
            g_ref[0] = g
            slope_ref[0] = (cdf + u * (jnp.exp(-0.5 * u * u) * DENSITY_NORM)).astype(BF16)
        acc[...] += nn(g, w.dst["fc2"][slot])

        @pl.when(j + 2 < chunks)
        def _():
            w.start_fc(layer, j + 2)

        @pl.when((j + 2 >= chunks) & (layer == 0))
        def _():
            w.start_fc(1, j + 2 - chunks)

    @pl.when(j == chunks - 1)
    def _():
        @pl.loop(0, acc.shape[0] // TILE)
        def _(k):
            rows = row_tile(k)
            f = acc[rows, :] + vec(vec_ref, OUT_B)
            if keep:
                f_ref[0, rows, :] = f.astype(BF16)
            x[rows, :] = (m_now[rows, :] + vec(vec_ref, SCALE_B) * f).astype(BF16)

        @pl.when(layer == 1)
        def _():
            y_ref[...] = x[...]


def attn_bwd_kernel(pick_ref, ws_ref, da_ref, own_ref, other_ref, b_ref, et_ref, mask_ref, zt_ref, ot_ref, lse_ref,
                    dz_ref, db_ref, dat, dot, dzt):
    width = da_ref.shape[1]
    i = pl.program_id(0)

    @pl.when(i == 0)
    def _():
        dz_ref[...] = jnp.zeros_like(dz_ref)
        db_ref[...] = jnp.zeros_like(db_ref)
        dzt[...] = jnp.zeros_like(dzt)

    win = pl.ds(pl.multiple_of(ws_ref[i], 16), SLOTS)
    et = et_ref[0]
    dat[...] = tn(da_ref[win, :], et).astype(BF16)
    proj = jnp.where(pick_ref[0] == 1, own_ref[...], other_ref[...])
    dot[...] = nn(proj, dat[...]).astype(BF16)
    attn_back_image(et, mask_ref[0], zt_ref, ot_ref, lse_ref, b_ref, dat, dot, dzt, db_ref)
    for c in range(3):
        cols = slice(c * width, (c + 1) * width)
        dz_ref[win, cols] = (dz_ref[win, cols].astype(F32) + nt(et, dzt[cols, :])).astype(BF16)


def attn_back_image(et, mask, zt, ot, lse_ref, b, dat, dot, dzt, db_ref):
    heads = b.shape[0]
    width = dat.shape[0]
    hd = width // heads
    extra_k = extra_rows([mask, 1.0, 1.0, 1.0], SLOTS)
    extra_v = extra_rows([1.0, 1.0, 1.0], SLOTS)

    def parts(h):
        r = h * hd
        return (zt[r:r + hd, :], zt[width + r:width + r + hd, :SLOTS], zt[2 * width + r:2 * width + r + hd, :SLOTS],
                dot[r:r + hd, :])

    def products(h):
        qt, kt, vt, dt = parts(h)
        r = h * hd
        delta = jnp.sum(dt.astype(F32) * ot[r:r + hd, :].astype(F32), axis=0, keepdims=True)
        extra_q = extra_rows([1.0, *split3(-lse_ref[h:h + 1, :])], LANES)
        extra_d = extra_rows(split3(-delta), LANES)
        s = tn(jnp.concatenate([kt, extra_k], axis=0), jnp.concatenate([qt, extra_q], axis=0))
        dp = tn(jnp.concatenate([vt, extra_v], axis=0), jnp.concatenate([dt, extra_d], axis=0))
        return s, dp

    def middle(h, s, dp):
        p = jnp.exp(s + b[h])
        ds = p * dp
        if db_ref is not None:
            db_ref[h] += ds
        return p.astype(BF16), ds.astype(BF16)

    def finish(h, p, ds):
        qt, kt, vt, dt = parts(h)
        r = h * hd
        dzt[2 * width + r:2 * width + r + hd, :SLOTS] = nt(dt, p).astype(BF16)
        dzt[width + r:width + r + hd, :SLOTS] = nt(qt, ds).astype(BF16)
        dzt[r:r + hd, :] = (nn(kt, ds) * hd ** -0.5).astype(BF16)

    s, e = {}, {}
    for t in range(heads + 2 * LAG_BACK):
        if t < heads:
            s[t] = products(t)
        if 0 <= t - LAG_BACK < heads:
            e[t - LAG_BACK] = middle(t - LAG_BACK, *s.pop(t - LAG_BACK))
        if t - 2 * LAG_BACK >= 0:
            finish(t - 2 * LAG_BACK, *e.pop(t - 2 * LAG_BACK))


def backward_kernel(core_ref, ws_ref, dy_ref, vec_refs, *refs):
    b_refs, et_ref, mask_ref = refs[8:10], refs[10], refs[11]
    m_ref, x_ref, slope_ref, zt_ref, ot_ref, lse_ref, dx_ref = refs[12:19]
    scratch = refs[19:]
    w = weights_of(core_ref[0], refs[:8], scratch[:8])
    dy, df, acc, dm, da, dz, dat, dot, dzt, b, b_sem = scratch[8:]
    step, t = pl.program_id(0), pl.program_id(1)
    layer = 1 - step
    imgs = et_ref.shape[0]
    width = dy.shape[1]
    chunks = pl.num_programs(1) - imgs - 1
    vec_ref = vec_refs.at[layer]

    def start_b(k):
        pltpu.make_async_copy(b_refs[k], b, b_sem).start()

    @pl.when((step == 0) & (t == 0))
    def _():
        w.start_fc(1, 0)
        w.start_fc(1, 1)
        w.start("proj", 1)
        start_b(1)
        w.start("qkv", 1)
        dy[...] = dy_ref[...]

    @pl.when((step == 1) & (t == 0))
    def _():
        w.start("qkv", 0)

    @pl.when(t == 0)
    def _():
        acc[...] = jnp.zeros_like(acc)

        @pl.loop(0, df.shape[0] // TILE)
        def _(k):
            rows = row_tile(k)
            df[rows, :] = (dy[rows, :].astype(F32) * vec(vec_ref, SCALE_B)).astype(BF16)

    @pl.when(t < chunks)
    def _():
        slot = lax.rem(t, 2)
        w.wait("fc1", t)
        w.wait("fc2", t)
        du = (nt(df[...], w.dst["fc2"][slot]) * slope_ref[...].astype(F32)).astype(BF16)
        acc[...] += nt(du, w.dst["fc1"][slot])

        @pl.when(t + 2 < chunks)
        def _():
            w.start_fc(layer, t + 2)

        @pl.when((t + 2 >= chunks) & (step == 0))
        def _():
            w.start_fc(0, t + 2 - chunks)

    @pl.when(t == chunks - 1)
    def _():
        def emit(rows, dv):
            value = dy[rows, :].astype(F32) + dv
            dm[rows, :] = value
            da[rows, :] = (value * vec(vec_ref, SCALE_A)).astype(BF16)
            return ()

        norm_back_tiles(0, m_ref, acc, vec_ref, GAIN_B, emit)
        dz[...] = jnp.zeros_like(dz)
        dzt[...] = jnp.zeros_like(dzt)
        w.wait("proj")
        pltpu.make_async_copy(b, b, b_sem).wait()

    @pl.when((t >= chunks) & (t < chunks + imgs))
    def _():
        i = t - chunks
        et = et_ref[i]
        win = pl.ds(pl.multiple_of(ws_ref[i], 16), SLOTS)
        dat[...] = tn(da[win, :], et).astype(BF16)
        dot[...] = nn(w.dst["proj"][...], dat[...]).astype(BF16)
        attn_back_image(et, mask_ref[i], zt_ref, ot_ref, lse_ref, b, dat, dot, dzt, None)
        for c in range(3):
            cols = slice(c * width, (c + 1) * width)
            dz[win, cols] = (dz[win, cols].astype(F32) + nt(et, dzt[cols, :])).astype(BF16)

    @pl.when(t == chunks + imgs)
    def _():
        @pl.when(step == 0)
        def _():
            w.start("proj", 0)
            start_b(0)

        w.wait("qkv")
        acc[...] = nt(dz[:, :width], w.dst["qkv"][:, :width])
        for c in range(1, 3):
            cols = slice(c * width, (c + 1) * width)
            acc[...] += nt(dz[:, cols], w.dst["qkv"][:, cols])

        def emit(rows, dv):
            dy[rows, :] = (dm[rows, :] + dv).astype(BF16)
            return ()

        norm_back_tiles(0, x_ref, acc, vec_ref, GAIN_A, emit)

        @pl.when(step == 1)
        def _():
            dx_ref[...] = dy[...]


def spread(count):
    entry = iota((count, SPAN * WIDE), 0)
    lane = iota((count, SPAN * WIDE), 1)
    return jnp.where((entry == lane // WIDE * SPAN + lane % WIDE) & (lane % WIDE < SPAN), 1.0, 0.0).astype(BF16)


def squeeze():
    lane = iota((SPAN * WIDE, STRIP), 0)
    to = iota((SPAN * WIDE, STRIP), 1)
    return jnp.where(lane == to // PITCH * WIDE + to % PITCH, 1.0, 0.0).astype(BF16)


def placed(product, v, onehot):
    hi = v.astype(BF16)
    return product(hi, onehot) + product((v - hi.astype(F32)).astype(BF16), onehot)


def strip_rows(layer, head):
    return pl.ds(layer * HEAD_ROWS + head, PITCH, stride=2 * HEAD_ROWS)


def bias_kernel(table_ref, *refs):
    b_refs, (shifted, strips) = refs[:2], refs[2:]
    rows = table_ref.shape[0]
    heads = b_refs[0].shape[0]
    wide = placed(nn, table_ref[...], spread(table_ref.shape[1]))
    for c in range(PITCH):
        shifted[c * rows:(c + 1) * rows, :] = pltpu.roll(wide, (c - GRID + 1) % (SPAN * WIDE), 1)
    packed = placed(nn, shifted[...], squeeze())
    for k in range(strips.shape[0]):
        strips[k] = packed[:, k * 128:(k + 1) * 128]
    row = iota((SLOTS, LANES), 0)
    col = iota((SLOTS, LANES), 1)
    for layer, b_ref in enumerate(b_refs):
        for h in range(heads):
            strip = jnp.concatenate([strips[k, strip_rows(layer, h), :] for k in range(strips.shape[0])], axis=1)
            for r in range(GRID):
                at = PITCH * (GRID - 1 - r)
                b_ref[h, r * PITCH:(r + 1) * PITCH, :] = strip[:, at:at + LANES]
            mine = layer * HEAD_ROWS + h
            query, key, both = [table_ref[mine:mine + 1, SPAN * SPAN + k:SPAN * SPAN + k + 1] for k in range(3)]
            full = jnp.where(col == CLASS_SLOT, query, b_ref[h])
            b_ref[h] = jnp.where(row == CLASS_SLOT, jnp.where(col == CLASS_SLOT, both, key), full)


def bias_back_kernel(db_ref, table_ref, strips, classes):
    table_ref[...] = folded(db_ref, strips, classes)


def folded(db_ref, strips, classes):
    heads = db_ref.shape[0]
    row = iota((SLOTS, LANES), 0)
    col = iota((SLOTS, LANES), 1)
    is_row = row == CLASS_SLOT
    is_col = col == CLASS_SLOT
    entry = iota((1, classes.shape[1]), 1) - SPAN * SPAN
    strips[...] = jnp.zeros_like(strips)
    classes[...] = jnp.zeros_like(classes)
    for h in range(heads):
        full = db_ref[h]
        query = jnp.sum(jnp.where(is_col & ~is_row, full, 0.0), keepdims=True)
        key = jnp.sum(jnp.where(is_row & ~is_col, full, 0.0), keepdims=True)
        both = jnp.sum(jnp.where(is_row & is_col, full, 0.0), keepdims=True)
        classes[h:h + 1, :] = jnp.where(
            entry == 0, query, jnp.where(entry == 1, key, jnp.where(entry == 2, both, 0.0)))
        plain = jnp.where(is_row | is_col, 0.0, full)
        total = jnp.zeros((PITCH, STRIP), F32)
        for r in range(GRID):
            part = jnp.concatenate([plain[r * PITCH:(r + 1) * PITCH, :], jnp.zeros((PITCH, STRIP - LANES), F32)],
                                   axis=1)
            total = total + pltpu.roll(part, PITCH * (GRID - 1 - r), 1)
        for k in range(strips.shape[0]):
            strips[k, pl.ds(h, PITCH, stride=HEAD_ROWS), :] = total[:, k * 128:(k + 1) * 128]
    rows = classes.shape[0]
    wide = placed(nt, jnp.concatenate([strips[k] for k in range(strips.shape[0])], axis=1), squeeze())
    gathered = jnp.zeros((rows, SPAN * WIDE), F32)
    for c in range(GRID):
        gathered = gathered + pltpu.roll(wide[c * rows:(c + 1) * rows, :], (GRID - 1 - c) % (SPAN * WIDE), 1)
    return placed(nt, gathered, spread(classes.shape[1])) + classes[...]


def norm_back_tiles(count, src_ref, grad_ref, vec_ref, gain, emit):
    def body(t, sums):
        rows = row_tile(t)
        unit, inverse = row_stats(src_ref[rows, :].astype(F32))
        grad = grad_ref[rows, :]
        scaled = grad * vec(vec_ref, gain)
        mean_one = jnp.mean(scaled, axis=-1, keepdims=True)
        mean_two = jnp.mean(scaled * unit, axis=-1, keepdims=True)
        more = emit(rows, inverse * (scaled - mean_one - unit * mean_two))
        if not count:
            return sums
        return tuple(s + jnp.sum(v, axis=0, keepdims=True) for s, v in zip(sums, (grad * unit, grad) + more))

    zero = jnp.zeros((1, grad_ref.shape[1]), F32)
    return lax.fori_loop(0, grad_ref.shape[0] // TILE, body, (zero,) * count)


def mlp_bwd_kernel(want, pick_ref, dy_ref, m_ref, vec_ref, slope_ref, fc1_own, fc1_other, fc2_own, fc2_other, *rest):
    if want:
        (n2_ref, g_ref, a_ref, f_ref, dm_ref, da_ref, fc1_give, fc1_keep, fc2_give, fc2_keep, sums_ref, df, acc) = rest
    else:
        dm_ref, da_ref, df, acc = rest
    j = pl.program_id(0)
    steps = pl.num_programs(0)
    mine = pick_ref[0] == 1
    core = pick_ref[1]
    width = dy_ref.shape[1]

    @pl.when(j == 0)
    def _():
        acc[...] = jnp.zeros_like(acc)
        if want:
            sums_ref[...] = jnp.zeros_like(sums_ref)
        zero = jnp.zeros((1, width), F32)

        def body(t, sums):
            rows = row_tile(t)
            dy = dy_ref[rows, :].astype(F32)
            scaled = (dy * vec(vec_ref, SCALE_B)).astype(BF16)
            df[rows, :] = scaled
            if not want:
                return sums
            return (sums[0] + jnp.sum(scaled.astype(F32), axis=0, keepdims=True),
                    sums[1] + jnp.sum(dy * f_ref[rows, :].astype(F32), axis=0, keepdims=True))

        sums = lax.fori_loop(0, df.shape[0] // TILE, body, (zero, zero) if want else ())
        if want:
            sums_ref[SUM_DF:SUM_DF + 1, :] = sums[0]
            sums_ref[SUM_SCALE_B:SUM_SCALE_B + 1, :] = sums[1]

    fc1 = jnp.where(mine, fc1_own[...], fc1_other[...])
    fc2 = jnp.where(mine, fc2_own[...], fc2_other[...])
    du = (nt(df[...], fc2) * slope_ref[...].astype(F32)).astype(BF16)
    acc[...] += nt(du, fc1)
    if want:
        at = lax.rem(j + (1 - core) * (steps // 2), steps)
        sums_ref[pl.ds(FC1_BIAS + at, 1), :] = jnp.sum(du.astype(F32), axis=0, keepdims=True)
        grad = tn(g_ref[...], df[...]).astype(BF16)
        low, high = grad[:, :width // 2], grad[:, width // 2:]
        fc2_keep[...] = jnp.where(core == 0, low, high)
        fc2_give[...] = jnp.where(core == 0, high, low)
        grad1 = tn(n2_ref[...], du).astype(BF16)

        @pl.when(j < steps // 2)
        def _():
            fc1_give[...] = grad1

        @pl.when(j >= steps // 2)
        def _():
            fc1_keep[...] = grad1

    @pl.when(j == steps - 1)
    def _():
        def emit(rows, dv):
            dm = dy_ref[rows, :].astype(F32) + dv
            da = (dm * vec(vec_ref, SCALE_A)).astype(BF16)
            dm_ref[rows, :] = dm
            da_ref[rows, :] = da
            return (da.astype(F32), dm * a_ref[rows, :].astype(F32)) if want else ()

        sums = norm_back_tiles(4 if want else 0, m_ref, acc, vec_ref, GAIN_B, emit)
        for k, s in zip((SUM_GAIN_B, SUM_SHIFT_B, SUM_DA, SUM_SCALE_A), sums):
            sums_ref[k:k + 1, :] = s


def attn_tail_kernel(pick_ref, vec_ref, dz_ref, own_ref, other_ref, dm_ref, da_ref, x_refs, n1_refs, o_refs, dx_ref,
                     sums_ref, give_ref, keep_ref, o, da, n1, dz, wt, dm, x, give, keep, acc, sems, layer):
    core = pick_ref[1]
    width = x.shape[1]
    part = 3 * width // 2
    arrays = dict(o=(o_refs.at[layer], o), da=(da_ref, da), n1=(n1_refs.at[layer], n1), dm=(dm_ref, dm),
                  x=(x_refs.at[layer], x))
    place = {name: k for k, name in enumerate(arrays)}

    def load(name):
        src, dst = arrays[name]
        return pltpu.make_async_copy(src, dst, sems.at[place[name]])

    def columns(ref, k):
        half = core if k else 1 - core
        return ref.at[:, pl.ds(pl.multiple_of(half * part, 128), part)]

    def load_dz(k):
        return pltpu.make_async_copy(columns(dz_ref, k), dz.at[k], sems.at[5 + k])

    def load_wt(k):
        @pl.when(pick_ref[0] == 1)
        def _():
            pltpu.make_async_copy(columns(own_ref, k), wt.at[k], sems.at[7 + k]).start()

        @pl.when(pick_ref[0] == 0)
        def _():
            pltpu.make_async_copy(columns(other_ref, k), wt.at[k], sems.at[7 + k]).start()

    load("o").start()
    load("da").start()
    load("n1").start()
    load_dz(0).start()
    load_wt(0)
    load_dz(1).start()
    load_wt(1)
    load("dm").start()
    load("x").start()
    sums_ref[...] = jnp.zeros_like(sums_ref)
    load("o").wait()
    load("da").wait()
    grad = tn(o[...], da[...]).astype(BF16)
    low, high = grad[:, :width // 2], grad[:, width // 2:]
    give[:, part:] = jnp.where(core == 0, high, low)
    keep[:, part:] = jnp.where(core == 0, low, high)
    load("n1").wait()
    stores = []
    for k, (to, out) in enumerate(((give, give_ref), (keep, keep_ref))):
        load_dz(k).wait()
        half = core if k else 1 - core
        to[:, :part] = tn(n1[...], dz[k]).astype(BF16)
        stores.append(pltpu.make_async_copy(to, out, sems.at[9 + k]))
        stores[-1].start()
        totals = jnp.sum(dz[k].astype(F32), axis=0, keepdims=True)

        @pl.when(half == 0)
        def _():
            sums_ref[SUM_Q:SUM_Q + 1, :] = totals[:, :width]

        @pl.when(half == 1)
        def _():
            sums_ref[SUM_V:SUM_V + 1, :] = totals[:, width // 2:]

        pltpu.make_async_copy(wt.at[k], wt.at[k], sems.at[7 + k]).wait()
        if k == 0:
            acc[...] = nt(dz[k], wt[k])
        else:
            acc[...] += nt(dz[k], wt[k])
    load("dm").wait()
    load("x").wait()

    def emit(rows, dv):
        dx_ref[rows, :] = (dm[rows, :] + dv).astype(BF16)
        return ()

    sums = norm_back_tiles(2, x, acc, vec_ref, GAIN_A, emit)
    for k, v in zip((SUM_GAIN_A, SUM_SHIFT_A), sums):
        sums_ref[k:k + 1, :] = v
    for c in stores:
        c.wait()


TAKES = dict(backward=85, forward=75, forward_keep=85, mlp_bwd=15, mlp_bwd_all=27, attn_bwd=20, attn_bwd_all=21, attn_tail=9,
             attn_tail_all=16, bias_build=6, bias_back=9)


VMEM = dict(backward=60, forward=60, forward_keep=60, mlp_bwd=60, mlp_bwd_all=60, attn_bwd=60, attn_bwd_all=60, attn_tail=60,
            attn_tail_all=60, bias_build=60, bias_back=60)


def cost(name):
    return pl.CostEstimate(flops=TAKES[name] * 800_000_000, bytes_accessed=TAKES[name] * 3_000_000, transcendentals=0)


def params(name):
    return pltpu.CompilerParams(vmem_limit_bytes=VMEM[name] * 1024 * 1024)


def shaped(*arrays):
    return [jax.ShapeDtypeStruct(s, d) for s, d in arrays]


def whole(shape):
    return pl.BlockSpec(shape, lambda *_: (0,) * len(shape))


def once(shape):
    return pl.BlockSpec(shape, lambda *_: (0,) * len(shape), pipeline_mode=pl.Buffered(1))


def per_image(shape):
    return pl.BlockSpec((1,) + shape, lambda i, *_: (i,) + (0,) * len(shape))


def call(kernel, name, prefetched, grid, inputs, outputs, scratch, after=()):
    count = len(prefetched) + len(inputs)

    def body(*refs):
        kernel(*refs[:count], *refs[count + len(after):])

    inputs = inputs + [(a, pl.BlockSpec(memory_space=pl.ANY)) for a in after]
    return pl.pallas_call(
        body,
        grid_spec=pltpu.PrefetchScalarGridSpec(
            num_scalar_prefetch=len(prefetched), grid=grid, in_specs=[s for _, s in inputs],
            out_specs=[s for _, _, s in outputs], scratch_shapes=scratch),
        out_shape=[jax.ShapeDtypeStruct(s, d) for s, d, _ in outputs],
        compiler_params=params(name), name=name, cost_estimate=cost(name),
    )(*prefetched, *[a for a, _ in inputs])


def forward(keep, x_pair, section, meta):
    core, ws, et, mask = meta
    rows, width = x_pair[0].shape
    biases = section["bias"]
    heads = biases[0].shape[0]
    hidden = section["own"]["fc1"].shape[1]
    imgs = et.shape[0]
    chunks = hidden // width
    anywhere = pl.BlockSpec(memory_space=pl.ANY)
    vectors = section["vectors"]
    inputs = [(x, anywhere) for x in x_pair] + [(vectors, once(vectors.shape))]
    inputs += [(section[side][name], anywhere) for side in ("own", "other") for name in MATRICES]
    inputs += [(v, anywhere) for v in biases] + [(et, once(et.shape)), (mask, once(mask.shape))]
    outputs = [((rows, width), BF16, whole((rows, width)))]
    low = [pltpu.VMEM((rows, width), BF16)]
    scratch = weight_scratch(width) + low + [
        pltpu.VMEM(biases[0].shape, F32), pltpu.VMEM((3 * width, 128), F32), pltpu.VMEM((width, LANES), BF16),
        pltpu.VMEM((rows, width), F32), pltpu.VMEM((3 * width, width), BF16), pltpu.SemaphoreType.DMA, pltpu.SemaphoreType.DMA]
    if keep:
        def of_layer(kind):
            return (2, rows, width), kind, pl.BlockSpec((1, rows, width), lambda l, t, *_: (l, 0, 0))

        def of_image(*shape, kind=BF16):
            return ((2, imgs) + shape, kind,
                    pl.BlockSpec((1, 1) + shape, lambda l, t, *_: (l, jnp.minimum(t, imgs - 1), 0, 0)))

        of_chunk = ((2, rows, hidden), BF16,
                    pl.BlockSpec((1, rows, width), lambda l, t, *_: (l, 0, jnp.maximum(t - imgs, 0))))
        outputs += [of_layer(BF16), of_layer(BF16), of_layer(BF16), of_layer(F32), of_layer(BF16), of_layer(BF16),
                    of_layer(BF16), of_image(3 * width, LANES), of_image(width, LANES),
                    of_image(heads, LANES, kind=F32), of_chunk, of_chunk]
    else:
        scratch = low * 2 + [pltpu.VMEM((rows, width), F32)] + low + [
            pltpu.VMEM((3 * width, LANES), BF16), pltpu.VMEM((width, LANES), BF16)] + scratch
    return call(functools.partial(forward_kernel, keep), "forward_keep" if keep else "forward", [core, ws],
                (2, imgs + chunks), inputs, outputs, scratch)


def backward(dy, section, meta, kept):
    core, ws, et, mask = meta
    rows, width = dy.shape
    biases = section["bias"]
    imgs = et.shape[0]
    chunks = section["own"]["fc1"].shape[1] // width
    anywhere = pl.BlockSpec(memory_space=pl.ANY)
    vectors = section["vectors"]
    inputs = [(dy, once(dy.shape)), (vectors, once(vectors.shape))]
    inputs += [(section[side][name], anywhere) for side in ("own", "other") for name in MATRICES]
    inputs += [(v, anywhere) for v in biases] + [(et, once(et.shape)), (mask, once(mask.shape))]
    of_layer = pl.BlockSpec((None, rows, width), lambda l, t, *_: (1 - l, 0, 0))
    inputs += [(kept["m"], of_layer), (kept["x"], of_layer)]
    inputs += [(kept["slope"], pl.BlockSpec((None, rows, width),
                                            lambda l, t, *_: (1 - l, 0, jnp.minimum(t, chunks - 1))))]
    for name in ("zt", "ot", "lse"):
        v = kept[name]
        inputs += [(v, pl.BlockSpec((None, None) + v.shape[2:],
                                    lambda l, t, *_: (1 - l, jnp.clip(t - chunks, 0, imgs - 1), 0, 0)))]
    low, high = pltpu.VMEM((rows, width), BF16), pltpu.VMEM((rows, width), F32)
    slots = pltpu.VMEM((width, LANES), BF16)
    scratch = weight_scratch(width) + [
        low, low, high, high, low, pltpu.VMEM((rows, 3 * width), BF16), slots, slots,
        pltpu.VMEM((3 * width, LANES), BF16), pltpu.VMEM(biases[0].shape, F32), pltpu.SemaphoreType.DMA]
    return call(backward_kernel, "backward", [core, ws], (2, chunks + imgs + 1), inputs,
                [((rows, width), BF16, whole((rows, width)))], scratch)[0]


def attn_bwd(da, w, meta, kept, after=()):
    _, ws, et, mask = meta
    rows, width = da.shape
    bias = w["bias"]
    imgs = et.shape[0]
    single_proj = once((width, width))
    layer = w["layer"]

    def kept_image(name):
        v = kept[name]
        return v, pl.BlockSpec((None, None) + v.shape[2:], lambda i, *_: (layer, i, 0, 0))

    inputs = [(da, once(da.shape)), (w["proj"][0], single_proj), (w["proj"][1], single_proj), (bias, once(bias.shape)),
              (et, per_image(et.shape[1:])), (mask, per_image(mask.shape[1:])), kept_image("zt"),
              kept_image("ot"), kept_image("lse")]
    outputs = [((rows, 3 * width), BF16, whole((rows, 3 * width)))]
    outputs += [(bias.shape, F32, whole(bias.shape))]
    scratch = [pltpu.VMEM((width, LANES), BF16), pltpu.VMEM((width, LANES), BF16), pltpu.VMEM((3 * width, LANES), BF16)]
    return call(attn_bwd_kernel, "attn_bwd_all", [w["pick"], ws],
                (imgs,), inputs, outputs, scratch, after)


def build_bias(tables, heads):
    shape = (heads, SLOTS, LANES)
    rows = tables.shape[0]
    return call(bias_kernel, "bias_build", [], (1,), [(tables, once(tables.shape))], [(shape, F32, whole(shape))] * 2,
                [pltpu.VMEM((PITCH * rows, SPAN * WIDE), F32), pltpu.VMEM((STRIP // 128, PITCH * rows, 128), F32)])


def table_back(db, lanes, after=()):
    return call(bias_back_kernel, "bias_back", [], (1,), [(db, once(db.shape))],
                [((HEAD_ROWS, lanes), F32, whole((HEAD_ROWS, lanes)))],
                [pltpu.VMEM((STRIP // 128, PITCH * HEAD_ROWS, 128), F32), pltpu.VMEM((HEAD_ROWS, lanes), F32)],
                after)[0]


def chosen(which, block, to_index):
    def index(j, pick):
        used = pick[0] if which == 0 else 1 - pick[0]
        return tuple(k * used for k in to_index(j, pick))
    return pl.BlockSpec(block, index)


def both(pair, block, to_index):
    return [(pair[k], chosen(k, block, to_index)) for k in range(2)]


def kept_whole(kept, name, w):
    v, layer = kept[name], w["layer"]
    return v, pl.BlockSpec((None,) + v.shape[1:], lambda *_: (layer, 0, 0), pipeline_mode=pl.Buffered(1))


def mlp_bwd(want, dy, w, kept, after=()):
    rows, width = dy.shape
    hidden = w["fc1"][0].shape[1]
    steps = hidden // width
    full = whole((rows, width))
    single = once((rows, width))

    def at(j, pick):
        return lax.rem(j + (1 - pick[1]) * (steps // 2), steps)

    layer = w["layer"]
    part = pl.BlockSpec((None, rows, width), lambda j, p: (layer, 0, at(j, p)))
    inputs = [(dy, single), kept_whole(kept, "m", w), (w["vectors"], once(w["vectors"].shape)), (kept["slope"], part),
              *both(w["fc1"], (width, width), lambda j, p: (0, at(j, p))),
              *both(w["fc2"], (width, width), lambda j, p: (at(j, p), 0))]
    outputs = [((rows, width), F32, full), ((rows, width), BF16, full)]
    if want:
        inputs += [kept_whole(kept, "n2", w), (kept["g"], part), kept_whole(kept, "a", w), kept_whole(kept, "f", w)]
        half = pl.BlockSpec((width, width // 2), lambda j, p: (at(j, p), 0))
        give = pl.BlockSpec((width, width), lambda j, p: (0, jnp.minimum(j, steps // 2 - 1)))
        stay = pl.BlockSpec((width, width), lambda j, p: (0, jnp.maximum(j - steps // 2, 0)))
        outputs += [((width, hidden // 2), BF16, give), ((width, hidden // 2), BF16, stay),
                    ((hidden, width // 2), BF16, half), ((hidden, width // 2), BF16, half),
                    ((16, width), F32, whole((16, width)))]
    scratch = [pltpu.VMEM((rows, width), BF16), pltpu.VMEM((rows, width), F32)]
    return call(functools.partial(mlp_bwd_kernel, want), "mlp_bwd_all" if want else "mlp_bwd", [w["pick"]],
                (steps,), inputs, outputs, scratch, after)


def attn_tail(dm, dz, da, w, kept, after=()):
    rows, width = dm.shape
    part = 3 * width // 2
    layer = w["layer"]
    anywhere = pl.BlockSpec(memory_space=pl.ANY)
    inputs = [(w["vectors"], once(w["vectors"].shape))]
    inputs += [(v, anywhere) for v in (dz, *w["qkv"], dm, da, kept["x"], kept["n1"], kept["o"])]
    outputs = [((rows, width), BF16, whole((rows, width))), ((8, width), F32, whole((8, width)))]
    outputs += [((width, 2 * width), BF16, anywhere)] * 2
    low, high = pltpu.VMEM((rows, width), BF16), pltpu.VMEM((rows, width), F32)
    scratch = [low, low, low, pltpu.VMEM((2, rows, part), BF16), pltpu.VMEM((2, width, part), BF16), high, low,
               pltpu.VMEM((width, 2 * width), BF16), pltpu.VMEM((width, 2 * width), BF16), high,
               pltpu.SemaphoreType.DMA((11,))]
    dx, sums, give, keep = call(functools.partial(attn_tail_kernel, layer=layer), "attn_tail_all", [w["pick"]], (1,),
                                inputs, outputs, scratch, after)
    return dx, give, keep, sums


def sequence_meta(ids, order, rows):
    imgs, patches = order.shape
    image = jnp.arange(imgs, dtype=jnp.int32)
    start = jnp.sum((ids[None, :] < image[:, None]).astype(jnp.int32), axis=1)
    count = jnp.sum((ids[None, :] == image[:, None]).astype(jnp.int32), axis=1)
    ws = jnp.minimum(start // 16 * 16, rows - SLOTS)
    slot = jnp.arange(LANES, dtype=jnp.int32)
    is_class = slot == CLASS_SLOT
    is_patch = (slot % PITCH < GRID) & (slot < SLOTS)
    patch = jnp.where(is_patch, slot // PITCH * GRID + slot % PITCH, -1)
    place = jnp.arange(1, patches + 1, dtype=jnp.int32)
    offset = jnp.sum(jnp.where(order[:, None, :] == patch[None, :, None], place, 0), axis=2)
    valid = (is_class | is_patch)[None, :] & (offset < count[:, None])
    local = jnp.where(valid, offset + (start - ws)[:, None], -1)
    row = jnp.arange(SLOTS, dtype=jnp.int32)
    et = (local[:, None, :] == row[None, :, None]).astype(BF16)
    mask = jnp.where(valid, 0.0, NEGATIVE).astype(F32)[:, None, :SLOTS]
    return ws, et, mask


KEPT = ("x", "n1", "o", "m", "n2", "a", "f", "zt", "ot", "lse", "g", "slope")


def later(arrays, token):
    if token is None:
        return list(arrays)
    return list(lax.optimization_barrier((*arrays, token)))[:-1]


class Reducer:
    def __init__(self, keep, give, swap_core, swap_wide, at_wide, wide, at_once=None):
        self.swap_wide, self.at_wide = swap_wide, at_wide
        if at_once is not None:
            send, stay = at_once
            self.sent, self.parts = [send], [stay]
            self.left, self.bit = wide // 2, 2
            return
        shape = (wide, keep.shape[0] // wide, keep.shape[1])
        self.parts = [v.reshape(shape) for v in (keep, swap_core(give))]
        self.left, self.bit = wide, 1
        self.sent = []

    def launch(self, token=None):
        self.parts.append(self.swap_wide(later(self.sent, token)[0], 1))
        return self

    def hold(self, token):
        self.parts[-1], = later([self.parts[-1]], token)

    def added(self, parts):
        return sum(v.astype(F32) for v in parts)

    def step(self, token=None):
        if self.left == 1:
            return
        self.hold(token)
        mine = self.at_wide // self.bit % 2
        pairs = [v.reshape((self.left // 2, 2) + v.shape[1:]) for v in self.parts]
        self.sent = [self.added(lax.dynamic_index_in_dim(v, 1 - mine, 1, keepdims=False) for v in pairs).astype(BF16)]
        self.parts = [lax.dynamic_index_in_dim(v, mine, 1, keepdims=False) for v in pairs]
        self.parts.append(self.swap_wide(self.sent[0], self.bit))
        self.left, self.bit = self.left // 2, 2 * self.bit

    def two(self):
        return [self.added(self.parts[:-1]).astype(BF16), self.parts[-1]]

    def finish(self, token=None):
        while self.left > 1:
            self.step(token)
        self.hold(token)
        return self.added(self.parts)[0]


def swap_sums_kernel(count, *refs):
    keeps, gives, outs = refs[:count], refs[count:2 * count], refs[2 * count:4 * count]
    mine, come = refs[4 * count:5 * count], refs[5 * count:6 * count]
    local_sem, send_sem, recv_sem = refs[6 * count:]
    me = lax.axis_index("narrow")
    b = lax.axis_index("wide") % 2
    partner = {"narrow": me + 1 - 2 * (me % 2)}
    barrier = pltpu.get_barrier_semaphore()
    pl.semaphore_signal(barrier, inc=1, device_id=partner, device_id_type=pl.DeviceIdType.MESH)
    pl.semaphore_wait(barrier, 1)
    copies = []
    for k in range(count):
        remote = pltpu.make_async_remote_copy(
            src_ref=gives[k], dst_ref=come[k], send_sem=send_sem.at[k], recv_sem=recv_sem.at[k], device_id=partner,
            device_id_type=pl.DeviceIdType.MESH)
        local = pltpu.make_async_copy(keeps[k], mine[k], local_sem.at[k])
        remote.start()
        local.start()
        copies.append((remote, local))
    for k in range(count):
        for copy in copies[k]:
            copy.wait()
        send, stay = outs[2 * k:2 * k + 2]

        @pl.loop(0, send.shape[0])
        def _(i):
            for to, index in ((send, 2 * i + 1 - b), (stay, 2 * i + b)):
                to[i] = (mine[k][index].astype(F32) + come[k][index].astype(F32)).astype(BF16)


def swap_sums(halves, wide):
    count = len(halves)
    blocks = [(keep.shape[0] // wide, keep.shape[1]) for keep, _ in halves]
    anywhere = pl.BlockSpec(memory_space=pl.ANY)
    dma = pltpu.SemaphoreType.DMA
    out = pl.pallas_call(
        functools.partial(swap_sums_kernel, count), in_specs=[anywhere] * 2 * count,
        out_specs=[pl.BlockSpec(memory_space=pltpu.VMEM)] * 2 * count,
        out_shape=[jax.ShapeDtypeStruct((wide // 2,) + block, BF16) for block in blocks for _ in range(2)],
        scratch_shapes=[pltpu.VMEM((wide,) + block, BF16) for _ in range(2) for block in blocks]
        + [dma((count,))] * 3,
        compiler_params=pltpu.CompilerParams(vmem_limit_bytes=60 * 1024 * 1024, collective_id=count,
                                             has_side_effects=True),
        cost_estimate=pl.CostEstimate(flops=0, bytes_accessed=30_000_000, transcendentals=0), name="swap_sums",
    )(*[h[k].reshape((wide,) + block) for k in range(2) for h, block in zip(halves, blocks)])
    return [(out[2 * k], out[2 * k + 1]) for k in range(count)]


FC2, FC1, FC1_MORE, ATTN, ATTN_MORE, SMALL, ROWS = range(7)
ROW_STEP, ROW_WINDOW = 192, 224
CORE, Y, Z0, Z1, FINAL = range(5)


def last_sums_kernel(cuts, counts, *refs):
    pairs, twos, small_refs, db_refs, row_refs = refs[:6], refs[6:12], refs[12:16], refs[16:18], refs[18:20]
    out_fc2, out_fc1, out_attn, small_out, rows_out = refs[20:25]
    scratch = list(refs[25:])
    db, strips, classes, db_sem, row_buf, row_sem, small_low = scratch[-11:-4]
    small_got, send_sem, recv_sem, local_sem = scratch[-4:]
    me = lax.axis_index("narrow")
    at = lax.axis_index("wide")
    core = me % 2
    half = {hop: at // bit % 2 for hop, bit in ((Y, 1), (Z0, 2), (Z1, 4))}
    core_partner = {"narrow": me + 1 - 2 * core}
    across = {"narrow": me + 2 - 4 * (me // 2)}
    corner = {"narrow": 3 - me}
    partners = {CORE: core_partner, FINAL: core_partner}
    for hop, bit in ((Y, 1), (Z0, 2), (Z1, 4)):
        partners[hop] = {"wide": at + bit * (1 - 2 * half[hop])}
    greeted = [core_partner, across, corner] + [partners[hop] for hop in (Y, Z0, Z1)]
    barrier = pltpu.get_barrier_semaphore()
    for partner in greeted:
        pl.semaphore_signal(barrier, inc=1, device_id=partner, device_id_type=pl.DeviceIdType.MESH)
    pl.semaphore_wait(barrier, len(greeted))

    def remote(src, dst, row, hop, device=None):
        return pltpu.make_async_remote_copy(
            src_ref=src, dst_ref=dst, send_sem=send_sem.at[row, hop], recv_sem=recv_sem.at[row, hop],
            device_id=partners[hop] if device is None else device, device_id_type=pl.DeviceIdType.MESH)

    first, second, levels, last = {}, {}, {}, {}
    for p, (k, cut) in enumerate(cuts):
        n = counts[p]
        mine, come = scratch.pop(0), scratch.pop(0)
        first[p] = (pairs[2 * k].at[:, :, cut], mine)
        second[p] = (pairs[2 * k + 1].at[:, :, cut], come)
        levels[p] = [(None, mine, come)]
        while n > 1:
            n //= 2
            levels[p].append((scratch.pop(0), scratch.pop(0), scratch.pop(0)))
        last[p] = (scratch.pop(0), scratch.pop(0))
    pending = {}

    def begin(p):
        pending[p] = [pltpu.make_async_copy(*first[p], local_sem.at[p, 0])]
        if p in (ATTN, ATTN_MORE):
            pending[p].append(remote(*second[p], p, CORE))
        else:
            pending[p].append(pltpu.make_async_copy(*second[p], local_sem.at[p, 1]))
        for c in pending[p]:
            c.start()

    def wait(p):
        for c in pending[p]:
            c.wait()

    def hop(p, n):
        wait(p)
        level = counts[p].bit_length() - n.bit_length()
        _, mine, come = levels[p][level]
        send, stay, next_come = levels[p][level + 1]
        which = {8: Y, 4: Z0, 2: Z1}[n]
        b = half[which]

        def add(to, i, index):
            to[i] = (mine[index].astype(F32) + come[index].astype(F32)).astype(BF16)

        @pl.loop(0, n // 2)
        def _(i):
            add(send, i, 2 * i + 1 - b)

        copy = remote(send, next_come, p, which)
        copy.start()
        pending[p] = [copy]

        @pl.loop(0, n // 2)
        def _(i):
            add(stay, i, 2 * i + b)

    def total(p):
        wait(p)
        _, stay, come = levels[p][-1]
        return stay[0].astype(F32) + come[0].astype(F32)

    outs = {FC2: out_fc2, FC1: out_fc1, FC1_MORE: out_fc1, ATTN: out_attn, ATTN_MORE: out_attn}
    others = {FC2: twos[:2], FC1: twos[2:4], FC1_MORE: twos[2:4], ATTN: twos[4:], ATTN_MORE: twos[4:]}

    def end(p):
        cut = cuts[p][1]
        one = total(p)
        two = sum(ref[0, :, cut].astype(F32) for ref in others[p])
        give, come = last[p]
        give[...] = jnp.where(core == 0, two, one).astype(BF16)
        copy = remote(give, come, p, FINAL)
        copy.start()
        pending[p] = [copy]
        outs[p][core, :, cut] = jnp.where(core == 0, one, two)

    def close(p):
        wait(p)
        outs[p][1 - core, :, cuts[p][1]] = last[p][1][...].astype(F32)

    small = {}

    def small_send(h):
        small_low[...] = small_out[...].astype(BF16)
        small[h] = remote(small_low, small_got.at[h], SMALL, h)
        small[h].start()

    def small_take(h):
        small[h].wait()
        small_out[...] = small_low[...].astype(F32) + small_got[h].astype(F32)

    for p in (ATTN, ATTN_MORE, FC2, FC1, FC1_MORE):
        begin(p)
    db_copies = [pltpu.make_async_copy(ref, db.at[k], db_sem.at[k]) for k, ref in enumerate(db_refs)]
    for c in db_copies:
        c.start()
    row_copies = []
    for k, (device, block) in enumerate(((core_partner, me + 1 - 2 * core), (across, me + 2 - 4 * (me // 2)),
                                         (corner, 3 - me))):
        window = pl.ds(pl.multiple_of(block * ROW_STEP, 16), ROW_WINDOW)
        row_copies.append(remote(row_buf.at[window, :], rows_out.at[k], ROWS, k, device))
    for k in range(2):
        @pl.when(me // 2 == k)
        def _():
            pltpu.make_async_copy(row_refs[k], row_buf, row_sem).start()

    hop(FC2, 2)
    hop(FC1, 4)
    hop(FC1_MORE, 4)
    hop(ATTN, 8)
    hop(ATTN_MORE, 8)
    pltpu.make_async_copy(row_refs[0], row_buf, row_sem).wait()
    for c in row_copies:
        c.start()
    row = 0
    for ref in small_refs:
        small_out[row:row + ref.shape[0], :] = ref[...]
        row += ref.shape[0]
    db_copies[0].wait()
    small_out[row:row + HEAD_ROWS, :] = folded(db.at[0], strips, classes)
    db_copies[1].wait()
    small_out[row + HEAD_ROWS:, :] = folded(db.at[1], strips, classes)
    small_send(CORE)
    end(FC2)
    hop(FC1, 2)
    hop(FC1_MORE, 2)
    small_take(CORE)
    small_send(Y)
    hop(ATTN, 4)
    end(FC1)
    end(FC1_MORE)
    hop(ATTN_MORE, 4)
    hop(ATTN, 2)
    for p in (FC2, FC1, FC1_MORE):
        close(p)
    small_take(Y)
    small_send(Z0)
    hop(ATTN_MORE, 2)
    end(ATTN)
    small_take(Z0)
    small_send(Z1)
    for c in row_copies:
        c.wait()
    end(ATTN_MORE)
    small_take(Z1)
    close(ATTN)
    close(ATTN_MORE)


def last_sums(pairs, two, small, db, rows):
    anywhere = pl.BlockSpec(memory_space=pl.ANY)
    vmem = pl.BlockSpec(memory_space=pltpu.VMEM)
    scratch, cuts, counts = [], [], []
    for k, many in enumerate((1, 2, 2)):
        p = pairs[k][0]
        size = p.shape[2] // many
        for c in range(many):
            n, block = p.shape[0], (p.shape[1], size)
            cuts.append((k, slice(c * size, (c + 1) * size)))
            counts.append(n)
            scratch += [pltpu.VMEM((n,) + block, BF16)] * 2
            while n > 1:
                n //= 2
                scratch += [pltpu.VMEM((n,) + block, BF16)] * 3
            scratch += [pltpu.VMEM(block, BF16)] * 2
    lanes = small[0].shape[1]
    count = sum(v.shape[0] for v in small) + 2 * HEAD_ROWS
    scratch += [pltpu.VMEM((2,) + db[0].shape, F32), pltpu.VMEM((STRIP // 128, PITCH * HEAD_ROWS, 128), F32),
                pltpu.VMEM((HEAD_ROWS, lanes), F32), pltpu.SemaphoreType.DMA((2,)),
                pltpu.VMEM(rows[0].shape, BF16), pltpu.SemaphoreType.DMA, pltpu.VMEM((count, lanes), BF16),
                pltpu.VMEM((4, count, lanes), BF16)]
    scratch += [pltpu.SemaphoreType.DMA((7, 5)), pltpu.SemaphoreType.DMA((7, 5)), pltpu.SemaphoreType.DMA((5, 2))]
    return pl.pallas_call(
        functools.partial(last_sums_kernel, cuts, counts),
        in_specs=[anywhere] * 6 + [vmem] * 10 + [anywhere] * 4,
        out_specs=[vmem] * 5,
        out_shape=[jax.ShapeDtypeStruct((2,) + p.shape[1:], F32) for p, _ in pairs]
        + [jax.ShapeDtypeStruct((count, lanes), F32), jax.ShapeDtypeStruct((3, ROW_WINDOW, lanes), BF16)],
        scratch_shapes=scratch,
        compiler_params=pltpu.CompilerParams(vmem_limit_bytes=60 * 1024 * 1024, collective_id=0, has_side_effects=True),
        cost_estimate=pl.CostEstimate(flops=0, bytes_accessed=300_000_000, transcendentals=0), name="last_sums",
    )(*[v for pair in pairs for v in pair], *two, *small, *db, *rows)


def shards(images, cotangent, image_ids, patch_order, qkv_weight, qv_bias, proj_weight, rel_table, layer_scales,
           layer_norm_gains, norm_biases, fc1_weight, fc1_bias, fc2_weight, out_biases):
    me = lax.axis_index("narrow")
    at_wide = lax.axis_index("wide")
    wide = lax.axis_size("wide")
    core = me % 2
    first = me < 2
    quarter, width = images.shape[1:]
    rows = 4 * quarter
    padded = -(-rows // TILE) * TILE
    entries, heads = rel_table.shape[1:]
    flips = {k: [(d, d ^ k) for d in range(4)] for k in (1, 2, 3)}

    def swap(v, k):
        return lax.ppermute(v, "narrow", flips[k])

    def swap_wide(v, k):
        return lax.ppermute(v, "wide", [(d, d ^ k) for d in range(wide)])

    def pick(v, index):
        return lax.dynamic_index_in_dim(v, index, 0, keepdims=False)

    smalls = jnp.concatenate([layer_norm_gains[0, :1], norm_biases[0, :1], layer_norm_gains[0, 1:], norm_biases[0, 1:],
                              layer_scales[0], out_biases[0], fc1_bias.reshape(-1, width), qv_bias[0],
                              jnp.zeros((2, width), F32)])
    table = jnp.pad(rel_table[0].T, ((0, HEAD_ROWS - heads), (0, width - entries)))
    own_small = jnp.concatenate([smalls, table])
    other_small = swap(own_small, 1)
    own = dict(qkv=qkv_weight[0])
    own["proj"], own["fc1"], own["fc2"] = later([proj_weight[0], fc1_weight[0], fc2_weight[0]], other_small)
    other = {name: swap(own[name], 1) for name in MATRICES}
    bias_at = FC1_BIAS + fc1_bias.shape[1] // width
    both = [jnp.where(core == k, own_small, other_small) for k in range(2)]
    biases = build_bias(jnp.concatenate([v[16:] for v in both]), heads)
    weights = []
    for layer in range(2):
        vectors = both[layer][:16]
        weights.append(dict(
            layer=layer, pick=jnp.stack([(core == layer).astype(jnp.int32), core]), vectors=vectors, bias=biases[layer],
            **{name: (own[name], other[name]) for name in MATRICES}))

    section = dict(
        vectors=jnp.stack([w["vectors"] for w in weights]), bias=[w["bias"] for w in weights],
        own=own, other=other)

    mine = jnp.where(first, images, cotangent)
    theirs = jnp.where(first, cotangent, images)
    pieces = [pick(mine, core), swap(pick(mine, 1 - core), 1), swap(pick(theirs, core), 2),
              swap(pick(theirs, 1 - core), 3)]
    ids, order = later([pick(image_ids, core), pick(patch_order, core)], pieces[2])
    meta = (jnp.stack([core, 1 - first.astype(jnp.int32)]),) + sequence_meta(ids, order, padded)
    rows_in = jnp.zeros((padded, width), BF16)
    for k, piece in enumerate(pieces):
        rows_in = lax.dynamic_update_slice(rows_in, piece, ((me ^ k) * quarter, 0))

    middle, = forward(False, (rows_in, rows_in), section, meta)
    y_out, *parts = forward(True, (rows_in, swap(middle, 2)), section, meta)
    kept = dict(zip(KEPT, parts))

    back = backward(rows_in, section, meta, kept)
    dy_in = jnp.where(first, swap(back, 2), rows_in)

    def reducer(keep, give, at_once=None):
        return Reducer(keep, give, lambda v: swap(v, 1), swap_wide, at_wide, wide, at_once)

    def mlp_part(dy, w, kept_one, after=()):
        dm, da, fc1_give, fc1_keep, fc2_give, fc2_keep, sums = mlp_bwd(True, dy, w, kept_one, after)
        return dm, da, [(fc2_keep, fc2_give), (fc1_keep, fc1_give)], sums

    def tail_part(dm, da, dz, w, kept_one, after=()):
        dx, give, keep, sums = attn_tail(dm, dz, da, w, kept_one, after)
        return dx, keep, give, sums

    def sent(*reducers):
        return [v for r in reducers for v in r.sent]

    def reducers(halves):
        return [reducer(*h, at_once) for h, at_once in zip(halves, swap_sums(halves, wide))]

    dm, da, halves, sums_two = mlp_part(dy_in, weights[1], kept)
    fc_two = [r.launch() for r in reducers(halves)]
    dz, db_two = attn_bwd(da, weights[1], meta, kept, sent(*fc_two))
    mid, *halves, tail_two = tail_part(dm, da, dz, weights[1], kept)
    attn_two = reducers([halves])[0].launch()
    for r in fc_two:
        r.step(mid)
    dm, da, halves, sums_one = mlp_part(mid, weights[0], kept, sent(attn_two, *fc_two))
    fc_one = reducers(halves)
    fc_one[0].launch()
    for r in fc_two + [attn_two]:
        r.step(fc_one[0].sent[0])
    dz, db_one = attn_bwd(da, weights[0], meta, kept, sent(*fc_two, *fc_one, attn_two))
    fc_one[0].step(dz)
    fc_one[1].launch(dz)
    attn_two.step(dz)
    ready = [r.two()[0] for r in fc_one + fc_two + [attn_two]]
    dx, *halves, tail_one = tail_part(dm, da, dz, weights[0], kept, sent(*fc_one, attn_two) + ready)

    if wide == 8:
        pairs = [(ready[0], fc_one[0].parts[-1]), (ready[1], fc_one[1].parts[-1]),
                 [v.reshape(wide, -1, v.shape[1]) for v in halves]]
        two = [v for k, r in enumerate(fc_two + [attn_two]) for v in (ready[2 + k], r.parts[-1])]
        *shares, small, others = last_sums(pairs, two, [sums_two, tail_two, sums_one, tail_one], [db_two, db_one],
                                           [dx, y_out])
        fc2, fc1, attn = [(v[0], v[1]) for v in shares]
        mine = lax.dynamic_slice_in_dim(jnp.where(first, dx, y_out), quarter * me, quarter, 0)
        others = lax.dynamic_slice_in_dim(others, (quarter - ROW_STEP) * me, quarter, 1)
    else:
        result = jnp.where(first, dx, y_out)[:rows].reshape(4, quarter, width)
        mine, others = pick(result, me), [swap(pick(result, me ^ k), k) for k in (1, 2, 3)]
        small = jnp.concatenate([sums_two, tail_two, sums_one, tail_one, table_back(db_two, width),
                                 table_back(db_one, width)])
        small = small + swap(small, 1)
        for k in range(wide.bit_length() - 1):
            small = small + swap_wide(small, 1 << k)
        shares = []
        for one, two in zip(fc_one + [reducer(*halves)], fc_two + [attn_two]):
            one, two = one.finish(), two.finish()
            stay = jnp.where(core == 0, one, two)
            got = swap(jnp.where(core == 0, two, one).astype(BF16), 1).astype(F32)
            shares.append((jnp.where(core == 0, stay, got), jnp.where(core == 0, got, stay)))
        fc2, fc1, attn = shares
    same, across = [mine, others[0]], others[1:]
    same = jnp.where(core == 0, jnp.stack(same), jnp.stack(same[::-1]))
    across = jnp.where(core == 0, jnp.stack(across), jnp.stack(across[::-1]))
    encoded = jnp.where(first, across, same)
    images_grad = jnp.where(first, same, across)
    qkv = jnp.concatenate([v[:, :3 * width // 2] for v in attn], axis=1)
    proj = jnp.concatenate([v[:, 3 * width // 2:] for v in attn], axis=1)
    tables = small[48:].reshape(2, HEAD_ROWS, width)
    totals = jnp.where(core == 0, small[24:48], small[:24])
    table_grad = jnp.where(core == 0, tables[1], tables[0])
    tail = totals[16:]
    return (
        encoded,
        images_grad,
        qkv[None],
        tail[SUM_Q:SUM_V + 1][None],
        proj[None],
        table_grad[:heads, :entries].T[None],
        jnp.stack([totals[SUM_SCALE_A], totals[SUM_SCALE_B]])[None],
        jnp.stack([tail[SUM_GAIN_A], totals[SUM_GAIN_B]])[None],
        jnp.stack([tail[SUM_SHIFT_A], totals[SUM_SHIFT_B]])[None],
        jnp.concatenate(fc1, axis=1)[None],
        totals[FC1_BIAS:bias_at].reshape(1, -1),
        jnp.concatenate(fc2, axis=1)[None],
        jnp.stack([totals[SUM_DA], totals[SUM_DF]])[None],
    )


def solution(mesh):
    by_layer = P("narrow", None, None)
    by_rows = P("wide", "narrow", None)
    by_both = P("narrow", "wide", None)
    in_specs = (by_rows, by_rows, P("wide", None), P("wide", None, None)) + (by_layer,) * 8 + (
        P("narrow", None), by_layer, by_layer)
    out_specs = (by_rows, by_rows, by_both, by_layer, by_both, by_layer, by_layer, by_layer, by_layer, by_both,
                 P("narrow", None), by_both, by_layer)
    return jax.shard_map(shards, mesh=mesh, in_specs=in_specs, out_specs=out_specs, check_vma=False)
```
